32 devices in a mesh: section: 2 (over core), tm: 8 (over z, x), tile: 2 (over y).
Axes of the slice: x: 2, y: 2, z: 4, core: 2. Of those that a mesh axis runs over, the one named last changes fastest.
Arguments:
- features: bfloat16 [16, 16, 64, 256], P('tm', 'tile', None, 'section'), may hold values from -320 to 320
- norm_gain_in: float32 [256], replicated, may hold values from 0.1 to 1.9
- norm_shift_in: float32 [256], replicated, may hold values from -0.8 to 0.8
- conv_in_weight: bfloat16 [3, 3, 3, 256, 128], replicated, may hold values from -0.078125 to 0.078125
- conv_in_bias: float32 [128], replicated, may hold values from -1 to 1
- norm_gain_mid: float32 [128], replicated, may hold values from 0.1 to 1.9
- norm_shift_mid: float32 [128], replicated, may hold values from -0.8 to 0.8
- conv_mid_weight: bfloat16 [3, 3, 3, 128, 128], replicated, may hold values from -0.109375 to 0.109375
- conv_mid_bias: float32 [128], replicated, may hold values from -0.6 to 0.6
- skip_weight: bfloat16 [256, 128], replicated, may hold values from -0.09375 to 0.09375
- skip_bias: float32 [128], replicated, may hold values from -0.6 to 0.6
Outputs:
- block_out: bfloat16 [16, 16, 64, 128], P('tm', 'tile', 'section')
The draws below stay inside these ranges and needn't reach their ends.
All inputs are finite; a program needn't handle non-finite values.
Results may differ from the reference program's by a relative error of at most 0.008.
Values may be sent and summed in bfloat16 or wider, within the bound.
No kernel may reach another device: no remote copies, remote signals or barrier semaphores. Data moves between devices by JAX's collectives and lax.ppermute only.
A program may use at most 64 MiB of HBM per device.

```python
import jax
import jax.numpy as jnp
from jax import lax

CIN = 256
COUT = 128
GROUPS = 32
FR_DEV = 2
ROWS_DEV = 8
FRAMES = 16
ROWS = 16
COLS = 64


log_ten = 2.302585093


two_pi = 6.283185307


def amplitude_profile(key, count):
    key_slope, key_sign, key_phase, key_rough = jax.random.split(key, 4)
    position = jnp.arange(count, dtype=jnp.float32) / max(count - 1, 1)
    slope = jax.random.uniform(key_slope, (), jnp.float32, 0.3, 0.5)
    flip = (2 * jax.random.randint(key_sign, (), 0, 2) - 1).astype(jnp.float32)
    phase = jax.random.uniform(key_phase, (), jnp.float32, 0.0, 1.0)
    rough = jax.random.uniform(key_rough, (count,), jnp.float32, 0.0, 1.0)
    return flip * slope * (position - 0.5) + 0.12 * jnp.sin(two_pi * (1.5 * position + phase)) + 0.12 * rough


def draw_features(key, part):
    keys = jax.random.split(key, 8)
    shape = (FRAMES, ROWS, COLS, CIN)
    noise = jnp.clip(jax.random.normal(keys[0], shape, jnp.float32), -5.0, 5.0)
    offset = jax.random.uniform(keys[1], (CIN,), jnp.float32, -1.0, 1.0)
    time_offset = jax.random.uniform(keys[2], (FRAMES // FR_DEV, CIN), jnp.float32, -0.8, 0.8)
    tile_offset = jax.random.uniform(keys[3], (ROWS // ROWS_DEV, CIN), jnp.float32, -0.5, 0.5)
    time_offset = jnp.repeat(time_offset, FR_DEV, axis=0)
    tile_offset = jnp.repeat(tile_offset, ROWS_DEV, axis=0)
    frame_exp = amplitude_profile(keys[4], FRAMES)
    row_exp = amplitude_profile(keys[5], ROWS)
    col_pos = jnp.arange(COLS, dtype=jnp.float32) / max(COLS - 1, 1)
    rough = jax.random.uniform(keys[6], (FRAMES, ROWS, COLS, 1), jnp.float32)
    chan_pos = jax.random.uniform(keys[7], (CIN,), jnp.float32)
    exponent = frame_exp[:, None, None, None] + row_exp[None, :, None, None] + 0.5 * col_pos[None, None, :, None] + 0.25 * rough
    scale = jnp.exp(log_ten * exponent) * jnp.exp(log_ten * 0.1 * chan_pos)
    shifted = noise + offset + time_offset[:, None, None, :] + tile_offset[None, :, None, :]
    return (scale * shifted).astype(jnp.bfloat16)


def normal_values(rng, extent, scale, most, kind=jnp.bfloat16):
    return jnp.clip(scale * jax.random.normal(rng, extent, jnp.float32), -most, most).astype(kind)


def setup_inputs(seed: int = 0) -> dict:
    seeds = jax.random.split(jax.random.key(seed), 12)
    features = draw_features(jax.random.fold_in(seeds[11], 71), 0)
    norm_gain_in = jnp.clip(1.0 + 0.18 * jax.random.normal(seeds[1], (CIN,), jnp.float32), 0.1, 1.9)
    norm_shift_in = jnp.clip(jax.random.uniform(seeds[2], (CIN,), jnp.float32, -0.8, 0.8), -0.8, 0.8)
    conv_in_weight = normal_values(seeds[3], (3, 3, 3, CIN, COUT), (27 * CIN) ** -0.5, 0.078125)
    conv_in_bias = jnp.clip(jax.random.uniform(seeds[4], (COUT,), jnp.float32, -1.0, 1.0), -1.0, 1.0)
    norm_gain_mid = jnp.clip(1.0 + 0.18 * jax.random.normal(seeds[5], (COUT,), jnp.float32), 0.1, 1.9)
    norm_shift_mid = jnp.clip(jax.random.uniform(seeds[6], (COUT,), jnp.float32, -0.8, 0.8), -0.8, 0.8)
    conv_mid_weight = normal_values(seeds[7], (3, 3, 3, COUT, COUT), (27 * COUT) ** -0.5, 0.109375)
    conv_mid_bias = jnp.clip(jax.random.uniform(seeds[8], (COUT,), jnp.float32, -0.6, 0.6), -0.6, 0.6)
    skip_weight = normal_values(seeds[9], (CIN, COUT), (16 * CIN) ** -0.5, 0.09375)
    skip_bias = jnp.clip(jax.random.uniform(seeds[10], (COUT,), jnp.float32, -0.6, 0.6), -0.6, 0.6)
    return {"features": features, "norm_gain_in": norm_gain_in, "norm_shift_in": norm_shift_in, "conv_in_weight": conv_in_weight, "conv_in_bias": conv_in_bias, "norm_gain_mid": norm_gain_mid, "norm_shift_mid": norm_shift_mid, "conv_mid_weight": conv_mid_weight, "conv_mid_bias": conv_mid_bias, "skip_weight": skip_weight, "skip_bias": skip_bias}


def group_norm_act(values, norm_gain, norm_shift):
    frames, rows, columns, channels = values.shape
    grouped = values.reshape(frames, rows, columns, GROUPS, channels // GROUPS)
    group_mean = lax.optimization_barrier(jnp.mean(grouped, axis=(0, 1, 2, 4), keepdims=True))
    centered = grouped - group_mean
    spread = lax.optimization_barrier(jnp.mean(centered * centered, axis=(0, 1, 2, 4), keepdims=True))
    normed = (centered * lax.rsqrt(spread + 1e-06)).reshape(values.shape)
    return jax.nn.silu(normed * norm_gain + norm_shift).astype(jnp.bfloat16)

def convolve(active, weights, conv_bias):
    padded = jnp.pad(active.astype(jnp.float32), ((2, 0), (1, 1), (1, 1), (0, 0)), mode='edge')
    summed = lax.conv_general_dilated(padded[None], weights.astype(jnp.float32), (1, 1, 1), 'VALID', dimension_numbers=('NDHWC', 'DHWIO', 'NDHWC'), precision=lax.Precision.HIGHEST)
    return summed[0] + conv_bias

def reference(features, norm_gain_in, norm_shift_in, conv_in_weight, conv_in_bias, norm_gain_mid, norm_shift_mid, conv_mid_weight, conv_mid_bias, skip_weight, skip_bias):
    act_in = group_norm_act(features.astype(jnp.float32), norm_gain_in, norm_shift_in)
    hidden = convolve(act_in, conv_in_weight, conv_in_bias).astype(jnp.bfloat16)
    act_mid = group_norm_act(hidden.astype(jnp.float32), norm_gain_mid, norm_shift_mid)
    residual = convolve(act_mid, conv_mid_weight, conv_mid_bias)
    shortcut = jnp.einsum('frck,ko->frco', features.astype(jnp.float32), skip_weight.astype(jnp.float32), precision=lax.Precision.HIGHEST) + skip_bias
    return (residual + shortcut).astype(jnp.bfloat16)
```

```python
import jax
import jax.numpy as jnp
from jax import lax
from jax.sharding import PartitionSpec as P

GROUPS = 32
AXES = ("section", "tm", "tile")


def local_moments(values):
    cells = values.astype(jnp.float32)
    mean = jnp.mean(cells, axis=(0, 1, 2))
    centered = cells - mean
    return jnp.stack([mean, jnp.sum(centered * centered, axis=(0, 1, 2))])


def combine(moments, cells, group_width):
    devices, _, channels = moments.shape
    groups = channels // group_width
    means = moments[:, 0].reshape(devices, groups, group_width)
    spreads = moments[:, 1].reshape(devices, groups, group_width)
    group_mean = jnp.mean(means, axis=(0, 2))
    off = means - group_mean[None, :, None]
    spread = jnp.sum(spreads + cells * off * off, axis=(0, 2)) / (cells * devices * group_width)
    inv = lax.rsqrt(spread + 1e-6)
    return jnp.repeat(group_mean, group_width), jnp.repeat(inv, group_width)


def normalize(values, mean, inv, gain, shift):
    normed = (values.astype(jnp.float32) - mean) * inv * gain + shift
    return jax.nn.silu(normed).astype(jnp.bfloat16)


def convolve(padded, weights):
    frames, rows, columns = (padded.shape[0] - 2, padded.shape[1] - 2, padded.shape[2] - 2)
    channels, outputs = weights.shape[3:]
    summed = jnp.zeros((frames, rows, columns, outputs), jnp.float32)
    for t in range(3):
        for h in range(3):
            slab = padded[t : t + frames, h : h + rows]
            window = jnp.concatenate([slab[:, :, w : w + columns] for w in range(3)], axis=-1)
            summed = summed + jnp.einsum(
                "frck,ko->frco",
                window,
                weights[t, h].reshape(3 * channels, outputs),
                preferred_element_type=jnp.float32,
            )
    return summed


def pairs_for(tm_count, tile_count, tm_step, tile_step):
    out = []
    for a in range(tm_count):
        for b in range(tile_count):
            c, d = a + tm_step, b + tile_step
            if 0 <= c < tm_count and 0 <= d < tile_count:
                out.append((a * tile_count + b, c * tile_count + d))
    return out


def shards(
    features,
    norm_gain_in,
    norm_shift_in,
    conv_in_weight,
    conv_in_bias,
    norm_gain_mid,
    norm_shift_mid,
    conv_mid_weight,
    conv_mid_bias,
    skip_weight,
    skip_bias,
):
    sections, tms, tiles = (lax.axis_size(axis) for axis in AXES)
    devices = sections * tms * tiles
    section, tm, tile = (lax.axis_index(axis) for axis in AXES)
    frames, rows, columns, half = features.shape
    own = columns // sections
    group_in = half * sections // GROUPS

    previous = lax.ppermute(features, ("tm", "tile"), pairs_for(tms, tiles, 1, 0))
    top, bottom = features[:, :2], features[:, -2:]
    up = lax.ppermute(bottom, ("tm", "tile"), pairs_for(tms, tiles, 0, 1))
    down = lax.ppermute(top, ("tm", "tile"), pairs_for(tms, tiles, 0, -1))
    up_prev = lax.ppermute(bottom, ("tm", "tile"), pairs_for(tms, tiles, 1, 1))
    down_prev = lax.ppermute(top, ("tm", "tile"), pairs_for(tms, tiles, 1, -1))

    gathered = lax.all_gather(local_moments(features), AXES)
    gathered = gathered.reshape(sections, tms * tiles, 2, half)
    gathered = jnp.concatenate([gathered[s] for s in range(sections)], axis=-1)
    mean_in, inv_in = combine(gathered, frames * rows * columns, group_in)

    now = jnp.concatenate([up, features, down], axis=1)
    before = jnp.concatenate([up_prev, previous, down_prev], axis=1)
    block = jnp.concatenate([jnp.where(tm == 0, now[:1], before), now], axis=0)
    row_ids = jnp.arange(rows + 4)[None, :, None, None]
    block = jnp.where((tile == 0) & (row_ids < 2), block[:, 2:3], block)
    block = jnp.where((tile == tiles - 1) & (row_ids >= rows + 2), block[:, -3:-2], block)
    left = block[:, :, : own + 2]
    right = block[:, :, own - 2 :]
    got = lax.ppermute(
        jnp.where(section == 0, right, left), "section", [(0, 1), (1, 0)]
    )
    kept = jnp.where(section == 0, left, right)
    whole = jnp.where(
        section == 0,
        jnp.concatenate([kept, got], axis=-1),
        jnp.concatenate([got, kept], axis=-1),
    )
    at_left = jnp.concatenate([whole[:, :, :1], whole[:, :, :1], whole], axis=2)
    at_right = jnp.concatenate([whole, whole[:, :, -1:], whole[:, :, -1:]], axis=2)
    whole = jnp.where(section == 0, at_left, at_right)

    act_in = normalize(whole, mean_in, inv_in, norm_gain_in, norm_shift_in)
    hidden = (convolve(act_in, conv_in_weight) + conv_in_bias).astype(jnp.bfloat16)
    row_ids = jnp.arange(rows + 2)[None, :, None, None]
    col_ids = jnp.arange(own + 2)[None, None, :, None]
    hidden = jnp.where((tile == 0) & (row_ids == 0), hidden[:, 1:2], hidden)
    hidden = jnp.where((tile == tiles - 1) & (row_ids == rows + 1), hidden[:, -2:-1], hidden)
    hidden = jnp.where((section == 0) & (col_ids == 0), hidden[:, :, 1:2], hidden)
    hidden = jnp.where(
        (section == sections - 1) & (col_ids == own + 1), hidden[:, :, -2:-1], hidden
    )
    before = lax.ppermute(hidden, "tm", [(i, i + 1) for i in range(tms - 1)])
    moments = local_moments(hidden[:, 1:-1, 1:-1])
    moments = lax.all_to_all(
        jnp.broadcast_to(moments, (devices, *moments.shape)), AXES, 0, 0, tiled=True
    )
    mean_mid, inv_mid = combine(moments, frames * rows * own, hidden.shape[-1] // GROUPS)
    block = jnp.concatenate([jnp.where(tm == 0, hidden[:1], before), hidden], axis=0)
    act_mid = normalize(block, mean_mid, inv_mid, norm_gain_mid, norm_shift_mid)
    residual = convolve(act_mid, conv_mid_weight) + conv_mid_bias
    shortcut = jnp.einsum(
        "frck,ko->frco",
        whole[frames:, 2:-2, 2:-2],
        skip_weight,
        preferred_element_type=jnp.float32,
    )
    return (residual + (shortcut + skip_bias)).astype(jnp.bfloat16)


def solution(mesh):
    in_specs = (P("tm", "tile", None, "section"),) + (P(),) * 10
    out_specs = P("tm", "tile", "section", None)
    return jax.shard_map(shards, mesh=mesh, in_specs=in_specs, out_specs=out_specs, check_vma=False)
```

```python
import functools

import jax
import jax.numpy as jnp
from jax import lax
from jax.experimental import pallas as pl
from jax.experimental.pallas import tpu as pltpu
from jax.sharding import PartitionSpec as P

GROUPS = 32
AXES = ("section", "tm", "tile")
VMEM_LIMIT = 48 * 1024 * 1024
RIM = 16


def params():
    return pltpu.CompilerParams(vmem_limit_bytes=VMEM_LIMIT)


def vmem_specs(count):
    return [pl.BlockSpec(memory_space=pltpu.VMEM)] * count


def silu(u):
    half = 0.5 * u
    return half + half * jnp.tanh(half)


def moments_of(cells):
    mean = jnp.sum(cells, axis=0, keepdims=True) * (1.0 / cells.shape[0])
    off = cells - mean
    return jnp.concatenate([mean, jnp.sum(off * off, axis=0, keepdims=True)], axis=0)


def group_matrix(channels, width):
    shape = (channels, channels)
    row = lax.broadcasted_iota(jnp.int32, shape, 0) // width
    col = lax.broadcasted_iota(jnp.int32, shape, 1) // width
    return jnp.where(row == col, 1.0, 0.0).astype(jnp.float32)


def group_sum(values, matrix):
    tall = jnp.broadcast_to(values, (8, values.shape[-1]))
    return jnp.dot(
        tall, matrix, preferred_element_type=jnp.float32, precision=lax.Precision.HIGHEST
    )[:1]


def scale_and_offset(moments, cells, width, gain, shift):
    devices, _, channels = moments.shape
    matrix = group_matrix(channels, width)
    means = moments[:, 0, :]
    spreads = moments[:, 1, :]
    mean = group_sum(jnp.sum(means, axis=0, keepdims=True), matrix) * (1.0 / (devices * width))
    off = means - mean
    total = jnp.sum(spreads + float(cells) * (off * off), axis=0, keepdims=True)
    spread = group_sum(total, matrix) * (1.0 / (cells * devices * width))
    scale = lax.rsqrt(spread + 1e-6) * gain
    return mean, scale, shift


def apply_norm(values, norm):
    mean, scale, shift = norm
    return silu((values.astype(jnp.float32) - mean) * scale + shift).astype(jnp.bfloat16)


def first_kernel(x_ref, moments_ref, top_ref, bottom_ref):
    x = x_ref[...]
    cells = x.astype(jnp.float32).reshape(-1, x.shape[-1])
    own = moments_of(cells)
    moments_ref[...] = jnp.broadcast_to(own[None], moments_ref.shape)
    top_ref[...] = x_ref[:, :2]
    bottom_ref[...] = x_ref[:, -2:]


def conv_rows(act_ref, weight_ref, frame, rows, width):
    total = None
    for t in range(3):
        for h in range(3):
            cells = act_ref[frame + t, h : h + rows]
            cells = cells.reshape(rows * width, cells.shape[-1])
            taps = jnp.concatenate([weight_ref[t, h, w] for w in range(3)], axis=-1)
            part = jnp.dot(cells, taps, preferred_element_type=jnp.float32)
            total = part if total is None else total + part
    outputs = weight_ref.shape[-1]
    total = total.reshape(rows, width, 3 * outputs)
    before, middle, after = (total[..., k * outputs : (k + 1) * outputs] for k in range(3))
    before = jnp.concatenate([before[:, :1], before[:, :-1]], axis=1)
    after = jnp.concatenate([after[:, 1:], after[:, -1:]], axis=1)
    return middle + before + after


def middle_kernel(
    tiles,
    x_ref,
    prev_ref,
    up_ref,
    down_ref,
    up_prev_ref,
    down_prev_ref,
    other_x_ref,
    other_prev_ref,
    other_up_ref,
    other_down_ref,
    other_up_prev_ref,
    other_down_prev_ref,
    moments_ref,
    gain_ref,
    shift_ref,
    weight_ref,
    bias_ref,
    hidden_ref,
    out_moments_ref,
    act_ref,
):
    section, tm, tile = (lax.axis_index(axis) for axis in AXES)
    frames, rows, columns, half = x_ref.shape
    width = columns // 2 + RIM
    first = pl.multiple_of(section * (columns - width), RIM)
    cols = pl.ds(first, width)
    per_section = moments_ref.shape[0] // 2
    pieces = (
        (
            section,
            ((x_ref, up_ref, down_ref), (prev_ref, up_prev_ref, down_prev_ref)),
        ),
        (
            1 - section,
            (
                (other_x_ref, other_up_ref, other_down_ref),
                (other_prev_ref, other_up_prev_ref, other_down_prev_ref),
            ),
        ),
    )
    for which, (now, before) in pieces:
        norm = scale_and_offset(
            moments_ref[pl.ds(which * per_section, per_section)],
            frames * rows * columns,
            2 * half // GROUPS,
            gain_ref[pl.ds(which, 1), :],
            shift_ref[pl.ds(which, 1), :],
        )
        lanes = pl.ds(pl.multiple_of(which * half, half), half)
        for start, (body, up, down) in ((frames, now), (0, before)):
            for f in range(frames):
                act_ref[start + f, 2 : 2 + rows, :, lanes] = apply_norm(body[f, :, cols, :], norm)
                act_ref[start + f, 0:2, :, lanes] = apply_norm(up[f, :, cols, :], norm)
                act_ref[start + f, 2 + rows :, :, lanes] = apply_norm(down[f, :, cols, :], norm)

    @pl.when(tile == 0)
    def _():
        for f in range(2 * frames):
            act_ref[f, 1] = act_ref[f, 2]

    @pl.when(tile == tiles - 1)
    def _():
        for f in range(2 * frames):
            act_ref[f, rows + 2] = act_ref[f, rows + 1]

    @pl.when(tm == 0)
    def _():
        for f in range(frames):
            act_ref[f] = act_ref[frames]

    for f in range(frames):
        hidden = conv_rows(act_ref, weight_ref, f, rows + 2, width) + bias_ref[...]
        hidden_ref[f] = hidden.astype(jnp.bfloat16)

    cells = hidden_ref[:, 1 : 1 + rows, pl.ds(first, columns // 2), :]
    cells = cells.astype(jnp.float32).reshape(-1, cells.shape[-1])
    own = moments_of(cells)
    out_moments_ref[...] = jnp.broadcast_to(own[None], out_moments_ref.shape)


def last_kernel(
    tiles,
    hidden_ref,
    before_ref,
    moments_ref,
    gain_ref,
    shift_ref,
    weight_ref,
    bias_ref,
    x_ref,
    other_x_ref,
    skip_ref,
    skip_bias_ref,
    out_ref,
    act_ref,
):
    section, tm, tile = (lax.axis_index(axis) for axis in AXES)
    frames, padded, width, outputs = hidden_ref.shape
    rows = padded - 2
    columns = x_ref.shape[2]
    half = x_ref.shape[3]
    own = columns // 2
    norm = scale_and_offset(
        moments_ref[...],
        frames * rows * own,
        outputs // GROUPS,
        gain_ref[...],
        shift_ref[...],
    )
    for f in range(frames):
        act_ref[f] = apply_norm(before_ref[f], norm)
        act_ref[frames + f] = apply_norm(hidden_ref[f], norm)

    @pl.when(tile == 0)
    def _():
        for f in range(2 * frames):
            act_ref[f, 0] = act_ref[f, 1]

    @pl.when(tile == tiles - 1)
    def _():
        for f in range(2 * frames):
            act_ref[f, rows + 1] = act_ref[f, rows]

    @pl.when(tm == 0)
    def _():
        for f in range(frames):
            act_ref[f] = act_ref[frames]

    mine = pl.ds(pl.multiple_of(section * own, own), own)
    skip_here = skip_ref[pl.ds(pl.multiple_of(section * half, half), half), :]
    skip_there = skip_ref[pl.ds(pl.multiple_of((1 - section) * half, half), half), :]
    for f in range(frames):
        residual = conv_rows(act_ref, weight_ref, f, rows, width)
        residual = jnp.where(section == 0, residual[:, :own], residual[:, width - own :])
        here = x_ref[f, :, mine, :].reshape(rows * own, half)
        there = other_x_ref[f, :, mine, :].reshape(rows * own, half)
        shortcut = jnp.dot(here, skip_here, preferred_element_type=jnp.float32)
        shortcut = shortcut + jnp.dot(there, skip_there, preferred_element_type=jnp.float32)
        total = (residual + bias_ref[...]) + (
            shortcut.reshape(rows, own, outputs) + skip_bias_ref[...]
        )
        out_ref[f] = total.astype(jnp.bfloat16)


def pairs_for(tm_count, tile_count, tm_step, tile_step):
    out = []
    for a in range(tm_count):
        for b in range(tile_count):
            c, d = a + tm_step, b + tile_step
            if 0 <= c < tm_count and 0 <= d < tile_count:
                out.append((a * tile_count + b, c * tile_count + d))
    return out


def to_everyone(moments):
    return lax.all_to_all(moments, AXES, 0, 0, tiled=True)


def shards(
    features,
    norm_gain_in,
    norm_shift_in,
    conv_in_weight,
    conv_in_bias,
    norm_gain_mid,
    norm_shift_mid,
    conv_mid_weight,
    conv_mid_bias,
    skip_weight,
    skip_bias,
):
    sections, tms, tiles = (lax.axis_size(axis) for axis in AXES)
    devices = sections * tms * tiles
    tile = lax.axis_index("tile")
    frames, rows, columns, half = features.shape
    own = columns // sections
    width = own + RIM
    middle = conv_in_weight.shape[-1]
    outputs = conv_mid_weight.shape[-1]
    grid_axes = ("tm", "tile")

    def shift(value, tm_step, tile_step):
        return lax.ppermute(value, grid_axes, pairs_for(tms, tiles, tm_step, tile_step))

    def swap(value):
        return lax.ppermute(value, "section", [(0, 1), (1, 0)])

    previous = shift(features, 1, 0)
    edge = jax.ShapeDtypeStruct((frames, 2, columns, half), features.dtype)
    moments, top, bottom = pl.pallas_call(
        first_kernel,
        out_shape=(jax.ShapeDtypeStruct((devices, 2, half), jnp.float32), edge, edge),
        in_specs=vmem_specs(1),
        out_specs=tuple(vmem_specs(3)),
        compiler_params=params(),
        name="feature_moments",
    )(features)
    if tiles == 2:
        facing = jnp.where(tile == 0, bottom, top)
        up = down = lax.ppermute(facing, "tile", [(0, 1), (1, 0)])
        crossing = [
            (a * 2 + b, (a + 1) * 2 + 1 - b) for a in range(tms - 1) for b in range(2)
        ]
        up_prev = down_prev = lax.ppermute(facing, grid_axes, crossing)
        rims = [up, up_prev]
        other_up, other_up_prev = (swap(rim) for rim in rims)
        other_down, other_down_prev = other_up, other_up_prev
    else:
        up, down = shift(bottom, 0, 1), shift(top, 0, -1)
        up_prev, down_prev = shift(bottom, 1, 1), shift(top, 1, -1)
        other_up, other_down = swap(up), swap(down)
        other_up_prev, other_down_prev = swap(up_prev), swap(down_prev)
    moments = to_everyone(moments)
    other = swap(features)
    other_previous = swap(previous)

    hidden, moments_mid = pl.pallas_call(
        functools.partial(middle_kernel, tiles),
        out_shape=(
            jax.ShapeDtypeStruct((frames, rows + 2, width, middle), jnp.bfloat16),
            jax.ShapeDtypeStruct((devices, 2, middle), jnp.float32),
        ),
        in_specs=vmem_specs(17),
        out_specs=tuple(vmem_specs(2)),
        scratch_shapes=[pltpu.VMEM((2 * frames, rows + 4, width, 2 * half), jnp.bfloat16)],
        compiler_params=params(),
        name="norm_conv_in",
    )(
        features,
        previous,
        up,
        down,
        up_prev,
        down_prev,
        other,
        other_previous,
        other_up,
        other_down,
        other_up_prev,
        other_down_prev,
        moments,
        norm_gain_in.reshape(2, half),
        norm_shift_in.reshape(2, half),
        conv_in_weight,
        conv_in_bias.reshape(1, middle),
    )
    before = shift(hidden, 1, 0)
    moments_mid = to_everyone(moments_mid)
    return pl.pallas_call(
        functools.partial(last_kernel, tiles),
        out_shape=jax.ShapeDtypeStruct((frames, rows, own, outputs), jnp.bfloat16),
        in_specs=vmem_specs(11),
        out_specs=pl.BlockSpec(memory_space=pltpu.VMEM),
        scratch_shapes=[pltpu.VMEM((2 * frames, rows + 2, width, middle), jnp.bfloat16)],
        compiler_params=params(),
        name="norm_conv_mid",
    )(
        hidden,
        before,
        moments_mid,
        norm_gain_mid.reshape(1, middle),
        norm_shift_mid.reshape(1, middle),
        conv_mid_weight,
        conv_mid_bias.reshape(1, outputs),
        features,
        other,
        skip_weight,
        skip_bias.reshape(1, outputs),
    )


def solution(mesh):
    in_specs = (P("tm", "tile", None, "section"),) + (P(),) * 10
    out_specs = P("tm", "tile", "section", None)
    return jax.shard_map(shards, mesh=mesh, in_specs=in_specs, out_specs=out_specs, check_vma=False)
```

```python
import functools

import jax
import jax.numpy as jnp
from jax import lax
from jax.experimental import pallas as pl
from jax.experimental.pallas import tpu as pltpu
from jax.sharding import PartitionSpec as P

GROUPS = 32
AXES = ("section", "tm", "tile")
VMEM_LIMIT = 48 * 1024 * 1024
RIM = 16


def params():
    return pltpu.CompilerParams(vmem_limit_bytes=VMEM_LIMIT)


def cost(flops, moved):
    return pl.CostEstimate(flops=flops, bytes_accessed=moved, transcendentals=0)


def vmem_specs(count):
    return [pl.BlockSpec(memory_space=pltpu.VMEM)] * count


def silu(u):
    half = 0.5 * u
    return half + half * jnp.tanh(half)


def moments_of(cells):
    mean = jnp.sum(cells, axis=0, keepdims=True) * (1.0 / cells.shape[0])
    off = cells - mean
    return jnp.concatenate([mean, jnp.sum(off * off, axis=0, keepdims=True)], axis=0)


def group_matrix(channels, width):
    shape = (channels, channels)
    row = lax.broadcasted_iota(jnp.int32, shape, 0) // width
    col = lax.broadcasted_iota(jnp.int32, shape, 1) // width
    return jnp.where(row == col, 1.0, 0.0).astype(jnp.float32)


def group_sum(values, matrix):
    tall = jnp.broadcast_to(values, (8, values.shape[-1]))
    return jnp.dot(
        tall, matrix, preferred_element_type=jnp.float32, precision=lax.Precision.HIGHEST
    )[:1]


def scale_and_offset(moments, cells, width, gain, shift):
    devices, _, channels = moments.shape
    matrix = group_matrix(channels, width)
    means = moments[:, 0, :]
    spreads = moments[:, 1, :]
    mean = group_sum(jnp.sum(means, axis=0, keepdims=True), matrix) * (1.0 / (devices * width))
    off = means - mean
    total = jnp.sum(spreads + float(cells) * (off * off), axis=0, keepdims=True)
    spread = group_sum(total, matrix) * (1.0 / (cells * devices * width))
    scale = lax.rsqrt(spread + 1e-6) * gain
    return mean, scale, shift


def apply_norm(values, norm):
    mean, scale, shift = norm
    return silu((values.astype(jnp.float32) - mean) * scale + shift).astype(jnp.bfloat16)


def first_kernel(x_ref, moments_ref, top_ref, bottom_ref):
    x = x_ref[...]
    cells = x.astype(jnp.float32).reshape(-1, x.shape[-1])
    own = moments_of(cells)
    moments_ref[...] = jnp.broadcast_to(own[None], moments_ref.shape)
    top_ref[...] = x_ref[:, :2]
    bottom_ref[...] = x_ref[:, -2:]


def conv_rows(act_ref, weight_ref, frame, rows, width):
    total = None
    for t in range(3):
        for h in range(3):
            cells = act_ref[frame + t, h : h + rows]
            cells = cells.reshape(rows * width, cells.shape[-1])
            taps = jnp.concatenate([weight_ref[t, h, w] for w in range(3)], axis=-1)
            part = jnp.dot(cells, taps, preferred_element_type=jnp.float32)
            total = part if total is None else total + part
    outputs = weight_ref.shape[-1]
    total = total.reshape(rows, width, 3 * outputs)
    before, middle, after = (total[..., k * outputs : (k + 1) * outputs] for k in range(3))
    before = jnp.concatenate([before[:, :1], before[:, :-1]], axis=1)
    after = jnp.concatenate([after[:, 1:], after[:, -1:]], axis=1)
    return middle + before + after


def middle_kernel(
    tiles,
    x_ref,
    prev_ref,
    up_ref,
    down_ref,
    up_prev_ref,
    down_prev_ref,
    other_x_ref,
    other_prev_ref,
    other_up_ref,
    other_down_ref,
    other_up_prev_ref,
    other_down_prev_ref,
    moments_ref,
    vectors_ref,
    weight_ref,
    hidden_ref,
    out_moments_ref,
    act_ref,
):
    section, tm, tile = (lax.axis_index(axis) for axis in AXES)
    frames, rows, columns, half = x_ref.shape
    width = columns // 2 + RIM
    first = pl.multiple_of(section * (columns - width), RIM)
    cols = pl.ds(first, width)
    per_section = moments_ref.shape[0] // 2
    pieces = (
        (
            section,
            ((x_ref, up_ref, down_ref), (prev_ref, up_prev_ref, down_prev_ref)),
        ),
        (
            1 - section,
            (
                (other_x_ref, other_up_ref, other_down_ref),
                (other_prev_ref, other_up_prev_ref, other_down_prev_ref),
            ),
        ),
    )
    for which, (now, before) in pieces:
        norm = scale_and_offset(
            moments_ref[pl.ds(which * per_section, per_section)],
            frames * rows * columns,
            2 * half // GROUPS,
            vectors_ref[pl.ds(which, 1), :],
            vectors_ref[pl.ds(2 + which, 1), :],
        )
        lanes = pl.ds(pl.multiple_of(which * half, half), half)
        for start, (body, up, down) in ((frames, now), (0, before)):
            for f in range(frames):
                act_ref[start + f, 2 : 2 + rows, :, lanes] = apply_norm(body[f, :, cols, :], norm)
                act_ref[start + f, 0:2, :, lanes] = apply_norm(up[f, :, cols, :], norm)
                act_ref[start + f, 2 + rows :, :, lanes] = apply_norm(down[f, :, cols, :], norm)

    @pl.when(tile == 0)
    def _():
        for f in range(2 * frames):
            act_ref[f, 1] = act_ref[f, 2]

    @pl.when(tile == tiles - 1)
    def _():
        for f in range(2 * frames):
            act_ref[f, rows + 2] = act_ref[f, rows + 1]

    @pl.when(tm == 0)
    def _():
        for f in range(frames):
            act_ref[f] = act_ref[frames]

    for f in range(frames):
        hidden = conv_rows(act_ref, weight_ref, f, rows + 2, width) + vectors_ref[4:5]
        hidden_ref[f] = hidden.astype(jnp.bfloat16)

    cells = hidden_ref[:, 1 : 1 + rows, pl.ds(first, columns // 2), :]
    cells = cells.astype(jnp.float32).reshape(-1, cells.shape[-1])
    own = moments_of(cells)
    out_moments_ref[...] = jnp.broadcast_to(own[None], out_moments_ref.shape)


def last_kernel(
    tiles,
    hidden_ref,
    before_ref,
    moments_ref,
    vectors_ref,
    weight_ref,
    x_ref,
    other_x_ref,
    skip_ref,
    out_ref,
    act_ref,
):
    section, tm, tile = (lax.axis_index(axis) for axis in AXES)
    frames, padded, width, outputs = hidden_ref.shape
    rows = padded - 2
    columns = x_ref.shape[2]
    half = x_ref.shape[3]
    own = columns // 2
    norm = scale_and_offset(
        moments_ref[...],
        frames * rows * own,
        outputs // GROUPS,
        vectors_ref[5:6],
        vectors_ref[6:7],
    )
    for f in range(frames):
        act_ref[f] = apply_norm(before_ref[f], norm)
        act_ref[frames + f] = apply_norm(hidden_ref[f], norm)

    @pl.when(tile == 0)
    def _():
        for f in range(2 * frames):
            act_ref[f, 0] = act_ref[f, 1]

    @pl.when(tile == tiles - 1)
    def _():
        for f in range(2 * frames):
            act_ref[f, rows + 1] = act_ref[f, rows]

    @pl.when(tm == 0)
    def _():
        for f in range(frames):
            act_ref[f] = act_ref[frames]

    mine = pl.ds(pl.multiple_of(section * own, own), own)
    skip_here = skip_ref[pl.ds(pl.multiple_of(section * half, half), half), :]
    skip_there = skip_ref[pl.ds(pl.multiple_of((1 - section) * half, half), half), :]
    for f in range(frames):
        residual = conv_rows(act_ref, weight_ref, f, rows, width)
        residual = jnp.where(section == 0, residual[:, :own], residual[:, width - own :])
        here = x_ref[f, :, mine, :].reshape(rows * own, half)
        there = other_x_ref[f, :, mine, :].reshape(rows * own, half)
        shortcut = jnp.dot(here, skip_here, preferred_element_type=jnp.float32)
        shortcut = shortcut + jnp.dot(there, skip_there, preferred_element_type=jnp.float32)
        total = (residual + vectors_ref[7:8]) + (
            shortcut.reshape(rows, own, outputs) + vectors_ref[8:9]
        )
        out_ref[f] = total.astype(jnp.bfloat16)


def pairs_for(tm_count, tile_count, tm_step, tile_step):
    out = []
    for a in range(tm_count):
        for b in range(tile_count):
            c, d = a + tm_step, b + tile_step
            if 0 <= c < tm_count and 0 <= d < tile_count:
                out.append((a * tile_count + b, c * tile_count + d))
    return out


def to_everyone(moments):
    return lax.all_to_all(moments, AXES, 0, 0, tiled=True)


def shards(
    features,
    norm_gain_in,
    norm_shift_in,
    conv_in_weight,
    conv_in_bias,
    norm_gain_mid,
    norm_shift_mid,
    conv_mid_weight,
    conv_mid_bias,
    skip_weight,
    skip_bias,
):
    sections, tms, tiles = (lax.axis_size(axis) for axis in AXES)
    devices = sections * tms * tiles
    tile = lax.axis_index("tile")
    frames, rows, columns, half = features.shape
    own = columns // sections
    width = own + RIM
    middle = conv_in_weight.shape[-1]
    outputs = conv_mid_weight.shape[-1]
    grid_axes = ("tm", "tile")

    def shift(value, tm_step, tile_step):
        return lax.ppermute(value, grid_axes, pairs_for(tms, tiles, tm_step, tile_step))

    def swap(value):
        return lax.ppermute(value, "section", [(0, 1), (1, 0)])

    previous = shift(features, 1, 0)
    edge = jax.ShapeDtypeStruct((frames, 2, columns, half), features.dtype)
    moments, top, bottom = pl.pallas_call(
        first_kernel,
        out_shape=(jax.ShapeDtypeStruct((devices, 2, half), jnp.float32), edge, edge),
        in_specs=vmem_specs(1),
        out_specs=tuple(vmem_specs(3)),
        compiler_params=params(),
        cost_estimate=cost(1_000_000_000, 1_000_000),
        name="feature_moments",
    )(features)
    vectors = jnp.concatenate(
        [
            norm_gain_in,
            norm_shift_in,
            conv_in_bias,
            norm_gain_mid,
            norm_shift_mid,
            conv_mid_bias,
            skip_bias,
        ]
    ).reshape(-1, half)
    if tiles == 2:
        facing = jnp.where(tile == 0, bottom, top)
        crossing = [
            (a * 2 + b, (a + 1) * 2 + 1 - b) for a in range(tms - 1) for b in range(2)
        ]
        rims = [
            lax.ppermute(facing, "tile", [(0, 1), (1, 0)]),
            lax.ppermute(facing, grid_axes, crossing),
        ]
    else:
        rims = [
            shift(bottom, 0, 1),
            shift(bottom, 1, 1),
            shift(top, 0, -1),
            shift(top, 1, -1),
        ]
    other = swap(features)
    moments = to_everyone(moments)
    previous, moments, *rims = lax.optimization_barrier((previous, moments, *rims))
    other_previous = swap(previous)
    other_rims = [swap(rim) for rim in rims]
    up, up_prev, down, down_prev = (rims * 2)[:4]
    other_up, other_up_prev, other_down, other_down_prev = (other_rims * 2)[:4]

    hidden, moments_mid = pl.pallas_call(
        functools.partial(middle_kernel, tiles),
        out_shape=(
            jax.ShapeDtypeStruct((frames, rows + 2, width, middle), jnp.bfloat16),
            jax.ShapeDtypeStruct((devices, 2, middle), jnp.float32),
        ),
        in_specs=vmem_specs(15),
        out_specs=tuple(vmem_specs(2)),
        scratch_shapes=[pltpu.VMEM((2 * frames, rows + 4, width, 2 * half), jnp.bfloat16)],
        compiler_params=params(),
        name="norm_conv_in",
    )(
        features,
        previous,
        up,
        down,
        up_prev,
        down_prev,
        other,
        other_previous,
        other_up,
        other_down,
        other_up_prev,
        other_down_prev,
        moments,
        vectors,
        conv_in_weight,
    )
    before = shift(hidden, 1, 0)
    moments_mid = to_everyone(moments_mid)
    return pl.pallas_call(
        functools.partial(last_kernel, tiles),
        out_shape=jax.ShapeDtypeStruct((frames, rows, own, outputs), jnp.bfloat16),
        in_specs=vmem_specs(8),
        out_specs=pl.BlockSpec(memory_space=pltpu.VMEM),
        scratch_shapes=[pltpu.VMEM((2 * frames, rows + 2, width, middle), jnp.bfloat16)],
        compiler_params=params(),
        name="norm_conv_mid",
    )(
        hidden,
        before,
        moments_mid,
        vectors,
        conv_mid_weight,
        features,
        other,
        skip_weight,
    )


def solution(mesh):
    in_specs = (P("tm", "tile", None, "section"),) + (P(),) * 10
    out_specs = P("tm", "tile", "section", None)
    return jax.shard_map(shards, mesh=mesh, in_specs=in_specs, out_specs=out_specs, check_vma=False)
```

```python
import functools

import jax
import jax.numpy as jnp
from jax import lax
from jax.experimental import pallas as pl
from jax.experimental.pallas import tpu as pltpu
from jax.sharding import PartitionSpec as P

GROUPS = 32
AXES = ("section", "tm", "tile")
VMEM_LIMIT = 48 * 1024 * 1024
RIM = 16


def params():
    return pltpu.CompilerParams(vmem_limit_bytes=VMEM_LIMIT)


def cost(flops, moved):
    return pl.CostEstimate(flops=flops, bytes_accessed=moved, transcendentals=0)


def vmem_specs(count):
    return [pl.BlockSpec(memory_space=pltpu.VMEM)] * count


def silu(u):
    half = 0.5 * u
    return half + half * jnp.tanh(half)


def moments_of(cells):
    mean = jnp.sum(cells, axis=0, keepdims=True) * (1.0 / cells.shape[0])
    off = cells - mean
    return jnp.concatenate([mean, jnp.sum(off * off, axis=0, keepdims=True)], axis=0)


def group_matrix(channels, width):
    shape = (channels, channels)
    row = lax.broadcasted_iota(jnp.int32, shape, 0) // width
    col = lax.broadcasted_iota(jnp.int32, shape, 1) // width
    return jnp.where(row == col, 1.0, 0.0).astype(jnp.float32)


def group_sum(values, matrix):
    tall = jnp.broadcast_to(values, (8, values.shape[-1]))
    return jnp.dot(
        tall, matrix, preferred_element_type=jnp.float32, precision=lax.Precision.HIGHEST
    )[:1]


def scale_and_offset(moments, cells, width, gain, shift):
    devices, _, channels = moments.shape
    matrix = group_matrix(channels, width)
    means = moments[:, 0, :]
    spreads = moments[:, 1, :]
    mean = group_sum(jnp.sum(means, axis=0, keepdims=True), matrix) * (1.0 / (devices * width))
    off = means - mean
    total = jnp.sum(spreads + float(cells) * (off * off), axis=0, keepdims=True)
    spread = group_sum(total, matrix) * (1.0 / (cells * devices * width))
    scale = lax.rsqrt(spread + 1e-6) * gain
    return mean, scale, shift


def apply_norm(values, norm):
    mean, scale, shift = norm
    return silu((values.astype(jnp.float32) - mean) * scale + shift).astype(jnp.bfloat16)


def first_kernel(pairs, x_ref, moments_ref, *edge_refs):
    x = x_ref[...]
    cells = x.astype(jnp.float32).reshape(-1, x.shape[-1])
    own = moments_of(cells)
    moments_ref[...] = jnp.broadcast_to(own[None], moments_ref.shape)
    rows = x_ref.shape[1]
    if pairs:
        first = (rows - 2) * (1 - lax.axis_index("tile"))
        edge_refs[0][...] = x_ref[:, pl.ds(first, 2)]
    else:
        edge_refs[0][...] = x_ref[:, :2]
        edge_refs[1][...] = x_ref[:, -2:]


def conv_rows(act_ref, weight_ref, frame, rows, width):
    total = None
    for t in range(3):
        for h in range(3):
            cells = act_ref[frame + t, h : h + rows]
            cells = cells.reshape(rows * width, cells.shape[-1])
            taps = jnp.concatenate([weight_ref[t, h, w] for w in range(3)], axis=-1)
            part = jnp.dot(cells, taps, preferred_element_type=jnp.float32)
            total = part if total is None else total + part
    outputs = weight_ref.shape[-1]
    total = total.reshape(rows, width, 3 * outputs)
    before, middle, after = (total[..., k * outputs : (k + 1) * outputs] for k in range(3))
    before = jnp.concatenate([before[:, :1], before[:, :-1]], axis=1)
    after = jnp.concatenate([after[:, 1:], after[:, -1:]], axis=1)
    return middle + before + after


def middle_kernel(
    tiles,
    x_ref,
    prev_ref,
    up_ref,
    down_ref,
    up_prev_ref,
    down_prev_ref,
    other_x_ref,
    other_prev_ref,
    other_up_ref,
    other_down_ref,
    other_up_prev_ref,
    other_down_prev_ref,
    moments_ref,
    gain_ref,
    shift_ref,
    weight_ref,
    bias_ref,
    hidden_ref,
    out_moments_ref,
    act_ref,
):
    section, tm, tile = (lax.axis_index(axis) for axis in AXES)
    frames, rows, columns, half = x_ref.shape
    width = columns // 2 + RIM
    first = pl.multiple_of(section * (columns - width), RIM)
    cols = pl.ds(first, width)
    per_section = moments_ref.shape[0] // 2
    pieces = (
        (
            section,
            ((x_ref, up_ref, down_ref), (prev_ref, up_prev_ref, down_prev_ref)),
        ),
        (
            1 - section,
            (
                (other_x_ref, other_up_ref, other_down_ref),
                (other_prev_ref, other_up_prev_ref, other_down_prev_ref),
            ),
        ),
    )
    for which, (now, before) in pieces:
        norm = scale_and_offset(
            moments_ref[pl.ds(which * per_section, per_section)],
            frames * rows * columns,
            2 * half // GROUPS,
            gain_ref[pl.ds(which, 1), :],
            shift_ref[pl.ds(which, 1), :],
        )
        lanes = pl.ds(pl.multiple_of(which * half, half), half)
        for start, (body, up, down) in ((frames, now), (0, before)):
            for f in range(frames):
                act_ref[start + f, 2 : 2 + rows, :, lanes] = apply_norm(body[f, :, cols, :], norm)
                act_ref[start + f, 0:2, :, lanes] = apply_norm(up[f, :, cols, :], norm)
                act_ref[start + f, 2 + rows :, :, lanes] = apply_norm(down[f, :, cols, :], norm)

    @pl.when(tile == 0)
    def _():
        for f in range(2 * frames):
            act_ref[f, 1] = act_ref[f, 2]

    @pl.when(tile == tiles - 1)
    def _():
        for f in range(2 * frames):
            act_ref[f, rows + 2] = act_ref[f, rows + 1]

    @pl.when(tm == 0)
    def _():
        for f in range(frames):
            act_ref[f] = act_ref[frames]

    for f in range(frames):
        hidden = conv_rows(act_ref, weight_ref, f, rows + 2, width) + bias_ref[...]
        hidden_ref[f] = hidden.astype(jnp.bfloat16)

    cells = hidden_ref[:, 1 : 1 + rows, pl.ds(first, columns // 2), :]
    cells = cells.astype(jnp.float32).reshape(-1, cells.shape[-1])
    own = moments_of(cells)
    out_moments_ref[...] = jnp.broadcast_to(own[None], out_moments_ref.shape)


def last_kernel(
    tiles,
    hidden_ref,
    before_ref,
    moments_ref,
    gain_ref,
    shift_ref,
    weight_ref,
    bias_ref,
    x_ref,
    other_x_ref,
    skip_ref,
    skip_bias_ref,
    out_ref,
    act_ref,
):
    section, tm, tile = (lax.axis_index(axis) for axis in AXES)
    frames, padded, width, outputs = hidden_ref.shape
    rows = padded - 2
    columns = x_ref.shape[2]
    half = x_ref.shape[3]
    own = columns // 2
    norm = scale_and_offset(
        moments_ref[...],
        frames * rows * own,
        outputs // GROUPS,
        gain_ref[...],
        shift_ref[...],
    )
    for f in range(frames):
        act_ref[f] = apply_norm(before_ref[f], norm)
        act_ref[frames + f] = apply_norm(hidden_ref[f], norm)

    @pl.when(tile == 0)
    def _():
        for f in range(2 * frames):
            act_ref[f, 0] = act_ref[f, 1]

    @pl.when(tile == tiles - 1)
    def _():
        for f in range(2 * frames):
            act_ref[f, rows + 1] = act_ref[f, rows]

    @pl.when(tm == 0)
    def _():
        for f in range(frames):
            act_ref[f] = act_ref[frames]

    mine = pl.ds(pl.multiple_of(section * own, own), own)
    skip_here = skip_ref[pl.ds(pl.multiple_of(section * half, half), half), :]
    skip_there = skip_ref[pl.ds(pl.multiple_of((1 - section) * half, half), half), :]
    for f in range(frames):
        residual = conv_rows(act_ref, weight_ref, f, rows, width)
        residual = jnp.where(section == 0, residual[:, :own], residual[:, width - own :])
        here = x_ref[f, :, mine, :].reshape(rows * own, half)
        there = other_x_ref[f, :, mine, :].reshape(rows * own, half)
        shortcut = jnp.dot(here, skip_here, preferred_element_type=jnp.float32)
        shortcut = shortcut + jnp.dot(there, skip_there, preferred_element_type=jnp.float32)
        total = (residual + bias_ref[...]) + (
            shortcut.reshape(rows, own, outputs) + skip_bias_ref[...]
        )
        out_ref[f] = total.astype(jnp.bfloat16)


def pairs_for(tm_count, tile_count, tm_step, tile_step):
    out = []
    for a in range(tm_count):
        for b in range(tile_count):
            c, d = a + tm_step, b + tile_step
            if 0 <= c < tm_count and 0 <= d < tile_count:
                out.append((a * tile_count + b, c * tile_count + d))
    return out


def to_everyone(moments):
    return lax.all_to_all(moments, AXES, 0, 0, tiled=True)


def shards(
    features,
    norm_gain_in,
    norm_shift_in,
    conv_in_weight,
    conv_in_bias,
    norm_gain_mid,
    norm_shift_mid,
    conv_mid_weight,
    conv_mid_bias,
    skip_weight,
    skip_bias,
):
    sections, tms, tiles = (lax.axis_size(axis) for axis in AXES)
    devices = sections * tms * tiles
    frames, rows, columns, half = features.shape
    own = columns // sections
    width = own + RIM
    middle = conv_in_weight.shape[-1]
    outputs = conv_mid_weight.shape[-1]
    grid_axes = ("tm", "tile")

    def shift(value, tm_step, tile_step):
        return lax.ppermute(value, grid_axes, pairs_for(tms, tiles, tm_step, tile_step))

    def swap(value):
        return lax.ppermute(value, "section", [(0, 1), (1, 0)])

    previous = shift(features, 1, 0)
    edge = jax.ShapeDtypeStruct((frames, 2, columns, half), features.dtype)
    edges = 1 if tiles == 2 else 2
    moments, *edge_rows = pl.pallas_call(
        functools.partial(first_kernel, tiles == 2),
        out_shape=(jax.ShapeDtypeStruct((devices, 2, half), jnp.float32),) + (edge,) * edges,
        in_specs=vmem_specs(1),
        out_specs=tuple(vmem_specs(1 + edges)),
        compiler_params=params(),
        cost_estimate=cost(1_000_000_000, 1_000_000),
        name="feature_moments",
    )(features)
    if tiles == 2:
        (facing,) = edge_rows
        crossing = [
            (a * 2 + b, (a + 1) * 2 + 1 - b) for a in range(tms - 1) for b in range(2)
        ]
        rims = [
            lax.ppermute(facing, "tile", [(0, 1), (1, 0)]),
            lax.ppermute(facing, grid_axes, crossing),
        ]
    else:
        top, bottom = edge_rows
        rims = [
            shift(bottom, 0, 1),
            shift(bottom, 1, 1),
            shift(top, 0, -1),
            shift(top, 1, -1),
        ]
    other = swap(features)
    moments = to_everyone(moments)
    previous, moments, *rims = lax.optimization_barrier((previous, moments, *rims))
    other_previous = swap(previous)
    other_rims = [swap(rim) for rim in rims]
    up, up_prev, down, down_prev = (rims * 2)[:4]
    other_up, other_up_prev, other_down, other_down_prev = (other_rims * 2)[:4]

    hidden, moments_mid = pl.pallas_call(
        functools.partial(middle_kernel, tiles),
        out_shape=(
            jax.ShapeDtypeStruct((frames, rows + 2, width, middle), jnp.bfloat16),
            jax.ShapeDtypeStruct((devices, 2, middle), jnp.float32),
        ),
        in_specs=vmem_specs(17),
        out_specs=tuple(vmem_specs(2)),
        scratch_shapes=[pltpu.VMEM((2 * frames, rows + 4, width, 2 * half), jnp.bfloat16)],
        compiler_params=params(),
        name="norm_conv_in",
    )(
        features,
        previous,
        up,
        down,
        up_prev,
        down_prev,
        other,
        other_previous,
        other_up,
        other_down,
        other_up_prev,
        other_down_prev,
        moments,
        norm_gain_in.reshape(2, half),
        norm_shift_in.reshape(2, half),
        conv_in_weight,
        conv_in_bias.reshape(1, middle),
    )
    before = shift(hidden, 1, 0)
    moments_mid = to_everyone(moments_mid)
    return pl.pallas_call(
        functools.partial(last_kernel, tiles),
        out_shape=jax.ShapeDtypeStruct((frames, rows, own, outputs), jnp.bfloat16),
        in_specs=vmem_specs(11),
        out_specs=pl.BlockSpec(memory_space=pltpu.VMEM),
        scratch_shapes=[pltpu.VMEM((2 * frames, rows + 2, width, middle), jnp.bfloat16)],
        compiler_params=params(),
        name="norm_conv_mid",
    )(
        hidden,
        before,
        moments_mid,
        norm_gain_mid.reshape(1, middle),
        norm_shift_mid.reshape(1, middle),
        conv_mid_weight,
        conv_mid_bias.reshape(1, outputs),
        features,
        other,
        skip_weight,
        skip_bias.reshape(1, outputs),
    )


def solution(mesh):
    in_specs = (P("tm", "tile", None, "section"),) + (P(),) * 10
    out_specs = P("tm", "tile", "section", None)
    return jax.shard_map(shards, mesh=mesh, in_specs=in_specs, out_specs=out_specs, check_vma=False)
```

```python
import functools

import jax
import jax.numpy as jnp
from jax import lax
from jax.experimental import pallas as pl
from jax.experimental.pallas import tpu as pltpu
from jax.sharding import PartitionSpec as P

GROUPS = 32
AXES = ("section", "tm", "tile")
VMEM_LIMIT = 48 * 1024 * 1024
RIM = 16


def params():
    return pltpu.CompilerParams(vmem_limit_bytes=VMEM_LIMIT)


def cost(flops, moved):
    return pl.CostEstimate(flops=flops, bytes_accessed=moved, transcendentals=0)


def vmem_specs(count):
    return [pl.BlockSpec(memory_space=pltpu.VMEM)] * count


def silu(u):
    half = 0.5 * u
    return half + half * jnp.tanh(half)


def moments_of(cells):
    mean = jnp.sum(cells, axis=0, keepdims=True) * (1.0 / cells.shape[0])
    off = cells - mean
    return jnp.concatenate([mean, jnp.sum(off * off, axis=0, keepdims=True)], axis=0)


def group_matrix(channels, width):
    shape = (channels, channels)
    row = lax.broadcasted_iota(jnp.int32, shape, 0) // width
    col = lax.broadcasted_iota(jnp.int32, shape, 1) // width
    return jnp.where(row == col, 1.0, 0.0).astype(jnp.float32)


def group_sum(values, matrix):
    tall = jnp.broadcast_to(values, (8, values.shape[-1]))
    return jnp.dot(
        tall, matrix, preferred_element_type=jnp.float32, precision=lax.Precision.HIGHEST
    )[:1]


def scale_and_offset(refs, cells, width, gain, shift):
    channels = refs[0].shape[-1]
    devices = sum(ref.shape[0] for ref in refs)
    matrix = group_matrix(channels, width)
    moments = [ref[...] for ref in refs]
    summed = sum(jnp.sum(part[:, 0, :], axis=0, keepdims=True) for part in moments)
    mean = group_sum(summed, matrix) * (1.0 / (devices * width))
    total = 0.0
    for part in moments:
        off = part[:, 0, :] - mean
        total = total + jnp.sum(
            part[:, 1, :] + float(cells) * (off * off), axis=0, keepdims=True
        )
    spread = group_sum(total, matrix) * (1.0 / (cells * devices * width))
    scale = lax.rsqrt(spread + 1e-6) * gain
    return mean, scale, shift


def apply_norm(values, norm):
    mean, scale, shift = norm
    return silu((values.astype(jnp.float32) - mean) * scale + shift).astype(jnp.bfloat16)


def first_kernel(pairs, x_ref, moments_ref, *edge_refs):
    x = x_ref[...]
    cells = x.astype(jnp.float32).reshape(-1, x.shape[-1])
    own = moments_of(cells)
    moments_ref[...] = jnp.broadcast_to(own[None], moments_ref.shape)
    rows = x_ref.shape[1]
    if pairs:
        first = (rows - 2) * (1 - lax.axis_index("tile"))
        edge_refs[0][...] = x_ref[:, pl.ds(first, 2)]
    else:
        edge_refs[0][...] = x_ref[:, :2]
        edge_refs[1][...] = x_ref[:, -2:]


def conv_rows(act_ref, weight_ref, frame, rows, width):
    total = None
    for t in range(3):
        for h in range(3):
            cells = act_ref[frame + t, h : h + rows]
            cells = cells.reshape(rows * width, cells.shape[-1])
            taps = jnp.concatenate([weight_ref[t, h, w] for w in range(3)], axis=-1)
            part = jnp.dot(cells, taps, preferred_element_type=jnp.float32)
            total = part if total is None else total + part
    outputs = weight_ref.shape[-1]
    total = total.reshape(rows, width, 3 * outputs)
    before, middle, after = (total[..., k * outputs : (k + 1) * outputs] for k in range(3))
    before = jnp.concatenate([before[:, :1], before[:, :-1]], axis=1)
    after = jnp.concatenate([after[:, 1:], after[:, -1:]], axis=1)
    return middle + before + after


def middle_kernel(
    tiles,
    x_ref,
    prev_ref,
    up_ref,
    down_ref,
    up_prev_ref,
    down_prev_ref,
    other_x_ref,
    other_prev_ref,
    other_up_ref,
    other_down_ref,
    other_up_prev_ref,
    other_down_prev_ref,
    moments_ref,
    other_moments_ref,
    gain_ref,
    shift_ref,
    weight_ref,
    bias_ref,
    hidden_ref,
    sent_ref,
    out_moments_ref,
    act_ref,
):
    section, tm, tile = (lax.axis_index(axis) for axis in AXES)
    frames, rows, columns, half = x_ref.shape
    width = columns // 2 + RIM
    first = pl.multiple_of(section * (columns - width), RIM)
    cols = pl.ds(first, width)
    pieces = (
        (
            section,
            moments_ref,
            ((x_ref, up_ref, down_ref), (prev_ref, up_prev_ref, down_prev_ref)),
        ),
        (
            1 - section,
            other_moments_ref,
            (
                (other_x_ref, other_up_ref, other_down_ref),
                (other_prev_ref, other_up_prev_ref, other_down_prev_ref),
            ),
        ),
    )
    for which, moments, (now, before) in pieces:
        norm = scale_and_offset(
            [moments],
            frames * rows * columns,
            2 * half // GROUPS,
            gain_ref[pl.ds(which, 1), :],
            shift_ref[pl.ds(which, 1), :],
        )
        lanes = pl.ds(pl.multiple_of(which * half, half), half)
        for start, (body, up, down) in ((frames, now), (0, before)):
            for f in range(frames):
                act_ref[start + f, 2 : 2 + rows, :, lanes] = apply_norm(body[f, :, cols, :], norm)
                act_ref[start + f, 0:2, :, lanes] = apply_norm(up[f, :, cols, :], norm)
                act_ref[start + f, 2 + rows :, :, lanes] = apply_norm(down[f, :, cols, :], norm)

    @pl.when(tile == 0)
    def _():
        for f in range(2 * frames):
            act_ref[f, 1] = act_ref[f, 2]

    @pl.when(tile == tiles - 1)
    def _():
        for f in range(2 * frames):
            act_ref[f, rows + 2] = act_ref[f, rows + 1]

    @pl.when(tm == 0)
    def _():
        for f in range(frames):
            act_ref[f] = act_ref[frames]

    own = columns // 2
    sent_rows = sent_ref.shape[1] - 1
    top = sent_start(tiles, tile)
    for f in range(frames):
        hidden = conv_rows(act_ref, weight_ref, f, rows + 2, width) + bias_ref[...]
        hidden_ref[f] = hidden.astype(jnp.bfloat16)
        sent_ref[f, :sent_rows] = hidden_ref[f, pl.ds(top, sent_rows), pl.ds(first, own), :]
        rim = jnp.where(section == 0, hidden[:, own, :], hidden[:, width - own - 1, :])
        spare = jnp.zeros((own - rim.shape[0], rim.shape[1]), jnp.float32)
        sent_ref[f, sent_rows] = jnp.concatenate([rim, spare], axis=0).astype(jnp.bfloat16)

    cells = hidden_ref[:, 1 : 1 + rows, pl.ds(first, own), :]
    cells = cells.astype(jnp.float32).reshape(-1, cells.shape[-1])
    out_moments_ref[...] = jnp.broadcast_to(moments_of(cells)[None], out_moments_ref.shape)


def sent_start(tiles, tile):
    return 1 - tile if tiles == 2 else 0


def last_kernel(
    tiles,
    hidden_ref,
    before_ref,
    moments_ref,
    other_moments_ref,
    gain_ref,
    shift_ref,
    weight_ref,
    bias_ref,
    x_ref,
    other_x_ref,
    skip_ref,
    skip_bias_ref,
    out_ref,
    act_ref,
):
    section, tm, tile = (lax.axis_index(axis) for axis in AXES)
    frames, padded, width, outputs = hidden_ref.shape
    rows = padded - 2
    columns = x_ref.shape[2]
    half = x_ref.shape[3]
    own = columns // 2
    sent_rows = before_ref.shape[1] - 1
    top = sent_start(tiles, tile)
    first = pl.multiple_of(section * (width - own), RIM)
    beside = pl.multiple_of((1 - section) * own, RIM)
    norm = scale_and_offset(
        [moments_ref, other_moments_ref],
        frames * rows * own,
        outputs // GROUPS,
        gain_ref[...],
        shift_ref[...],
    )
    for f in range(frames):
        act_ref[frames + f] = apply_norm(hidden_ref[f], norm)
        act_ref[f, pl.ds(top, sent_rows), pl.ds(first, own), :] = apply_norm(
            before_ref[f, :sent_rows], norm
        )
        rim = apply_norm(before_ref[f, sent_rows], norm).astype(jnp.float32)[:padded]
        rim = jnp.broadcast_to(rim[:, None, :], (padded, width - own, outputs))
        act_ref[f, :, pl.ds(beside, width - own), :] = rim.astype(jnp.bfloat16)

    @pl.when(tile == 0)
    def _():
        for f in range(2 * frames):
            act_ref[f, 0] = act_ref[f, 1]

    @pl.when(tile == tiles - 1)
    def _():
        for f in range(2 * frames):
            act_ref[f, rows + 1] = act_ref[f, rows]

    @pl.when(tm == 0)
    def _():
        for f in range(frames):
            act_ref[f] = act_ref[frames]

    mine = pl.ds(pl.multiple_of(section * own, own), own)
    skip_here = skip_ref[pl.ds(pl.multiple_of(section * half, half), half), :]
    skip_there = skip_ref[pl.ds(pl.multiple_of((1 - section) * half, half), half), :]
    for f in range(frames):
        residual = conv_rows(act_ref, weight_ref, f, rows, width)
        residual = jnp.where(section == 0, residual[:, :own], residual[:, width - own :])
        here = x_ref[f, :, mine, :].reshape(rows * own, half)
        there = other_x_ref[f, :, mine, :].reshape(rows * own, half)
        shortcut = jnp.dot(here, skip_here, preferred_element_type=jnp.float32)
        shortcut = shortcut + jnp.dot(there, skip_there, preferred_element_type=jnp.float32)
        total = (residual + bias_ref[...]) + (
            shortcut.reshape(rows, own, outputs) + skip_bias_ref[...]
        )
        out_ref[f] = total.astype(jnp.bfloat16)


def pairs_for(tm_count, tile_count, tm_step, tile_step):
    out = []
    for a in range(tm_count):
        for b in range(tile_count):
            c, d = a + tm_step, b + tile_step
            if 0 <= c < tm_count and 0 <= d < tile_count:
                out.append((a * tile_count + b, c * tile_count + d))
    return out


def to_everyone(moments):
    return lax.all_to_all(moments, ("tm", "tile"), 0, 0, tiled=True)


def shards(
    features,
    norm_gain_in,
    norm_shift_in,
    conv_in_weight,
    conv_in_bias,
    norm_gain_mid,
    norm_shift_mid,
    conv_mid_weight,
    conv_mid_bias,
    skip_weight,
    skip_bias,
):
    sections, tms, tiles = (lax.axis_size(axis) for axis in AXES)
    parties = tms * tiles
    frames, rows, columns, half = features.shape
    own = columns // sections
    width = own + RIM
    middle = conv_in_weight.shape[-1]
    outputs = conv_mid_weight.shape[-1]
    grid_axes = ("tm", "tile")

    def shift(value, tm_step, tile_step):
        return lax.ppermute(value, grid_axes, pairs_for(tms, tiles, tm_step, tile_step))

    def swap(value):
        return lax.ppermute(value, "section", [(0, 1), (1, 0)])

    previous = shift(features, 1, 0)
    edge = jax.ShapeDtypeStruct((frames, 2, columns, half), features.dtype)
    edges = 1 if tiles == 2 else 2
    moments, *edge_rows = pl.pallas_call(
        functools.partial(first_kernel, tiles == 2),
        out_shape=(jax.ShapeDtypeStruct((parties, 2, half), jnp.float32),) + (edge,) * edges,
        in_specs=vmem_specs(1),
        out_specs=tuple(vmem_specs(1 + edges)),
        compiler_params=params(),
        cost_estimate=cost(1_000_000_000, 1_000_000),
        name="feature_moments",
    )(features)
    if tiles == 2:
        (facing,) = edge_rows
        crossing = [
            (a * 2 + b, (a + 1) * 2 + 1 - b) for a in range(tms - 1) for b in range(2)
        ]
        rims = [
            lax.ppermute(facing, "tile", [(0, 1), (1, 0)]),
            lax.ppermute(facing, grid_axes, crossing),
        ]
    else:
        top, bottom = edge_rows
        rims = [
            shift(bottom, 0, 1),
            shift(bottom, 1, 1),
            shift(top, 0, -1),
            shift(top, 1, -1),
        ]
    other = swap(features)
    moments = to_everyone(moments)
    previous, moments, *rims = lax.optimization_barrier((previous, moments, *rims))
    other_moments = swap(moments)
    other_previous = swap(previous)
    other_rims = [swap(rim) for rim in rims]
    up, up_prev, down, down_prev = (rims * 2)[:4]
    other_up, other_up_prev, other_down, other_down_prev = (other_rims * 2)[:4]

    sent_rows = rows + (1 if tiles == 2 else 2)
    hidden, sent, moments_mid = pl.pallas_call(
        functools.partial(middle_kernel, tiles),
        out_shape=(
            jax.ShapeDtypeStruct((frames, rows + 2, width, middle), jnp.bfloat16),
            jax.ShapeDtypeStruct((frames, sent_rows + 1, own, middle), jnp.bfloat16),
            jax.ShapeDtypeStruct((parties, 2, middle), jnp.float32),
        ),
        in_specs=vmem_specs(18),
        out_specs=tuple(vmem_specs(3)),
        scratch_shapes=[pltpu.VMEM((2 * frames, rows + 4, width, 2 * half), jnp.bfloat16)],
        compiler_params=params(),
        cost_estimate=cost(4_000_000_000, 1_000_000),
        name="norm_conv_in",
    )(
        features,
        previous,
        up,
        down,
        up_prev,
        down_prev,
        other,
        other_previous,
        other_up,
        other_down,
        other_up_prev,
        other_down_prev,
        moments,
        other_moments,
        norm_gain_in.reshape(2, half),
        norm_shift_in.reshape(2, half),
        conv_in_weight,
        conv_in_bias.reshape(1, middle),
    )
    before = shift(sent, 1, 0)
    moments_mid = to_everyone(moments_mid)
    return pl.pallas_call(
        functools.partial(last_kernel, tiles),
        out_shape=jax.ShapeDtypeStruct((frames, rows, own, outputs), jnp.bfloat16),
        in_specs=vmem_specs(12),
        out_specs=pl.BlockSpec(memory_space=pltpu.VMEM),
        scratch_shapes=[pltpu.VMEM((2 * frames, rows + 2, width, middle), jnp.bfloat16)],
        compiler_params=params(),
        name="norm_conv_mid",
    )(
        hidden,
        before,
        moments_mid,
        swap(moments_mid),
        norm_gain_mid.reshape(1, middle),
        norm_shift_mid.reshape(1, middle),
        conv_mid_weight,
        conv_mid_bias.reshape(1, outputs),
        features,
        other,
        skip_weight,
        skip_bias.reshape(1, outputs),
    )


def solution(mesh):
    in_specs = (P("tm", "tile", None, "section"),) + (P(),) * 10
    out_specs = P("tm", "tile", "section", None)
    return jax.shard_map(shards, mesh=mesh, in_specs=in_specs, out_specs=out_specs, check_vma=False)
```

```python
import functools

import jax
import jax.numpy as jnp
from jax import lax
from jax.experimental import pallas as pl
from jax.experimental.pallas import tpu as pltpu
from jax.sharding import PartitionSpec as P

GROUPS = 32
AXES = ("section", "tm", "tile")
VMEM_LIMIT = 48 * 1024 * 1024
RIM = 16


def params():
    return pltpu.CompilerParams(vmem_limit_bytes=VMEM_LIMIT)


def cost(flops, moved):
    return pl.CostEstimate(flops=flops, bytes_accessed=moved, transcendentals=0)


def vmem_specs(count):
    return [pl.BlockSpec(memory_space=pltpu.VMEM)] * count


def silu(u):
    half = 0.5 * u
    return half + half * jnp.tanh(half)


def moments_of(cells):
    mean = jnp.sum(cells, axis=0, keepdims=True) * (1.0 / cells.shape[0])
    off = cells - mean
    return jnp.concatenate([mean, jnp.sum(off * off, axis=0, keepdims=True)], axis=0)


def group_matrix(channels, width):
    shape = (channels, channels)
    row = lax.broadcasted_iota(jnp.int32, shape, 0) // width
    col = lax.broadcasted_iota(jnp.int32, shape, 1) // width
    return jnp.where(row == col, 1.0, 0.0).astype(jnp.float32)


def group_sum(values, matrix):
    tall = jnp.broadcast_to(values, (8, values.shape[-1]))
    return jnp.dot(
        tall, matrix, preferred_element_type=jnp.float32, precision=lax.Precision.HIGHEST
    )[:1]


def scale_and_offset(moments, cells, width, gain, shift):
    devices, _, channels = moments.shape
    matrix = group_matrix(channels, width)
    means = moments[:, 0, :]
    mean = group_sum(jnp.sum(means, axis=0, keepdims=True), matrix) * (1.0 / (devices * width))
    off = means - mean
    total = jnp.sum(moments[:, 1, :] + float(cells) * (off * off), axis=0, keepdims=True)
    spread = group_sum(total, matrix) * (1.0 / (cells * devices * width))
    scale = lax.rsqrt(spread + 1e-6) * gain
    return mean, scale, shift


def apply_norm(values, norm):
    mean, scale, shift = norm
    return silu((values.astype(jnp.float32) - mean) * scale + shift).astype(jnp.bfloat16)


def first_kernel(x_ref, moments_ref):
    x = x_ref[...]
    cells = x.astype(jnp.float32).reshape(-1, x.shape[-1])
    moments_ref[...] = jnp.broadcast_to(moments_of(cells)[None], moments_ref.shape)


def outgoing_kernel(pairs, x_ref, order_ref, block_ref, *edge_refs):
    block_ref[...] = x_ref[...]
    rows = x_ref.shape[1]
    if pairs:
        first = (rows - 2) * (1 - lax.axis_index("tile"))
        edge_refs[0][...] = x_ref[:, pl.ds(first, 2)]
    else:
        edge_refs[0][...] = x_ref[:, :2]
        edge_refs[1][...] = x_ref[:, -2:]


def conv_rows(act_ref, weight_ref, frames, rows, width):
    total = None
    for t, frame in enumerate(frames):
        for h in range(3) if frame is not None else ():
            cells = act_ref[frame, h : h + rows]
            cells = cells.reshape(rows * width, cells.shape[-1])
            taps = jnp.concatenate([weight_ref[t, h, w] for w in range(3)], axis=-1)
            part = jnp.dot(cells, taps, preferred_element_type=jnp.float32)
            total = part if total is None else total + part
    outputs = weight_ref.shape[-1]
    total = total.reshape(rows, width, 3 * outputs)
    before, middle, after = (total[..., k * outputs : (k + 1) * outputs] for k in range(3))
    before = jnp.concatenate([before[:, :1], before[:, :-1]], axis=1)
    after = jnp.concatenate([after[:, 1:], after[:, -1:]], axis=1)
    return middle + before + after


def middle_kernel(
    tiles,
    x_ref,
    prev_ref,
    up_ref,
    down_ref,
    up_prev_ref,
    down_prev_ref,
    other_x_ref,
    other_prev_ref,
    other_up_ref,
    other_down_ref,
    other_up_prev_ref,
    other_down_prev_ref,
    moments_ref,
    gain_ref,
    shift_ref,
    weight_ref,
    bias_ref,
    hidden_ref,
    out_moments_ref,
    act_ref,
):
    section, tm, tile = (lax.axis_index(axis) for axis in AXES)
    frames, rows, columns, half = x_ref.shape
    width = columns // 2 + RIM
    first = pl.multiple_of(section * (columns - width), RIM)
    cols = pl.ds(first, width)
    pieces = (
        (
            section,
            ((x_ref, up_ref, down_ref), (prev_ref, up_prev_ref, down_prev_ref)),
        ),
        (
            1 - section,
            (
                (other_x_ref, other_up_ref, other_down_ref),
                (other_prev_ref, other_up_prev_ref, other_down_prev_ref),
            ),
        ),
    )
    per_section = moments_ref.shape[0] // 2
    for which, (now, before) in pieces:
        norm = scale_and_offset(
            moments_ref[pl.ds(which * per_section, per_section)],
            frames * rows * columns,
            2 * half // GROUPS,
            gain_ref[pl.ds(which, 1), :],
            shift_ref[pl.ds(which, 1), :],
        )
        lanes = pl.ds(pl.multiple_of(which * half, half), half)
        for start, (body, up, down) in ((frames, now), (0, before)):
            for f in range(frames):
                act_ref[start + f, 2 : 2 + rows, :, lanes] = apply_norm(body[f, :, cols, :], norm)
                act_ref[start + f, 0:2, :, lanes] = apply_norm(up[f, :, cols, :], norm)
                act_ref[start + f, 2 + rows :, :, lanes] = apply_norm(down[f, :, cols, :], norm)

    @pl.when(tile == 0)
    def _():
        for f in range(2 * frames):
            act_ref[f, 1] = act_ref[f, 2]

    @pl.when(tile == tiles - 1)
    def _():
        for f in range(2 * frames):
            act_ref[f, rows + 2] = act_ref[f, rows + 1]

    @pl.when(tm == 0)
    def _():
        for f in range(frames):
            act_ref[f] = act_ref[frames]

    own = columns // 2
    for f in range(frames):
        hidden = conv_rows(act_ref, weight_ref, (f, f + 1, f + 2), rows + 2, width)
        hidden_ref[f] = (hidden + bias_ref[...]).astype(jnp.bfloat16)

    cells = hidden_ref[:, 1 : 1 + rows, pl.ds(first, own), :]
    cells = cells.astype(jnp.float32).reshape(-1, cells.shape[-1])
    out_moments_ref[...] = jnp.broadcast_to(moments_of(cells)[None], out_moments_ref.shape)


def sent_start(tiles, tile):
    return 1 - tile if tiles == 2 else 0


def pack_kernel(tiles, hidden_ref, sent_ref):
    section, tile = lax.axis_index("section"), lax.axis_index("tile")
    frames, padded, width, channels = hidden_ref.shape
    own = sent_ref.shape[2]
    first = pl.multiple_of(section * (width - own), RIM)
    sent_rows = sent_ref.shape[1] - 1
    top = sent_start(tiles, tile)
    for f in range(frames):
        sent_ref[f, :sent_rows] = hidden_ref[f, pl.ds(top, sent_rows), pl.ds(first, own), :]
        hidden = hidden_ref[f].astype(jnp.float32)
        rim = jnp.where(section == 0, hidden[:, own, :], hidden[:, width - own - 1, :])
        spare = jnp.zeros((own - padded, channels), jnp.float32)
        sent_ref[f, sent_rows] = jnp.concatenate([rim, spare], axis=0).astype(jnp.bfloat16)


def repeat_edges(act_ref, count, tiles, rows):
    tile = lax.axis_index("tile")

    @pl.when(tile == 0)
    def _():
        for f in range(count):
            act_ref[f, 0] = act_ref[f, 1]

    @pl.when(tile == tiles - 1)
    def _():
        for f in range(count):
            act_ref[f, rows + 1] = act_ref[f, rows]


def own_columns(values, own):
    section = lax.axis_index("section")
    width = values.shape[1]
    return jnp.where(section == 0, values[:, :own], values[:, width - own :])


def own_frames_kernel(
    tiles,
    hidden_ref,
    moments_ref,
    gain_ref,
    shift_ref,
    weight_ref,
    bias_ref,
    x_ref,
    other_x_ref,
    skip_ref,
    skip_bias_ref,
    part_ref,
    norm_ref,
    act_ref,
):
    section = lax.axis_index("section")
    frames, padded, width, outputs = hidden_ref.shape
    rows = padded - 2
    half = x_ref.shape[3]
    own = x_ref.shape[2] // 2
    norm = scale_and_offset(
        moments_ref[...],
        frames * rows * own,
        outputs // GROUPS,
        gain_ref[...],
        shift_ref[...],
    )
    norm_ref[...] = jnp.concatenate(norm, axis=0)
    for f in range(frames):
        act_ref[f] = apply_norm(hidden_ref[f], norm)
    repeat_edges(act_ref, frames, tiles, rows)
    mine = pl.ds(pl.multiple_of(section * own, own), own)
    skip_here = skip_ref[pl.ds(pl.multiple_of(section * half, half), half), :]
    skip_there = skip_ref[pl.ds(pl.multiple_of((1 - section) * half, half), half), :]
    for f in range(frames):
        taps = [k if k >= 0 else None for k in range(f - 2, f + 1)]
        residual = own_columns(conv_rows(act_ref, weight_ref, taps, rows, width), own)
        here = x_ref[f, :, mine, :].reshape(rows * own, half)
        there = other_x_ref[f, :, mine, :].reshape(rows * own, half)
        shortcut = jnp.dot(here, skip_here, preferred_element_type=jnp.float32)
        shortcut = shortcut + jnp.dot(there, skip_there, preferred_element_type=jnp.float32)
        part_ref[f] = (residual + bias_ref[...]) + (
            shortcut.reshape(rows, own, outputs) + skip_bias_ref[...]
        )


def last_kernel(
    tiles, hidden_ref, before_ref, norm_ref, weight_ref, part_ref, out_ref, act_ref
):
    section, tm, tile = (lax.axis_index(axis) for axis in AXES)
    frames, padded, width, outputs = hidden_ref.shape
    rows = padded - 2
    own = part_ref.shape[2]
    sent_rows = before_ref.shape[1] - 1
    top = sent_start(tiles, tile)
    first = pl.multiple_of(section * (width - own), RIM)
    beside = pl.multiple_of((1 - section) * own, RIM)
    norm = tuple(norm_ref[k : k + 1] for k in range(3))
    for f in range(frames):
        act_ref[f, pl.ds(top, sent_rows), pl.ds(first, own), :] = apply_norm(
            before_ref[f, :sent_rows], norm
        )
        rim = apply_norm(before_ref[f, sent_rows], norm).astype(jnp.float32)[:padded]
        rim = jnp.broadcast_to(rim[:, None, :], (padded, width - own, outputs))
        act_ref[f, :, pl.ds(beside, width - own), :] = rim.astype(jnp.bfloat16)

    @pl.when(tm == 0)
    def _():
        start = apply_norm(hidden_ref[0], norm)
        for f in range(frames):
            act_ref[f] = start

    repeat_edges(act_ref, frames, tiles, rows)
    for f in range(frames):
        taps = [k if k < frames else None for k in range(f, f + 3)]
        residual = own_columns(conv_rows(act_ref, weight_ref, taps, rows, width), own)
        out_ref[f] = (part_ref[f] + residual).astype(jnp.bfloat16)


def pairs_for(tm_count, tile_count, tm_step, tile_step):
    out = []
    for a in range(tm_count):
        for b in range(tile_count):
            c, d = a + tm_step, b + tile_step
            if 0 <= c < tm_count and 0 <= d < tile_count:
                out.append((a * tile_count + b, c * tile_count + d))
    return out


def to_everyone(moments):
    return lax.all_to_all(moments, AXES, 0, 0, tiled=True)


def shards(
    features,
    norm_gain_in,
    norm_shift_in,
    conv_in_weight,
    conv_in_bias,
    norm_gain_mid,
    norm_shift_mid,
    conv_mid_weight,
    conv_mid_bias,
    skip_weight,
    skip_bias,
):
    sections, tms, tiles = (lax.axis_size(axis) for axis in AXES)
    parties = sections * tms * tiles
    frames, rows, columns, half = features.shape
    own = columns // sections
    width = own + RIM
    middle = conv_in_weight.shape[-1]
    outputs = conv_mid_weight.shape[-1]
    grid_axes = ("tm", "tile")

    def shift(value, tm_step, tile_step):
        return lax.ppermute(value, grid_axes, pairs_for(tms, tiles, tm_step, tile_step))

    def swap(value):
        return lax.ppermute(value, "section", [(0, 1), (1, 0)])

    moments = pl.pallas_call(
        first_kernel,
        out_shape=jax.ShapeDtypeStruct((parties, 2, half), jnp.float32),
        in_specs=vmem_specs(1),
        out_specs=pl.BlockSpec(memory_space=pltpu.VMEM),
        compiler_params=params(),
        name="feature_moments",
    )(features)
    edge = jax.ShapeDtypeStruct((frames, 2, columns, half), features.dtype)
    edges = 1 if tiles == 2 else 2
    block, *edge_rows = pl.pallas_call(
        functools.partial(outgoing_kernel, tiles == 2),
        out_shape=(jax.ShapeDtypeStruct(features.shape, features.dtype),) + (edge,) * edges,
        in_specs=[*vmem_specs(1), pl.BlockSpec(memory_space=pl.ANY)],
        out_specs=tuple(vmem_specs(1 + edges)),
        compiler_params=params(),
        cost_estimate=cost(1_000_000_000, 1_000_000),
        name="outgoing_rows",
    )(features, moments)
    previous = shift(block, 1, 0)
    if tiles == 2:
        (facing,) = edge_rows
        crossing = [
            (a * 2 + b, (a + 1) * 2 + 1 - b) for a in range(tms - 1) for b in range(2)
        ]
        rims = [
            lax.ppermute(facing, "tile", [(0, 1), (1, 0)]),
            lax.ppermute(facing, grid_axes, crossing),
        ]
    else:
        top, bottom = edge_rows
        rims = [
            shift(bottom, 0, 1),
            shift(bottom, 1, 1),
            shift(top, 0, -1),
            shift(top, 1, -1),
        ]
    other = swap(block)
    moments = to_everyone(moments)
    previous, moments, *rims = lax.optimization_barrier((previous, moments, *rims))
    other_previous = swap(previous)
    other_rims = [swap(rim) for rim in rims]
    up, up_prev, down, down_prev = (rims * 2)[:4]
    other_up, other_up_prev, other_down, other_down_prev = (other_rims * 2)[:4]

    sent_rows = rows + (1 if tiles == 2 else 2)
    hidden, moments_mid = pl.pallas_call(
        functools.partial(middle_kernel, tiles),
        out_shape=(
            jax.ShapeDtypeStruct((frames, rows + 2, width, middle), jnp.bfloat16),
            jax.ShapeDtypeStruct((parties, 2, middle), jnp.float32),
        ),
        in_specs=vmem_specs(17),
        out_specs=tuple(vmem_specs(2)),
        scratch_shapes=[pltpu.VMEM((2 * frames, rows + 4, width, 2 * half), jnp.bfloat16)],
        compiler_params=params(),
        cost_estimate=cost(4_000_000_000, 1_000_000),
        name="norm_conv_in",
    )(
        features,
        previous,
        up,
        down,
        up_prev,
        down_prev,
        other,
        other_previous,
        other_up,
        other_down,
        other_up_prev,
        other_down_prev,
        moments,
        norm_gain_in.reshape(2, half),
        norm_shift_in.reshape(2, half),
        conv_in_weight,
        conv_in_bias.reshape(1, middle),
    )
    moments_mid = to_everyone(moments_mid)
    sent = pl.pallas_call(
        functools.partial(pack_kernel, tiles),
        out_shape=jax.ShapeDtypeStruct((frames, sent_rows + 1, own, middle), jnp.bfloat16),
        in_specs=vmem_specs(1),
        out_specs=pl.BlockSpec(memory_space=pltpu.VMEM),
        compiler_params=params(),
        cost_estimate=cost(1_000_000_000, 1_000_000),
        name="pack_hidden",
    )(hidden)
    before = shift(sent, 1, 0)
    part, norm_mid = pl.pallas_call(
        functools.partial(own_frames_kernel, tiles),
        out_shape=(
            jax.ShapeDtypeStruct((frames, rows, own, outputs), jnp.float32),
            jax.ShapeDtypeStruct((3, middle), jnp.float32),
        ),
        in_specs=vmem_specs(10),
        out_specs=tuple(vmem_specs(2)),
        scratch_shapes=[pltpu.VMEM((frames, rows + 2, width, middle), jnp.bfloat16)],
        compiler_params=params(),
        cost_estimate=cost(2_000_000_000, 1_000_000),
        name="conv_mid_own_frames",
    )(
        hidden,
        moments_mid,
        norm_gain_mid.reshape(1, middle),
        norm_shift_mid.reshape(1, middle),
        conv_mid_weight,
        conv_mid_bias.reshape(1, outputs),
        features,
        other,
        skip_weight,
        skip_bias.reshape(1, outputs),
    )
    return pl.pallas_call(
        functools.partial(last_kernel, tiles),
        out_shape=jax.ShapeDtypeStruct((frames, rows, own, outputs), jnp.bfloat16),
        in_specs=vmem_specs(5),
        out_specs=pl.BlockSpec(memory_space=pltpu.VMEM),
        scratch_shapes=[pltpu.VMEM((frames, rows + 2, width, middle), jnp.bfloat16)],
        compiler_params=params(),
        cost_estimate=cost(2_000_000_000, 1_000_000),
        name="conv_mid_previous_frames",
    )(hidden, before, norm_mid, conv_mid_weight, part)


def solution(mesh):
    in_specs = (P("tm", "tile", None, "section"),) + (P(),) * 10
    out_specs = P("tm", "tile", "section", None)
    return jax.shard_map(shards, mesh=mesh, in_specs=in_specs, out_specs=out_specs, check_vma=False)
```

```python
import functools

import jax
import jax.numpy as jnp
from jax import lax
from jax.experimental import pallas as pl
from jax.experimental.pallas import tpu as pltpu
from jax.sharding import PartitionSpec as P

GROUPS = 32
AXES = ("section", "tm", "tile")
VMEM_LIMIT = 48 * 1024 * 1024
RIM = 16


def params():
    return pltpu.CompilerParams(vmem_limit_bytes=VMEM_LIMIT)


def cost(flops, moved):
    return pl.CostEstimate(flops=flops, bytes_accessed=moved, transcendentals=0)


def vmem_specs(count):
    return [pl.BlockSpec(memory_space=pltpu.VMEM)] * count


def silu(u):
    half = 0.5 * u
    return half + half * jnp.tanh(half)


def moments_of(cells):
    mean = jnp.sum(cells, axis=0, keepdims=True) * (1.0 / cells.shape[0])
    off = cells - mean
    return jnp.concatenate([mean, jnp.sum(off * off, axis=0, keepdims=True)], axis=0)


def group_matrix(channels, width):
    shape = (channels, channels)
    row = lax.broadcasted_iota(jnp.int32, shape, 0) // width
    col = lax.broadcasted_iota(jnp.int32, shape, 1) // width
    return jnp.where(row == col, 1.0, 0.0).astype(jnp.float32)


def group_sum(values, matrix):
    tall = jnp.broadcast_to(values, (8, values.shape[-1]))
    return jnp.dot(
        tall, matrix, preferred_element_type=jnp.float32, precision=lax.Precision.HIGHEST
    )[:1]


def scale_and_offset(moments, cells, width, gain, shift):
    devices, _, channels = moments.shape
    matrix = group_matrix(channels, width)
    means = moments[:, 0, :]
    mean = group_sum(jnp.sum(means, axis=0, keepdims=True), matrix) * (1.0 / (devices * width))
    off = means - mean
    total = jnp.sum(moments[:, 1, :] + float(cells) * (off * off), axis=0, keepdims=True)
    spread = group_sum(total, matrix) * (1.0 / (cells * devices * width))
    scale = lax.rsqrt(spread + 1e-6) * gain
    return mean, scale, shift


def apply_norm(values, norm):
    mean, scale, shift = norm
    return silu((values.astype(jnp.float32) - mean) * scale + shift).astype(jnp.bfloat16)


def first_kernel(x_ref, moments_ref):
    x = x_ref[...]
    cells = x.astype(jnp.float32).reshape(-1, x.shape[-1])
    moments_ref[...] = jnp.broadcast_to(moments_of(cells)[None], moments_ref.shape)


def outgoing_kernel(pairs, x_ref, order_ref, block_ref, *edge_refs):
    block_ref[...] = x_ref[...]
    rows = x_ref.shape[1]
    if pairs:
        first = (rows - 2) * (1 - lax.axis_index("tile"))
        edge_refs[0][...] = x_ref[:, pl.ds(first, 2)]
    else:
        edge_refs[0][...] = x_ref[:, :2]
        edge_refs[1][...] = x_ref[:, -2:]


def scales_kernel(cells, moments_ref, gain_ref, shift_ref, norm_ref):
    sections, half = gain_ref.shape
    per_section = moments_ref.shape[0] // sections
    for k in range(sections):
        norm = scale_and_offset(
            moments_ref[k * per_section : (k + 1) * per_section],
            cells,
            sections * half // GROUPS,
            gain_ref[k : k + 1],
            shift_ref[k : k + 1],
        )
        norm_ref[k] = jnp.concatenate(norm, axis=0)


def conv_rows(act_ref, weight_ref, frames, rows, width):
    total = None
    for t, frame in enumerate(frames):
        for h in range(3) if frame is not None else ():
            cells = act_ref[frame, h : h + rows]
            cells = cells.reshape(rows * width, cells.shape[-1])
            taps = jnp.concatenate([weight_ref[t, h, w] for w in range(3)], axis=-1)
            part = jnp.dot(cells, taps, preferred_element_type=jnp.float32)
            total = part if total is None else total + part
    outputs = weight_ref.shape[-1]
    total = total.reshape(rows, width, 3 * outputs)
    before, middle, after = (total[..., k * outputs : (k + 1) * outputs] for k in range(3))
    before = jnp.concatenate([before[:, :1], before[:, :-1]], axis=1)
    after = jnp.concatenate([after[:, 1:], after[:, -1:]], axis=1)
    return middle + before + after


def middle_kernel(
    tiles,
    x_ref,
    prev_ref,
    up_ref,
    down_ref,
    up_prev_ref,
    down_prev_ref,
    other_x_ref,
    other_prev_ref,
    other_up_ref,
    other_down_ref,
    other_up_prev_ref,
    other_down_prev_ref,
    norm_ref,
    weight_ref,
    bias_ref,
    hidden_ref,
    out_moments_ref,
    act_ref,
):
    section, tm, tile = (lax.axis_index(axis) for axis in AXES)
    frames, rows, columns, half = x_ref.shape
    width = columns // 2 + RIM
    first = pl.multiple_of(section * (columns - width), RIM)
    cols = pl.ds(first, width)
    pieces = (
        (
            section,
            ((x_ref, up_ref, down_ref), (prev_ref, up_prev_ref, down_prev_ref)),
        ),
        (
            1 - section,
            (
                (other_x_ref, other_up_ref, other_down_ref),
                (other_prev_ref, other_up_prev_ref, other_down_prev_ref),
            ),
        ),
    )
    for which, (now, before) in pieces:
        norm = tuple(norm_ref[which, k : k + 1] for k in range(3))
        lanes = pl.ds(pl.multiple_of(which * half, half), half)
        for start, (body, up, down) in ((frames, now), (0, before)):
            for f in range(frames):
                act_ref[start + f, 2 : 2 + rows, :, lanes] = apply_norm(body[f, :, cols, :], norm)
                act_ref[start + f, 0:2, :, lanes] = apply_norm(up[f, :, cols, :], norm)
                act_ref[start + f, 2 + rows :, :, lanes] = apply_norm(down[f, :, cols, :], norm)

    @pl.when(tile == 0)
    def _():
        for f in range(2 * frames):
            act_ref[f, 1] = act_ref[f, 2]

    @pl.when(tile == tiles - 1)
    def _():
        for f in range(2 * frames):
            act_ref[f, rows + 2] = act_ref[f, rows + 1]

    @pl.when(tm == 0)
    def _():
        for f in range(frames):
            act_ref[f] = act_ref[frames]

    own = columns // 2
    for f in range(frames):
        hidden = conv_rows(act_ref, weight_ref, (f, f + 1, f + 2), rows + 2, width)
        hidden_ref[f] = (hidden + bias_ref[...]).astype(jnp.bfloat16)

    cells = hidden_ref[:, 1 : 1 + rows, pl.ds(first, own), :]
    cells = cells.astype(jnp.float32).reshape(-1, cells.shape[-1])
    out_moments_ref[...] = jnp.broadcast_to(moments_of(cells)[None], out_moments_ref.shape)


def sent_start(tiles, tile):
    return 1 - tile if tiles == 2 else 0


def pack_kernel(tiles, hidden_ref, sent_ref):
    section, tile = lax.axis_index("section"), lax.axis_index("tile")
    frames, padded, width, channels = hidden_ref.shape
    own = sent_ref.shape[2]
    first = pl.multiple_of(section * (width - own), RIM)
    sent_rows = sent_ref.shape[1] - 1
    top = sent_start(tiles, tile)
    for f in range(frames):
        sent_ref[f, :sent_rows] = hidden_ref[f, pl.ds(top, sent_rows), pl.ds(first, own), :]
        hidden = hidden_ref[f].astype(jnp.float32)
        rim = jnp.where(section == 0, hidden[:, own, :], hidden[:, width - own - 1, :])
        spare = jnp.zeros((own - padded, channels), jnp.float32)
        sent_ref[f, sent_rows] = jnp.concatenate([rim, spare], axis=0).astype(jnp.bfloat16)


def repeat_edges(act_ref, count, tiles, rows):
    tile = lax.axis_index("tile")

    @pl.when(tile == 0)
    def _():
        for f in range(count):
            act_ref[f, 0] = act_ref[f, 1]

    @pl.when(tile == tiles - 1)
    def _():
        for f in range(count):
            act_ref[f, rows + 1] = act_ref[f, rows]


def own_columns(values, own):
    section = lax.axis_index("section")
    width = values.shape[1]
    return jnp.where(section == 0, values[:, :own], values[:, width - own :])


def own_frames_kernel(
    tiles,
    hidden_ref,
    moments_ref,
    gain_ref,
    shift_ref,
    weight_ref,
    bias_ref,
    x_ref,
    other_x_ref,
    skip_ref,
    skip_bias_ref,
    part_ref,
    norm_ref,
    act_ref,
):
    section = lax.axis_index("section")
    frames, padded, width, outputs = hidden_ref.shape
    rows = padded - 2
    half = x_ref.shape[3]
    own = x_ref.shape[2] // 2
    norm = scale_and_offset(
        moments_ref[...],
        frames * rows * own,
        outputs // GROUPS,
        gain_ref[...],
        shift_ref[...],
    )
    norm_ref[...] = jnp.concatenate(norm, axis=0)
    for f in range(frames):
        act_ref[f] = apply_norm(hidden_ref[f], norm)
    repeat_edges(act_ref, frames, tiles, rows)
    mine = pl.ds(pl.multiple_of(section * own, own), own)
    skip_here = skip_ref[pl.ds(pl.multiple_of(section * half, half), half), :]
    skip_there = skip_ref[pl.ds(pl.multiple_of((1 - section) * half, half), half), :]
    for f in range(frames):
        taps = [k if k >= 0 else None for k in range(f - 2, f + 1)]
        residual = own_columns(conv_rows(act_ref, weight_ref, taps, rows, width), own)
        here = x_ref[f, :, mine, :].reshape(rows * own, half)
        there = other_x_ref[f, :, mine, :].reshape(rows * own, half)
        shortcut = jnp.dot(here, skip_here, preferred_element_type=jnp.float32)
        shortcut = shortcut + jnp.dot(there, skip_there, preferred_element_type=jnp.float32)
        part_ref[f] = (residual + bias_ref[...]) + (
            shortcut.reshape(rows, own, outputs) + skip_bias_ref[...]
        )


def last_kernel(
    tiles, hidden_ref, before_ref, norm_ref, weight_ref, part_ref, out_ref, act_ref
):
    section, tm, tile = (lax.axis_index(axis) for axis in AXES)
    frames, padded, width, outputs = hidden_ref.shape
    rows = padded - 2
    own = part_ref.shape[2]
    sent_rows = before_ref.shape[1] - 1
    top = sent_start(tiles, tile)
    first = pl.multiple_of(section * (width - own), RIM)
    beside = pl.multiple_of((1 - section) * own, RIM)
    norm = tuple(norm_ref[k : k + 1] for k in range(3))
    for f in range(frames):
        act_ref[f, pl.ds(top, sent_rows), pl.ds(first, own), :] = apply_norm(
            before_ref[f, :sent_rows], norm
        )
        rim = apply_norm(before_ref[f, sent_rows], norm).astype(jnp.float32)[:padded]
        rim = jnp.broadcast_to(rim[:, None, :], (padded, width - own, outputs))
        act_ref[f, :, pl.ds(beside, width - own), :] = rim.astype(jnp.bfloat16)

    @pl.when(tm == 0)
    def _():
        start = apply_norm(hidden_ref[0], norm)
        for f in range(frames):
            act_ref[f] = start

    repeat_edges(act_ref, frames, tiles, rows)
    for f in range(frames):
        taps = [k if k < frames else None for k in range(f, f + 3)]
        residual = own_columns(conv_rows(act_ref, weight_ref, taps, rows, width), own)
        out_ref[f] = (part_ref[f] + residual).astype(jnp.bfloat16)


def pairs_for(tm_count, tile_count, tm_step, tile_step):
    out = []
    for a in range(tm_count):
        for b in range(tile_count):
            c, d = a + tm_step, b + tile_step
            if 0 <= c < tm_count and 0 <= d < tile_count:
                out.append((a * tile_count + b, c * tile_count + d))
    return out


def to_everyone(moments):
    return lax.all_to_all(moments, AXES, 0, 0, tiled=True)


def shards(
    features,
    norm_gain_in,
    norm_shift_in,
    conv_in_weight,
    conv_in_bias,
    norm_gain_mid,
    norm_shift_mid,
    conv_mid_weight,
    conv_mid_bias,
    skip_weight,
    skip_bias,
):
    sections, tms, tiles = (lax.axis_size(axis) for axis in AXES)
    parties = sections * tms * tiles
    frames, rows, columns, half = features.shape
    own = columns // sections
    width = own + RIM
    middle = conv_in_weight.shape[-1]
    outputs = conv_mid_weight.shape[-1]
    grid_axes = ("tm", "tile")

    def shift(value, tm_step, tile_step):
        return lax.ppermute(value, grid_axes, pairs_for(tms, tiles, tm_step, tile_step))

    def swap(value):
        return lax.ppermute(value, "section", [(0, 1), (1, 0)])

    moments = pl.pallas_call(
        first_kernel,
        out_shape=jax.ShapeDtypeStruct((parties, 2, half), jnp.float32),
        in_specs=vmem_specs(1),
        out_specs=pl.BlockSpec(memory_space=pltpu.VMEM),
        compiler_params=params(),
        name="feature_moments",
    )(features)
    edge = jax.ShapeDtypeStruct((frames, 2, columns, half), features.dtype)
    edges = 1 if tiles == 2 else 2
    block, *edge_rows = pl.pallas_call(
        functools.partial(outgoing_kernel, tiles == 2),
        out_shape=(jax.ShapeDtypeStruct(features.shape, features.dtype),) + (edge,) * edges,
        in_specs=[*vmem_specs(1), pl.BlockSpec(memory_space=pl.ANY)],
        out_specs=tuple(vmem_specs(1 + edges)),
        compiler_params=params(),
        cost_estimate=cost(1_000_000_000, 1_000_000),
        name="outgoing_rows",
    )(features, moments)
    previous = shift(block, 1, 0)
    if tiles == 2:
        (facing,) = edge_rows
        crossing = [
            (a * 2 + b, (a + 1) * 2 + 1 - b) for a in range(tms - 1) for b in range(2)
        ]
        rims = [
            lax.ppermute(facing, "tile", [(0, 1), (1, 0)]),
            lax.ppermute(facing, grid_axes, crossing),
        ]
    else:
        top, bottom = edge_rows
        rims = [
            shift(bottom, 0, 1),
            shift(bottom, 1, 1),
            shift(top, 0, -1),
            shift(top, 1, -1),
        ]
    other = swap(block)
    moments = to_everyone(moments)
    norm_in = pl.pallas_call(
        functools.partial(scales_kernel, frames * rows * columns),
        out_shape=jax.ShapeDtypeStruct((sections, 3, half), jnp.float32),
        in_specs=vmem_specs(3),
        out_specs=pl.BlockSpec(memory_space=pltpu.VMEM),
        compiler_params=params(),
        cost_estimate=cost(4_000_000_000, 1_000_000),
        name="feature_scales",
    )(moments, norm_gain_in.reshape(sections, half), norm_shift_in.reshape(sections, half))
    previous, norm_in, *rims = lax.optimization_barrier((previous, norm_in, *rims))
    other_previous = swap(previous)
    other_rims = [swap(rim) for rim in rims]
    up, up_prev, down, down_prev = (rims * 2)[:4]
    other_up, other_up_prev, other_down, other_down_prev = (other_rims * 2)[:4]

    sent_rows = rows + (1 if tiles == 2 else 2)
    hidden, moments_mid = pl.pallas_call(
        functools.partial(middle_kernel, tiles),
        out_shape=(
            jax.ShapeDtypeStruct((frames, rows + 2, width, middle), jnp.bfloat16),
            jax.ShapeDtypeStruct((parties, 2, middle), jnp.float32),
        ),
        in_specs=vmem_specs(15),
        out_specs=tuple(vmem_specs(2)),
        scratch_shapes=[pltpu.VMEM((2 * frames, rows + 4, width, 2 * half), jnp.bfloat16)],
        compiler_params=params(),
        cost_estimate=cost(4_000_000_000, 1_000_000),
        name="norm_conv_in",
    )(
        features,
        previous,
        up,
        down,
        up_prev,
        down_prev,
        other,
        other_previous,
        other_up,
        other_down,
        other_up_prev,
        other_down_prev,
        norm_in,
        conv_in_weight,
        conv_in_bias.reshape(1, middle),
    )
    moments_mid = to_everyone(moments_mid)
    sent = pl.pallas_call(
        functools.partial(pack_kernel, tiles),
        out_shape=jax.ShapeDtypeStruct((frames, sent_rows + 1, own, middle), jnp.bfloat16),
        in_specs=vmem_specs(1),
        out_specs=pl.BlockSpec(memory_space=pltpu.VMEM),
        compiler_params=params(),
        cost_estimate=cost(1_000_000_000, 1_000_000),
        name="pack_hidden",
    )(hidden)
    before = shift(sent, 1, 0)
    part, norm_mid = pl.pallas_call(
        functools.partial(own_frames_kernel, tiles),
        out_shape=(
            jax.ShapeDtypeStruct((frames, rows, own, outputs), jnp.float32),
            jax.ShapeDtypeStruct((3, middle), jnp.float32),
        ),
        in_specs=vmem_specs(10),
        out_specs=tuple(vmem_specs(2)),
        scratch_shapes=[pltpu.VMEM((frames, rows + 2, width, middle), jnp.bfloat16)],
        compiler_params=params(),
        cost_estimate=cost(2_000_000_000, 1_000_000),
        name="conv_mid_own_frames",
    )(
        hidden,
        moments_mid,
        norm_gain_mid.reshape(1, middle),
        norm_shift_mid.reshape(1, middle),
        conv_mid_weight,
        conv_mid_bias.reshape(1, outputs),
        features,
        other,
        skip_weight,
        skip_bias.reshape(1, outputs),
    )
    return pl.pallas_call(
        functools.partial(last_kernel, tiles),
        out_shape=jax.ShapeDtypeStruct((frames, rows, own, outputs), jnp.bfloat16),
        in_specs=vmem_specs(5),
        out_specs=pl.BlockSpec(memory_space=pltpu.VMEM),
        scratch_shapes=[pltpu.VMEM((frames, rows + 2, width, middle), jnp.bfloat16)],
        compiler_params=params(),
        cost_estimate=cost(2_000_000_000, 1_000_000),
        name="conv_mid_previous_frames",
    )(hidden, before, norm_mid, conv_mid_weight, part)


def solution(mesh):
    in_specs = (P("tm", "tile", None, "section"),) + (P(),) * 10
    out_specs = P("tm", "tile", "section", None)
    return jax.shard_map(shards, mesh=mesh, in_specs=in_specs, out_specs=out_specs, check_vma=False)
```

```python
import functools

import jax
import jax.numpy as jnp
from jax import lax
from jax.experimental import pallas as pl
from jax.experimental.pallas import tpu as pltpu
from jax.sharding import PartitionSpec as P

GROUPS = 32
AXES = ("section", "tm", "tile")
VMEM_LIMIT = 48 * 1024 * 1024
RIM = 16


def params():
    return pltpu.CompilerParams(vmem_limit_bytes=VMEM_LIMIT)


def cost(flops, moved):
    return pl.CostEstimate(flops=flops, bytes_accessed=moved, transcendentals=0)


def vmem_specs(count):
    return [pl.BlockSpec(memory_space=pltpu.VMEM)] * count


def silu(u):
    half = 0.5 * u
    return half + half * jnp.tanh(half)


def moments_of(cells):
    mean = jnp.sum(cells, axis=0, keepdims=True) * (1.0 / cells.shape[0])
    off = cells - mean
    return jnp.concatenate([mean, jnp.sum(off * off, axis=0, keepdims=True)], axis=0)


def group_matrix(channels, width):
    shape = (channels, channels)
    row = lax.broadcasted_iota(jnp.int32, shape, 0) // width
    col = lax.broadcasted_iota(jnp.int32, shape, 1) // width
    return jnp.where(row == col, 1.0, 0.0).astype(jnp.float32)


def group_sum(values, matrix):
    tall = jnp.broadcast_to(values, (8, values.shape[-1]))
    return jnp.dot(
        tall, matrix, preferred_element_type=jnp.float32, precision=lax.Precision.HIGHEST
    )[:1]


def scale_and_offset(moments, cells, width, gain, shift):
    devices, _, channels = moments.shape
    matrix = group_matrix(channels, width)
    means = moments[:, 0, :]
    mean = group_sum(jnp.sum(means, axis=0, keepdims=True), matrix) * (1.0 / (devices * width))
    off = means - mean
    total = jnp.sum(moments[:, 1, :] + float(cells) * (off * off), axis=0, keepdims=True)
    spread = group_sum(total, matrix) * (1.0 / (cells * devices * width))
    scale = lax.rsqrt(spread + 1e-6) * gain
    return mean, scale, shift


def apply_norm(values, norm):
    mean, scale, shift = norm
    return silu((values.astype(jnp.float32) - mean) * scale + shift).astype(jnp.bfloat16)


def first_kernel(pairs, x_ref, moments_ref, *edge_refs):
    x = x_ref[...]
    cells = x.astype(jnp.float32).reshape(-1, x.shape[-1])
    moments_ref[...] = jnp.broadcast_to(moments_of(cells)[None], moments_ref.shape)
    rows = x_ref.shape[1]
    if pairs:
        first = (rows - 2) * (1 - lax.axis_index("tile"))
        edge_refs[0][...] = x_ref[:, pl.ds(first, 2)]
    else:
        edge_refs[0][...] = x_ref[:, :2]
        edge_refs[1][...] = x_ref[:, -2:]


def scales_kernel(cells, moments_ref, gain_ref, shift_ref, norm_ref):
    sections, half = gain_ref.shape
    per_section = moments_ref.shape[0] // sections
    for k in range(sections):
        norm = scale_and_offset(
            moments_ref[k * per_section : (k + 1) * per_section],
            cells,
            sections * half // GROUPS,
            gain_ref[k : k + 1],
            shift_ref[k : k + 1],
        )
        norm_ref[k] = jnp.concatenate(norm, axis=0)


def conv_rows(act_ref, weight_ref, frames, rows, width):
    total = None
    for t, frame in enumerate(frames):
        for h in range(3) if frame is not None else ():
            cells = act_ref[frame, h : h + rows]
            cells = cells.reshape(rows * width, cells.shape[-1])
            taps = jnp.concatenate([weight_ref[t, h, w] for w in range(3)], axis=-1)
            part = jnp.dot(cells, taps, preferred_element_type=jnp.float32)
            total = part if total is None else total + part
    outputs = weight_ref.shape[-1]
    total = total.reshape(rows, width, 3 * outputs)
    before, middle, after = (total[..., k * outputs : (k + 1) * outputs] for k in range(3))
    before = jnp.concatenate([before[:, :1], before[:, :-1]], axis=1)
    after = jnp.concatenate([after[:, 1:], after[:, -1:]], axis=1)
    return middle + before + after


def middle_kernel(
    tiles,
    x_ref,
    prev_ref,
    up_ref,
    down_ref,
    up_prev_ref,
    down_prev_ref,
    other_x_ref,
    other_prev_ref,
    other_up_ref,
    other_down_ref,
    other_up_prev_ref,
    other_down_prev_ref,
    norm_ref,
    weight_ref,
    bias_ref,
    hidden_ref,
    out_moments_ref,
    act_ref,
):
    section, tm, tile = (lax.axis_index(axis) for axis in AXES)
    frames, rows, columns, half = x_ref.shape
    width = columns // 2 + RIM
    first = pl.multiple_of(section * (columns - width), RIM)
    cols = pl.ds(first, width)
    pieces = (
        (
            section,
            ((x_ref, up_ref, down_ref), (prev_ref, up_prev_ref, down_prev_ref)),
        ),
        (
            1 - section,
            (
                (other_x_ref, other_up_ref, other_down_ref),
                (other_prev_ref, other_up_prev_ref, other_down_prev_ref),
            ),
        ),
    )
    for which, (now, before) in pieces:
        norm = tuple(norm_ref[which, k : k + 1] for k in range(3))
        lanes = pl.ds(pl.multiple_of(which * half, half), half)
        for start, (body, up, down) in ((frames, now), (0, before)):
            for f in range(frames):
                act_ref[start + f, 2 : 2 + rows, :, lanes] = apply_norm(body[f, :, cols, :], norm)
                act_ref[start + f, 0:2, :, lanes] = apply_norm(up[f, :, cols, :], norm)
                act_ref[start + f, 2 + rows :, :, lanes] = apply_norm(down[f, :, cols, :], norm)

    @pl.when(tile == 0)
    def _():
        for f in range(2 * frames):
            act_ref[f, 1] = act_ref[f, 2]

    @pl.when(tile == tiles - 1)
    def _():
        for f in range(2 * frames):
            act_ref[f, rows + 2] = act_ref[f, rows + 1]

    @pl.when(tm == 0)
    def _():
        for f in range(frames):
            act_ref[f] = act_ref[frames]

    own = columns // 2
    for f in range(frames):
        hidden = conv_rows(act_ref, weight_ref, (f, f + 1, f + 2), rows + 2, width)
        hidden_ref[f] = (hidden + bias_ref[...]).astype(jnp.bfloat16)

    cells = hidden_ref[:, 1 : 1 + rows, pl.ds(first, own), :]
    cells = cells.astype(jnp.float32).reshape(-1, cells.shape[-1])
    out_moments_ref[...] = jnp.broadcast_to(moments_of(cells)[None], out_moments_ref.shape)


def sent_start(tiles, tile):
    return 1 - tile if tiles == 2 else 0


def pack_kernel(tiles, hidden_ref, sent_ref):
    section, tile = lax.axis_index("section"), lax.axis_index("tile")
    frames, padded, width, channels = hidden_ref.shape
    own = sent_ref.shape[2]
    first = pl.multiple_of(section * (width - own), RIM)
    sent_rows = sent_ref.shape[1] - 1
    top = sent_start(tiles, tile)
    for f in range(frames):
        sent_ref[f, :sent_rows] = hidden_ref[f, pl.ds(top, sent_rows), pl.ds(first, own), :]
        hidden = hidden_ref[f].astype(jnp.float32)
        rim = jnp.where(section == 0, hidden[:, own, :], hidden[:, width - own - 1, :])
        spare = jnp.zeros((own - padded, channels), jnp.float32)
        sent_ref[f, sent_rows] = jnp.concatenate([rim, spare], axis=0).astype(jnp.bfloat16)


def repeat_edges(act_ref, count, tiles, rows):
    tile = lax.axis_index("tile")

    @pl.when(tile == 0)
    def _():
        for f in range(count):
            act_ref[f, 0] = act_ref[f, 1]

    @pl.when(tile == tiles - 1)
    def _():
        for f in range(count):
            act_ref[f, rows + 1] = act_ref[f, rows]


def own_columns(values, own):
    section = lax.axis_index("section")
    width = values.shape[1]
    return jnp.where(section == 0, values[:, :own], values[:, width - own :])


def own_frames_kernel(
    tiles,
    hidden_ref,
    moments_ref,
    gain_ref,
    shift_ref,
    weight_ref,
    bias_ref,
    x_ref,
    other_x_ref,
    skip_ref,
    skip_bias_ref,
    part_ref,
    norm_ref,
    act_ref,
):
    section = lax.axis_index("section")
    frames, padded, width, outputs = hidden_ref.shape
    rows = padded - 2
    half = x_ref.shape[3]
    own = x_ref.shape[2] // 2
    norm = scale_and_offset(
        moments_ref[...],
        frames * rows * own,
        outputs // GROUPS,
        gain_ref[...],
        shift_ref[...],
    )
    norm_ref[...] = jnp.concatenate(norm, axis=0)
    for f in range(frames):
        act_ref[f] = apply_norm(hidden_ref[f], norm)
    repeat_edges(act_ref, frames, tiles, rows)
    mine = pl.ds(pl.multiple_of(section * own, own), own)
    skip_here = skip_ref[pl.ds(pl.multiple_of(section * half, half), half), :]
    skip_there = skip_ref[pl.ds(pl.multiple_of((1 - section) * half, half), half), :]
    for f in range(frames):
        taps = [k if k >= 0 else None for k in range(f - 2, f + 1)]
        residual = own_columns(conv_rows(act_ref, weight_ref, taps, rows, width), own)
        here = x_ref[f, :, mine, :].reshape(rows * own, half)
        there = other_x_ref[f, :, mine, :].reshape(rows * own, half)
        shortcut = jnp.dot(here, skip_here, preferred_element_type=jnp.float32)
        shortcut = shortcut + jnp.dot(there, skip_there, preferred_element_type=jnp.float32)
        part_ref[f] = (residual + bias_ref[...]) + (
            shortcut.reshape(rows, own, outputs) + skip_bias_ref[...]
        )


def last_kernel(
    tiles, hidden_ref, before_ref, norm_ref, weight_ref, part_ref, out_ref, act_ref
):
    section, tm, tile = (lax.axis_index(axis) for axis in AXES)
    frames, padded, width, outputs = hidden_ref.shape
    rows = padded - 2
    own = part_ref.shape[2]
    sent_rows = before_ref.shape[1] - 1
    top = sent_start(tiles, tile)
    first = pl.multiple_of(section * (width - own), RIM)
    beside = pl.multiple_of((1 - section) * own, RIM)
    norm = tuple(norm_ref[k : k + 1] for k in range(3))
    for f in range(frames):
        act_ref[f, pl.ds(top, sent_rows), pl.ds(first, own), :] = apply_norm(
            before_ref[f, :sent_rows], norm
        )
        rim = apply_norm(before_ref[f, sent_rows], norm).astype(jnp.float32)[:padded]
        rim = jnp.broadcast_to(rim[:, None, :], (padded, width - own, outputs))
        act_ref[f, :, pl.ds(beside, width - own), :] = rim.astype(jnp.bfloat16)

    @pl.when(tm == 0)
    def _():
        start = apply_norm(hidden_ref[0], norm)
        for f in range(frames):
            act_ref[f] = start

    repeat_edges(act_ref, frames, tiles, rows)
    for f in range(frames):
        taps = [k if k < frames else None for k in range(f, f + 3)]
        residual = own_columns(conv_rows(act_ref, weight_ref, taps, rows, width), own)
        out_ref[f] = (part_ref[f] + residual).astype(jnp.bfloat16)


def pairs_for(tm_count, tile_count, tm_step, tile_step):
    out = []
    for a in range(tm_count):
        for b in range(tile_count):
            c, d = a + tm_step, b + tile_step
            if 0 <= c < tm_count and 0 <= d < tile_count:
                out.append((a * tile_count + b, c * tile_count + d))
    return out


def to_everyone(moments):
    return lax.all_to_all(moments, AXES, 0, 0, tiled=True)


def shards(
    features,
    norm_gain_in,
    norm_shift_in,
    conv_in_weight,
    conv_in_bias,
    norm_gain_mid,
    norm_shift_mid,
    conv_mid_weight,
    conv_mid_bias,
    skip_weight,
    skip_bias,
):
    sections, tms, tiles = (lax.axis_size(axis) for axis in AXES)
    parties = sections * tms * tiles
    frames, rows, columns, half = features.shape
    own = columns // sections
    width = own + RIM
    middle = conv_in_weight.shape[-1]
    outputs = conv_mid_weight.shape[-1]
    grid_axes = ("tm", "tile")

    def shift(value, tm_step, tile_step):
        return lax.ppermute(value, grid_axes, pairs_for(tms, tiles, tm_step, tile_step))

    def swap(value):
        return lax.ppermute(value, "section", [(0, 1), (1, 0)])

    previous = shift(features, 1, 0)
    edge = jax.ShapeDtypeStruct((frames, 2, columns, half), features.dtype)
    edges = 1 if tiles == 2 else 2
    moments, *edge_rows = pl.pallas_call(
        functools.partial(first_kernel, tiles == 2),
        out_shape=(jax.ShapeDtypeStruct((parties, 2, half), jnp.float32),) + (edge,) * edges,
        in_specs=vmem_specs(1),
        out_specs=tuple(vmem_specs(1 + edges)),
        compiler_params=params(),
        cost_estimate=cost(1_000_000_000, 1_000_000),
        name="feature_moments",
    )(features)
    if tiles == 2:
        (facing,) = edge_rows
        crossing = [
            (a * 2 + b, (a + 1) * 2 + 1 - b) for a in range(tms - 1) for b in range(2)
        ]
        rims = [
            lax.ppermute(facing, "tile", [(0, 1), (1, 0)]),
            lax.ppermute(facing, grid_axes, crossing),
        ]
    else:
        top, bottom = edge_rows
        rims = [
            shift(bottom, 0, 1),
            shift(bottom, 1, 1),
            shift(top, 0, -1),
            shift(top, 1, -1),
        ]
    other = swap(features)
    moments = to_everyone(moments)
    norm_in = pl.pallas_call(
        functools.partial(scales_kernel, frames * rows * columns),
        out_shape=jax.ShapeDtypeStruct((sections, 3, half), jnp.float32),
        in_specs=vmem_specs(3),
        out_specs=pl.BlockSpec(memory_space=pltpu.VMEM),
        compiler_params=params(),
        cost_estimate=cost(1_000_000_000, 1_000_000),
        name="feature_scales",
    )(moments, norm_gain_in.reshape(sections, half), norm_shift_in.reshape(sections, half))
    previous, norm_in, *rims = lax.optimization_barrier((previous, norm_in, *rims))
    other_previous = swap(previous)
    other_rims = [swap(rim) for rim in rims]
    up, up_prev, down, down_prev = (rims * 2)[:4]
    other_up, other_up_prev, other_down, other_down_prev = (other_rims * 2)[:4]

    sent_rows = rows + (1 if tiles == 2 else 2)
    hidden, moments_mid = pl.pallas_call(
        functools.partial(middle_kernel, tiles),
        out_shape=(
            jax.ShapeDtypeStruct((frames, rows + 2, width, middle), jnp.bfloat16),
            jax.ShapeDtypeStruct((parties, 2, middle), jnp.float32),
        ),
        in_specs=vmem_specs(15),
        out_specs=tuple(vmem_specs(2)),
        scratch_shapes=[pltpu.VMEM((2 * frames, rows + 4, width, 2 * half), jnp.bfloat16)],
        compiler_params=params(),
        cost_estimate=cost(4_000_000_000, 1_000_000),
        name="norm_conv_in",
    )(
        features,
        previous,
        up,
        down,
        up_prev,
        down_prev,
        other,
        other_previous,
        other_up,
        other_down,
        other_up_prev,
        other_down_prev,
        norm_in,
        conv_in_weight,
        conv_in_bias.reshape(1, middle),
    )
    moments_mid = to_everyone(moments_mid)
    sent = pl.pallas_call(
        functools.partial(pack_kernel, tiles),
        out_shape=jax.ShapeDtypeStruct((frames, sent_rows + 1, own, middle), jnp.bfloat16),
        in_specs=vmem_specs(1),
        out_specs=pl.BlockSpec(memory_space=pltpu.VMEM),
        compiler_params=params(),
        cost_estimate=cost(1_000_000_000, 1_000_000),
        name="pack_hidden",
    )(hidden)
    before = shift(sent, 1, 0)
    part, norm_mid = pl.pallas_call(
        functools.partial(own_frames_kernel, tiles),
        out_shape=(
            jax.ShapeDtypeStruct((frames, rows, own, outputs), jnp.float32),
            jax.ShapeDtypeStruct((3, middle), jnp.float32),
        ),
        in_specs=vmem_specs(10),
        out_specs=tuple(vmem_specs(2)),
        scratch_shapes=[pltpu.VMEM((frames, rows + 2, width, middle), jnp.bfloat16)],
        compiler_params=params(),
        cost_estimate=cost(2_000_000_000, 1_000_000),
        name="conv_mid_own_frames",
    )(
        hidden,
        moments_mid,
        norm_gain_mid.reshape(1, middle),
        norm_shift_mid.reshape(1, middle),
        conv_mid_weight,
        conv_mid_bias.reshape(1, outputs),
        features,
        other,
        skip_weight,
        skip_bias.reshape(1, outputs),
    )
    return pl.pallas_call(
        functools.partial(last_kernel, tiles),
        out_shape=jax.ShapeDtypeStruct((frames, rows, own, outputs), jnp.bfloat16),
        in_specs=vmem_specs(5),
        out_specs=pl.BlockSpec(memory_space=pltpu.VMEM),
        scratch_shapes=[pltpu.VMEM((frames, rows + 2, width, middle), jnp.bfloat16)],
        compiler_params=params(),
        cost_estimate=cost(2_000_000_000, 1_000_000),
        name="conv_mid_previous_frames",
    )(hidden, before, norm_mid, conv_mid_weight, part)


def solution(mesh):
    in_specs = (P("tm", "tile", None, "section"),) + (P(),) * 10
    out_specs = P("tm", "tile", "section", None)
    return jax.shard_map(shards, mesh=mesh, in_specs=in_specs, out_specs=out_specs, check_vma=False)
```

```python
import functools

import jax
import jax.numpy as jnp
from jax import lax
from jax.experimental import pallas as pl
from jax.experimental.pallas import tpu as pltpu
from jax.sharding import PartitionSpec as P

GROUPS = 32
AXES = ("section", "tm", "tile")
VMEM_LIMIT = 48 * 1024 * 1024
RIM = 16


def params():
    return pltpu.CompilerParams(vmem_limit_bytes=VMEM_LIMIT)


def cost(flops, moved):
    return pl.CostEstimate(flops=flops, bytes_accessed=moved, transcendentals=0)


def vmem_specs(count):
    return [pl.BlockSpec(memory_space=pltpu.VMEM)] * count


def silu(u):
    half = 0.5 * u
    return half + half * jnp.tanh(half)


def moments_of(cells):
    mean = jnp.sum(cells, axis=0, keepdims=True) * (1.0 / cells.shape[0])
    off = cells - mean
    return jnp.concatenate([mean, jnp.sum(off * off, axis=0, keepdims=True)], axis=0)


def group_matrix(channels, width):
    shape = (channels, channels)
    row = lax.broadcasted_iota(jnp.int32, shape, 0) // width
    col = lax.broadcasted_iota(jnp.int32, shape, 1) // width
    return jnp.where(row == col, 1.0, 0.0).astype(jnp.float32)


def group_sum(values, matrix):
    tall = jnp.broadcast_to(values, (8, values.shape[-1]))
    return jnp.dot(
        tall, matrix, preferred_element_type=jnp.float32, precision=lax.Precision.HIGHEST
    )[:1]


def scale_and_offset(moments, cells, width, gain, shift):
    devices, _, channels = moments.shape
    matrix = group_matrix(channels, width)
    means = moments[:, 0, :]
    mean = group_sum(jnp.sum(means, axis=0, keepdims=True), matrix) * (1.0 / (devices * width))
    off = means - mean
    total = jnp.sum(moments[:, 1, :] + float(cells) * (off * off), axis=0, keepdims=True)
    spread = group_sum(total, matrix) * (1.0 / (cells * devices * width))
    scale = lax.rsqrt(spread + 1e-6) * gain
    return mean, scale, shift


def apply_norm(values, norm):
    mean, scale, shift = norm
    return silu((values.astype(jnp.float32) - mean) * scale + shift).astype(jnp.bfloat16)


def first_kernel(x_ref, moments_ref):
    x = x_ref[...]
    cells = x.astype(jnp.float32).reshape(-1, x.shape[-1])
    moments_ref[...] = jnp.broadcast_to(moments_of(cells)[None], moments_ref.shape)


def rows_kernel(pairs, x_ref, prev_ref, *edge_refs):
    frames, rows = x_ref.shape[:2]
    if pairs:
        starts = [(rows - 2) * (1 - lax.axis_index("tile"))]
    else:
        starts = [0, rows - 2]
    for start, edge_ref in zip(starts, edge_refs):
        edge_ref[:frames] = prev_ref[:, pl.ds(start, 2)]
        edge_ref[frames:] = x_ref[:, pl.ds(start, 2)]


def scales_kernel(cells, moments_ref, gain_ref, shift_ref, norm_ref):
    sections, half = gain_ref.shape
    per_section = moments_ref.shape[0] // sections
    for k in range(sections):
        norm = scale_and_offset(
            moments_ref[k * per_section : (k + 1) * per_section],
            cells,
            sections * half // GROUPS,
            gain_ref[k : k + 1],
            shift_ref[k : k + 1],
        )
        norm_ref[k] = jnp.concatenate(norm, axis=0)


def conv_rows(act_ref, weight_ref, frames, rows, width):
    total = None
    for t, frame in enumerate(frames):
        for h in range(3) if frame is not None else ():
            cells = act_ref[frame, h : h + rows]
            cells = cells.reshape(rows * width, cells.shape[-1])
            taps = jnp.concatenate([weight_ref[t, h, w] for w in range(3)], axis=-1)
            part = jnp.dot(cells, taps, preferred_element_type=jnp.float32)
            total = part if total is None else total + part
    outputs = weight_ref.shape[-1]
    total = total.reshape(rows, width, 3 * outputs)
    before, middle, after = (total[..., k * outputs : (k + 1) * outputs] for k in range(3))
    before = jnp.concatenate([before[:, :1], before[:, :-1]], axis=1)
    after = jnp.concatenate([after[:, 1:], after[:, -1:]], axis=1)
    return middle + before + after


def middle_kernel(
    tiles,
    x_ref,
    prev_ref,
    up_ref,
    down_ref,
    other_x_ref,
    other_prev_ref,
    other_up_ref,
    other_down_ref,
    norm_ref,
    weight_ref,
    bias_ref,
    hidden_ref,
    out_moments_ref,
    act_ref,
):
    section, tm, tile = (lax.axis_index(axis) for axis in AXES)
    frames, rows, columns, half = x_ref.shape
    width = columns // 2 + RIM
    first = pl.multiple_of(section * (columns - width), RIM)
    cols = pl.ds(first, width)
    pieces = (
        (section, prev_ref, x_ref, up_ref, down_ref),
        (1 - section, other_prev_ref, other_x_ref, other_up_ref, other_down_ref),
    )
    for which, before, now, up, down in pieces:
        norm = tuple(norm_ref[which, k : k + 1] for k in range(3))
        lanes = pl.ds(pl.multiple_of(which * half, half), half)
        for f in range(2 * frames):
            body = before[f, :, cols, :] if f < frames else now[f - frames, :, cols, :]
            act_ref[f, 2 : 2 + rows, :, lanes] = apply_norm(body, norm)
            act_ref[f, 0:2, :, lanes] = apply_norm(up[f, :, cols, :], norm)
            act_ref[f, 2 + rows :, :, lanes] = apply_norm(down[f, :, cols, :], norm)

    @pl.when(tile == 0)
    def _():
        for f in range(2 * frames):
            act_ref[f, 1] = act_ref[f, 2]

    @pl.when(tile == tiles - 1)
    def _():
        for f in range(2 * frames):
            act_ref[f, rows + 2] = act_ref[f, rows + 1]

    @pl.when(tm == 0)
    def _():
        for f in range(frames):
            act_ref[f] = act_ref[frames]

    own = columns // 2
    for f in range(frames):
        hidden = conv_rows(act_ref, weight_ref, (f, f + 1, f + 2), rows + 2, width)
        hidden_ref[f] = (hidden + bias_ref[...]).astype(jnp.bfloat16)

    cells = hidden_ref[:, 1 : 1 + rows, pl.ds(first, own), :]
    cells = cells.astype(jnp.float32).reshape(-1, cells.shape[-1])
    out_moments_ref[...] = jnp.broadcast_to(moments_of(cells)[None], out_moments_ref.shape)


def sent_start(tiles, tile):
    return 1 - tile if tiles == 2 else 0


def pack_kernel(tiles, hidden_ref, sent_ref):
    section, tile = lax.axis_index("section"), lax.axis_index("tile")
    frames, padded, width, channels = hidden_ref.shape
    own = sent_ref.shape[2]
    first = pl.multiple_of(section * (width - own), RIM)
    sent_rows = sent_ref.shape[1] - 1
    top = sent_start(tiles, tile)
    for f in range(frames):
        sent_ref[f, :sent_rows] = hidden_ref[f, pl.ds(top, sent_rows), pl.ds(first, own), :]
        hidden = hidden_ref[f].astype(jnp.float32)
        rim = jnp.where(section == 0, hidden[:, own, :], hidden[:, width - own - 1, :])
        spare = jnp.zeros((own - padded, channels), jnp.float32)
        sent_ref[f, sent_rows] = jnp.concatenate([rim, spare], axis=0).astype(jnp.bfloat16)


def repeat_edges(act_ref, count, tiles, rows):
    tile = lax.axis_index("tile")

    @pl.when(tile == 0)
    def _():
        for f in range(count):
            act_ref[f, 0] = act_ref[f, 1]

    @pl.when(tile == tiles - 1)
    def _():
        for f in range(count):
            act_ref[f, rows + 1] = act_ref[f, rows]


def own_columns(values, own):
    section = lax.axis_index("section")
    width = values.shape[1]
    return jnp.where(section == 0, values[:, :own], values[:, width - own :])


def own_frames_kernel(
    tiles,
    hidden_ref,
    moments_ref,
    gain_ref,
    shift_ref,
    weight_ref,
    bias_ref,
    x_ref,
    other_x_ref,
    skip_ref,
    skip_bias_ref,
    part_ref,
    norm_ref,
    act_ref,
):
    section = lax.axis_index("section")
    frames, padded, width, outputs = hidden_ref.shape
    rows = padded - 2
    half = x_ref.shape[3]
    own = x_ref.shape[2] // 2
    norm = scale_and_offset(
        moments_ref[...],
        frames * rows * own,
        outputs // GROUPS,
        gain_ref[...],
        shift_ref[...],
    )
    norm_ref[...] = jnp.concatenate(norm, axis=0)
    for f in range(frames):
        act_ref[f] = apply_norm(hidden_ref[f], norm)
    repeat_edges(act_ref, frames, tiles, rows)
    mine = pl.ds(pl.multiple_of(section * own, own), own)
    skip_here = skip_ref[pl.ds(pl.multiple_of(section * half, half), half), :]
    skip_there = skip_ref[pl.ds(pl.multiple_of((1 - section) * half, half), half), :]
    for f in range(frames):
        taps = [k if k >= 0 else None for k in range(f - 2, f + 1)]
        residual = own_columns(conv_rows(act_ref, weight_ref, taps, rows, width), own)
        here = x_ref[f, :, mine, :].reshape(rows * own, half)
        there = other_x_ref[f, :, mine, :].reshape(rows * own, half)
        shortcut = jnp.dot(here, skip_here, preferred_element_type=jnp.float32)
        shortcut = shortcut + jnp.dot(there, skip_there, preferred_element_type=jnp.float32)
        part_ref[f] = (residual + bias_ref[...]) + (
            shortcut.reshape(rows, own, outputs) + skip_bias_ref[...]
        )


def last_kernel(
    tiles, hidden_ref, before_ref, norm_ref, weight_ref, part_ref, out_ref, act_ref
):
    section, tm, tile = (lax.axis_index(axis) for axis in AXES)
    frames, padded, width, outputs = hidden_ref.shape
    rows = padded - 2
    own = part_ref.shape[2]
    sent_rows = before_ref.shape[1] - 1
    top = sent_start(tiles, tile)
    first = pl.multiple_of(section * (width - own), RIM)
    beside = pl.multiple_of((1 - section) * own, RIM)
    norm = tuple(norm_ref[k : k + 1] for k in range(3))
    for f in range(frames):
        act_ref[f, pl.ds(top, sent_rows), pl.ds(first, own), :] = apply_norm(
            before_ref[f, :sent_rows], norm
        )
        rim = apply_norm(before_ref[f, sent_rows], norm).astype(jnp.float32)[:padded]
        rim = jnp.broadcast_to(rim[:, None, :], (padded, width - own, outputs))
        act_ref[f, :, pl.ds(beside, width - own), :] = rim.astype(jnp.bfloat16)

    @pl.when(tm == 0)
    def _():
        start = apply_norm(hidden_ref[0], norm)
        for f in range(frames):
            act_ref[f] = start

    repeat_edges(act_ref, frames, tiles, rows)
    for f in range(frames):
        taps = [k if k < frames else None for k in range(f, f + 3)]
        residual = own_columns(conv_rows(act_ref, weight_ref, taps, rows, width), own)
        out_ref[f] = (part_ref[f] + residual).astype(jnp.bfloat16)


def pairs_for(tm_count, tile_count, tm_step, tile_step):
    out = []
    for a in range(tm_count):
        for b in range(tile_count):
            c, d = a + tm_step, b + tile_step
            if 0 <= c < tm_count and 0 <= d < tile_count:
                out.append((a * tile_count + b, c * tile_count + d))
    return out


def to_everyone(moments):
    return lax.all_to_all(moments, AXES, 0, 0, tiled=True)


def shards(
    features,
    norm_gain_in,
    norm_shift_in,
    conv_in_weight,
    conv_in_bias,
    norm_gain_mid,
    norm_shift_mid,
    conv_mid_weight,
    conv_mid_bias,
    skip_weight,
    skip_bias,
):
    sections, tms, tiles = (lax.axis_size(axis) for axis in AXES)
    parties = sections * tms * tiles
    frames, rows, columns, half = features.shape
    own = columns // sections
    width = own + RIM
    middle = conv_in_weight.shape[-1]
    outputs = conv_mid_weight.shape[-1]
    grid_axes = ("tm", "tile")

    def shift(value, tm_step, tile_step):
        return lax.ppermute(value, grid_axes, pairs_for(tms, tiles, tm_step, tile_step))

    def swap(value):
        return lax.ppermute(value, "section", [(0, 1), (1, 0)])

    previous = shift(features, 1, 0)
    moments = pl.pallas_call(
        first_kernel,
        out_shape=jax.ShapeDtypeStruct((parties, 2, half), jnp.float32),
        in_specs=vmem_specs(1),
        out_specs=pl.BlockSpec(memory_space=pltpu.VMEM),
        compiler_params=params(),
        cost_estimate=cost(1_000_000_000, 1_000_000),
        name="feature_moments",
    )(features)
    moments = to_everyone(moments)
    other = swap(features)
    edges = 1 if tiles == 2 else 2
    edge_rows = pl.pallas_call(
        functools.partial(rows_kernel, tiles == 2),
        out_shape=(jax.ShapeDtypeStruct((2 * frames, 2, columns, half), features.dtype),) * edges,
        in_specs=vmem_specs(2),
        out_specs=tuple(vmem_specs(edges)),
        compiler_params=params(),
        cost_estimate=cost(500_000_000, 1_000_000),
        name="facing_rows",
    )(features, previous)
    if tiles == 2:
        rims = [lax.ppermute(edge_rows[0], "tile", [(0, 1), (1, 0)])]
    else:
        rims = [shift(edge_rows[1], 0, 1), shift(edge_rows[0], 0, -1)]
    other_previous = swap(previous)
    norm_in = pl.pallas_call(
        functools.partial(scales_kernel, frames * rows * columns),
        out_shape=jax.ShapeDtypeStruct((sections, 3, half), jnp.float32),
        in_specs=vmem_specs(3),
        out_specs=pl.BlockSpec(memory_space=pltpu.VMEM),
        compiler_params=params(),
        cost_estimate=cost(1_000_000_000, 1_000_000),
        name="feature_scales",
    )(moments, norm_gain_in.reshape(sections, half), norm_shift_in.reshape(sections, half))
    norm_in, *rims = lax.optimization_barrier((norm_in, *rims))
    other_rims = [swap(rim) for rim in rims]
    up, down = (rims * 2)[:2]
    other_up, other_down = (other_rims * 2)[:2]

    sent_rows = rows + (1 if tiles == 2 else 2)
    hidden, moments_mid = pl.pallas_call(
        functools.partial(middle_kernel, tiles),
        out_shape=(
            jax.ShapeDtypeStruct((frames, rows + 2, width, middle), jnp.bfloat16),
            jax.ShapeDtypeStruct((parties, 2, middle), jnp.float32),
        ),
        in_specs=vmem_specs(11),
        out_specs=tuple(vmem_specs(2)),
        scratch_shapes=[pltpu.VMEM((2 * frames, rows + 4, width, 2 * half), jnp.bfloat16)],
        compiler_params=params(),
        cost_estimate=cost(4_000_000_000, 1_000_000),
        name="norm_conv_in",
    )(
        features,
        previous,
        up,
        down,
        other,
        other_previous,
        other_up,
        other_down,
        norm_in,
        conv_in_weight,
        conv_in_bias.reshape(1, middle),
    )
    moments_mid = to_everyone(moments_mid)
    sent = pl.pallas_call(
        functools.partial(pack_kernel, tiles),
        out_shape=jax.ShapeDtypeStruct((frames, sent_rows + 1, own, middle), jnp.bfloat16),
        in_specs=vmem_specs(1),
        out_specs=pl.BlockSpec(memory_space=pltpu.VMEM),
        compiler_params=params(),
        cost_estimate=cost(1_000_000_000, 1_000_000),
        name="pack_hidden",
    )(hidden)
    before = shift(sent, 1, 0)
    part, norm_mid = pl.pallas_call(
        functools.partial(own_frames_kernel, tiles),
        out_shape=(
            jax.ShapeDtypeStruct((frames, rows, own, outputs), jnp.float32),
            jax.ShapeDtypeStruct((3, middle), jnp.float32),
        ),
        in_specs=vmem_specs(10),
        out_specs=tuple(vmem_specs(2)),
        scratch_shapes=[pltpu.VMEM((frames, rows + 2, width, middle), jnp.bfloat16)],
        compiler_params=params(),
        cost_estimate=cost(2_000_000_000, 1_000_000),
        name="conv_mid_own_frames",
    )(
        hidden,
        moments_mid,
        norm_gain_mid.reshape(1, middle),
        norm_shift_mid.reshape(1, middle),
        conv_mid_weight,
        conv_mid_bias.reshape(1, outputs),
        features,
        other,
        skip_weight,
        skip_bias.reshape(1, outputs),
    )
    return pl.pallas_call(
        functools.partial(last_kernel, tiles),
        out_shape=jax.ShapeDtypeStruct((frames, rows, own, outputs), jnp.bfloat16),
        in_specs=vmem_specs(5),
        out_specs=pl.BlockSpec(memory_space=pltpu.VMEM),
        scratch_shapes=[pltpu.VMEM((frames, rows + 2, width, middle), jnp.bfloat16)],
        compiler_params=params(),
        cost_estimate=cost(2_000_000_000, 1_000_000),
        name="conv_mid_previous_frames",
    )(hidden, before, norm_mid, conv_mid_weight, part)


def solution(mesh):
    in_specs = (P("tm", "tile", None, "section"),) + (P(),) * 10
    out_specs = P("tm", "tile", "section", None)
    return jax.shard_map(shards, mesh=mesh, in_specs=in_specs, out_specs=out_specs, check_vma=False)
```

```python
import functools

import jax
import jax.numpy as jnp
from jax import lax
from jax.experimental import pallas as pl
from jax.experimental.pallas import tpu as pltpu
from jax.sharding import PartitionSpec as P

GROUPS = 32
AXES = ("section", "tm", "tile")
VMEM_LIMIT = 48 * 1024 * 1024
FULL_LIMIT = 63 * 1024 * 1024
RIM = 16


def params(limit=VMEM_LIMIT):
    return pltpu.CompilerParams(vmem_limit_bytes=limit)


def cost(flops, moved):
    return pl.CostEstimate(flops=flops, bytes_accessed=moved, transcendentals=0)


def vmem_specs(count):
    return [pl.BlockSpec(memory_space=pltpu.VMEM)] * count


def silu(u):
    half = 0.5 * u
    return half + half * jnp.tanh(half)


def moments_of(cells):
    mean = jnp.sum(cells, axis=0, keepdims=True) * (1.0 / cells.shape[0])
    off = cells - mean
    return jnp.concatenate([mean, jnp.sum(off * off, axis=0, keepdims=True)], axis=0)


def group_matrix(channels, width):
    shape = (channels, channels)
    row = lax.broadcasted_iota(jnp.int32, shape, 0) // width
    col = lax.broadcasted_iota(jnp.int32, shape, 1) // width
    return jnp.where(row == col, 1.0, 0.0).astype(jnp.bfloat16)


def group_sum(values, matrix):
    parts = []
    for _ in range(3):
        part = values.astype(jnp.bfloat16).astype(jnp.float32)
        parts.append(jnp.broadcast_to(part, (8, part.shape[-1])))
        values = values - part
    stacked = jnp.concatenate(parts + [jnp.zeros_like(parts[0])], axis=0).astype(jnp.bfloat16)
    summed = jnp.dot(stacked, matrix, preferred_element_type=jnp.float32)
    return summed[0:1] + summed[8:9] + summed[16:17]


def scale_and_offset(moments, cells, width, gain, shift):
    devices, _, channels = moments.shape
    matrix = group_matrix(channels, width)
    means = moments[:, 0, :]
    mean = group_sum(jnp.sum(means, axis=0, keepdims=True), matrix) * (1.0 / (devices * width))
    off = means - mean
    total = jnp.sum(moments[:, 1, :] + float(cells) * (off * off), axis=0, keepdims=True)
    spread = group_sum(total, matrix) * (1.0 / (cells * devices * width))
    scale = lax.rsqrt(spread + 1e-6) * gain
    return mean, scale, shift


def apply_norm(values, norm):
    mean, scale, shift = norm
    return silu((values.astype(jnp.float32) - mean) * scale + shift).astype(jnp.bfloat16)


def first_kernel(x_hbm, moments_ref, x_ref, sem):
    copy = pltpu.make_async_copy(x_hbm, x_ref, sem)
    copy.start()
    copy.wait()
    x = x_ref[...]
    cells = x.astype(jnp.float32).reshape(-1, x.shape[-1])
    moments_ref[...] = jnp.broadcast_to(moments_of(cells)[None], moments_ref.shape)


def rows_kernel(pairs, x_ref, prev_ref, *edge_refs):
    frames, rows = x_ref.shape[:2]
    if pairs:
        starts = [(rows - 2) * (1 - lax.axis_index("tile"))]
    else:
        starts = [0, rows - 2]
    for start, edge_ref in zip(starts, edge_refs):
        edge_ref[:frames] = prev_ref[:, pl.ds(start, 2)]
        edge_ref[frames:] = x_ref[:, pl.ds(start, 2)]


def scales_kernel(cells, moments_ref, gain_ref, shift_ref, norm_ref):
    sections, half = gain_ref.shape
    per_section = moments_ref.shape[0] // sections
    for k in range(sections):
        norm = scale_and_offset(
            moments_ref[k * per_section : (k + 1) * per_section],
            cells,
            sections * half // GROUPS,
            gain_ref[k : k + 1],
            shift_ref[k : k + 1],
        )
        norm_ref[k] = jnp.concatenate(norm, axis=0)


def column_taps(weight_ref, t, h):
    return jnp.concatenate([weight_ref[t, h, w] for w in range(3)], axis=-1)


def shift_and_add(total, rows, width):
    outputs = total.shape[-1] // 3
    total = total.reshape(rows, width, 3 * outputs)
    before, middle, after = (total[..., k * outputs : (k + 1) * outputs] for k in range(3))
    before = jnp.concatenate([before[:, :1], before[:, :-1]], axis=1)
    after = jnp.concatenate([after[:, 1:], after[:, -1:]], axis=1)
    return middle + before + after


def conv_in_rows(act_ref, weight_ref, frames, top, rows, width):
    totals = [None] * frames
    for a in range(act_ref.shape[0]):
        reached = [f for f in range(frames) if 0 <= a - f <= 2]
        for h in range(3):
            cells = act_ref[a, pl.ds(top + h, rows)]
            cells = cells.reshape(rows * width, cells.shape[-1])
            taps = [column_taps(weight_ref, a - f, h) for f in reached]
            sums = jnp.dot(
                cells, jnp.concatenate(taps, axis=-1), preferred_element_type=jnp.float32
            )
            n = sums.shape[-1] // len(reached)
            for k, f in enumerate(reached):
                part = sums[:, k * n : (k + 1) * n]
                totals[f] = part if totals[f] is None else totals[f] + part
    return [shift_and_add(total, rows, width) for total in totals]


def conv_mid_rows(act_ref, weight_ref, taken, rows, width):
    cells, taps = [], []
    for t, frame in taken:
        for h in range(3):
            block = act_ref[frame, h : h + rows]
            cells.append(block.reshape(rows * width, block.shape[-1]))
            taps.append(column_taps(weight_ref, t, h))
    total = jnp.dot(
        jnp.concatenate(cells, axis=-1),
        jnp.concatenate(taps, axis=0),
        preferred_element_type=jnp.float32,
    )
    return shift_and_add(total, rows, width)


def first_row(tiles, tile):
    return 1 - tile if tiles == 2 else 0


def middle_kernel(tiles, sides, *refs):
    x_ref, prev_ref, other_x_ref, other_prev_ref = refs[:4]
    rim_refs, other_rim_refs = refs[4 : 4 + sides], refs[4 + sides : 4 + 2 * sides]
    norm_ref, weight_ref, bias_ref, hidden_ref, out_moments_ref, act_ref = refs[4 + 2 * sides :]
    section, tm, tile = (lax.axis_index(axis) for axis in AXES)
    frames, rows, columns, half = x_ref.shape
    kept = hidden_ref.shape[1]
    own = columns // 2
    width = own + RIM
    first = pl.multiple_of(section * (columns - width), RIM)
    cols = pl.ds(first, width)
    top = first_row(tiles, tile)
    rim_rows = (0, rows + 2) if sides == 2 else ((rows + 2) * (1 - tile),)
    pieces = (
        (section, prev_ref, x_ref, rim_refs),
        (1 - section, other_prev_ref, other_x_ref, other_rim_refs),
    )
    for which, before, now, rims in pieces:
        norm = tuple(norm_ref[which, k : k + 1] for k in range(3))
        lanes = pl.ds(pl.multiple_of(which * half, half), half)
        for f in range(2 * frames):
            body = before[f, :, cols, :] if f < frames else now[f - frames, :, cols, :]
            act_ref[f, 2 : 2 + rows, :, lanes] = apply_norm(body, norm)
            for row, rim in zip(rim_rows, rims):
                act_ref[f, pl.ds(row, 2), :, lanes] = apply_norm(rim[f, :, cols, :], norm)

    @pl.when(tile == 0)
    def _():
        for f in range(2 * frames):
            act_ref[f, 1] = act_ref[f, 2]

    @pl.when(tile == tiles - 1)
    def _():
        for f in range(2 * frames):
            act_ref[f, rows + 2] = act_ref[f, rows + 1]

    @pl.when(tm == 0)
    def _():
        for f in range(frames):
            act_ref[f] = act_ref[frames]

    for f, hidden in enumerate(conv_in_rows(act_ref, weight_ref, frames, top, kept, width)):
        hidden_ref[f] = (hidden + bias_ref[...]).astype(jnp.bfloat16)

    cells = hidden_ref[:, pl.ds(1 - top, rows), pl.ds(first, own), :]
    cells = cells.astype(jnp.float32).reshape(-1, cells.shape[-1])
    out_moments_ref[...] = jnp.broadcast_to(moments_of(cells)[None], out_moments_ref.shape)


def pack_kernel(hidden_ref, sent_ref):
    section = lax.axis_index("section")
    frames, kept, width, channels = hidden_ref.shape
    own = sent_ref.shape[2]
    first = pl.multiple_of(section * (width - own), RIM)
    for f in range(frames):
        sent_ref[f, :kept] = hidden_ref[f, :, pl.ds(first, own), :]
        hidden = hidden_ref[f].astype(jnp.float32)
        rim = jnp.where(section == 0, hidden[:, own, :], hidden[:, width - own - 1, :])
        spare = jnp.zeros((own - kept, channels), jnp.float32)
        sent_ref[f, kept] = jnp.concatenate([rim, spare], axis=0).astype(jnp.bfloat16)


def repeat_edges(act_ref, count, tiles, rows):
    tile = lax.axis_index("tile")

    @pl.when(tile == 0)
    def _():
        for f in range(count):
            act_ref[f, 0] = act_ref[f, 1]

    @pl.when(tile == tiles - 1)
    def _():
        for f in range(count):
            act_ref[f, rows + 1] = act_ref[f, rows]


def own_columns(values, own):
    section = lax.axis_index("section")
    width = values.shape[1]
    return jnp.where(section == 0, values[:, :own], values[:, width - own :])


def own_frames_kernel(
    tiles,
    hidden_ref,
    moments_ref,
    gain_ref,
    shift_ref,
    weight_ref,
    bias_ref,
    x_ref,
    other_x_ref,
    skip_ref,
    skip_bias_ref,
    part_ref,
    norm_ref,
    act_ref,
):
    section, tile = lax.axis_index("section"), lax.axis_index("tile")
    frames, kept, width, outputs = hidden_ref.shape
    rows, half = x_ref.shape[1], x_ref.shape[3]
    own = x_ref.shape[2] // 2
    top = first_row(tiles, tile)
    norm = scale_and_offset(
        moments_ref[...],
        frames * rows * own,
        outputs // GROUPS,
        gain_ref[...],
        shift_ref[...],
    )
    norm_ref[...] = jnp.concatenate(norm, axis=0)
    for f in range(frames):
        act_ref[f, pl.ds(top, kept)] = apply_norm(hidden_ref[f], norm)
    repeat_edges(act_ref, frames, tiles, rows)
    mine = pl.ds(pl.multiple_of(section * own, own), own)
    skip_here = skip_ref[pl.ds(pl.multiple_of(section * half, half), half), :]
    skip_there = skip_ref[pl.ds(pl.multiple_of((1 - section) * half, half), half), :]
    for f in range(frames):
        taken = [(k - f + 2, k) for k in range(f - 2, f + 1) if k >= 0]
        residual = own_columns(conv_mid_rows(act_ref, weight_ref, taken, rows, width), own)
        here = x_ref[f, :, mine, :].reshape(rows * own, half)
        there = other_x_ref[f, :, mine, :].reshape(rows * own, half)
        shortcut = jnp.dot(here, skip_here, preferred_element_type=jnp.float32)
        shortcut = shortcut + jnp.dot(there, skip_there, preferred_element_type=jnp.float32)
        part_ref[f] = (residual + bias_ref[...]) + (
            shortcut.reshape(rows, own, outputs) + skip_bias_ref[...]
        )


def last_kernel(
    tiles, hidden_ref, before_ref, norm_ref, weight_ref, part_ref, out_ref, act_ref
):
    section, tm, tile = (lax.axis_index(axis) for axis in AXES)
    frames, kept, width, outputs = hidden_ref.shape
    rows, own = part_ref.shape[1:3]
    top = first_row(tiles, tile)
    first = pl.multiple_of(section * (width - own), RIM)
    beside = pl.multiple_of((1 - section) * own, RIM)
    norm = tuple(norm_ref[k : k + 1] for k in range(3))
    for f in range(frames):
        act_ref[f, pl.ds(top, kept), pl.ds(first, own), :] = apply_norm(before_ref[f, :kept], norm)
        rim = apply_norm(before_ref[f, kept], norm).astype(jnp.float32)[:kept]
        rim = jnp.broadcast_to(rim[:, None, :], (kept, width - own, outputs))
        act_ref[f, pl.ds(top, kept), pl.ds(beside, width - own), :] = rim.astype(jnp.bfloat16)

    @pl.when(tm == 0)
    def _():
        start = apply_norm(hidden_ref[0], norm)
        for f in range(frames):
            act_ref[f, pl.ds(top, kept)] = start

    repeat_edges(act_ref, frames, tiles, rows)
    for f in range(frames):
        taken = [(k - f, k) for k in range(f, f + 3) if k < frames]
        residual = own_columns(conv_mid_rows(act_ref, weight_ref, taken, rows, width), own)
        out_ref[f] = (part_ref[f] + residual).astype(jnp.bfloat16)


def pairs_for(tm_count, tile_count, tm_step, tile_step):
    out = []
    for a in range(tm_count):
        for b in range(tile_count):
            c, d = a + tm_step, b + tile_step
            if 0 <= c < tm_count and 0 <= d < tile_count:
                out.append((a * tile_count + b, c * tile_count + d))
    return out


def to_everyone(moments):
    return lax.all_to_all(moments, AXES, 0, 0, tiled=True)


def shards(
    features,
    norm_gain_in,
    norm_shift_in,
    conv_in_weight,
    conv_in_bias,
    norm_gain_mid,
    norm_shift_mid,
    conv_mid_weight,
    conv_mid_bias,
    skip_weight,
    skip_bias,
):
    sections, tms, tiles = (lax.axis_size(axis) for axis in AXES)
    parties = sections * tms * tiles
    frames, rows, columns, half = features.shape
    own = columns // sections
    width = own + RIM
    middle = conv_in_weight.shape[-1]
    outputs = conv_mid_weight.shape[-1]
    grid_axes = ("tm", "tile")

    def shift(value, tm_step, tile_step):
        return lax.ppermute(value, grid_axes, pairs_for(tms, tiles, tm_step, tile_step))

    def swap(value):
        return lax.ppermute(value, "section", [(0, 1), (1, 0)])

    previous = shift(features, 1, 0)
    moments = pl.pallas_call(
        first_kernel,
        out_shape=jax.ShapeDtypeStruct((parties, 2, half), jnp.float32),
        in_specs=[pl.BlockSpec(memory_space=pl.ANY)],
        out_specs=pl.BlockSpec(memory_space=pltpu.VMEM),
        scratch_shapes=[
            pltpu.VMEM(features.shape, features.dtype),
            pltpu.SemaphoreType.DMA,
        ],
        compiler_params=params(FULL_LIMIT),
        cost_estimate=cost(1_000_000_000, 1_000_000),
        name="feature_moments",
    )(features)
    moments = to_everyone(moments)
    other = swap(features)
    edges = 1 if tiles == 2 else 2
    edge_rows = pl.pallas_call(
        functools.partial(rows_kernel, tiles == 2),
        out_shape=(jax.ShapeDtypeStruct((2 * frames, 2, columns, half), features.dtype),) * edges,
        in_specs=vmem_specs(2),
        out_specs=tuple(vmem_specs(edges)),
        compiler_params=params(),
        cost_estimate=cost(500_000_000, 1_000_000),
        name="facing_rows",
    )(features, previous)
    if tiles == 2:
        rims = [lax.ppermute(edge_rows[0], "tile", [(0, 1), (1, 0)])]
    else:
        rims = [shift(edge_rows[1], 0, 1), shift(edge_rows[0], 0, -1)]
    other_previous = swap(previous)
    norm_in = pl.pallas_call(
        functools.partial(scales_kernel, frames * rows * columns),
        out_shape=jax.ShapeDtypeStruct((sections, 3, half), jnp.float32),
        in_specs=vmem_specs(3),
        out_specs=pl.BlockSpec(memory_space=pltpu.VMEM),
        compiler_params=params(),
        cost_estimate=cost(1_000_000_000, 1_000_000),
        name="feature_scales",
    )(moments, norm_gain_in.reshape(sections, half), norm_shift_in.reshape(sections, half))
    norm_in, *rims = lax.optimization_barrier((norm_in, *rims))
    other_rims = [swap(rim) for rim in rims]

    kept = rows + edges
    hidden, moments_mid = pl.pallas_call(
        functools.partial(middle_kernel, tiles, edges),
        out_shape=(
            jax.ShapeDtypeStruct((frames, kept, width, middle), jnp.bfloat16),
            jax.ShapeDtypeStruct((parties, 2, middle), jnp.float32),
        ),
        in_specs=vmem_specs(7 + 2 * edges),
        out_specs=tuple(vmem_specs(2)),
        scratch_shapes=[pltpu.VMEM((2 * frames, rows + 4, width, 2 * half), jnp.bfloat16)],
        compiler_params=params(),
        cost_estimate=cost(4_000_000_000, 1_000_000),
        name="norm_conv_in",
    )(
        features,
        previous,
        other,
        other_previous,
        *rims,
        *other_rims,
        norm_in,
        conv_in_weight,
        conv_in_bias.reshape(1, middle),
    )
    moments_mid = to_everyone(moments_mid)
    sent = pl.pallas_call(
        pack_kernel,
        out_shape=jax.ShapeDtypeStruct((frames, kept + 1, own, middle), jnp.bfloat16),
        in_specs=vmem_specs(1),
        out_specs=pl.BlockSpec(memory_space=pltpu.VMEM),
        compiler_params=params(),
        cost_estimate=cost(1_000_000_000, 1_000_000),
        name="pack_hidden",
    )(hidden)
    before = shift(sent, 1, 0)
    part, norm_mid = pl.pallas_call(
        functools.partial(own_frames_kernel, tiles),
        out_shape=(
            jax.ShapeDtypeStruct((frames, rows, own, outputs), jnp.float32),
            jax.ShapeDtypeStruct((3, middle), jnp.float32),
        ),
        in_specs=vmem_specs(10),
        out_specs=tuple(vmem_specs(2)),
        scratch_shapes=[pltpu.VMEM((frames, rows + 2, width, middle), jnp.bfloat16)],
        compiler_params=params(),
        cost_estimate=cost(2_000_000_000, 1_000_000),
        name="conv_mid_own_frames",
    )(
        hidden,
        moments_mid,
        norm_gain_mid.reshape(1, middle),
        norm_shift_mid.reshape(1, middle),
        conv_mid_weight,
        conv_mid_bias.reshape(1, outputs),
        features,
        other,
        skip_weight,
        skip_bias.reshape(1, outputs),
    )
    return pl.pallas_call(
        functools.partial(last_kernel, tiles),
        out_shape=jax.ShapeDtypeStruct((frames, rows, own, outputs), jnp.bfloat16),
        in_specs=vmem_specs(5),
        out_specs=pl.BlockSpec(memory_space=pltpu.VMEM),
        scratch_shapes=[pltpu.VMEM((frames, rows + 2, width, middle), jnp.bfloat16)],
        compiler_params=params(),
        cost_estimate=cost(2_000_000_000, 1_000_000),
        name="conv_mid_previous_frames",
    )(hidden, before, norm_mid, conv_mid_weight, part)


def solution(mesh):
    in_specs = (P("tm", "tile", None, "section"),) + (P(),) * 10
    out_specs = P("tm", "tile", "section", None)
    return jax.shard_map(shards, mesh=mesh, in_specs=in_specs, out_specs=out_specs, check_vma=False)
```

```python
import functools

import jax
import jax.numpy as jnp
from jax import lax
from jax.experimental import pallas as pl
from jax.experimental.pallas import tpu as pltpu
from jax.sharding import PartitionSpec as P

GROUPS = 32
AXES = ("section", "tm", "tile")
VMEM_LIMIT = 48 * 1024 * 1024
FULL_LIMIT = 63 * 1024 * 1024
RIM = 16


def params(limit=VMEM_LIMIT):
    return pltpu.CompilerParams(vmem_limit_bytes=limit)


def cost(flops, moved):
    return pl.CostEstimate(flops=flops, bytes_accessed=moved, transcendentals=0)


def vmem_specs(count):
    return [pl.BlockSpec(memory_space=pltpu.VMEM)] * count


def silu(u):
    half = 0.5 * u
    return half + half * jnp.tanh(half)


def moments_of(cells):
    mean = jnp.sum(cells, axis=0, keepdims=True) * (1.0 / cells.shape[0])
    off = cells - mean
    return jnp.concatenate([mean, jnp.sum(off * off, axis=0, keepdims=True)], axis=0)


def group_matrix(channels, width):
    shape = (channels, channels)
    row = lax.broadcasted_iota(jnp.int32, shape, 0) // width
    col = lax.broadcasted_iota(jnp.int32, shape, 1) // width
    return jnp.where(row == col, 1.0, 0.0).astype(jnp.bfloat16)


def group_sum(values, matrix):
    parts = []
    for _ in range(3):
        part = values.astype(jnp.bfloat16).astype(jnp.float32)
        parts.append(jnp.broadcast_to(part, (8, part.shape[-1])))
        values = values - part
    stacked = jnp.concatenate(parts + [jnp.zeros_like(parts[0])], axis=0).astype(jnp.bfloat16)
    summed = jnp.dot(stacked, matrix, preferred_element_type=jnp.float32)
    return summed[0:1] + summed[8:9] + summed[16:17]


def scale_and_offset(moments, cells, width, gain, shift):
    devices, _, channels = moments.shape
    matrix = group_matrix(channels, width)
    means = moments[:, 0, :]
    mean = group_sum(jnp.sum(means, axis=0, keepdims=True), matrix) * (1.0 / (devices * width))
    off = means - mean
    total = jnp.sum(moments[:, 1, :] + float(cells) * (off * off), axis=0, keepdims=True)
    spread = group_sum(total, matrix) * (1.0 / (cells * devices * width))
    scale = lax.rsqrt(spread + 1e-6) * gain
    return mean, scale, shift


def apply_norm(values, norm):
    mean, scale, shift = norm
    return silu((values.astype(jnp.float32) - mean) * scale + shift).astype(jnp.bfloat16)


def first_kernel(x_hbm, moments_ref, x_ref, sem):
    copy = pltpu.make_async_copy(x_hbm, x_ref, sem)
    copy.start()
    copy.wait()
    x = x_ref[...]
    cells = x.astype(jnp.float32).reshape(-1, x.shape[-1])
    moments_ref[...] = jnp.broadcast_to(moments_of(cells)[None], moments_ref.shape)


def rows_kernel(pairs, x_ref, prev_ref, *edge_refs):
    frames, rows = x_ref.shape[:2]
    if pairs:
        starts = [(rows - 2) * (1 - lax.axis_index("tile"))]
    else:
        starts = [0, rows - 2]
    for start, edge_ref in zip(starts, edge_refs):
        edge_ref[:frames] = prev_ref[:, pl.ds(start, 2)]
        edge_ref[frames:] = x_ref[:, pl.ds(start, 2)]


def scales_kernel(cells, moments_ref, gain_ref, shift_ref, norm_ref):
    sections, half = gain_ref.shape
    per_section = moments_ref.shape[0] // sections
    for k in range(sections):
        norm = scale_and_offset(
            moments_ref[k * per_section : (k + 1) * per_section],
            cells,
            sections * half // GROUPS,
            gain_ref[k : k + 1],
            shift_ref[k : k + 1],
        )
        norm_ref[k] = jnp.concatenate(norm, axis=0)


def column_taps(weight_ref, t, h):
    return jnp.concatenate([weight_ref[t, h, w] for w in range(3)], axis=-1)


def shift_and_add(total, rows, width):
    outputs = total.shape[-1] // 3
    total = total.reshape(rows, width, 3 * outputs)
    before, middle, after = (total[..., k * outputs : (k + 1) * outputs] for k in range(3))
    before = jnp.concatenate([before[:, :1], before[:, :-1]], axis=1)
    after = jnp.concatenate([after[:, 1:], after[:, -1:]], axis=1)
    return middle + before + after


def conv_in_rows(act_ref, weight_ref, frames, top, rows, width):
    totals = [None] * frames
    for a in range(act_ref.shape[0]):
        reached = [f for f in range(frames) if 0 <= a - f <= 2]
        for h in range(3):
            cells = act_ref[a, pl.ds(top + h, rows)]
            cells = cells.reshape(rows * width, cells.shape[-1])
            taps = [column_taps(weight_ref, a - f, h) for f in reached]
            sums = jnp.dot(
                cells, jnp.concatenate(taps, axis=-1), preferred_element_type=jnp.float32
            )
            n = sums.shape[-1] // len(reached)
            for k, f in enumerate(reached):
                part = sums[:, k * n : (k + 1) * n]
                totals[f] = part if totals[f] is None else totals[f] + part
    return [shift_and_add(total, rows, width) for total in totals]


def conv_mid_rows(act_ref, weight_ref, taken, rows, width):
    cells, taps = [], []
    for t, frame in taken:
        for h in range(3):
            block = act_ref[frame, h : h + rows]
            cells.append(block.reshape(rows * width, block.shape[-1]))
            taps.append(column_taps(weight_ref, t, h))
    total = jnp.dot(
        jnp.concatenate(cells, axis=-1),
        jnp.concatenate(taps, axis=0),
        preferred_element_type=jnp.float32,
    )
    return shift_and_add(total, rows, width)


def first_row(tiles, tile):
    return 1 - tile if tiles == 2 else 0


def body_kernel(x_ref, prev_ref, other_x_ref, other_prev_ref, norm_ref, body_ref):
    section = lax.axis_index("section")
    frames, _, columns, half = x_ref.shape
    width = body_ref.shape[2]
    cols = pl.ds(pl.multiple_of(section * (columns - width), RIM), width)
    pieces = ((section, prev_ref, x_ref), (1 - section, other_prev_ref, other_x_ref))
    for which, before, now in pieces:
        norm = tuple(norm_ref[which, k : k + 1] for k in range(3))
        lanes = pl.ds(pl.multiple_of(which * half, half), half)
        for f in range(2 * frames):
            rows = before[f, :, cols, :] if f < frames else now[f - frames, :, cols, :]
            body_ref[f, :, :, lanes] = apply_norm(rows, norm)


def middle_kernel(tiles, sides, *refs):
    body_ref = refs[0]
    rim_refs, other_rim_refs = refs[1 : 1 + sides], refs[1 + sides : 1 + 2 * sides]
    norm_ref, weight_ref, bias_ref, hidden_ref, out_moments_ref, act_ref = refs[1 + 2 * sides :]
    section, tm, tile = (lax.axis_index(axis) for axis in AXES)
    columns, half = rim_refs[0].shape[2:]
    frames, rows, width = body_ref.shape[0] // 2, body_ref.shape[1], body_ref.shape[2]
    kept = hidden_ref.shape[1]
    own = columns // 2
    first = pl.multiple_of(section * (columns - width), RIM)
    cols = pl.ds(first, width)
    top = first_row(tiles, tile)
    rim_rows = (0, rows + 2) if sides == 2 else ((rows + 2) * (1 - tile),)
    act_ref[:, 2 : 2 + rows] = body_ref[...]
    for which, rims in ((section, rim_refs), (1 - section, other_rim_refs)):
        norm = tuple(norm_ref[which, k : k + 1] for k in range(3))
        lanes = pl.ds(pl.multiple_of(which * half, half), half)
        for f in range(2 * frames):
            for row, rim in zip(rim_rows, rims):
                act_ref[f, pl.ds(row, 2), :, lanes] = apply_norm(rim[f, :, cols, :], norm)

    @pl.when(tile == 0)
    def _():
        for f in range(2 * frames):
            act_ref[f, 1] = act_ref[f, 2]

    @pl.when(tile == tiles - 1)
    def _():
        for f in range(2 * frames):
            act_ref[f, rows + 2] = act_ref[f, rows + 1]

    @pl.when(tm == 0)
    def _():
        for f in range(frames):
            act_ref[f] = act_ref[frames]

    for f, hidden in enumerate(conv_in_rows(act_ref, weight_ref, frames, top, kept, width)):
        hidden_ref[f] = (hidden + bias_ref[...]).astype(jnp.bfloat16)

    cells = hidden_ref[:, pl.ds(1 - top, rows), pl.ds(first, own), :]
    cells = cells.astype(jnp.float32).reshape(-1, cells.shape[-1])
    out_moments_ref[...] = jnp.broadcast_to(moments_of(cells)[None], out_moments_ref.shape)


def pack_kernel(hidden_ref, sent_ref):
    section = lax.axis_index("section")
    frames, kept, width, channels = hidden_ref.shape
    own = sent_ref.shape[2]
    first = pl.multiple_of(section * (width - own), RIM)
    for f in range(frames):
        sent_ref[f, :kept] = hidden_ref[f, :, pl.ds(first, own), :]
        hidden = hidden_ref[f].astype(jnp.float32)
        rim = jnp.where(section == 0, hidden[:, own, :], hidden[:, width - own - 1, :])
        spare = jnp.zeros((own - kept, channels), jnp.float32)
        sent_ref[f, kept] = jnp.concatenate([rim, spare], axis=0).astype(jnp.bfloat16)


def repeat_edges(act_ref, count, tiles, rows):
    tile = lax.axis_index("tile")

    @pl.when(tile == 0)
    def _():
        for f in range(count):
            act_ref[f, 0] = act_ref[f, 1]

    @pl.when(tile == tiles - 1)
    def _():
        for f in range(count):
            act_ref[f, rows + 1] = act_ref[f, rows]


def own_columns(values, own):
    section = lax.axis_index("section")
    width = values.shape[1]
    return jnp.where(section == 0, values[:, :own], values[:, width - own :])


def shortcut_kernel(x_ref, other_x_ref, skip_ref, skip_bias_ref, bias_ref, part_ref):
    section = lax.axis_index("section")
    frames, rows, columns, half = x_ref.shape
    own = columns // 2
    mine = pl.ds(pl.multiple_of(section * own, own), own)
    skip_here = skip_ref[pl.ds(pl.multiple_of(section * half, half), half), :]
    skip_there = skip_ref[pl.ds(pl.multiple_of((1 - section) * half, half), half), :]
    for f in range(frames):
        here = x_ref[f, :, mine, :].reshape(rows * own, half)
        there = other_x_ref[f, :, mine, :].reshape(rows * own, half)
        shortcut = jnp.dot(here, skip_here, preferred_element_type=jnp.float32)
        shortcut = shortcut + jnp.dot(there, skip_there, preferred_element_type=jnp.float32)
        part_ref[f] = (shortcut + (skip_bias_ref[...] + bias_ref[...])).reshape(rows, own, -1)


def own_frames_kernel(
    tiles,
    hidden_ref,
    moments_ref,
    gain_ref,
    shift_ref,
    weight_ref,
    shortcut_ref,
    part_ref,
    norm_ref,
    act_ref,
):
    frames, kept, width, outputs = hidden_ref.shape
    rows, own = part_ref.shape[1:3]
    top = first_row(tiles, lax.axis_index("tile"))
    norm = scale_and_offset(
        moments_ref[...],
        frames * rows * own,
        outputs // GROUPS,
        gain_ref[...],
        shift_ref[...],
    )
    norm_ref[...] = jnp.concatenate(norm, axis=0)
    for f in range(frames):
        act_ref[f, pl.ds(top, kept)] = apply_norm(hidden_ref[f], norm)
    repeat_edges(act_ref, frames, tiles, rows)
    for f in range(frames):
        taken = [(k - f + 2, k) for k in range(f - 2, f + 1) if k >= 0]
        residual = own_columns(conv_mid_rows(act_ref, weight_ref, taken, rows, width), own)
        part_ref[f] = shortcut_ref[f] + residual


def last_kernel(
    tiles, hidden_ref, before_ref, norm_ref, weight_ref, part_ref, out_hbm, act_ref, out_ref, sems
):
    section, tm, tile = (lax.axis_index(axis) for axis in AXES)
    frames, kept, width, outputs = hidden_ref.shape
    rows, own = part_ref.shape[1:3]
    top = first_row(tiles, tile)
    first = pl.multiple_of(section * (width - own), RIM)
    beside = pl.multiple_of((1 - section) * own, RIM)
    norm = tuple(norm_ref[k : k + 1] for k in range(3))
    for f in range(frames):
        act_ref[f, pl.ds(top, kept), pl.ds(first, own), :] = apply_norm(before_ref[f, :kept], norm)
        rim = apply_norm(before_ref[f, kept], norm).astype(jnp.float32)[:kept]
        rim = jnp.broadcast_to(rim[:, None, :], (kept, width - own, outputs))
        act_ref[f, pl.ds(top, kept), pl.ds(beside, width - own), :] = rim.astype(jnp.bfloat16)

    @pl.when(tm == 0)
    def _():
        start = apply_norm(hidden_ref[0], norm)
        for f in range(frames):
            act_ref[f, pl.ds(top, kept)] = start

    repeat_edges(act_ref, frames, tiles, rows)
    copies = []
    for f in range(frames):
        taken = [(k - f, k) for k in range(f, f + 3) if k < frames]
        residual = own_columns(conv_mid_rows(act_ref, weight_ref, taken, rows, width), own)
        out_ref[f] = (part_ref[f] + residual).astype(jnp.bfloat16)
        copies.append(pltpu.make_async_copy(out_ref.at[f], out_hbm.at[f], sems.at[f]))
        copies[-1].start()
    for copy in copies:
        copy.wait()


def pairs_for(tm_count, tile_count, tm_step, tile_step):
    out = []
    for a in range(tm_count):
        for b in range(tile_count):
            c, d = a + tm_step, b + tile_step
            if 0 <= c < tm_count and 0 <= d < tile_count:
                out.append((a * tile_count + b, c * tile_count + d))
    return out


def to_everyone(moments):
    return lax.all_to_all(moments, AXES, 0, 0, tiled=True)


def shards(
    features,
    norm_gain_in,
    norm_shift_in,
    conv_in_weight,
    conv_in_bias,
    norm_gain_mid,
    norm_shift_mid,
    conv_mid_weight,
    conv_mid_bias,
    skip_weight,
    skip_bias,
):
    sections, tms, tiles = (lax.axis_size(axis) for axis in AXES)
    parties = sections * tms * tiles
    frames, rows, columns, half = features.shape
    own = columns // sections
    width = own + RIM
    middle = conv_in_weight.shape[-1]
    outputs = conv_mid_weight.shape[-1]
    grid_axes = ("tm", "tile")

    def shift(value, tm_step, tile_step):
        return lax.ppermute(value, grid_axes, pairs_for(tms, tiles, tm_step, tile_step))

    def swap(value):
        return lax.ppermute(value, "section", [(0, 1), (1, 0)])

    previous = shift(features, 1, 0)
    sums = pl.pallas_call(
        first_kernel,
        out_shape=jax.ShapeDtypeStruct((parties, 2, half), jnp.float32),
        in_specs=[pl.BlockSpec(memory_space=pl.ANY)],
        out_specs=pl.BlockSpec(memory_space=pltpu.VMEM),
        scratch_shapes=[
            pltpu.VMEM(features.shape, features.dtype),
            pltpu.SemaphoreType.DMA,
        ],
        compiler_params=params(FULL_LIMIT),
        cost_estimate=cost(1_000_000_000, 1_000_000),
        name="feature_moments",
    )(features)
    moments = to_everyone(sums)
    previous, _ = lax.optimization_barrier((previous, sums))
    other = swap(features)
    edges = 1 if tiles == 2 else 2
    edge_rows = pl.pallas_call(
        functools.partial(rows_kernel, tiles == 2),
        out_shape=(jax.ShapeDtypeStruct((2 * frames, 2, columns, half), features.dtype),) * edges,
        in_specs=vmem_specs(2),
        out_specs=tuple(vmem_specs(edges)),
        compiler_params=params(),
        cost_estimate=cost(500_000_000, 1_000_000),
        name="facing_rows",
    )(features, previous)
    if tiles == 2:
        rims = [lax.ppermute(edge_rows[0], "tile", [(0, 1), (1, 0)])]
    else:
        rims = [shift(edge_rows[1], 0, 1), shift(edge_rows[0], 0, -1)]
    other_previous = swap(previous)
    norm_in = pl.pallas_call(
        functools.partial(scales_kernel, frames * rows * columns),
        out_shape=jax.ShapeDtypeStruct((sections, 3, half), jnp.float32),
        in_specs=vmem_specs(3),
        out_specs=pl.BlockSpec(memory_space=pltpu.VMEM),
        compiler_params=params(),
        cost_estimate=cost(1_000_000_000, 1_000_000),
        name="feature_scales",
    )(moments, norm_gain_in.reshape(sections, half), norm_shift_in.reshape(sections, half))
    norm_in, *rims = lax.optimization_barrier((norm_in, *rims))
    other_rims = [swap(rim) for rim in rims]

    kept = rows + edges
    body = pl.pallas_call(
        body_kernel,
        out_shape=jax.ShapeDtypeStruct((2 * frames, rows, width, 2 * half), jnp.bfloat16),
        in_specs=vmem_specs(5),
        out_specs=pl.BlockSpec(memory_space=pltpu.VMEM),
        compiler_params=params(),
        cost_estimate=cost(1_000_000_000, 1_000_000),
        name="norm_body",
    )(features, previous, other, other_previous, norm_in)
    hidden, moments_mid = pl.pallas_call(
        functools.partial(middle_kernel, tiles, edges),
        out_shape=(
            jax.ShapeDtypeStruct((frames, kept, width, middle), jnp.bfloat16),
            jax.ShapeDtypeStruct((parties, 2, middle), jnp.float32),
        ),
        in_specs=vmem_specs(4 + 2 * edges),
        out_specs=tuple(vmem_specs(2)),
        scratch_shapes=[pltpu.VMEM((2 * frames, rows + 4, width, 2 * half), jnp.bfloat16)],
        compiler_params=params(),
        cost_estimate=cost(4_000_000_000, 1_000_000),
        name="conv_in",
    )(
        body,
        *rims,
        *other_rims,
        norm_in,
        conv_in_weight,
        conv_in_bias.reshape(1, middle),
    )
    moments_mid = to_everyone(moments_mid)
    sent = pl.pallas_call(
        pack_kernel,
        out_shape=jax.ShapeDtypeStruct((frames, kept + 1, own, middle), jnp.bfloat16),
        in_specs=vmem_specs(1),
        out_specs=pl.BlockSpec(memory_space=pltpu.VMEM),
        compiler_params=params(),
        cost_estimate=cost(1_000_000_000, 1_000_000),
        name="pack_hidden",
    )(hidden)
    before = shift(sent, 1, 0)
    shown, _ = lax.optimization_barrier((other, sent))
    shortcut = pl.pallas_call(
        shortcut_kernel,
        out_shape=jax.ShapeDtypeStruct((frames, rows, own, outputs), jnp.float32),
        in_specs=vmem_specs(5),
        out_specs=pl.BlockSpec(memory_space=pltpu.VMEM),
        compiler_params=params(),
        cost_estimate=cost(300_000_000, 1_000_000),
        name="shortcut",
    )(
        features,
        shown,
        skip_weight,
        skip_bias.reshape(1, outputs),
        conv_mid_bias.reshape(1, outputs),
    )
    part, norm_mid = pl.pallas_call(
        functools.partial(own_frames_kernel, tiles),
        out_shape=(
            jax.ShapeDtypeStruct((frames, rows, own, outputs), jnp.float32),
            jax.ShapeDtypeStruct((3, middle), jnp.float32),
        ),
        in_specs=vmem_specs(6),
        out_specs=tuple(vmem_specs(2)),
        scratch_shapes=[pltpu.VMEM((frames, rows + 2, width, middle), jnp.bfloat16)],
        compiler_params=params(),
        cost_estimate=cost(2_000_000_000, 1_000_000),
        name="conv_mid_own_frames",
    )(
        hidden,
        moments_mid,
        norm_gain_mid.reshape(1, middle),
        norm_shift_mid.reshape(1, middle),
        conv_mid_weight,
        shortcut,
    )
    return pl.pallas_call(
        functools.partial(last_kernel, tiles),
        out_shape=jax.ShapeDtypeStruct((frames, rows, own, outputs), jnp.bfloat16),
        in_specs=vmem_specs(5),
        out_specs=pl.BlockSpec(memory_space=pl.ANY),
        scratch_shapes=[
            pltpu.VMEM((frames, rows + 2, width, middle), jnp.bfloat16),
            pltpu.VMEM((frames, rows, own, outputs), jnp.bfloat16),
            pltpu.SemaphoreType.DMA((frames,)),
        ],
        compiler_params=params(),
        cost_estimate=cost(2_000_000_000, 1_000_000),
        name="conv_mid_previous_frames",
    )(hidden, before, norm_mid, conv_mid_weight, part)


def solution(mesh):
    in_specs = (P("tm", "tile", None, "section"),) + (P(),) * 10
    out_specs = P("tm", "tile", "section", None)
    return jax.shard_map(shards, mesh=mesh, in_specs=in_specs, out_specs=out_specs, check_vma=False)
```

```python
import functools

import jax
import jax.numpy as jnp
from jax import lax
from jax.experimental import pallas as pl
from jax.experimental.pallas import tpu as pltpu
from jax.sharding import PartitionSpec as P

GROUPS = 32
AXES = ("section", "tm", "tile")
VMEM_LIMIT = 48 * 1024 * 1024
FULL_LIMIT = 63 * 1024 * 1024
RIM = 16


def params(limit=VMEM_LIMIT):
    return pltpu.CompilerParams(vmem_limit_bytes=limit)


def cost(flops, moved):
    return pl.CostEstimate(flops=flops, bytes_accessed=moved, transcendentals=0)


def vmem_specs(count):
    return [pl.BlockSpec(memory_space=pltpu.VMEM)] * count


def silu(u):
    half = 0.5 * u
    return half + half * jnp.tanh(half)


def moments_of(cells):
    mean = jnp.sum(cells, axis=0, keepdims=True) * (1.0 / cells.shape[0])
    off = cells - mean
    return jnp.concatenate([mean, jnp.sum(off * off, axis=0, keepdims=True)], axis=0)


def group_matrix(channels, width):
    shape = (channels, channels)
    row = lax.broadcasted_iota(jnp.int32, shape, 0) // width
    col = lax.broadcasted_iota(jnp.int32, shape, 1) // width
    return jnp.where(row == col, 1.0, 0.0).astype(jnp.bfloat16)


def group_sum(values, matrix):
    parts = []
    for _ in range(3):
        part = values.astype(jnp.bfloat16).astype(jnp.float32)
        parts.append(jnp.broadcast_to(part, (8, part.shape[-1])))
        values = values - part
    stacked = jnp.concatenate(parts + [jnp.zeros_like(parts[0])], axis=0).astype(jnp.bfloat16)
    summed = jnp.dot(stacked, matrix, preferred_element_type=jnp.float32)
    return summed[0:1] + summed[8:9] + summed[16:17]


def scale_and_offset(moments, cells, width, gain, shift):
    devices, _, channels = moments.shape
    matrix = group_matrix(channels, width)
    means = moments[:, 0, :]
    mean = group_sum(jnp.sum(means, axis=0, keepdims=True), matrix) * (1.0 / (devices * width))
    off = means - mean
    total = jnp.sum(moments[:, 1, :] + float(cells) * (off * off), axis=0, keepdims=True)
    spread = group_sum(total, matrix) * (1.0 / (cells * devices * width))
    scale = lax.rsqrt(spread + 1e-6) * gain
    return mean, scale, shift


def apply_norm(values, norm):
    mean, scale, shift = norm
    return silu((values.astype(jnp.float32) - mean) * scale + shift).astype(jnp.bfloat16)


def first_kernel(x_hbm, moments_ref, x_ref, sem):
    copy = pltpu.make_async_copy(x_hbm, x_ref, sem)
    copy.start()
    copy.wait()
    x = x_ref[...]
    cells = x.astype(jnp.float32).reshape(-1, x.shape[-1])
    moments_ref[...] = jnp.broadcast_to(moments_of(cells)[None], moments_ref.shape)


def rows_kernel(pairs, x_ref, prev_ref, *edge_refs):
    frames, rows = x_ref.shape[:2]
    if pairs:
        starts = [(rows - 2) * (1 - lax.axis_index("tile"))]
    else:
        starts = [0, rows - 2]
    for start, edge_ref in zip(starts, edge_refs):
        edge_ref[:frames] = prev_ref[:, pl.ds(start, 2)]
        edge_ref[frames:] = x_ref[:, pl.ds(start, 2)]


def scales_kernel(cells, moments_ref, gain_ref, shift_ref, norm_ref):
    sections, half = gain_ref.shape
    per_section = moments_ref.shape[0] // sections
    for k in range(sections):
        norm = scale_and_offset(
            moments_ref[k * per_section : (k + 1) * per_section],
            cells,
            sections * half // GROUPS,
            gain_ref[k : k + 1],
            shift_ref[k : k + 1],
        )
        norm_ref[k] = jnp.concatenate(norm, axis=0)


def column_taps(weight_ref, t, h):
    return jnp.concatenate([weight_ref[t, h, w] for w in range(3)], axis=-1)


def shift_and_add(total, rows, width):
    outputs = total.shape[-1] // 3
    total = total.reshape(rows, width, 3 * outputs)
    before, middle, after = (total[..., k * outputs : (k + 1) * outputs] for k in range(3))
    before = jnp.concatenate([before[:, :1], before[:, :-1]], axis=1)
    after = jnp.concatenate([after[:, 1:], after[:, -1:]], axis=1)
    return middle + before + after


def conv_in_rows(act_ref, weight_ref, frames, top, rows, width):
    totals = [None] * frames
    for a in range(act_ref.shape[0]):
        reached = [f for f in range(frames) if 0 <= a - f <= 2]
        for h in range(3):
            cells = act_ref[a, pl.ds(top + h, rows)]
            cells = cells.reshape(rows * width, cells.shape[-1])
            taps = [column_taps(weight_ref, a - f, h) for f in reached]
            sums = jnp.dot(
                cells, jnp.concatenate(taps, axis=-1), preferred_element_type=jnp.float32
            )
            n = sums.shape[-1] // len(reached)
            for k, f in enumerate(reached):
                part = sums[:, k * n : (k + 1) * n]
                totals[f] = part if totals[f] is None else totals[f] + part
    return [shift_and_add(total, rows, width) for total in totals]


def conv_mid_rows(act_ref, weight_ref, taken, rows, width):
    cells, taps = [], []
    for t, frame in taken:
        for h in range(3):
            block = act_ref[frame, h : h + rows]
            cells.append(block.reshape(rows * width, block.shape[-1]))
            taps.append(column_taps(weight_ref, t, h))
    total = jnp.dot(
        jnp.concatenate(cells, axis=-1),
        jnp.concatenate(taps, axis=0),
        preferred_element_type=jnp.float32,
    )
    return shift_and_add(total, rows, width)


def first_row(tiles, tile):
    return 1 - tile if tiles == 2 else 0


def body_kernel(x_ref, prev_ref, other_x_ref, norm_ref, body_ref):
    section = lax.axis_index("section")
    frames, _, columns, half = x_ref.shape
    width = body_ref.shape[2]
    cols = pl.ds(pl.multiple_of(section * (columns - width), RIM), width)
    for which, first, ref in (
        (section, 0, prev_ref),
        (section, frames, x_ref),
        (1 - section, frames, other_x_ref),
    ):
        norm = tuple(norm_ref[which, k : k + 1] for k in range(3))
        lanes = pl.ds(pl.multiple_of(which * half, half), half)
        for f in range(frames):
            body_ref[first + f, :, :, lanes] = apply_norm(ref[f, :, cols, :], norm)


def middle_kernel(tiles, sides, *refs):
    body_ref, other_prev_ref = refs[:2]
    rim_refs, other_rim_refs = refs[2 : 2 + sides], refs[2 + sides : 2 + 2 * sides]
    norm_ref, weight_ref, bias_ref, hidden_ref, out_moments_ref, act_ref = refs[2 + 2 * sides :]
    section, tm, tile = (lax.axis_index(axis) for axis in AXES)
    columns, half = rim_refs[0].shape[2:]
    frames, rows, width = body_ref.shape[0] // 2, body_ref.shape[1], body_ref.shape[2]
    kept = hidden_ref.shape[1]
    own = columns // 2
    first = pl.multiple_of(section * (columns - width), RIM)
    cols = pl.ds(first, width)
    top = first_row(tiles, tile)
    rim_rows = (0, rows + 2) if sides == 2 else ((rows + 2) * (1 - tile),)
    act_ref[:, 2 : 2 + rows] = body_ref[...]
    for which, rims in ((section, rim_refs), (1 - section, other_rim_refs)):
        norm = tuple(norm_ref[which, k : k + 1] for k in range(3))
        lanes = pl.ds(pl.multiple_of(which * half, half), half)
        for f in range(2 * frames):
            for row, rim in zip(rim_rows, rims):
                act_ref[f, pl.ds(row, 2), :, lanes] = apply_norm(rim[f, :, cols, :], norm)
    for f in range(frames):
        act_ref[f, 2 : 2 + rows, :, lanes] = apply_norm(other_prev_ref[f, :, cols, :], norm)

    @pl.when(tile == 0)
    def _():
        for f in range(2 * frames):
            act_ref[f, 1] = act_ref[f, 2]

    @pl.when(tile == tiles - 1)
    def _():
        for f in range(2 * frames):
            act_ref[f, rows + 2] = act_ref[f, rows + 1]

    @pl.when(tm == 0)
    def _():
        for f in range(frames):
            act_ref[f] = act_ref[frames]

    for f, hidden in enumerate(conv_in_rows(act_ref, weight_ref, frames, top, kept, width)):
        hidden_ref[f] = (hidden + bias_ref[...]).astype(jnp.bfloat16)

    cells = hidden_ref[:, pl.ds(1 - top, rows), pl.ds(first, own), :]
    cells = cells.astype(jnp.float32).reshape(-1, cells.shape[-1])
    out_moments_ref[...] = jnp.broadcast_to(moments_of(cells)[None], out_moments_ref.shape)


def pack_kernel(hidden_ref, sent_ref):
    section = lax.axis_index("section")
    frames, kept, width, channels = hidden_ref.shape
    own = sent_ref.shape[2]
    first = pl.multiple_of(section * (width - own), RIM)
    for f in range(frames):
        sent_ref[f, :kept] = hidden_ref[f, :, pl.ds(first, own), :]
        hidden = hidden_ref[f].astype(jnp.float32)
        rim = jnp.where(section == 0, hidden[:, own, :], hidden[:, width - own - 1, :])
        spare = jnp.zeros((own - kept, channels), jnp.float32)
        sent_ref[f, kept] = jnp.concatenate([rim, spare], axis=0).astype(jnp.bfloat16)


def repeat_edges(act_ref, count, tiles, rows):
    tile = lax.axis_index("tile")

    @pl.when(tile == 0)
    def _():
        for f in range(count):
            act_ref[f, 0] = act_ref[f, 1]

    @pl.when(tile == tiles - 1)
    def _():
        for f in range(count):
            act_ref[f, rows + 1] = act_ref[f, rows]


def own_columns(values, own):
    section = lax.axis_index("section")
    width = values.shape[1]
    return jnp.where(section == 0, values[:, :own], values[:, width - own :])


def shortcut_kernel(x_ref, other_x_ref, skip_ref, skip_bias_ref, bias_ref, part_ref):
    section = lax.axis_index("section")
    frames, rows, columns, half = x_ref.shape
    own = columns // 2
    mine = pl.ds(pl.multiple_of(section * own, own), own)
    skip_here = skip_ref[pl.ds(pl.multiple_of(section * half, half), half), :]
    skip_there = skip_ref[pl.ds(pl.multiple_of((1 - section) * half, half), half), :]
    for f in range(frames):
        here = x_ref[f, :, mine, :].reshape(rows * own, half)
        there = other_x_ref[f, :, mine, :].reshape(rows * own, half)
        shortcut = jnp.dot(here, skip_here, preferred_element_type=jnp.float32)
        shortcut = shortcut + jnp.dot(there, skip_there, preferred_element_type=jnp.float32)
        part_ref[f] = (shortcut + (skip_bias_ref[...] + bias_ref[...])).reshape(rows, own, -1)


def own_frames_kernel(
    tiles,
    hidden_ref,
    moments_ref,
    gain_ref,
    shift_ref,
    weight_ref,
    shortcut_ref,
    part_ref,
    norm_ref,
    act_ref,
):
    frames, kept, width, outputs = hidden_ref.shape
    rows, own = part_ref.shape[1:3]
    top = first_row(tiles, lax.axis_index("tile"))
    norm = scale_and_offset(
        moments_ref[...],
        frames * rows * own,
        outputs // GROUPS,
        gain_ref[...],
        shift_ref[...],
    )
    norm_ref[...] = jnp.concatenate(norm, axis=0)
    for f in range(frames):
        act_ref[f, pl.ds(top, kept)] = apply_norm(hidden_ref[f], norm)
    repeat_edges(act_ref, frames, tiles, rows)
    for f in range(frames):
        taken = [(k - f + 2, k) for k in range(f - 2, f + 1) if k >= 0]
        residual = own_columns(conv_mid_rows(act_ref, weight_ref, taken, rows, width), own)
        part_ref[f] = shortcut_ref[f] + residual


def last_kernel(
    tiles, hidden_ref, before_ref, norm_ref, weight_ref, part_ref, out_hbm, act_ref, out_ref, sems
):
    section, tm, tile = (lax.axis_index(axis) for axis in AXES)
    frames, kept, width, outputs = hidden_ref.shape
    rows, own = part_ref.shape[1:3]
    top = first_row(tiles, tile)
    first = pl.multiple_of(section * (width - own), RIM)
    beside = pl.multiple_of((1 - section) * own, RIM)
    norm = tuple(norm_ref[k : k + 1] for k in range(3))
    for f in range(frames):
        act_ref[f, pl.ds(top, kept), pl.ds(first, own), :] = apply_norm(before_ref[f, :kept], norm)
        rim = apply_norm(before_ref[f, kept], norm).astype(jnp.float32)[:kept]
        rim = jnp.broadcast_to(rim[:, None, :], (kept, width - own, outputs))
        act_ref[f, pl.ds(top, kept), pl.ds(beside, width - own), :] = rim.astype(jnp.bfloat16)

    @pl.when(tm == 0)
    def _():
        start = apply_norm(hidden_ref[0], norm)
        for f in range(frames):
            act_ref[f, pl.ds(top, kept)] = start

    repeat_edges(act_ref, frames, tiles, rows)
    copies = []
    for f in range(frames):
        taken = [(k - f, k) for k in range(f, f + 3) if k < frames]
        residual = own_columns(conv_mid_rows(act_ref, weight_ref, taken, rows, width), own)
        out_ref[f] = (part_ref[f] + residual).astype(jnp.bfloat16)
        copies.append(pltpu.make_async_copy(out_ref.at[f], out_hbm.at[f], sems.at[f]))
        copies[-1].start()
    for copy in copies:
        copy.wait()


def pairs_for(tm_count, tile_count, tm_step, tile_step):
    out = []
    for a in range(tm_count):
        for b in range(tile_count):
            c, d = a + tm_step, b + tile_step
            if 0 <= c < tm_count and 0 <= d < tile_count:
                out.append((a * tile_count + b, c * tile_count + d))
    return out


def to_everyone(moments):
    return lax.all_to_all(moments, AXES, 0, 0, tiled=True)


def shards(
    features,
    norm_gain_in,
    norm_shift_in,
    conv_in_weight,
    conv_in_bias,
    norm_gain_mid,
    norm_shift_mid,
    conv_mid_weight,
    conv_mid_bias,
    skip_weight,
    skip_bias,
):
    sections, tms, tiles = (lax.axis_size(axis) for axis in AXES)
    parties = sections * tms * tiles
    frames, rows, columns, half = features.shape
    own = columns // sections
    width = own + RIM
    middle = conv_in_weight.shape[-1]
    outputs = conv_mid_weight.shape[-1]
    grid_axes = ("tm", "tile")

    def shift(value, tm_step, tile_step):
        return lax.ppermute(value, grid_axes, pairs_for(tms, tiles, tm_step, tile_step))

    def swap(value):
        return lax.ppermute(value, "section", [(0, 1), (1, 0)])

    previous = shift(features, 1, 0)
    sums = pl.pallas_call(
        first_kernel,
        out_shape=jax.ShapeDtypeStruct((parties, 2, half), jnp.float32),
        in_specs=[pl.BlockSpec(memory_space=pl.ANY)],
        out_specs=pl.BlockSpec(memory_space=pltpu.VMEM),
        scratch_shapes=[
            pltpu.VMEM(features.shape, features.dtype),
            pltpu.SemaphoreType.DMA,
        ],
        compiler_params=params(FULL_LIMIT),
        cost_estimate=cost(1_000_000_000, 1_000_000),
        name="feature_moments",
    )(features)
    moments = to_everyone(sums)
    previous, _ = lax.optimization_barrier((previous, sums))
    other = swap(features)
    edges = 1 if tiles == 2 else 2
    edge_rows = pl.pallas_call(
        functools.partial(rows_kernel, tiles == 2),
        out_shape=(jax.ShapeDtypeStruct((2 * frames, 2, columns, half), features.dtype),) * edges,
        in_specs=vmem_specs(2),
        out_specs=tuple(vmem_specs(edges)),
        compiler_params=params(),
        cost_estimate=cost(500_000_000, 1_000_000),
        name="facing_rows",
    )(features, previous)
    if tiles == 2:
        rims = [lax.ppermute(edge_rows[0], "tile", [(0, 1), (1, 0)])]
    else:
        rims = [shift(edge_rows[1], 0, 1), shift(edge_rows[0], 0, -1)]
    other_previous = swap(previous)
    norm_in = pl.pallas_call(
        functools.partial(scales_kernel, frames * rows * columns),
        out_shape=jax.ShapeDtypeStruct((sections, 3, half), jnp.float32),
        in_specs=vmem_specs(3),
        out_specs=pl.BlockSpec(memory_space=pltpu.VMEM),
        compiler_params=params(),
        cost_estimate=cost(2_000_000_000, 1_000_000),
        name="feature_scales",
    )(moments, norm_gain_in.reshape(sections, half), norm_shift_in.reshape(sections, half))
    norm_in, *rims = lax.optimization_barrier((norm_in, *rims))
    other_rims = [swap(rim) for rim in rims]

    kept = rows + edges
    body = pl.pallas_call(
        body_kernel,
        out_shape=jax.ShapeDtypeStruct((2 * frames, rows, width, 2 * half), jnp.bfloat16),
        in_specs=vmem_specs(4),
        out_specs=pl.BlockSpec(memory_space=pltpu.VMEM),
        compiler_params=params(),
        cost_estimate=cost(1_000_000_000, 1_000_000),
        name="norm_body",
    )(features, previous, other, norm_in)
    hidden, moments_mid = pl.pallas_call(
        functools.partial(middle_kernel, tiles, edges),
        out_shape=(
            jax.ShapeDtypeStruct((frames, kept, width, middle), jnp.bfloat16),
            jax.ShapeDtypeStruct((parties, 2, middle), jnp.float32),
        ),
        in_specs=vmem_specs(5 + 2 * edges),
        out_specs=tuple(vmem_specs(2)),
        scratch_shapes=[pltpu.VMEM((2 * frames, rows + 4, width, 2 * half), jnp.bfloat16)],
        compiler_params=params(),
        cost_estimate=cost(4_000_000_000, 1_000_000),
        name="conv_in",
    )(
        body,
        other_previous,
        *rims,
        *other_rims,
        norm_in,
        conv_in_weight,
        conv_in_bias.reshape(1, middle),
    )
    moments_mid = to_everyone(moments_mid)
    sent = pl.pallas_call(
        pack_kernel,
        out_shape=jax.ShapeDtypeStruct((frames, kept + 1, own, middle), jnp.bfloat16),
        in_specs=vmem_specs(1),
        out_specs=pl.BlockSpec(memory_space=pltpu.VMEM),
        compiler_params=params(),
        cost_estimate=cost(1_000_000_000, 1_000_000),
        name="pack_hidden",
    )(hidden)
    before = shift(sent, 1, 0)
    shown, _ = lax.optimization_barrier((other, sent))
    shortcut = pl.pallas_call(
        shortcut_kernel,
        out_shape=jax.ShapeDtypeStruct((frames, rows, own, outputs), jnp.float32),
        in_specs=vmem_specs(5),
        out_specs=pl.BlockSpec(memory_space=pltpu.VMEM),
        compiler_params=params(),
        cost_estimate=cost(300_000_000, 1_000_000),
        name="shortcut",
    )(
        features,
        shown,
        skip_weight,
        skip_bias.reshape(1, outputs),
        conv_mid_bias.reshape(1, outputs),
    )
    part, norm_mid = pl.pallas_call(
        functools.partial(own_frames_kernel, tiles),
        out_shape=(
            jax.ShapeDtypeStruct((frames, rows, own, outputs), jnp.float32),
            jax.ShapeDtypeStruct((3, middle), jnp.float32),
        ),
        in_specs=vmem_specs(6),
        out_specs=tuple(vmem_specs(2)),
        scratch_shapes=[pltpu.VMEM((frames, rows + 2, width, middle), jnp.bfloat16)],
        compiler_params=params(),
        cost_estimate=cost(2_000_000_000, 1_000_000),
        name="conv_mid_own_frames",
    )(
        hidden,
        moments_mid,
        norm_gain_mid.reshape(1, middle),
        norm_shift_mid.reshape(1, middle),
        conv_mid_weight,
        shortcut,
    )
    return pl.pallas_call(
        functools.partial(last_kernel, tiles),
        out_shape=jax.ShapeDtypeStruct((frames, rows, own, outputs), jnp.bfloat16),
        in_specs=vmem_specs(5),
        out_specs=pl.BlockSpec(memory_space=pl.ANY),
        scratch_shapes=[
            pltpu.VMEM((frames, rows + 2, width, middle), jnp.bfloat16),
            pltpu.VMEM((frames, rows, own, outputs), jnp.bfloat16),
            pltpu.SemaphoreType.DMA((frames,)),
        ],
        compiler_params=params(),
        cost_estimate=cost(2_000_000_000, 1_000_000),
        name="conv_mid_previous_frames",
    )(hidden, before, norm_mid, conv_mid_weight, part)


def solution(mesh):
    in_specs = (P("tm", "tile", None, "section"),) + (P(),) * 10
    out_specs = P("tm", "tile", "section", None)
    return jax.shard_map(shards, mesh=mesh, in_specs=in_specs, out_specs=out_specs, check_vma=False)
```

```python
import functools

import jax
import jax.numpy as jnp
from jax import lax
from jax.experimental import pallas as pl
from jax.experimental.pallas import tpu as pltpu
from jax.sharding import PartitionSpec as P

GROUPS = 32
AXES = ("section", "tm", "tile")
VMEM_LIMIT = 48 * 1024 * 1024
FULL_LIMIT = 63 * 1024 * 1024
RIM = 16


def params(limit=VMEM_LIMIT):
    return pltpu.CompilerParams(vmem_limit_bytes=limit)


def cost(flops, moved):
    return pl.CostEstimate(flops=flops, bytes_accessed=moved, transcendentals=0)


def vmem_specs(count):
    return [pl.BlockSpec(memory_space=pltpu.VMEM)] * count


def silu(u):
    half = 0.5 * u
    return half + half * jnp.tanh(half)


def moments_of(cells):
    mean = jnp.sum(cells, axis=0, keepdims=True) * (1.0 / cells.shape[0])
    off = cells - mean
    return jnp.concatenate([mean, jnp.sum(off * off, axis=0, keepdims=True)], axis=0)


def group_matrix(channels, width):
    shape = (channels, channels)
    row = lax.broadcasted_iota(jnp.int32, shape, 0) // width
    col = lax.broadcasted_iota(jnp.int32, shape, 1) // width
    return jnp.where(row == col, 1.0, 0.0).astype(jnp.bfloat16)


def group_sum(values, matrix):
    parts = []
    for _ in range(3):
        part = values.astype(jnp.bfloat16).astype(jnp.float32)
        parts.append(jnp.broadcast_to(part, (8, part.shape[-1])))
        values = values - part
    stacked = jnp.concatenate(parts + [jnp.zeros_like(parts[0])], axis=0).astype(jnp.bfloat16)
    summed = jnp.dot(stacked, matrix, preferred_element_type=jnp.float32)
    return summed[0:1] + summed[8:9] + summed[16:17]


def scale_and_offset(moments, cells, width, gain, shift):
    devices, _, channels = moments.shape
    matrix = group_matrix(channels, width)
    means = moments[:, 0, :]
    mean = group_sum(jnp.sum(means, axis=0, keepdims=True), matrix) * (1.0 / (devices * width))
    off = means - mean
    total = jnp.sum(moments[:, 1, :] + float(cells) * (off * off), axis=0, keepdims=True)
    spread = group_sum(total, matrix) * (1.0 / (cells * devices * width))
    scale = lax.rsqrt(spread + 1e-6) * gain
    return mean, scale, shift


def apply_norm(values, norm):
    mean, scale, shift = norm
    return silu((values.astype(jnp.float32) - mean) * scale + shift).astype(jnp.bfloat16)


def first_kernel(x_hbm, moments_ref, x_ref, sem):
    copy = pltpu.make_async_copy(x_hbm, x_ref, sem)
    copy.start()
    copy.wait()
    x = x_ref[...]
    cells = x.astype(jnp.float32).reshape(-1, x.shape[-1])
    moments_ref[...] = jnp.broadcast_to(moments_of(cells)[None], moments_ref.shape)


def rows_kernel(pairs, x_ref, prev_ref, for_x_ref, for_prev_ref, *edge_refs):
    frames, rows, columns = x_ref.shape[:3]
    width = for_x_ref.shape[2]
    start = (1 - lax.axis_index("section")) * (columns - width)
    theirs = pl.ds(pl.multiple_of(start, RIM), width)
    for_x_ref[...] = x_ref[:, :, theirs, :]
    for_prev_ref[...] = prev_ref[:, :, theirs, :]
    if pairs:
        starts = [(rows - 2) * (1 - lax.axis_index("tile"))]
    else:
        starts = [0, rows - 2]
    for start, edge_ref in zip(starts, edge_refs):
        edge_ref[:frames] = prev_ref[:, pl.ds(start, 2)]
        edge_ref[frames:] = x_ref[:, pl.ds(start, 2)]


def scales_kernel(cells, moments_ref, gain_ref, shift_ref, norm_ref):
    sections, half = gain_ref.shape
    per_section = moments_ref.shape[0] // sections
    for k in range(sections):
        norm = scale_and_offset(
            moments_ref[k * per_section : (k + 1) * per_section],
            cells,
            sections * half // GROUPS,
            gain_ref[k : k + 1],
            shift_ref[k : k + 1],
        )
        norm_ref[k] = jnp.concatenate(norm, axis=0)


def column_taps(weight_ref, t, h):
    return jnp.concatenate([weight_ref[t, h, w] for w in range(3)], axis=-1)


def shift_and_add(total, rows, width):
    outputs = total.shape[-1] // 3
    total = total.reshape(rows, width, 3 * outputs)
    before, middle, after = (total[..., k * outputs : (k + 1) * outputs] for k in range(3))
    before = jnp.concatenate([before[:, :1], before[:, :-1]], axis=1)
    after = jnp.concatenate([after[:, 1:], after[:, -1:]], axis=1)
    return middle + before + after


def conv_in_rows(act_ref, weight_ref, frames, top, rows, width):
    totals = [None] * frames
    for a in range(act_ref.shape[0]):
        reached = [f for f in range(frames) if 0 <= a - f <= 2]
        for h in range(3):
            cells = act_ref[a, pl.ds(top + h, rows)]
            cells = cells.reshape(rows * width, cells.shape[-1])
            taps = [column_taps(weight_ref, a - f, h) for f in reached]
            sums = jnp.dot(
                cells, jnp.concatenate(taps, axis=-1), preferred_element_type=jnp.float32
            )
            n = sums.shape[-1] // len(reached)
            for k, f in enumerate(reached):
                part = sums[:, k * n : (k + 1) * n]
                totals[f] = part if totals[f] is None else totals[f] + part
    return [shift_and_add(total, rows, width) for total in totals]


def conv_mid_rows(act_ref, weight_ref, taken, rows, width):
    cells, taps = [], []
    for t, frame in taken:
        for h in range(3):
            block = act_ref[frame, h : h + rows]
            cells.append(block.reshape(rows * width, block.shape[-1]))
            taps.append(column_taps(weight_ref, t, h))
    total = jnp.dot(
        jnp.concatenate(cells, axis=-1),
        jnp.concatenate(taps, axis=0),
        preferred_element_type=jnp.float32,
    )
    return shift_and_add(total, rows, width)


def first_row(tiles, tile):
    return 1 - tile if tiles == 2 else 0


def body_kernel(x_ref, prev_ref, other_x_ref, norm_ref, body_ref):
    section = lax.axis_index("section")
    frames, _, columns, half = x_ref.shape
    width = body_ref.shape[2]
    mine = pl.ds(pl.multiple_of(section * (columns - width), RIM), width)
    for which, first, ref, cols in (
        (section, 0, prev_ref, mine),
        (section, frames, x_ref, mine),
        (1 - section, frames, other_x_ref, slice(None)),
    ):
        norm = tuple(norm_ref[which, k : k + 1] for k in range(3))
        lanes = pl.ds(pl.multiple_of(which * half, half), half)
        for f in range(frames):
            body_ref[first + f, :, :, lanes] = apply_norm(ref[f, :, cols, :], norm)


def middle_kernel(tiles, sides, *refs):
    body_ref, other_prev_ref = refs[:2]
    rim_refs, other_rim_refs = refs[2 : 2 + sides], refs[2 + sides : 2 + 2 * sides]
    norm_ref, weight_ref, bias_ref, hidden_ref, out_moments_ref, act_ref = refs[2 + 2 * sides :]
    section, tm, tile = (lax.axis_index(axis) for axis in AXES)
    columns, half = rim_refs[0].shape[2:]
    frames, rows, width = body_ref.shape[0] // 2, body_ref.shape[1], body_ref.shape[2]
    kept = hidden_ref.shape[1]
    own = columns // 2
    first = pl.multiple_of(section * (columns - width), RIM)
    cols = pl.ds(first, width)
    top = first_row(tiles, tile)
    rim_rows = (0, rows + 2) if sides == 2 else ((rows + 2) * (1 - tile),)
    act_ref[:, 2 : 2 + rows] = body_ref[...]
    for which, rims in ((section, rim_refs), (1 - section, other_rim_refs)):
        norm = tuple(norm_ref[which, k : k + 1] for k in range(3))
        lanes = pl.ds(pl.multiple_of(which * half, half), half)
        for f in range(2 * frames):
            for row, rim in zip(rim_rows, rims):
                act_ref[f, pl.ds(row, 2), :, lanes] = apply_norm(rim[f, :, cols, :], norm)
    for f in range(frames):
        act_ref[f, 2 : 2 + rows, :, lanes] = apply_norm(other_prev_ref[f], norm)

    @pl.when(tile == 0)
    def _():
        for f in range(2 * frames):
            act_ref[f, 1] = act_ref[f, 2]

    @pl.when(tile == tiles - 1)
    def _():
        for f in range(2 * frames):
            act_ref[f, rows + 2] = act_ref[f, rows + 1]

    @pl.when(tm == 0)
    def _():
        for f in range(frames):
            act_ref[f] = act_ref[frames]

    for f, hidden in enumerate(conv_in_rows(act_ref, weight_ref, frames, top, kept, width)):
        hidden_ref[f] = (hidden + bias_ref[...]).astype(jnp.bfloat16)

    cells = hidden_ref[:, pl.ds(1 - top, rows), pl.ds(first, own), :]
    cells = cells.astype(jnp.float32).reshape(-1, cells.shape[-1])
    out_moments_ref[...] = jnp.broadcast_to(moments_of(cells)[None], out_moments_ref.shape)


def pack_kernel(hidden_ref, sent_ref):
    section = lax.axis_index("section")
    frames, kept, width, channels = hidden_ref.shape
    own = sent_ref.shape[2]
    first = pl.multiple_of(section * (width - own), RIM)
    for f in range(frames):
        sent_ref[f, :kept] = hidden_ref[f, :, pl.ds(first, own), :]
        hidden = hidden_ref[f].astype(jnp.float32)
        rim = jnp.where(section == 0, hidden[:, own, :], hidden[:, width - own - 1, :])
        spare = jnp.zeros((own - kept, channels), jnp.float32)
        sent_ref[f, kept] = jnp.concatenate([rim, spare], axis=0).astype(jnp.bfloat16)


def repeat_edges(act_ref, count, tiles, rows):
    tile = lax.axis_index("tile")

    @pl.when(tile == 0)
    def _():
        for f in range(count):
            act_ref[f, 0] = act_ref[f, 1]

    @pl.when(tile == tiles - 1)
    def _():
        for f in range(count):
            act_ref[f, rows + 1] = act_ref[f, rows]


def own_columns(values, own):
    section = lax.axis_index("section")
    width = values.shape[1]
    return jnp.where(section == 0, values[:, :own], values[:, width - own :])


def shortcut_kernel(x_ref, other_x_ref, skip_ref, skip_bias_ref, bias_ref, part_ref):
    section = lax.axis_index("section")
    frames, rows, columns, half = x_ref.shape
    own = columns // 2
    mine = pl.ds(pl.multiple_of(section * own, own), own)
    within = pl.ds(pl.multiple_of(section * (other_x_ref.shape[2] - own), RIM), own)
    skip_here = skip_ref[pl.ds(pl.multiple_of(section * half, half), half), :]
    skip_there = skip_ref[pl.ds(pl.multiple_of((1 - section) * half, half), half), :]
    for f in range(frames):
        here = x_ref[f, :, mine, :].reshape(rows * own, half)
        there = other_x_ref[f, :, within, :].reshape(rows * own, half)
        shortcut = jnp.dot(here, skip_here, preferred_element_type=jnp.float32)
        shortcut = shortcut + jnp.dot(there, skip_there, preferred_element_type=jnp.float32)
        part_ref[f] = (shortcut + (skip_bias_ref[...] + bias_ref[...])).reshape(rows, own, -1)


def own_frames_kernel(
    tiles,
    hidden_ref,
    moments_ref,
    gain_ref,
    shift_ref,
    weight_ref,
    shortcut_ref,
    part_ref,
    norm_ref,
    act_ref,
):
    frames, kept, width, outputs = hidden_ref.shape
    rows, own = part_ref.shape[1:3]
    top = first_row(tiles, lax.axis_index("tile"))
    norm = scale_and_offset(
        moments_ref[...],
        frames * rows * own,
        outputs // GROUPS,
        gain_ref[...],
        shift_ref[...],
    )
    norm_ref[...] = jnp.concatenate(norm, axis=0)
    for f in range(frames):
        act_ref[f, pl.ds(top, kept)] = apply_norm(hidden_ref[f], norm)
    repeat_edges(act_ref, frames, tiles, rows)
    for f in range(frames):
        taken = [(k - f + 2, k) for k in range(f - 2, f + 1) if k >= 0]
        residual = own_columns(conv_mid_rows(act_ref, weight_ref, taken, rows, width), own)
        part_ref[f] = shortcut_ref[f] + residual


def last_kernel(
    tiles, hidden_ref, before_ref, norm_ref, weight_ref, part_ref, out_hbm, act_ref, out_ref, sems
):
    section, tm, tile = (lax.axis_index(axis) for axis in AXES)
    frames, kept, width, outputs = hidden_ref.shape
    rows, own = part_ref.shape[1:3]
    top = first_row(tiles, tile)
    first = pl.multiple_of(section * (width - own), RIM)
    beside = pl.multiple_of((1 - section) * own, RIM)
    norm = tuple(norm_ref[k : k + 1] for k in range(3))
    for f in range(frames):
        act_ref[f, pl.ds(top, kept), pl.ds(first, own), :] = apply_norm(before_ref[f, :kept], norm)
        rim = apply_norm(before_ref[f, kept], norm).astype(jnp.float32)[:kept]
        rim = jnp.broadcast_to(rim[:, None, :], (kept, width - own, outputs))
        act_ref[f, pl.ds(top, kept), pl.ds(beside, width - own), :] = rim.astype(jnp.bfloat16)

    @pl.when(tm == 0)
    def _():
        start = apply_norm(hidden_ref[0], norm)
        for f in range(frames):
            act_ref[f, pl.ds(top, kept)] = start

    repeat_edges(act_ref, frames, tiles, rows)
    copies = []
    for f in range(frames):
        taken = [(k - f, k) for k in range(f, f + 3) if k < frames]
        residual = own_columns(conv_mid_rows(act_ref, weight_ref, taken, rows, width), own)
        out_ref[f] = (part_ref[f] + residual).astype(jnp.bfloat16)
        copies.append(pltpu.make_async_copy(out_ref.at[f], out_hbm.at[f], sems.at[f]))
        copies[-1].start()
    for copy in copies:
        copy.wait()


def pairs_for(tm_count, tile_count, tm_step, tile_step):
    out = []
    for a in range(tm_count):
        for b in range(tile_count):
            c, d = a + tm_step, b + tile_step
            if 0 <= c < tm_count and 0 <= d < tile_count:
                out.append((a * tile_count + b, c * tile_count + d))
    return out


def to_everyone(moments):
    return lax.all_to_all(moments, AXES, 0, 0, tiled=True)


def shards(
    features,
    norm_gain_in,
    norm_shift_in,
    conv_in_weight,
    conv_in_bias,
    norm_gain_mid,
    norm_shift_mid,
    conv_mid_weight,
    conv_mid_bias,
    skip_weight,
    skip_bias,
):
    sections, tms, tiles = (lax.axis_size(axis) for axis in AXES)
    parties = sections * tms * tiles
    frames, rows, columns, half = features.shape
    own = columns // sections
    width = own + RIM
    middle = conv_in_weight.shape[-1]
    outputs = conv_mid_weight.shape[-1]
    grid_axes = ("tm", "tile")

    def shift(value, tm_step, tile_step):
        return lax.ppermute(value, grid_axes, pairs_for(tms, tiles, tm_step, tile_step))

    def swap(value):
        return lax.ppermute(value, "section", [(0, 1), (1, 0)])

    previous = shift(features, 1, 0)
    sums = pl.pallas_call(
        first_kernel,
        out_shape=jax.ShapeDtypeStruct((parties, 2, half), jnp.float32),
        in_specs=[pl.BlockSpec(memory_space=pl.ANY)],
        out_specs=pl.BlockSpec(memory_space=pltpu.VMEM),
        scratch_shapes=[
            pltpu.VMEM(features.shape, features.dtype),
            pltpu.SemaphoreType.DMA,
        ],
        compiler_params=params(FULL_LIMIT),
        cost_estimate=cost(1_000_000_000, 1_000_000),
        name="feature_moments",
    )(features)
    moments = to_everyone(sums)
    previous, _ = lax.optimization_barrier((previous, sums))
    edges = 1 if tiles == 2 else 2
    edge = jax.ShapeDtypeStruct((2 * frames, 2, columns, half), features.dtype)
    cut = jax.ShapeDtypeStruct((frames, rows, width, half), features.dtype)
    for_x, for_previous, *edge_rows = pl.pallas_call(
        functools.partial(rows_kernel, tiles == 2),
        out_shape=(cut, cut) + (edge,) * edges,
        in_specs=vmem_specs(2),
        out_specs=tuple(vmem_specs(2 + edges)),
        compiler_params=params(),
        cost_estimate=cost(500_000_000, 1_000_000),
        name="facing_rows",
    )(features, previous)
    if tiles == 2:
        rims = [lax.ppermute(edge_rows[0], "tile", [(0, 1), (1, 0)])]
    else:
        rims = [shift(edge_rows[1], 0, 1), shift(edge_rows[0], 0, -1)]
    other = swap(for_x)
    other_previous = swap(for_previous)
    norm_in = pl.pallas_call(
        functools.partial(scales_kernel, frames * rows * columns),
        out_shape=jax.ShapeDtypeStruct((sections, 3, half), jnp.float32),
        in_specs=vmem_specs(3),
        out_specs=pl.BlockSpec(memory_space=pltpu.VMEM),
        compiler_params=params(),
        cost_estimate=cost(2_000_000_000, 1_000_000),
        name="feature_scales",
    )(moments, norm_gain_in.reshape(sections, half), norm_shift_in.reshape(sections, half))
    norm_in, *rims = lax.optimization_barrier((norm_in, *rims))
    other_rims = [swap(rim) for rim in rims]

    kept = rows + edges
    body = pl.pallas_call(
        body_kernel,
        out_shape=jax.ShapeDtypeStruct((2 * frames, rows, width, 2 * half), jnp.bfloat16),
        in_specs=vmem_specs(4),
        out_specs=pl.BlockSpec(memory_space=pltpu.VMEM),
        compiler_params=params(),
        cost_estimate=cost(1_000_000_000, 1_000_000),
        name="norm_body",
    )(features, previous, other, norm_in)
    hidden, moments_mid = pl.pallas_call(
        functools.partial(middle_kernel, tiles, edges),
        out_shape=(
            jax.ShapeDtypeStruct((frames, kept, width, middle), jnp.bfloat16),
            jax.ShapeDtypeStruct((parties, 2, middle), jnp.float32),
        ),
        in_specs=vmem_specs(5 + 2 * edges),
        out_specs=tuple(vmem_specs(2)),
        scratch_shapes=[pltpu.VMEM((2 * frames, rows + 4, width, 2 * half), jnp.bfloat16)],
        compiler_params=params(),
        cost_estimate=cost(4_000_000_000, 1_000_000),
        name="conv_in",
    )(
        body,
        other_previous,
        *rims,
        *other_rims,
        norm_in,
        conv_in_weight,
        conv_in_bias.reshape(1, middle),
    )
    moments_mid = to_everyone(moments_mid)
    sent = pl.pallas_call(
        pack_kernel,
        out_shape=jax.ShapeDtypeStruct((frames, kept + 1, own, middle), jnp.bfloat16),
        in_specs=vmem_specs(1),
        out_specs=pl.BlockSpec(memory_space=pltpu.VMEM),
        compiler_params=params(),
        cost_estimate=cost(1_000_000_000, 1_000_000),
        name="pack_hidden",
    )(hidden)
    before = shift(sent, 1, 0)
    shown, _ = lax.optimization_barrier((other, sent))
    shortcut = pl.pallas_call(
        shortcut_kernel,
        out_shape=jax.ShapeDtypeStruct((frames, rows, own, outputs), jnp.float32),
        in_specs=vmem_specs(5),
        out_specs=pl.BlockSpec(memory_space=pltpu.VMEM),
        compiler_params=params(),
        cost_estimate=cost(300_000_000, 1_000_000),
        name="shortcut",
    )(
        features,
        shown,
        skip_weight,
        skip_bias.reshape(1, outputs),
        conv_mid_bias.reshape(1, outputs),
    )
    part, norm_mid = pl.pallas_call(
        functools.partial(own_frames_kernel, tiles),
        out_shape=(
            jax.ShapeDtypeStruct((frames, rows, own, outputs), jnp.float32),
            jax.ShapeDtypeStruct((3, middle), jnp.float32),
        ),
        in_specs=vmem_specs(6),
        out_specs=tuple(vmem_specs(2)),
        scratch_shapes=[pltpu.VMEM((frames, rows + 2, width, middle), jnp.bfloat16)],
        compiler_params=params(),
        cost_estimate=cost(2_000_000_000, 1_000_000),
        name="conv_mid_own_frames",
    )(
        hidden,
        moments_mid,
        norm_gain_mid.reshape(1, middle),
        norm_shift_mid.reshape(1, middle),
        conv_mid_weight,
        shortcut,
    )
    return pl.pallas_call(
        functools.partial(last_kernel, tiles),
        out_shape=jax.ShapeDtypeStruct((frames, rows, own, outputs), jnp.bfloat16),
        in_specs=vmem_specs(5),
        out_specs=pl.BlockSpec(memory_space=pl.ANY),
        scratch_shapes=[
            pltpu.VMEM((frames, rows + 2, width, middle), jnp.bfloat16),
            pltpu.VMEM((frames, rows, own, outputs), jnp.bfloat16),
            pltpu.SemaphoreType.DMA((frames,)),
        ],
        compiler_params=params(),
        cost_estimate=cost(2_000_000_000, 1_000_000),
        name="conv_mid_previous_frames",
    )(hidden, before, norm_mid, conv_mid_weight, part)


def solution(mesh):
    in_specs = (P("tm", "tile", None, "section"),) + (P(),) * 10
    out_specs = P("tm", "tile", "section", None)
    return jax.shard_map(shards, mesh=mesh, in_specs=in_specs, out_specs=out_specs, check_vma=False)
```

```python
import functools

import jax
import jax.numpy as jnp
from jax import lax
from jax.experimental import pallas as pl
from jax.experimental.pallas import tpu as pltpu
from jax.sharding import PartitionSpec as P

GROUPS = 32
AXES = ("section", "tm", "tile")
VMEM_LIMIT = 48 * 1024 * 1024
FULL_LIMIT = 63 * 1024 * 1024
RIM = 16


def params(limit=VMEM_LIMIT):
    return pltpu.CompilerParams(vmem_limit_bytes=limit)


def cost(flops, moved):
    return pl.CostEstimate(flops=flops, bytes_accessed=moved, transcendentals=0)


def vmem_specs(count):
    return [pl.BlockSpec(memory_space=pltpu.VMEM)] * count


def silu(u):
    half = 0.5 * u
    return half + half * jnp.tanh(half)


def moments_of(cells):
    mean = jnp.sum(cells, axis=0, keepdims=True) * (1.0 / cells.shape[0])
    off = cells - mean
    return jnp.concatenate([mean, jnp.sum(off * off, axis=0, keepdims=True)], axis=0)


def group_matrix(channels, width):
    shape = (channels, channels)
    row = lax.broadcasted_iota(jnp.int32, shape, 0) // width
    col = lax.broadcasted_iota(jnp.int32, shape, 1) // width
    return jnp.where(row == col, 1.0, 0.0).astype(jnp.bfloat16)


def group_sum(values, matrix):
    parts = []
    for _ in range(3):
        part = values.astype(jnp.bfloat16).astype(jnp.float32)
        parts.append(jnp.broadcast_to(part, (8, part.shape[-1])))
        values = values - part
    stacked = jnp.concatenate(parts + [jnp.zeros_like(parts[0])], axis=0).astype(jnp.bfloat16)
    summed = jnp.dot(stacked, matrix, preferred_element_type=jnp.float32)
    return summed[0:1] + summed[8:9] + summed[16:17]


def scale_and_offset(moments, cells, width, gain, shift):
    devices, _, channels = moments.shape
    matrix = group_matrix(channels, width)
    means = moments[:, 0, :]
    mean = group_sum(jnp.sum(means, axis=0, keepdims=True), matrix) * (1.0 / (devices * width))
    off = means - mean
    total = jnp.sum(moments[:, 1, :] + float(cells) * (off * off), axis=0, keepdims=True)
    spread = group_sum(total, matrix) * (1.0 / (cells * devices * width))
    scale = lax.rsqrt(spread + 1e-6) * gain
    return mean, scale, shift


def apply_norm(values, norm):
    mean, scale, shift = norm
    return silu((values.astype(jnp.float32) - mean) * scale + shift).astype(jnp.bfloat16)


def first_kernel(x_hbm, moments_ref, x_ref, sem):
    copy = pltpu.make_async_copy(x_hbm, x_ref, sem)
    copy.start()
    copy.wait()
    x = x_ref[...]
    cells = x.astype(jnp.float32).reshape(-1, x.shape[-1])
    moments_ref[...] = jnp.broadcast_to(moments_of(cells)[None], moments_ref.shape)


def facing(pairs, block_ref, edge_refs):
    rows = block_ref.shape[1]
    starts = [(rows - 2) * (1 - lax.axis_index("tile"))] if pairs else [0, rows - 2]
    for start, edge_ref in zip(starts, edge_refs):
        edge_ref[...] = block_ref[:, pl.ds(start, 2)]


def own_rows_kernel(pairs, x_ref, order_ref, *edge_refs):
    facing(pairs, x_ref, edge_refs)


def rows_kernel(pairs, x_ref, prev_ref, for_x_ref, for_prev_ref, *edge_refs):
    columns, width = x_ref.shape[2], for_x_ref.shape[2]
    start = (1 - lax.axis_index("section")) * (columns - width)
    theirs = pl.ds(pl.multiple_of(start, RIM), width)
    for_x_ref[...] = x_ref[:, :, theirs, :]
    for_prev_ref[...] = prev_ref[:, :, theirs, :]
    facing(pairs, prev_ref, edge_refs)


def scales_kernel(cells, moments_ref, gain_ref, shift_ref, norm_ref):
    sections, half = gain_ref.shape
    per_section = moments_ref.shape[0] // sections
    for k in range(sections):
        norm = scale_and_offset(
            moments_ref[k * per_section : (k + 1) * per_section],
            cells,
            sections * half // GROUPS,
            gain_ref[k : k + 1],
            shift_ref[k : k + 1],
        )
        norm_ref[k] = jnp.concatenate(norm, axis=0)


def column_taps(weight_ref, t, h):
    return jnp.concatenate([weight_ref[t, h, w] for w in range(3)], axis=-1)


def shift_and_add(total, rows, width):
    outputs = total.shape[-1] // 3
    total = total.reshape(rows, width, 3 * outputs)
    before, middle, after = (total[..., k * outputs : (k + 1) * outputs] for k in range(3))
    before = jnp.concatenate([before[:, :1], before[:, :-1]], axis=1)
    after = jnp.concatenate([after[:, 1:], after[:, -1:]], axis=1)
    return middle + before + after


def conv_in_rows(act_ref, weight_ref, frames, top, rows, width):
    totals = [None] * frames
    for a in range(act_ref.shape[0]):
        reached = [f for f in range(frames) if 0 <= a - f <= 2]
        for h in range(3):
            cells = act_ref[a, pl.ds(top + h, rows)]
            cells = cells.reshape(rows * width, cells.shape[-1])
            taps = [column_taps(weight_ref, a - f, h) for f in reached]
            sums = jnp.dot(
                cells, jnp.concatenate(taps, axis=-1), preferred_element_type=jnp.float32
            )
            n = sums.shape[-1] // len(reached)
            for k, f in enumerate(reached):
                part = sums[:, k * n : (k + 1) * n]
                totals[f] = part if totals[f] is None else totals[f] + part
    return [shift_and_add(total, rows, width) for total in totals]


def conv_mid_rows(act_ref, weight_ref, taken, rows, width):
    cells, taps = [], []
    for t, frame in taken:
        for h in range(3):
            block = act_ref[frame, h : h + rows]
            cells.append(block.reshape(rows * width, block.shape[-1]))
            taps.append(column_taps(weight_ref, t, h))
    total = jnp.dot(
        jnp.concatenate(cells, axis=-1),
        jnp.concatenate(taps, axis=0),
        preferred_element_type=jnp.float32,
    )
    return shift_and_add(total, rows, width)


def first_row(tiles, tile):
    return 1 - tile if tiles == 2 else 0


def body_kernel(x_ref, prev_ref, other_x_ref, norm_ref, body_ref):
    section = lax.axis_index("section")
    frames, _, columns, half = x_ref.shape
    width = body_ref.shape[2]
    mine = pl.ds(pl.multiple_of(section * (columns - width), RIM), width)
    for which, first, ref, cols in (
        (section, 0, prev_ref, mine),
        (section, frames, x_ref, mine),
        (1 - section, frames, other_x_ref, slice(None)),
    ):
        norm = tuple(norm_ref[which, k : k + 1] for k in range(3))
        lanes = pl.ds(pl.multiple_of(which * half, half), half)
        for f in range(frames):
            body_ref[first + f, :, :, lanes] = apply_norm(ref[f, :, cols, :], norm)


def middle_kernel(tiles, sides, *refs):
    body_ref, other_prev_ref = refs[:2]
    rim_refs, other_rim_refs = refs[2 : 2 + 2 * sides], refs[2 + 2 * sides : 2 + 4 * sides]
    norm_ref, weight_ref, bias_ref, hidden_ref, out_moments_ref, act_ref = refs[2 + 4 * sides :]
    section, tm, tile = (lax.axis_index(axis) for axis in AXES)
    columns, half = rim_refs[0].shape[2:]
    frames, rows, width = body_ref.shape[0] // 2, body_ref.shape[1], body_ref.shape[2]
    kept = hidden_ref.shape[1]
    own = columns // 2
    first = pl.multiple_of(section * (columns - width), RIM)
    cols = pl.ds(first, width)
    top = first_row(tiles, tile)
    rim_rows = (0, rows + 2) if sides == 2 else ((rows + 2) * (1 - tile),)
    act_ref[:, 2 : 2 + rows] = body_ref[...]
    for which, rims in ((section, rim_refs), (1 - section, other_rim_refs)):
        norm = tuple(norm_ref[which, k : k + 1] for k in range(3))
        lanes = pl.ds(pl.multiple_of(which * half, half), half)
        for k, rim in enumerate(rims):
            start, row = k // sides * frames, rim_rows[k % sides]
            for f in range(frames):
                act_ref[start + f, pl.ds(row, 2), :, lanes] = apply_norm(rim[f, :, cols, :], norm)
    for f in range(frames):
        act_ref[f, 2 : 2 + rows, :, lanes] = apply_norm(other_prev_ref[f], norm)

    @pl.when(tile == 0)
    def _():
        for f in range(2 * frames):
            act_ref[f, 1] = act_ref[f, 2]

    @pl.when(tile == tiles - 1)
    def _():
        for f in range(2 * frames):
            act_ref[f, rows + 2] = act_ref[f, rows + 1]

    @pl.when(tm == 0)
    def _():
        for f in range(frames):
            act_ref[f] = act_ref[frames]

    for f, hidden in enumerate(conv_in_rows(act_ref, weight_ref, frames, top, kept, width)):
        hidden_ref[f] = (hidden + bias_ref[...]).astype(jnp.bfloat16)

    cells = hidden_ref[:, pl.ds(1 - top, rows), pl.ds(first, own), :]
    cells = cells.astype(jnp.float32).reshape(-1, cells.shape[-1])
    out_moments_ref[...] = jnp.broadcast_to(moments_of(cells)[None], out_moments_ref.shape)


def pack_kernel(hidden_ref, sent_ref):
    section = lax.axis_index("section")
    frames, kept, width, channels = hidden_ref.shape
    own = sent_ref.shape[2]
    first = pl.multiple_of(section * (width - own), RIM)
    for f in range(frames):
        sent_ref[f, :kept] = hidden_ref[f, :, pl.ds(first, own), :]
        hidden = hidden_ref[f].astype(jnp.float32)
        rim = jnp.where(section == 0, hidden[:, own, :], hidden[:, width - own - 1, :])
        spare = jnp.zeros((own - kept, channels), jnp.float32)
        sent_ref[f, kept] = jnp.concatenate([rim, spare], axis=0).astype(jnp.bfloat16)


def repeat_edges(act_ref, count, tiles, rows):
    tile = lax.axis_index("tile")

    @pl.when(tile == 0)
    def _():
        for f in range(count):
            act_ref[f, 0] = act_ref[f, 1]

    @pl.when(tile == tiles - 1)
    def _():
        for f in range(count):
            act_ref[f, rows + 1] = act_ref[f, rows]


def own_columns(values, own):
    section = lax.axis_index("section")
    width = values.shape[1]
    return jnp.where(section == 0, values[:, :own], values[:, width - own :])


def shortcut_kernel(x_ref, other_x_ref, skip_ref, skip_bias_ref, bias_ref, part_ref):
    section = lax.axis_index("section")
    frames, rows, columns, half = x_ref.shape
    own = columns // 2
    mine = pl.ds(pl.multiple_of(section * own, own), own)
    within = pl.ds(pl.multiple_of(section * (other_x_ref.shape[2] - own), RIM), own)
    skip_here = skip_ref[pl.ds(pl.multiple_of(section * half, half), half), :]
    skip_there = skip_ref[pl.ds(pl.multiple_of((1 - section) * half, half), half), :]
    for f in range(frames):
        here = x_ref[f, :, mine, :].reshape(rows * own, half)
        there = other_x_ref[f, :, within, :].reshape(rows * own, half)
        shortcut = jnp.dot(here, skip_here, preferred_element_type=jnp.float32)
        shortcut = shortcut + jnp.dot(there, skip_there, preferred_element_type=jnp.float32)
        part_ref[f] = (shortcut + (skip_bias_ref[...] + bias_ref[...])).reshape(rows, own, -1)


def own_frames_kernel(
    tiles,
    hidden_ref,
    moments_ref,
    gain_ref,
    shift_ref,
    weight_ref,
    shortcut_ref,
    part_ref,
    norm_ref,
    act_ref,
):
    frames, kept, width, outputs = hidden_ref.shape
    rows, own = part_ref.shape[1:3]
    top = first_row(tiles, lax.axis_index("tile"))
    norm = scale_and_offset(
        moments_ref[...],
        frames * rows * own,
        outputs // GROUPS,
        gain_ref[...],
        shift_ref[...],
    )
    norm_ref[...] = jnp.concatenate(norm, axis=0)
    for f in range(frames):
        act_ref[f, pl.ds(top, kept)] = apply_norm(hidden_ref[f], norm)
    repeat_edges(act_ref, frames, tiles, rows)
    for f in range(frames):
        taken = [(k - f + 2, k) for k in range(f - 2, f + 1) if k >= 0]
        residual = own_columns(conv_mid_rows(act_ref, weight_ref, taken, rows, width), own)
        part_ref[f] = shortcut_ref[f] + residual


def last_kernel(
    tiles, hidden_ref, before_ref, norm_ref, weight_ref, part_ref, out_hbm, act_ref, out_ref, sems
):
    section, tm, tile = (lax.axis_index(axis) for axis in AXES)
    frames, kept, width, outputs = hidden_ref.shape
    rows, own = part_ref.shape[1:3]
    top = first_row(tiles, tile)
    first = pl.multiple_of(section * (width - own), RIM)
    beside = pl.multiple_of((1 - section) * own, RIM)
    norm = tuple(norm_ref[k : k + 1] for k in range(3))
    for f in range(frames):
        act_ref[f, pl.ds(top, kept), pl.ds(first, own), :] = apply_norm(before_ref[f, :kept], norm)
        rim = apply_norm(before_ref[f, kept], norm).astype(jnp.float32)[:kept]
        rim = jnp.broadcast_to(rim[:, None, :], (kept, width - own, outputs))
        act_ref[f, pl.ds(top, kept), pl.ds(beside, width - own), :] = rim.astype(jnp.bfloat16)

    @pl.when(tm == 0)
    def _():
        start = apply_norm(hidden_ref[0], norm)
        for f in range(frames):
            act_ref[f, pl.ds(top, kept)] = start

    repeat_edges(act_ref, frames, tiles, rows)
    copies = []
    for f in range(frames):
        taken = [(k - f, k) for k in range(f, f + 3) if k < frames]
        residual = own_columns(conv_mid_rows(act_ref, weight_ref, taken, rows, width), own)
        out_ref[f] = (part_ref[f] + residual).astype(jnp.bfloat16)
        copies.append(pltpu.make_async_copy(out_ref.at[f], out_hbm.at[f], sems.at[f]))
        copies[-1].start()
    for copy in copies:
        copy.wait()


def pairs_for(tm_count, tile_count, tm_step, tile_step):
    out = []
    for a in range(tm_count):
        for b in range(tile_count):
            c, d = a + tm_step, b + tile_step
            if 0 <= c < tm_count and 0 <= d < tile_count:
                out.append((a * tile_count + b, c * tile_count + d))
    return out


def to_everyone(moments):
    return lax.all_to_all(moments, AXES, 0, 0, tiled=True)


def shards(
    features,
    norm_gain_in,
    norm_shift_in,
    conv_in_weight,
    conv_in_bias,
    norm_gain_mid,
    norm_shift_mid,
    conv_mid_weight,
    conv_mid_bias,
    skip_weight,
    skip_bias,
):
    sections, tms, tiles = (lax.axis_size(axis) for axis in AXES)
    parties = sections * tms * tiles
    frames, rows, columns, half = features.shape
    own = columns // sections
    width = own + RIM
    middle = conv_in_weight.shape[-1]
    outputs = conv_mid_weight.shape[-1]
    grid_axes = ("tm", "tile")

    def shift(value, tm_step, tile_step):
        return lax.ppermute(value, grid_axes, pairs_for(tms, tiles, tm_step, tile_step))

    def swap(value):
        return lax.ppermute(value, "section", [(0, 1), (1, 0)])

    previous = shift(features, 1, 0)
    sums = pl.pallas_call(
        first_kernel,
        out_shape=jax.ShapeDtypeStruct((parties, 2, half), jnp.float32),
        in_specs=[pl.BlockSpec(memory_space=pl.ANY)],
        out_specs=pl.BlockSpec(memory_space=pltpu.VMEM),
        scratch_shapes=[
            pltpu.VMEM(features.shape, features.dtype),
            pltpu.SemaphoreType.DMA,
        ],
        compiler_params=params(FULL_LIMIT),
        cost_estimate=cost(1_000_000_000, 1_000_000),
        name="feature_moments",
    )(features)
    moments = to_everyone(sums)
    previous, _ = lax.optimization_barrier((previous, sums))
    edges = 1 if tiles == 2 else 2
    edge = jax.ShapeDtypeStruct((frames, 2, columns, half), features.dtype)
    cut = jax.ShapeDtypeStruct((frames, rows, width, half), features.dtype)
    own_edges = pl.pallas_call(
        functools.partial(own_rows_kernel, tiles == 2),
        out_shape=(edge,) * edges,
        in_specs=[*vmem_specs(1), pl.BlockSpec(memory_space=pl.ANY)],
        out_specs=tuple(vmem_specs(edges)),
        compiler_params=params(),
        cost_estimate=cost(0, 1_000),
        name="own_facing_rows",
    )(features, sums)
    for_x, for_previous, *previous_edges = pl.pallas_call(
        functools.partial(rows_kernel, tiles == 2),
        out_shape=(cut, cut) + (edge,) * edges,
        in_specs=vmem_specs(2),
        out_specs=tuple(vmem_specs(2 + edges)),
        compiler_params=params(),
        cost_estimate=cost(500_000_000, 1_000_000),
        name="facing_rows",
    )(features, previous)

    def from_neighbours(edge_rows):
        if tiles == 2:
            return [lax.ppermute(edge_rows[0], "tile", [(0, 1), (1, 0)])]
        return [shift(edge_rows[1], 0, 1), shift(edge_rows[0], 0, -1)]

    own_rims = from_neighbours(own_edges)
    rims = from_neighbours(previous_edges) + own_rims
    other = swap(for_x)
    other_previous = swap(for_previous)
    norm_in = pl.pallas_call(
        functools.partial(scales_kernel, frames * rows * columns),
        out_shape=jax.ShapeDtypeStruct((sections, 3, half), jnp.float32),
        in_specs=vmem_specs(3),
        out_specs=pl.BlockSpec(memory_space=pltpu.VMEM),
        compiler_params=params(),
        cost_estimate=cost(2_000_000_000, 1_000_000),
        name="feature_scales",
    )(moments, norm_gain_in.reshape(sections, half), norm_shift_in.reshape(sections, half))
    norm_in, *rims = lax.optimization_barrier((norm_in, *rims))
    other_rims = [swap(rim) for rim in rims]

    kept = rows + edges
    body = pl.pallas_call(
        body_kernel,
        out_shape=jax.ShapeDtypeStruct((2 * frames, rows, width, 2 * half), jnp.bfloat16),
        in_specs=vmem_specs(4),
        out_specs=pl.BlockSpec(memory_space=pltpu.VMEM),
        compiler_params=params(),
        cost_estimate=cost(1_000_000_000, 1_000_000),
        name="norm_body",
    )(features, previous, other, norm_in)
    hidden, moments_mid = pl.pallas_call(
        functools.partial(middle_kernel, tiles, edges),
        out_shape=(
            jax.ShapeDtypeStruct((frames, kept, width, middle), jnp.bfloat16),
            jax.ShapeDtypeStruct((parties, 2, middle), jnp.float32),
        ),
        in_specs=vmem_specs(5 + 4 * edges),
        out_specs=tuple(vmem_specs(2)),
        scratch_shapes=[pltpu.VMEM((2 * frames, rows + 4, width, 2 * half), jnp.bfloat16)],
        compiler_params=params(),
        cost_estimate=cost(4_000_000_000, 1_000_000),
        name="conv_in",
    )(
        body,
        other_previous,
        *rims,
        *other_rims,
        norm_in,
        conv_in_weight,
        conv_in_bias.reshape(1, middle),
    )
    moments_mid = to_everyone(moments_mid)
    sent = pl.pallas_call(
        pack_kernel,
        out_shape=jax.ShapeDtypeStruct((frames, kept + 1, own, middle), jnp.bfloat16),
        in_specs=vmem_specs(1),
        out_specs=pl.BlockSpec(memory_space=pltpu.VMEM),
        compiler_params=params(),
        cost_estimate=cost(1_000_000_000, 1_000_000),
        name="pack_hidden",
    )(hidden)
    before = shift(sent, 1, 0)
    shown, _ = lax.optimization_barrier((other, sent))
    shortcut = pl.pallas_call(
        shortcut_kernel,
        out_shape=jax.ShapeDtypeStruct((frames, rows, own, outputs), jnp.float32),
        in_specs=vmem_specs(5),
        out_specs=pl.BlockSpec(memory_space=pltpu.VMEM),
        compiler_params=params(),
        cost_estimate=cost(300_000_000, 1_000_000),
        name="shortcut",
    )(
        features,
        shown,
        skip_weight,
        skip_bias.reshape(1, outputs),
        conv_mid_bias.reshape(1, outputs),
    )
    part, norm_mid = pl.pallas_call(
        functools.partial(own_frames_kernel, tiles),
        out_shape=(
            jax.ShapeDtypeStruct((frames, rows, own, outputs), jnp.float32),
            jax.ShapeDtypeStruct((3, middle), jnp.float32),
        ),
        in_specs=vmem_specs(6),
        out_specs=tuple(vmem_specs(2)),
        scratch_shapes=[pltpu.VMEM((frames, rows + 2, width, middle), jnp.bfloat16)],
        compiler_params=params(),
        cost_estimate=cost(2_000_000_000, 1_000_000),
        name="conv_mid_own_frames",
    )(
        hidden,
        moments_mid,
        norm_gain_mid.reshape(1, middle),
        norm_shift_mid.reshape(1, middle),
        conv_mid_weight,
        shortcut,
    )
    return pl.pallas_call(
        functools.partial(last_kernel, tiles),
        out_shape=jax.ShapeDtypeStruct((frames, rows, own, outputs), jnp.bfloat16),
        in_specs=vmem_specs(5),
        out_specs=pl.BlockSpec(memory_space=pl.ANY),
        scratch_shapes=[
            pltpu.VMEM((frames, rows + 2, width, middle), jnp.bfloat16),
            pltpu.VMEM((frames, rows, own, outputs), jnp.bfloat16),
            pltpu.SemaphoreType.DMA((frames,)),
        ],
        compiler_params=params(),
        cost_estimate=cost(2_000_000_000, 1_000_000),
        name="conv_mid_previous_frames",
    )(hidden, before, norm_mid, conv_mid_weight, part)


def solution(mesh):
    in_specs = (P("tm", "tile", None, "section"),) + (P(),) * 10
    out_specs = P("tm", "tile", "section", None)
    return jax.shard_map(shards, mesh=mesh, in_specs=in_specs, out_specs=out_specs, check_vma=False)
```

```python
import functools

import jax
import jax.numpy as jnp
from jax import lax
from jax.experimental import pallas as pl
from jax.experimental.pallas import tpu as pltpu
from jax.sharding import PartitionSpec as P

GROUPS = 32
AXES = ("section", "tm", "tile")
VMEM_LIMIT = 48 * 1024 * 1024
FULL_LIMIT = 63 * 1024 * 1024
RIM = 16


def params(limit=VMEM_LIMIT):
    return pltpu.CompilerParams(vmem_limit_bytes=limit)


def cost(flops, moved):
    return pl.CostEstimate(flops=flops, bytes_accessed=moved, transcendentals=0)


def vmem_specs(count):
    return [pl.BlockSpec(memory_space=pltpu.VMEM)] * count


def silu(u):
    half = 0.5 * u
    return half + half * jnp.tanh(half)


def moments_of(cells):
    mean = jnp.sum(cells, axis=0, keepdims=True) * (1.0 / cells.shape[0])
    off = cells - mean
    return jnp.concatenate([mean, jnp.sum(off * off, axis=0, keepdims=True)], axis=0)


def group_matrix(channels, width):
    shape = (channels, channels)
    row = lax.broadcasted_iota(jnp.int32, shape, 0) // width
    col = lax.broadcasted_iota(jnp.int32, shape, 1) // width
    return jnp.where(row == col, 1.0, 0.0).astype(jnp.bfloat16)


def group_sum(values, matrix):
    parts = []
    for _ in range(3):
        part = values.astype(jnp.bfloat16).astype(jnp.float32)
        parts.append(jnp.broadcast_to(part, (8, part.shape[-1])))
        values = values - part
    stacked = jnp.concatenate(parts + [jnp.zeros_like(parts[0])], axis=0).astype(jnp.bfloat16)
    summed = jnp.dot(stacked, matrix, preferred_element_type=jnp.float32)
    return summed[0:1] + summed[8:9] + summed[16:17]


def scale_and_offset(moments, cells, width, gain, shift):
    devices, _, channels = moments.shape
    matrix = group_matrix(channels, width)
    means = moments[:, 0, :]
    mean = group_sum(jnp.sum(means, axis=0, keepdims=True), matrix) * (1.0 / (devices * width))
    off = means - mean
    total = jnp.sum(moments[:, 1, :] + float(cells) * (off * off), axis=0, keepdims=True)
    spread = group_sum(total, matrix) * (1.0 / (cells * devices * width))
    scale = lax.rsqrt(spread + 1e-6) * gain
    return mean, scale, shift


def apply_norm(values, norm):
    mean, scale, shift = norm
    return silu((values.astype(jnp.float32) - mean) * scale + shift).astype(jnp.bfloat16)


def first_kernel(x_hbm, moments_ref, x_ref, sems):
    frames, rows = x_ref.shape[:2]
    pieces = [(f, slice(k, k + rows // 2)) for f in range(frames) for k in (0, rows // 2)]
    copies = [
        pltpu.make_async_copy(x_hbm.at[f, part], x_ref.at[f, part], sems.at[k])
        for k, (f, part) in enumerate(pieces)
    ]
    for copy in copies:
        copy.start()
    means, spreads = [], []
    for copy, (f, part) in zip(copies, pieces):
        copy.wait()
        cells = x_ref[f, part].astype(jnp.float32).reshape(-1, x_ref.shape[-1])
        mean = jnp.sum(cells, axis=0, keepdims=True) * (1.0 / cells.shape[0])
        off = cells - mean
        means.append(mean)
        spreads.append(jnp.sum(off * off, axis=0, keepdims=True))
    mean = sum(means) * (1.0 / len(pieces))
    spread = sum(spreads)
    for part in means:
        spread = spread + float(cells.shape[0]) * ((part - mean) * (part - mean))
    own = jnp.concatenate([mean, spread], axis=0)
    moments_ref[...] = jnp.broadcast_to(own[None], moments_ref.shape)


def rows_kernel(pairs, x_ref, prev_ref, for_x_ref, for_prev_ref, *edge_refs):
    frames, rows, columns = x_ref.shape[:3]
    width = for_x_ref.shape[2]
    start = (1 - lax.axis_index("section")) * (columns - width)
    theirs = pl.ds(pl.multiple_of(start, RIM), width)
    for_x_ref[...] = x_ref[:, :, theirs, :]
    for_prev_ref[...] = prev_ref[:, :, theirs, :]
    if pairs:
        starts = [(rows - 2) * (1 - lax.axis_index("tile"))]
    else:
        starts = [0, rows - 2]
    for start, edge_ref in zip(starts, edge_refs):
        edge_ref[:frames] = prev_ref[:, pl.ds(start, 2)]
        edge_ref[frames:] = x_ref[:, pl.ds(start, 2)]


def scales_kernel(cells, moments_ref, gain_ref, shift_ref, norm_ref):
    sections, half = gain_ref.shape
    per_section = moments_ref.shape[0] // sections
    for k in range(sections):
        norm = scale_and_offset(
            moments_ref[k * per_section : (k + 1) * per_section],
            cells,
            sections * half // GROUPS,
            gain_ref[k : k + 1],
            shift_ref[k : k + 1],
        )
        norm_ref[k] = jnp.concatenate(norm, axis=0)


def column_taps(weight_ref, t, h):
    return jnp.concatenate([weight_ref[t, h, w] for w in range(3)], axis=-1)


def shift_and_add(total, rows, width):
    outputs = total.shape[-1] // 3
    total = total.reshape(rows, width, 3 * outputs)
    before, middle, after = (total[..., k * outputs : (k + 1) * outputs] for k in range(3))
    before = jnp.concatenate([before[:, :1], before[:, :-1]], axis=1)
    after = jnp.concatenate([after[:, 1:], after[:, -1:]], axis=1)
    return middle + before + after


def conv_in_rows(act_ref, weight_ref, frames, top, rows, width):
    totals = [None] * frames
    for a in range(act_ref.shape[0]):
        reached = [f for f in range(frames) if 0 <= a - f <= 2]
        for h in range(3):
            cells = act_ref[a, pl.ds(top + h, rows)]
            cells = cells.reshape(rows * width, cells.shape[-1])
            taps = [column_taps(weight_ref, a - f, h) for f in reached]
            sums = jnp.dot(
                cells, jnp.concatenate(taps, axis=-1), preferred_element_type=jnp.float32
            )
            n = sums.shape[-1] // len(reached)
            for k, f in enumerate(reached):
                part = sums[:, k * n : (k + 1) * n]
                totals[f] = part if totals[f] is None else totals[f] + part
    return [shift_and_add(total, rows, width) for total in totals]


def conv_mid_rows(act_ref, weight_ref, taken, rows, width):
    cells, taps = [], []
    for t, frame in taken:
        for h in range(3):
            block = act_ref[frame, h : h + rows]
            cells.append(block.reshape(rows * width, block.shape[-1]))
            taps.append(column_taps(weight_ref, t, h))
    total = jnp.dot(
        jnp.concatenate(cells, axis=-1),
        jnp.concatenate(taps, axis=0),
        preferred_element_type=jnp.float32,
    )
    return shift_and_add(total, rows, width)


def first_row(tiles, tile):
    return 1 - tile if tiles == 2 else 0


def body_kernel(x_ref, prev_ref, other_x_ref, norm_ref, body_ref):
    section = lax.axis_index("section")
    frames, _, columns, half = x_ref.shape
    width = body_ref.shape[2]
    mine = pl.ds(pl.multiple_of(section * (columns - width), RIM), width)
    for which, first, ref, cols in (
        (section, 0, prev_ref, mine),
        (section, frames, x_ref, mine),
        (1 - section, frames, other_x_ref, slice(None)),
    ):
        norm = tuple(norm_ref[which, k : k + 1] for k in range(3))
        lanes = pl.ds(pl.multiple_of(which * half, half), half)
        for f in range(frames):
            body_ref[first + f, :, :, lanes] = apply_norm(ref[f, :, cols, :], norm)


def middle_kernel(tiles, sides, *refs):
    body_ref, other_prev_ref = refs[:2]
    rim_refs, other_rim_refs = refs[2 : 2 + sides], refs[2 + sides : 2 + 2 * sides]
    norm_ref, weight_ref, bias_ref, hidden_ref, out_moments_ref, act_ref = refs[2 + 2 * sides :]
    section, tm, tile = (lax.axis_index(axis) for axis in AXES)
    columns, half = rim_refs[0].shape[2:]
    frames, rows, width = body_ref.shape[0] // 2, body_ref.shape[1], body_ref.shape[2]
    kept = hidden_ref.shape[1]
    own = columns // 2
    first = pl.multiple_of(section * (columns - width), RIM)
    cols = pl.ds(first, width)
    top = first_row(tiles, tile)
    rim_rows = (0, rows + 2) if sides == 2 else ((rows + 2) * (1 - tile),)
    act_ref[:, 2 : 2 + rows] = body_ref[...]
    for which, rims in ((section, rim_refs), (1 - section, other_rim_refs)):
        norm = tuple(norm_ref[which, k : k + 1] for k in range(3))
        lanes = pl.ds(pl.multiple_of(which * half, half), half)
        for f in range(2 * frames):
            for row, rim in zip(rim_rows, rims):
                act_ref[f, pl.ds(row, 2), :, lanes] = apply_norm(rim[f, :, cols, :], norm)
    for f in range(frames):
        act_ref[f, 2 : 2 + rows, :, lanes] = apply_norm(other_prev_ref[f], norm)

    @pl.when(tile == 0)
    def _():
        for f in range(2 * frames):
            act_ref[f, 1] = act_ref[f, 2]

    @pl.when(tile == tiles - 1)
    def _():
        for f in range(2 * frames):
            act_ref[f, rows + 2] = act_ref[f, rows + 1]

    @pl.when(tm == 0)
    def _():
        for f in range(frames):
            act_ref[f] = act_ref[frames]

    for f, hidden in enumerate(conv_in_rows(act_ref, weight_ref, frames, top, kept, width)):
        hidden_ref[f] = (hidden + bias_ref[...]).astype(jnp.bfloat16)

    cells = hidden_ref[:, pl.ds(1 - top, rows), pl.ds(first, own), :]
    cells = cells.astype(jnp.float32).reshape(-1, cells.shape[-1])
    out_moments_ref[...] = jnp.broadcast_to(moments_of(cells)[None], out_moments_ref.shape)


def pack_kernel(hidden_ref, sent_ref):
    section = lax.axis_index("section")
    frames, kept, width, channels = hidden_ref.shape
    own = sent_ref.shape[2]
    first = pl.multiple_of(section * (width - own), RIM)
    for f in range(frames):
        sent_ref[f, :kept] = hidden_ref[f, :, pl.ds(first, own), :]
        hidden = hidden_ref[f].astype(jnp.float32)
        rim = jnp.where(section == 0, hidden[:, own, :], hidden[:, width - own - 1, :])
        spare = jnp.zeros((own - kept, channels), jnp.float32)
        sent_ref[f, kept] = jnp.concatenate([rim, spare], axis=0).astype(jnp.bfloat16)


def repeat_edges(act_ref, count, tiles, rows):
    tile = lax.axis_index("tile")

    @pl.when(tile == 0)
    def _():
        for f in range(count):
            act_ref[f, 0] = act_ref[f, 1]

    @pl.when(tile == tiles - 1)
    def _():
        for f in range(count):
            act_ref[f, rows + 1] = act_ref[f, rows]


def own_columns(values, own):
    section = lax.axis_index("section")
    width = values.shape[1]
    return jnp.where(section == 0, values[:, :own], values[:, width - own :])


def shortcut_kernel(x_ref, other_x_ref, skip_ref, skip_bias_ref, bias_ref, part_ref):
    section = lax.axis_index("section")
    frames, rows, columns, half = x_ref.shape
    own = columns // 2
    mine = pl.ds(pl.multiple_of(section * own, own), own)
    within = pl.ds(pl.multiple_of(section * (other_x_ref.shape[2] - own), RIM), own)
    skip_here = skip_ref[pl.ds(pl.multiple_of(section * half, half), half), :]
    skip_there = skip_ref[pl.ds(pl.multiple_of((1 - section) * half, half), half), :]
    for f in range(frames):
        here = x_ref[f, :, mine, :].reshape(rows * own, half)
        there = other_x_ref[f, :, within, :].reshape(rows * own, half)
        shortcut = jnp.dot(here, skip_here, preferred_element_type=jnp.float32)
        shortcut = shortcut + jnp.dot(there, skip_there, preferred_element_type=jnp.float32)
        part_ref[f] = (shortcut + (skip_bias_ref[...] + bias_ref[...])).reshape(rows, own, -1)


def own_frames_kernel(
    tiles,
    hidden_ref,
    moments_ref,
    gain_ref,
    shift_ref,
    weight_ref,
    shortcut_ref,
    part_ref,
    norm_ref,
    act_ref,
):
    frames, kept, width, outputs = hidden_ref.shape
    rows, own = part_ref.shape[1:3]
    top = first_row(tiles, lax.axis_index("tile"))
    norm = scale_and_offset(
        moments_ref[...],
        frames * rows * own,
        outputs // GROUPS,
        gain_ref[...],
        shift_ref[...],
    )
    norm_ref[...] = jnp.concatenate(norm, axis=0)
    for f in range(frames):
        act_ref[f, pl.ds(top, kept)] = apply_norm(hidden_ref[f], norm)
    repeat_edges(act_ref, frames, tiles, rows)
    for f in range(frames):
        taken = [(k - f + 2, k) for k in range(f - 2, f + 1) if k >= 0]
        residual = own_columns(conv_mid_rows(act_ref, weight_ref, taken, rows, width), own)
        part_ref[f] = shortcut_ref[f] + residual


def last_kernel(
    tiles, hidden_ref, before_ref, norm_ref, weight_ref, part_ref, out_hbm, act_ref, out_ref, sems
):
    section, tm, tile = (lax.axis_index(axis) for axis in AXES)
    frames, kept, width, outputs = hidden_ref.shape
    rows, own = part_ref.shape[1:3]
    top = first_row(tiles, tile)
    first = pl.multiple_of(section * (width - own), RIM)
    beside = pl.multiple_of((1 - section) * own, RIM)
    norm = tuple(norm_ref[k : k + 1] for k in range(3))
    for f in range(frames):
        act_ref[f, pl.ds(top, kept), pl.ds(first, own), :] = apply_norm(before_ref[f, :kept], norm)
        rim = apply_norm(before_ref[f, kept], norm).astype(jnp.float32)[:kept]
        rim = jnp.broadcast_to(rim[:, None, :], (kept, width - own, outputs))
        act_ref[f, pl.ds(top, kept), pl.ds(beside, width - own), :] = rim.astype(jnp.bfloat16)

    @pl.when(tm == 0)
    def _():
        start = apply_norm(hidden_ref[0], norm)
        for f in range(frames):
            act_ref[f, pl.ds(top, kept)] = start

    repeat_edges(act_ref, frames, tiles, rows)
    copies = []
    for f in range(frames):
        taken = [(k - f, k) for k in range(f, f + 3) if k < frames]
        residual = own_columns(conv_mid_rows(act_ref, weight_ref, taken, rows, width), own)
        out_ref[f] = (part_ref[f] + residual).astype(jnp.bfloat16)
        copies.append(pltpu.make_async_copy(out_ref.at[f], out_hbm.at[f], sems.at[f]))
        copies[-1].start()
    for copy in copies:
        copy.wait()


def pairs_for(tm_count, tile_count, tm_step, tile_step):
    out = []
    for a in range(tm_count):
        for b in range(tile_count):
            c, d = a + tm_step, b + tile_step
            if 0 <= c < tm_count and 0 <= d < tile_count:
                out.append((a * tile_count + b, c * tile_count + d))
    return out


def to_everyone(moments):
    return lax.all_to_all(moments, AXES, 0, 0, tiled=True)


def shards(
    features,
    norm_gain_in,
    norm_shift_in,
    conv_in_weight,
    conv_in_bias,
    norm_gain_mid,
    norm_shift_mid,
    conv_mid_weight,
    conv_mid_bias,
    skip_weight,
    skip_bias,
):
    sections, tms, tiles = (lax.axis_size(axis) for axis in AXES)
    parties = sections * tms * tiles
    frames, rows, columns, half = features.shape
    own = columns // sections
    width = own + RIM
    middle = conv_in_weight.shape[-1]
    outputs = conv_mid_weight.shape[-1]
    grid_axes = ("tm", "tile")

    def shift(value, tm_step, tile_step):
        return lax.ppermute(value, grid_axes, pairs_for(tms, tiles, tm_step, tile_step))

    def swap(value):
        return lax.ppermute(value, "section", [(0, 1), (1, 0)])

    previous = shift(features, 1, 0)
    sums = pl.pallas_call(
        first_kernel,
        out_shape=jax.ShapeDtypeStruct((parties, 2, half), jnp.float32),
        in_specs=[pl.BlockSpec(memory_space=pl.ANY)],
        out_specs=pl.BlockSpec(memory_space=pltpu.VMEM),
        scratch_shapes=[
            pltpu.VMEM(features.shape, features.dtype),
            pltpu.SemaphoreType.DMA((2 * frames,)),
        ],
        compiler_params=params(FULL_LIMIT),
        cost_estimate=cost(1_000_000_000, 1_000_000),
        name="feature_moments",
    )(features)
    moments = to_everyone(sums)
    previous, _ = lax.optimization_barrier((previous, sums))
    edges = 1 if tiles == 2 else 2
    edge = jax.ShapeDtypeStruct((2 * frames, 2, columns, half), features.dtype)
    cut = jax.ShapeDtypeStruct((frames, rows, width, half), features.dtype)
    for_x, for_previous, *edge_rows = pl.pallas_call(
        functools.partial(rows_kernel, tiles == 2),
        out_shape=(cut, cut) + (edge,) * edges,
        in_specs=vmem_specs(2),
        out_specs=tuple(vmem_specs(2 + edges)),
        compiler_params=params(),
        cost_estimate=cost(500_000_000, 1_000_000),
        name="facing_rows",
    )(features, previous)
    if tiles == 2:
        rims = [lax.ppermute(edge_rows[0], "tile", [(0, 1), (1, 0)])]
    else:
        rims = [shift(edge_rows[1], 0, 1), shift(edge_rows[0], 0, -1)]
    other = swap(for_x)
    other_previous = swap(for_previous)
    norm_in = pl.pallas_call(
        functools.partial(scales_kernel, frames * rows * columns),
        out_shape=jax.ShapeDtypeStruct((sections, 3, half), jnp.float32),
        in_specs=vmem_specs(3),
        out_specs=pl.BlockSpec(memory_space=pltpu.VMEM),
        compiler_params=params(),
        cost_estimate=cost(2_000_000_000, 1_000_000),
        name="feature_scales",
    )(moments, norm_gain_in.reshape(sections, half), norm_shift_in.reshape(sections, half))
    norm_in, *rims = lax.optimization_barrier((norm_in, *rims))
    other_rims = [swap(rim) for rim in rims]

    kept = rows + edges
    body = pl.pallas_call(
        body_kernel,
        out_shape=jax.ShapeDtypeStruct((2 * frames, rows, width, 2 * half), jnp.bfloat16),
        in_specs=vmem_specs(4),
        out_specs=pl.BlockSpec(memory_space=pltpu.VMEM),
        compiler_params=params(),
        cost_estimate=cost(1_000_000_000, 1_000_000),
        name="norm_body",
    )(features, previous, other, norm_in)
    hidden, moments_mid = pl.pallas_call(
        functools.partial(middle_kernel, tiles, edges),
        out_shape=(
            jax.ShapeDtypeStruct((frames, kept, width, middle), jnp.bfloat16),
            jax.ShapeDtypeStruct((parties, 2, middle), jnp.float32),
        ),
        in_specs=vmem_specs(5 + 2 * edges),
        out_specs=tuple(vmem_specs(2)),
        scratch_shapes=[pltpu.VMEM((2 * frames, rows + 4, width, 2 * half), jnp.bfloat16)],
        compiler_params=params(),
        cost_estimate=cost(4_000_000_000, 1_000_000),
        name="conv_in",
    )(
        body,
        other_previous,
        *rims,
        *other_rims,
        norm_in,
        conv_in_weight,
        conv_in_bias.reshape(1, middle),
    )
    moments_mid = to_everyone(moments_mid)
    sent = pl.pallas_call(
        pack_kernel,
        out_shape=jax.ShapeDtypeStruct((frames, kept + 1, own, middle), jnp.bfloat16),
        in_specs=vmem_specs(1),
        out_specs=pl.BlockSpec(memory_space=pltpu.VMEM),
        compiler_params=params(),
        cost_estimate=cost(1_000_000_000, 1_000_000),
        name="pack_hidden",
    )(hidden)
    before = shift(sent, 1, 0)
    shown, _ = lax.optimization_barrier((other, sent))
    shortcut = pl.pallas_call(
        shortcut_kernel,
        out_shape=jax.ShapeDtypeStruct((frames, rows, own, outputs), jnp.float32),
        in_specs=vmem_specs(5),
        out_specs=pl.BlockSpec(memory_space=pltpu.VMEM),
        compiler_params=params(),
        cost_estimate=cost(300_000_000, 1_000_000),
        name="shortcut",
    )(
        features,
        shown,
        skip_weight,
        skip_bias.reshape(1, outputs),
        conv_mid_bias.reshape(1, outputs),
    )
    part, norm_mid = pl.pallas_call(
        functools.partial(own_frames_kernel, tiles),
        out_shape=(
            jax.ShapeDtypeStruct((frames, rows, own, outputs), jnp.float32),
            jax.ShapeDtypeStruct((3, middle), jnp.float32),
        ),
        in_specs=vmem_specs(6),
        out_specs=tuple(vmem_specs(2)),
        scratch_shapes=[pltpu.VMEM((frames, rows + 2, width, middle), jnp.bfloat16)],
        compiler_params=params(),
        cost_estimate=cost(2_000_000_000, 1_000_000),
        name="conv_mid_own_frames",
    )(
        hidden,
        moments_mid,
        norm_gain_mid.reshape(1, middle),
        norm_shift_mid.reshape(1, middle),
        conv_mid_weight,
        shortcut,
    )
    return pl.pallas_call(
        functools.partial(last_kernel, tiles),
        out_shape=jax.ShapeDtypeStruct((frames, rows, own, outputs), jnp.bfloat16),
        in_specs=vmem_specs(5),
        out_specs=pl.BlockSpec(memory_space=pl.ANY),
        scratch_shapes=[
            pltpu.VMEM((frames, rows + 2, width, middle), jnp.bfloat16),
            pltpu.VMEM((frames, rows, own, outputs), jnp.bfloat16),
            pltpu.SemaphoreType.DMA((frames,)),
        ],
        compiler_params=params(),
        cost_estimate=cost(2_000_000_000, 1_000_000),
        name="conv_mid_previous_frames",
    )(hidden, before, norm_mid, conv_mid_weight, part)


def solution(mesh):
    in_specs = (P("tm", "tile", None, "section"),) + (P(),) * 10
    out_specs = P("tm", "tile", "section", None)
    return jax.shard_map(shards, mesh=mesh, in_specs=in_specs, out_specs=out_specs, check_vma=False)
```

```python
import functools

import jax
import jax.numpy as jnp
from jax import lax
from jax.experimental import pallas as pl
from jax.experimental.pallas import tpu as pltpu
from jax.sharding import PartitionSpec as P

GROUPS = 32
AXES = ("section", "tm", "tile")
VMEM_LIMIT = 48 * 1024 * 1024
RIM = 16


def params(limit=VMEM_LIMIT):
    return pltpu.CompilerParams(vmem_limit_bytes=limit)


def cost(flops, moved):
    return pl.CostEstimate(flops=flops, bytes_accessed=moved, transcendentals=0)


def vmem_specs(count):
    return [pl.BlockSpec(memory_space=pltpu.VMEM)] * count


def silu(u):
    half = 0.5 * u
    return half + half * jnp.tanh(half)


def moments_of(cells):
    mean = jnp.sum(cells, axis=0, keepdims=True) * (1.0 / cells.shape[0])
    off = cells - mean
    return jnp.concatenate([mean, jnp.sum(off * off, axis=0, keepdims=True)], axis=0)


def group_matrix(channels, width):
    shape = (channels, channels)
    row = lax.broadcasted_iota(jnp.int32, shape, 0) // width
    col = lax.broadcasted_iota(jnp.int32, shape, 1) // width
    return jnp.where(row == col, 1.0, 0.0).astype(jnp.bfloat16)


def group_sum(values, matrix):
    parts = []
    for _ in range(3):
        part = values.astype(jnp.bfloat16).astype(jnp.float32)
        parts.append(jnp.broadcast_to(part, (8, part.shape[-1])))
        values = values - part
    stacked = jnp.concatenate(parts + [jnp.zeros_like(parts[0])], axis=0).astype(jnp.bfloat16)
    summed = jnp.dot(stacked, matrix, preferred_element_type=jnp.float32)
    return summed[0:1] + summed[8:9] + summed[16:17]


def scale_and_offset(moments, cells, width, gain, shift, matrix):
    devices = moments.shape[0]
    means = moments[:, 0, :]
    mean = group_sum(jnp.sum(means, axis=0, keepdims=True), matrix) * (1.0 / (devices * width))
    off = means - mean
    total = jnp.sum(moments[:, 1, :] + float(cells) * (off * off), axis=0, keepdims=True)
    spread = group_sum(total, matrix) * (1.0 / (cells * devices * width))
    scale = lax.rsqrt(spread + 1e-6) * gain
    return mean, scale, shift


def apply_norm(values, norm):
    mean, scale, shift = norm
    return silu((values.astype(jnp.float32) - mean) * scale + shift).astype(jnp.bfloat16)


def matrix_kernel(width, matrix_ref):
    matrix_ref[...] = group_matrix(matrix_ref.shape[0], width)


def first_kernel(x_ref, order_ref, moments_ref):
    x = x_ref[...]
    cells = x.astype(jnp.float32).reshape(-1, x.shape[-1])
    moments_ref[...] = jnp.broadcast_to(moments_of(cells)[None], moments_ref.shape)


def rows_kernel(pairs, x_ref, prev_ref, for_x_ref, for_prev_ref, *edge_refs):
    frames, rows, columns = x_ref.shape[:3]
    width = for_x_ref.shape[2]
    start = (1 - lax.axis_index("section")) * (columns - width)
    theirs = pl.ds(pl.multiple_of(start, RIM), width)
    for_x_ref[...] = x_ref[:, :, theirs, :]
    for_prev_ref[...] = prev_ref[:, :, theirs, :]
    if pairs:
        starts = [(rows - 2) * (1 - lax.axis_index("tile"))]
    else:
        starts = [0, rows - 2]
    for start, edge_ref in zip(starts, edge_refs):
        edge_ref[:frames] = prev_ref[:, pl.ds(start, 2)]
        edge_ref[frames:] = x_ref[:, pl.ds(start, 2)]


def scales_kernel(cells, moments_ref, gain_ref, shift_ref, matrix_ref, norm_ref):
    sections, half = gain_ref.shape
    per_section = moments_ref.shape[0] // sections
    for k in range(sections):
        norm = scale_and_offset(
            moments_ref[k * per_section : (k + 1) * per_section],
            cells,
            sections * half // GROUPS,
            gain_ref[k : k + 1],
            shift_ref[k : k + 1],
            matrix_ref[...],
        )
        norm_ref[k] = jnp.concatenate(norm, axis=0)


def column_taps(weight_ref, t, h):
    return jnp.concatenate([weight_ref[t, h, w] for w in range(3)], axis=-1)


def shift_and_add(total, rows, width):
    outputs = total.shape[-1] // 3
    total = total.reshape(rows, width, 3 * outputs)
    before, middle, after = (total[..., k * outputs : (k + 1) * outputs] for k in range(3))
    before = jnp.concatenate([before[:, :1], before[:, :-1]], axis=1)
    after = jnp.concatenate([after[:, 1:], after[:, -1:]], axis=1)
    return middle + before + after


def conv_in_rows(act_ref, weight_ref, frames, top, rows, width):
    totals = [None] * frames
    for a in range(act_ref.shape[0]):
        reached = [f for f in range(frames) if 0 <= a - f <= 2]
        for h in range(3):
            cells = act_ref[a, pl.ds(top + h, rows)]
            cells = cells.reshape(rows * width, cells.shape[-1])
            taps = [column_taps(weight_ref, a - f, h) for f in reached]
            sums = jnp.dot(
                cells, jnp.concatenate(taps, axis=-1), preferred_element_type=jnp.float32
            )
            n = sums.shape[-1] // len(reached)
            for k, f in enumerate(reached):
                part = sums[:, k * n : (k + 1) * n]
                totals[f] = part if totals[f] is None else totals[f] + part
    return [shift_and_add(total, rows, width) for total in totals]


def conv_mid_rows(act_ref, weight_ref, taken, rows, width):
    cells, taps = [], []
    for t, frame in taken:
        for h in range(3):
            block = act_ref[frame, h : h + rows]
            cells.append(block.reshape(rows * width, block.shape[-1]))
            taps.append(column_taps(weight_ref, t, h))
    total = jnp.dot(
        jnp.concatenate(cells, axis=-1),
        jnp.concatenate(taps, axis=0),
        preferred_element_type=jnp.float32,
    )
    return shift_and_add(total, rows, width)


def first_row(tiles, tile):
    return 1 - tile if tiles == 2 else 0


def body_kernel(x_ref, prev_ref, other_x_ref, norm_ref, body_ref):
    section = lax.axis_index("section")
    frames, _, columns, half = x_ref.shape
    width = body_ref.shape[2]
    mine = pl.ds(pl.multiple_of(section * (columns - width), RIM), width)
    for which, first, ref, cols in (
        (section, 0, prev_ref, mine),
        (section, frames, x_ref, mine),
        (1 - section, frames, other_x_ref, slice(None)),
    ):
        norm = tuple(norm_ref[which, k : k + 1] for k in range(3))
        lanes = pl.ds(pl.multiple_of(which * half, half), half)
        for f in range(frames):
            body_ref[first + f, :, :, lanes] = apply_norm(ref[f, :, cols, :], norm)


def middle_kernel(tiles, sides, *refs):
    body_ref, other_prev_ref = refs[:2]
    rim_refs, other_rim_refs = refs[2 : 2 + sides], refs[2 + sides : 2 + 2 * sides]
    norm_ref, weight_ref, bias_ref, hidden_ref, out_moments_ref, act_ref = refs[2 + 2 * sides :]
    section, tm, tile = (lax.axis_index(axis) for axis in AXES)
    columns, half = rim_refs[0].shape[2:]
    frames, rows, width = body_ref.shape[0] // 2, body_ref.shape[1], body_ref.shape[2]
    kept = hidden_ref.shape[1]
    own = columns // 2
    first = pl.multiple_of(section * (columns - width), RIM)
    cols = pl.ds(first, width)
    top = first_row(tiles, tile)
    rim_rows = (0, rows + 2) if sides == 2 else ((rows + 2) * (1 - tile),)
    act_ref[:, 2 : 2 + rows] = body_ref[...]
    for which, rims in ((section, rim_refs), (1 - section, other_rim_refs)):
        norm = tuple(norm_ref[which, k : k + 1] for k in range(3))
        lanes = pl.ds(pl.multiple_of(which * half, half), half)
        for f in range(2 * frames):
            for row, rim in zip(rim_rows, rims):
                act_ref[f, pl.ds(row, 2), :, lanes] = apply_norm(rim[f, :, cols, :], norm)
    for f in range(frames):
        act_ref[f, 2 : 2 + rows, :, lanes] = apply_norm(other_prev_ref[f], norm)

    @pl.when(tile == 0)
    def _():
        for f in range(2 * frames):
            act_ref[f, 1] = act_ref[f, 2]

    @pl.when(tile == tiles - 1)
    def _():
        for f in range(2 * frames):
            act_ref[f, rows + 2] = act_ref[f, rows + 1]

    @pl.when(tm == 0)
    def _():
        for f in range(frames):
            act_ref[f] = act_ref[frames]

    for f, hidden in enumerate(conv_in_rows(act_ref, weight_ref, frames, top, kept, width)):
        hidden_ref[f] = (hidden + bias_ref[...]).astype(jnp.bfloat16)

    cells = hidden_ref[:, pl.ds(1 - top, rows), pl.ds(first, own), :]
    cells = cells.astype(jnp.float32).reshape(-1, cells.shape[-1])
    out_moments_ref[...] = jnp.broadcast_to(moments_of(cells)[None], out_moments_ref.shape)


def pack_kernel(hidden_ref, sent_ref):
    section = lax.axis_index("section")
    frames, kept, width, channels = hidden_ref.shape
    own = sent_ref.shape[2]
    first = pl.multiple_of(section * (width - own), RIM)
    for f in range(frames):
        sent_ref[f, :kept] = hidden_ref[f, :, pl.ds(first, own), :]
        hidden = hidden_ref[f].astype(jnp.float32)
        rim = jnp.where(section == 0, hidden[:, own, :], hidden[:, width - own - 1, :])
        spare = jnp.zeros((own - kept, channels), jnp.float32)
        sent_ref[f, kept] = jnp.concatenate([rim, spare], axis=0).astype(jnp.bfloat16)


def repeat_edges(act_ref, count, tiles, rows):
    tile = lax.axis_index("tile")

    @pl.when(tile == 0)
    def _():
        for f in range(count):
            act_ref[f, 0] = act_ref[f, 1]

    @pl.when(tile == tiles - 1)
    def _():
        for f in range(count):
            act_ref[f, rows + 1] = act_ref[f, rows]


def own_columns(values, own):
    section = lax.axis_index("section")
    width = values.shape[1]
    return jnp.where(section == 0, values[:, :own], values[:, width - own :])


def shortcut_kernel(x_ref, other_x_ref, skip_ref, skip_bias_ref, bias_ref, part_ref):
    section = lax.axis_index("section")
    frames, rows, columns, half = x_ref.shape
    own = columns // 2
    mine = pl.ds(pl.multiple_of(section * own, own), own)
    within = pl.ds(pl.multiple_of(section * (other_x_ref.shape[2] - own), RIM), own)
    skip_here = skip_ref[pl.ds(pl.multiple_of(section * half, half), half), :]
    skip_there = skip_ref[pl.ds(pl.multiple_of((1 - section) * half, half), half), :]
    for f in range(frames):
        here = x_ref[f, :, mine, :].reshape(rows * own, half)
        there = other_x_ref[f, :, within, :].reshape(rows * own, half)
        shortcut = jnp.dot(here, skip_here, preferred_element_type=jnp.float32)
        shortcut = shortcut + jnp.dot(there, skip_there, preferred_element_type=jnp.float32)
        part_ref[f] = (shortcut + (skip_bias_ref[...] + bias_ref[...])).reshape(rows, own, -1)


def own_frames_kernel(
    tiles,
    hidden_ref,
    moments_ref,
    gain_ref,
    shift_ref,
    weight_ref,
    shortcut_ref,
    part_ref,
    norm_ref,
    act_ref,
):
    frames, kept, width, outputs = hidden_ref.shape
    rows, own = part_ref.shape[1:3]
    top = first_row(tiles, lax.axis_index("tile"))
    norm = scale_and_offset(
        moments_ref[...],
        frames * rows * own,
        outputs // GROUPS,
        gain_ref[...],
        shift_ref[...],
        group_matrix(outputs, outputs // GROUPS),
    )
    norm_ref[...] = jnp.concatenate(norm, axis=0)
    for f in range(frames):
        act_ref[f, pl.ds(top, kept)] = apply_norm(hidden_ref[f], norm)
    repeat_edges(act_ref, frames, tiles, rows)
    for f in range(frames):
        taken = [(k - f + 2, k) for k in range(f - 2, f + 1) if k >= 0]
        residual = own_columns(conv_mid_rows(act_ref, weight_ref, taken, rows, width), own)
        part_ref[f] = shortcut_ref[f] + residual


def last_kernel(
    tiles, hidden_ref, before_ref, norm_ref, weight_ref, part_ref, out_hbm, act_ref, out_ref, sems
):
    section, tm, tile = (lax.axis_index(axis) for axis in AXES)
    frames, kept, width, outputs = hidden_ref.shape
    rows, own = part_ref.shape[1:3]
    top = first_row(tiles, tile)
    first = pl.multiple_of(section * (width - own), RIM)
    beside = pl.multiple_of((1 - section) * own, RIM)
    norm = tuple(norm_ref[k : k + 1] for k in range(3))
    for f in range(frames):
        act_ref[f, pl.ds(top, kept), pl.ds(first, own), :] = apply_norm(before_ref[f, :kept], norm)
        rim = apply_norm(before_ref[f, kept], norm).astype(jnp.float32)[:kept]
        rim = jnp.broadcast_to(rim[:, None, :], (kept, width - own, outputs))
        act_ref[f, pl.ds(top, kept), pl.ds(beside, width - own), :] = rim.astype(jnp.bfloat16)

    @pl.when(tm == 0)
    def _():
        start = apply_norm(hidden_ref[0], norm)
        for f in range(frames):
            act_ref[f, pl.ds(top, kept)] = start

    repeat_edges(act_ref, frames, tiles, rows)
    copies = []
    for f in range(frames):
        taken = [(k - f, k) for k in range(f, f + 3) if k < frames]
        residual = own_columns(conv_mid_rows(act_ref, weight_ref, taken, rows, width), own)
        out_ref[f] = (part_ref[f] + residual).astype(jnp.bfloat16)
        copies.append(pltpu.make_async_copy(out_ref.at[f], out_hbm.at[f], sems.at[f]))
        copies[-1].start()
    for copy in copies:
        copy.wait()


def pairs_for(tm_count, tile_count, tm_step, tile_step):
    out = []
    for a in range(tm_count):
        for b in range(tile_count):
            c, d = a + tm_step, b + tile_step
            if 0 <= c < tm_count and 0 <= d < tile_count:
                out.append((a * tile_count + b, c * tile_count + d))
    return out


def to_everyone(moments):
    return lax.all_to_all(moments, AXES, 0, 0, tiled=True)


def shards(
    features,
    norm_gain_in,
    norm_shift_in,
    conv_in_weight,
    conv_in_bias,
    norm_gain_mid,
    norm_shift_mid,
    conv_mid_weight,
    conv_mid_bias,
    skip_weight,
    skip_bias,
):
    sections, tms, tiles = (lax.axis_size(axis) for axis in AXES)
    parties = sections * tms * tiles
    frames, rows, columns, half = features.shape
    own = columns // sections
    width = own + RIM
    middle = conv_in_weight.shape[-1]
    outputs = conv_mid_weight.shape[-1]
    grid_axes = ("tm", "tile")

    def shift(value, tm_step, tile_step):
        return lax.ppermute(value, grid_axes, pairs_for(tms, tiles, tm_step, tile_step))

    def swap(value):
        return lax.ppermute(value, "section", [(0, 1), (1, 0)])

    previous = shift(features, 1, 0)
    matrix = pl.pallas_call(
        functools.partial(matrix_kernel, half * sections // GROUPS),
        out_shape=jax.ShapeDtypeStruct((half, half), jnp.bfloat16),
        out_specs=pl.BlockSpec(memory_space=pltpu.VMEM),
        compiler_params=params(),
        cost_estimate=cost(1_000_000_000, 1_000_000),
        name="group_matrix",
    )()
    sums = pl.pallas_call(
        first_kernel,
        out_shape=jax.ShapeDtypeStruct((parties, 2, half), jnp.float32),
        in_specs=[*vmem_specs(1), pl.BlockSpec(memory_space=pl.ANY)],
        out_specs=pl.BlockSpec(memory_space=pltpu.VMEM),
        compiler_params=params(),
        cost_estimate=cost(1_000_000_000, 1_000_000),
        name="feature_moments",
    )(features, matrix)
    moments = to_everyone(sums)
    previous, _ = lax.optimization_barrier((previous, sums))
    edges = 1 if tiles == 2 else 2
    edge = jax.ShapeDtypeStruct((2 * frames, 2, columns, half), features.dtype)
    cut = jax.ShapeDtypeStruct((frames, rows, width, half), features.dtype)
    for_x, for_previous, *edge_rows = pl.pallas_call(
        functools.partial(rows_kernel, tiles == 2),
        out_shape=(cut, cut) + (edge,) * edges,
        in_specs=vmem_specs(2),
        out_specs=tuple(vmem_specs(2 + edges)),
        compiler_params=params(),
        cost_estimate=cost(500_000_000, 1_000_000),
        name="facing_rows",
    )(features, previous)
    if tiles == 2:
        rims = [lax.ppermute(edge_rows[0], "tile", [(0, 1), (1, 0)])]
    else:
        rims = [shift(edge_rows[1], 0, 1), shift(edge_rows[0], 0, -1)]
    other = swap(for_x)
    other_previous = swap(for_previous)
    norm_in = pl.pallas_call(
        functools.partial(scales_kernel, frames * rows * columns),
        out_shape=jax.ShapeDtypeStruct((sections, 3, half), jnp.float32),
        in_specs=vmem_specs(4),
        out_specs=pl.BlockSpec(memory_space=pltpu.VMEM),
        compiler_params=params(),
        cost_estimate=cost(2_000_000_000, 1_000_000),
        name="feature_scales",
    )(moments, norm_gain_in.reshape(sections, half), norm_shift_in.reshape(sections, half), matrix)
    norm_in, *rims = lax.optimization_barrier((norm_in, *rims))
    other_rims = [swap(rim) for rim in rims]

    kept = rows + edges
    body = pl.pallas_call(
        body_kernel,
        out_shape=jax.ShapeDtypeStruct((2 * frames, rows, width, 2 * half), jnp.bfloat16),
        in_specs=vmem_specs(4),
        out_specs=pl.BlockSpec(memory_space=pltpu.VMEM),
        compiler_params=params(),
        cost_estimate=cost(1_000_000_000, 1_000_000),
        name="norm_body",
    )(features, previous, other, norm_in)
    hidden, moments_mid = pl.pallas_call(
        functools.partial(middle_kernel, tiles, edges),
        out_shape=(
            jax.ShapeDtypeStruct((frames, kept, width, middle), jnp.bfloat16),
            jax.ShapeDtypeStruct((parties, 2, middle), jnp.float32),
        ),
        in_specs=vmem_specs(5 + 2 * edges),
        out_specs=tuple(vmem_specs(2)),
        scratch_shapes=[pltpu.VMEM((2 * frames, rows + 4, width, 2 * half), jnp.bfloat16)],
        compiler_params=params(),
        cost_estimate=cost(4_000_000_000, 1_000_000),
        name="conv_in",
    )(
        body,
        other_previous,
        *rims,
        *other_rims,
        norm_in,
        conv_in_weight,
        conv_in_bias.reshape(1, middle),
    )
    moments_mid = to_everyone(moments_mid)
    sent = pl.pallas_call(
        pack_kernel,
        out_shape=jax.ShapeDtypeStruct((frames, kept + 1, own, middle), jnp.bfloat16),
        in_specs=vmem_specs(1),
        out_specs=pl.BlockSpec(memory_space=pltpu.VMEM),
        compiler_params=params(),
        cost_estimate=cost(1_000_000_000, 1_000_000),
        name="pack_hidden",
    )(hidden)
    before = shift(sent, 1, 0)
    shown, _ = lax.optimization_barrier((other, sent))
    shortcut = pl.pallas_call(
        shortcut_kernel,
        out_shape=jax.ShapeDtypeStruct((frames, rows, own, outputs), jnp.float32),
        in_specs=vmem_specs(5),
        out_specs=pl.BlockSpec(memory_space=pltpu.VMEM),
        compiler_params=params(),
        cost_estimate=cost(300_000_000, 1_000_000),
        name="shortcut",
    )(
        features,
        shown,
        skip_weight,
        skip_bias.reshape(1, outputs),
        conv_mid_bias.reshape(1, outputs),
    )
    part, norm_mid = pl.pallas_call(
        functools.partial(own_frames_kernel, tiles),
        out_shape=(
            jax.ShapeDtypeStruct((frames, rows, own, outputs), jnp.float32),
            jax.ShapeDtypeStruct((3, middle), jnp.float32),
        ),
        in_specs=vmem_specs(6),
        out_specs=tuple(vmem_specs(2)),
        scratch_shapes=[pltpu.VMEM((frames, rows + 2, width, middle), jnp.bfloat16)],
        compiler_params=params(),
        cost_estimate=cost(2_000_000_000, 1_000_000),
        name="conv_mid_own_frames",
    )(
        hidden,
        moments_mid,
        norm_gain_mid.reshape(1, middle),
        norm_shift_mid.reshape(1, middle),
        conv_mid_weight,
        shortcut,
    )
    return pl.pallas_call(
        functools.partial(last_kernel, tiles),
        out_shape=jax.ShapeDtypeStruct((frames, rows, own, outputs), jnp.bfloat16),
        in_specs=vmem_specs(5),
        out_specs=pl.BlockSpec(memory_space=pl.ANY),
        scratch_shapes=[
            pltpu.VMEM((frames, rows + 2, width, middle), jnp.bfloat16),
            pltpu.VMEM((frames, rows, own, outputs), jnp.bfloat16),
            pltpu.SemaphoreType.DMA((frames,)),
        ],
        compiler_params=params(),
        cost_estimate=cost(2_000_000_000, 1_000_000),
        name="conv_mid_previous_frames",
    )(hidden, before, norm_mid, conv_mid_weight, part)


def solution(mesh):
    in_specs = (P("tm", "tile", None, "section"),) + (P(),) * 10
    out_specs = P("tm", "tile", "section", None)
    return jax.shard_map(shards, mesh=mesh, in_specs=in_specs, out_specs=out_specs, check_vma=False)
```

```python
import functools

import jax
import jax.numpy as jnp
from jax import lax
from jax.experimental import pallas as pl
from jax.experimental.pallas import tpu as pltpu
from jax.sharding import PartitionSpec as P

GROUPS = 32
AXES = ("section", "tm", "tile")
VMEM_LIMIT = 48 * 1024 * 1024
RIM = 16


def params(limit=VMEM_LIMIT):
    return pltpu.CompilerParams(vmem_limit_bytes=limit)


def cost(flops, moved):
    return pl.CostEstimate(flops=flops, bytes_accessed=moved, transcendentals=0)


def vmem_specs(count):
    return [pl.BlockSpec(memory_space=pltpu.VMEM)] * count


def silu(u):
    half = 0.5 * u
    return half + half * jnp.tanh(half)


def moments_of(cells):
    mean = jnp.sum(cells, axis=0, keepdims=True) * (1.0 / cells.shape[0])
    off = cells - mean
    return jnp.concatenate([mean, jnp.sum(off * off, axis=0, keepdims=True)], axis=0)


def group_matrix(channels, width):
    shape = (channels, channels)
    row = lax.broadcasted_iota(jnp.int32, shape, 0) // width
    col = lax.broadcasted_iota(jnp.int32, shape, 1) // width
    return jnp.where(row == col, 1.0, 0.0).astype(jnp.bfloat16)


def group_sum(values, matrix):
    parts = []
    for _ in range(3):
        part = values.astype(jnp.bfloat16).astype(jnp.float32)
        parts.append(jnp.broadcast_to(part, (8, part.shape[-1])))
        values = values - part
    stacked = jnp.concatenate(parts + [jnp.zeros_like(parts[0])], axis=0).astype(jnp.bfloat16)
    summed = jnp.dot(stacked, matrix, preferred_element_type=jnp.float32)
    return summed[0:1] + summed[8:9] + summed[16:17]


def scale_and_offset(moments, cells, width, gain, shift, matrix):
    devices = moments.shape[0]
    means = moments[:, 0, :]
    mean = group_sum(jnp.sum(means, axis=0, keepdims=True), matrix) * (1.0 / (devices * width))
    off = means - mean
    total = jnp.sum(moments[:, 1, :] + float(cells) * (off * off), axis=0, keepdims=True)
    spread = group_sum(total, matrix) * (1.0 / (cells * devices * width))
    scale = lax.rsqrt(spread + 1e-6) * gain
    return mean, scale, shift


def apply_norm(values, norm):
    mean, scale, shift = norm
    return silu((values.astype(jnp.float32) - mean) * scale + shift).astype(jnp.bfloat16)


def matrix_kernel(width, matrix_ref):
    matrix_ref[...] = group_matrix(matrix_ref.shape[0], width)


def first_kernel(x_ref, order_ref, moments_ref):
    x = x_ref[...]
    cells = x.astype(jnp.float32).reshape(-1, x.shape[-1])
    moments_ref[...] = jnp.broadcast_to(moments_of(cells)[None], moments_ref.shape)


def facing_rows(pairs, block_ref, frame, edge_refs):
    rows = block_ref.shape[1]
    starts = [(rows - 1) * (1 - lax.axis_index("tile"))] if pairs else [0, rows - 1]
    for start, edge_ref in zip(starts, edge_refs):
        edge_ref[frame : frame + block_ref.shape[0]] = block_ref[:, pl.ds(start, 1)]


def rim_places(sides, rows):
    return (0, rows + 1) if sides == 2 else ((rows + 1) * (1 - lax.axis_index("tile")),)


def rows_kernel(pairs, x_ref, prev_ref, for_x_ref, for_prev_ref, *edge_refs):
    frames, _, columns = x_ref.shape[:3]
    width = for_x_ref.shape[2]
    start = (1 - lax.axis_index("section")) * (columns - width)
    theirs = pl.ds(pl.multiple_of(start, RIM), width)
    for_x_ref[...] = x_ref[:, :, theirs, :]
    for_prev_ref[...] = prev_ref[:, :, theirs, :]
    facing_rows(pairs, prev_ref, 0, edge_refs)
    facing_rows(pairs, x_ref, frames, edge_refs)


def scales_kernel(cells, moments_ref, gain_ref, shift_ref, matrix_ref, norm_ref):
    sections, half = gain_ref.shape
    per_section = moments_ref.shape[0] // sections
    for k in range(sections):
        norm = scale_and_offset(
            moments_ref[k * per_section : (k + 1) * per_section],
            cells,
            sections * half // GROUPS,
            gain_ref[k : k + 1],
            shift_ref[k : k + 1],
            matrix_ref[...],
        )
        norm_ref[k] = jnp.concatenate(norm, axis=0)


def column_taps(weight_ref, t, h):
    return jnp.concatenate([weight_ref[t, h, w] for w in range(3)], axis=-1)


def shift_and_add(total, rows, width):
    outputs = total.shape[-1] // 3
    total = total.reshape(rows, width, 3 * outputs)
    before, middle, after = (total[..., k * outputs : (k + 1) * outputs] for k in range(3))
    before = jnp.concatenate([before[:, :1], before[:, :-1]], axis=1)
    after = jnp.concatenate([after[:, 1:], after[:, -1:]], axis=1)
    return middle + before + after


def conv_in_rows(act_ref, weight_ref, frames, rows, width):
    totals = [None] * frames
    for a in range(act_ref.shape[0]):
        reached = [f for f in range(frames) if 0 <= a - f <= 2]
        for h in range(3):
            cells = act_ref[a, h : h + rows]
            cells = cells.reshape(rows * width, cells.shape[-1])
            taps = [column_taps(weight_ref, a - f, h) for f in reached]
            sums = jnp.dot(
                cells, jnp.concatenate(taps, axis=-1), preferred_element_type=jnp.float32
            )
            n = sums.shape[-1] // len(reached)
            for k, f in enumerate(reached):
                part = sums[:, k * n : (k + 1) * n]
                totals[f] = part if totals[f] is None else totals[f] + part
    return [shift_and_add(total, rows, width) for total in totals]


def conv_mid_rows(act_ref, weight_ref, taken, rows, width):
    cells, taps = [], []
    for t, frame in taken:
        for h in range(3):
            block = act_ref[frame, h : h + rows]
            cells.append(block.reshape(rows * width, block.shape[-1]))
            taps.append(column_taps(weight_ref, t, h))
    total = jnp.dot(
        jnp.concatenate(cells, axis=-1),
        jnp.concatenate(taps, axis=0),
        preferred_element_type=jnp.float32,
    )
    return shift_and_add(total, rows, width)


def body_kernel(x_ref, prev_ref, other_x_ref, norm_ref, body_ref):
    section = lax.axis_index("section")
    frames, _, columns, half = x_ref.shape
    width = body_ref.shape[2]
    mine = pl.ds(pl.multiple_of(section * (columns - width), RIM), width)
    for which, first, ref, cols in (
        (section, 0, prev_ref, mine),
        (section, frames, x_ref, mine),
        (1 - section, frames, other_x_ref, slice(None)),
    ):
        norm = tuple(norm_ref[which, k : k + 1] for k in range(3))
        lanes = pl.ds(pl.multiple_of(which * half, half), half)
        for f in range(frames):
            body_ref[first + f, :, :, lanes] = apply_norm(ref[f, :, cols, :], norm)


def middle_kernel(tiles, sides, *refs):
    body_ref, other_prev_ref = refs[:2]
    rim_refs, other_rim_refs = refs[2 : 2 + sides], refs[2 + sides : 2 + 2 * sides]
    norm_ref, weight_ref, bias_ref, hidden_ref, out_moments_ref, act_ref = refs[2 + 2 * sides :]
    section, tm = lax.axis_index("section"), lax.axis_index("tm")
    columns, half = rim_refs[0].shape[2:]
    frames, rows, width = body_ref.shape[0] // 2, body_ref.shape[1], body_ref.shape[2]
    own = columns // 2
    first = pl.multiple_of(section * (columns - width), RIM)
    cols = pl.ds(first, width)
    places = rim_places(sides, rows)
    act_ref[:, 1 : 1 + rows] = body_ref[...]
    for which, rims in ((section, rim_refs), (1 - section, other_rim_refs)):
        norm = tuple(norm_ref[which, k : k + 1] for k in range(3))
        lanes = pl.ds(pl.multiple_of(which * half, half), half)
        for f in range(2 * frames):
            for row, rim in zip(places, rims):
                act_ref[f, pl.ds(row, 1), :, lanes] = apply_norm(rim[f, :, cols, :], norm)
    for f in range(frames):
        act_ref[f, 1 : 1 + rows, :, lanes] = apply_norm(other_prev_ref[f], norm)
    repeat_edges(act_ref, 2 * frames, tiles, rows)

    @pl.when(tm == 0)
    def _():
        for f in range(frames):
            act_ref[f] = act_ref[frames]

    for f, hidden in enumerate(conv_in_rows(act_ref, weight_ref, frames, rows, width)):
        hidden_ref[f] = (hidden + bias_ref[...]).astype(jnp.bfloat16)

    cells = hidden_ref[:, :, pl.ds(first, own), :]
    cells = cells.astype(jnp.float32).reshape(-1, cells.shape[-1])
    out_moments_ref[...] = jnp.broadcast_to(moments_of(cells)[None], out_moments_ref.shape)


def pack_kernel(pairs, hidden_ref, sent_ref, *edge_refs):
    section = lax.axis_index("section")
    frames, rows, width, channels = hidden_ref.shape
    own = sent_ref.shape[2]
    first = pl.multiple_of(section * (width - own), RIM)
    for f in range(frames):
        sent_ref[f, :rows] = hidden_ref[f, :, pl.ds(first, own), :]
        hidden = hidden_ref[f].astype(jnp.float32)
        rim = jnp.where(section == 0, hidden[:, own, :], hidden[:, width - own - 1, :])
        spare = jnp.zeros((own - rows, channels), jnp.float32)
        sent_ref[f, rows] = jnp.concatenate([rim, spare], axis=0).astype(jnp.bfloat16)
    facing_rows(pairs, hidden_ref, 0, edge_refs)


def repeat_edges(act_ref, count, tiles, rows):
    tile = lax.axis_index("tile")

    @pl.when(tile == 0)
    def _():
        for f in range(count):
            act_ref[f, 0] = act_ref[f, 1]

    @pl.when(tile == tiles - 1)
    def _():
        for f in range(count):
            act_ref[f, rows + 1] = act_ref[f, rows]


def own_columns(values, own):
    section = lax.axis_index("section")
    width = values.shape[1]
    return jnp.where(section == 0, values[:, :own], values[:, width - own :])


def shortcut_kernel(x_ref, other_x_ref, skip_ref, skip_bias_ref, bias_ref, part_ref):
    section = lax.axis_index("section")
    frames, rows, columns, half = x_ref.shape
    own = columns // 2
    mine = pl.ds(pl.multiple_of(section * own, own), own)
    within = pl.ds(pl.multiple_of(section * (other_x_ref.shape[2] - own), RIM), own)
    skip_here = skip_ref[pl.ds(pl.multiple_of(section * half, half), half), :]
    skip_there = skip_ref[pl.ds(pl.multiple_of((1 - section) * half, half), half), :]
    for f in range(frames):
        here = x_ref[f, :, mine, :].reshape(rows * own, half)
        there = other_x_ref[f, :, within, :].reshape(rows * own, half)
        shortcut = jnp.dot(here, skip_here, preferred_element_type=jnp.float32)
        shortcut = shortcut + jnp.dot(there, skip_there, preferred_element_type=jnp.float32)
        part_ref[f] = (shortcut + (skip_bias_ref[...] + bias_ref[...])).reshape(rows, own, -1)


def own_frames_kernel(tiles, sides, *refs):
    rims, refs = refs[:sides], refs[sides:]
    hidden_ref, moments_ref, gain_ref, shift_ref, weight_ref, shortcut_ref = refs[:6]
    part_ref, norm_ref, act_ref = refs[6:]
    frames, rows, width, outputs = hidden_ref.shape
    own = part_ref.shape[2]
    norm = scale_and_offset(
        moments_ref[...],
        frames * rows * own,
        outputs // GROUPS,
        gain_ref[...],
        shift_ref[...],
        group_matrix(outputs, outputs // GROUPS),
    )
    norm_ref[...] = jnp.concatenate(norm, axis=0)
    for f in range(frames):
        act_ref[f, 1 : 1 + rows] = apply_norm(hidden_ref[f], norm)
        for row, rim in zip(rim_places(sides, rows), rims):
            act_ref[f, pl.ds(row, 1)] = apply_norm(rim[f], norm)
    repeat_edges(act_ref, frames, tiles, rows)
    for f in range(frames):
        taken = [(k - f + 2, k) for k in range(f - 2, f + 1) if k >= 0]
        residual = own_columns(conv_mid_rows(act_ref, weight_ref, taken, rows, width), own)
        part_ref[f] = shortcut_ref[f] + residual


def last_kernel(tiles, sides, *refs):
    own_rims, rims, refs = refs[:sides], refs[sides : 2 * sides], refs[2 * sides :]
    hidden_ref, before_ref, norm_ref, weight_ref, part_ref, out_hbm, act_ref, out_ref, sems = refs
    section, tm = lax.axis_index("section"), lax.axis_index("tm")
    frames, rows, width, outputs = hidden_ref.shape
    own = part_ref.shape[2]
    first = pl.multiple_of(section * (width - own), RIM)
    beside = pl.multiple_of((1 - section) * own, RIM)
    norm = tuple(norm_ref[k : k + 1] for k in range(3))
    places = rim_places(sides, rows)
    for f in range(frames):
        act_ref[f, 1 : 1 + rows, pl.ds(first, own), :] = apply_norm(before_ref[f, :rows], norm)
        column = apply_norm(before_ref[f, rows], norm).astype(jnp.float32)[:rows]
        column = jnp.broadcast_to(column[:, None, :], (rows, width - own, outputs))
        act_ref[f, 1 : 1 + rows, pl.ds(beside, width - own), :] = column.astype(jnp.bfloat16)
        for row, rim in zip(places, rims):
            act_ref[f, pl.ds(row, 1)] = apply_norm(rim[f], norm)

    @pl.when(tm == 0)
    def _():
        start = apply_norm(hidden_ref[0], norm)
        start_rims = [apply_norm(rim[0], norm) for rim in own_rims]
        for f in range(frames):
            act_ref[f, 1 : 1 + rows] = start
            for row, rim in zip(places, start_rims):
                act_ref[f, pl.ds(row, 1)] = rim

    repeat_edges(act_ref, frames, tiles, rows)
    copies = []
    for f in range(frames):
        taken = [(k - f, k) for k in range(f, f + 3) if k < frames]
        residual = own_columns(conv_mid_rows(act_ref, weight_ref, taken, rows, width), own)
        out_ref[f] = (part_ref[f] + residual).astype(jnp.bfloat16)
        copies.append(pltpu.make_async_copy(out_ref.at[f], out_hbm.at[f], sems.at[f]))
        copies[-1].start()
    for copy in copies:
        copy.wait()


def pairs_for(tm_count, tile_count, tm_step, tile_step):
    out = []
    for a in range(tm_count):
        for b in range(tile_count):
            c, d = a + tm_step, b + tile_step
            if 0 <= c < tm_count and 0 <= d < tile_count:
                out.append((a * tile_count + b, c * tile_count + d))
    return out


def to_everyone(moments):
    return lax.all_to_all(moments, AXES, 0, 0, tiled=True)


def shards(
    features,
    norm_gain_in,
    norm_shift_in,
    conv_in_weight,
    conv_in_bias,
    norm_gain_mid,
    norm_shift_mid,
    conv_mid_weight,
    conv_mid_bias,
    skip_weight,
    skip_bias,
):
    sections, tms, tiles = (lax.axis_size(axis) for axis in AXES)
    parties = sections * tms * tiles
    frames, rows, columns, half = features.shape
    own = columns // sections
    width = own + RIM
    middle = conv_in_weight.shape[-1]
    outputs = conv_mid_weight.shape[-1]
    grid_axes = ("tm", "tile")

    def shift(value, tm_step, tile_step):
        return lax.ppermute(value, grid_axes, pairs_for(tms, tiles, tm_step, tile_step))

    def swap(value):
        return lax.ppermute(value, "section", [(0, 1), (1, 0)])

    previous = shift(features, 1, 0)
    matrix = pl.pallas_call(
        functools.partial(matrix_kernel, half * sections // GROUPS),
        out_shape=jax.ShapeDtypeStruct((half, half), jnp.bfloat16),
        out_specs=pl.BlockSpec(memory_space=pltpu.VMEM),
        compiler_params=params(),
        cost_estimate=cost(1_000_000_000, 1_000_000),
        name="group_matrix",
    )()
    sums = pl.pallas_call(
        first_kernel,
        out_shape=jax.ShapeDtypeStruct((parties, 2, half), jnp.float32),
        in_specs=[*vmem_specs(1), pl.BlockSpec(memory_space=pl.ANY)],
        out_specs=pl.BlockSpec(memory_space=pltpu.VMEM),
        compiler_params=params(),
        cost_estimate=cost(1_000_000_000, 1_000_000),
        name="feature_moments",
    )(features, matrix)
    moments = to_everyone(sums)
    previous, _ = lax.optimization_barrier((previous, sums))
    edges = 1 if tiles == 2 else 2
    edge = jax.ShapeDtypeStruct((2 * frames, 1, columns, half), features.dtype)
    cut = jax.ShapeDtypeStruct((frames, rows, width, half), features.dtype)
    for_x, for_previous, *edge_rows = pl.pallas_call(
        functools.partial(rows_kernel, tiles == 2),
        out_shape=(cut, cut) + (edge,) * edges,
        in_specs=vmem_specs(2),
        out_specs=tuple(vmem_specs(2 + edges)),
        compiler_params=params(),
        cost_estimate=cost(500_000_000, 1_000_000),
        name="facing_rows",
    )(features, previous)

    def from_neighbours(facing):
        if tiles == 2:
            return [lax.ppermute(facing[0], "tile", [(0, 1), (1, 0)])]
        return [shift(facing[1], 0, 1), shift(facing[0], 0, -1)]

    rims = from_neighbours(edge_rows)
    other = swap(for_x)
    other_previous = swap(for_previous)
    norm_in = pl.pallas_call(
        functools.partial(scales_kernel, frames * rows * columns),
        out_shape=jax.ShapeDtypeStruct((sections, 3, half), jnp.float32),
        in_specs=vmem_specs(4),
        out_specs=pl.BlockSpec(memory_space=pltpu.VMEM),
        compiler_params=params(),
        cost_estimate=cost(3_000_000_000, 1_000_000),
        name="feature_scales",
    )(moments, norm_gain_in.reshape(sections, half), norm_shift_in.reshape(sections, half), matrix)
    norm_in, *rims = lax.optimization_barrier((norm_in, *rims))
    other_rims = [swap(rim) for rim in rims]

    body = pl.pallas_call(
        body_kernel,
        out_shape=jax.ShapeDtypeStruct((2 * frames, rows, width, 2 * half), jnp.bfloat16),
        in_specs=vmem_specs(4),
        out_specs=pl.BlockSpec(memory_space=pltpu.VMEM),
        compiler_params=params(),
        cost_estimate=cost(1_000_000_000, 1_000_000),
        name="norm_body",
    )(features, previous, other, norm_in)
    hidden, moments_mid = pl.pallas_call(
        functools.partial(middle_kernel, tiles, edges),
        out_shape=(
            jax.ShapeDtypeStruct((frames, rows, width, middle), jnp.bfloat16),
            jax.ShapeDtypeStruct((parties, 2, middle), jnp.float32),
        ),
        in_specs=vmem_specs(5 + 2 * edges),
        out_specs=tuple(vmem_specs(2)),
        scratch_shapes=[pltpu.VMEM((2 * frames, rows + 2, width, 2 * half), jnp.bfloat16)],
        compiler_params=params(),
        cost_estimate=cost(4_000_000_000, 1_000_000),
        name="conv_in",
    )(
        body,
        other_previous,
        *rims,
        *other_rims,
        norm_in,
        conv_in_weight,
        conv_in_bias.reshape(1, middle),
    )
    moments_mid = to_everyone(moments_mid)
    row = jax.ShapeDtypeStruct((frames, 1, width, middle), jnp.bfloat16)
    sent, *facing = pl.pallas_call(
        functools.partial(pack_kernel, tiles == 2),
        out_shape=(jax.ShapeDtypeStruct((frames, rows + 1, own, middle), jnp.bfloat16),)
        + (row,) * edges,
        in_specs=vmem_specs(1),
        out_specs=tuple(vmem_specs(1 + edges)),
        compiler_params=params(),
        cost_estimate=cost(1_000_000_000, 1_000_000),
        name="pack_hidden",
    )(hidden)
    before = shift(sent, 1, 0)
    hidden_rims = from_neighbours(facing)
    before_rims = [shift(rim, 1, 0) for rim in hidden_rims]
    shown, _ = lax.optimization_barrier((other, sent))
    shortcut = pl.pallas_call(
        shortcut_kernel,
        out_shape=jax.ShapeDtypeStruct((frames, rows, own, outputs), jnp.float32),
        in_specs=vmem_specs(5),
        out_specs=pl.BlockSpec(memory_space=pltpu.VMEM),
        compiler_params=params(),
        cost_estimate=cost(300_000_000, 1_000_000),
        name="shortcut",
    )(
        features,
        shown,
        skip_weight,
        skip_bias.reshape(1, outputs),
        conv_mid_bias.reshape(1, outputs),
    )
    part, norm_mid = pl.pallas_call(
        functools.partial(own_frames_kernel, tiles, edges),
        out_shape=(
            jax.ShapeDtypeStruct((frames, rows, own, outputs), jnp.float32),
            jax.ShapeDtypeStruct((3, middle), jnp.float32),
        ),
        in_specs=vmem_specs(6 + edges),
        out_specs=tuple(vmem_specs(2)),
        scratch_shapes=[pltpu.VMEM((frames, rows + 2, width, middle), jnp.bfloat16)],
        compiler_params=params(),
        cost_estimate=cost(2_000_000_000, 1_000_000),
        name="conv_mid_own_frames",
    )(
        *hidden_rims,
        hidden,
        moments_mid,
        norm_gain_mid.reshape(1, middle),
        norm_shift_mid.reshape(1, middle),
        conv_mid_weight,
        shortcut,
    )
    return pl.pallas_call(
        functools.partial(last_kernel, tiles, edges),
        out_shape=jax.ShapeDtypeStruct((frames, rows, own, outputs), jnp.bfloat16),
        in_specs=vmem_specs(5 + 2 * edges),
        out_specs=pl.BlockSpec(memory_space=pl.ANY),
        scratch_shapes=[
            pltpu.VMEM((frames, rows + 2, width, middle), jnp.bfloat16),
            pltpu.VMEM((frames, rows, own, outputs), jnp.bfloat16),
            pltpu.SemaphoreType.DMA((frames,)),
        ],
        compiler_params=params(),
        cost_estimate=cost(2_000_000_000, 1_000_000),
        name="conv_mid_previous_frames",
    )(*hidden_rims, *before_rims, hidden, before, norm_mid, conv_mid_weight, part)


def solution(mesh):
    in_specs = (P("tm", "tile", None, "section"),) + (P(),) * 10
    out_specs = P("tm", "tile", "section", None)
    return jax.shard_map(shards, mesh=mesh, in_specs=in_specs, out_specs=out_specs, check_vma=False)
```

```python
import functools

import jax
import jax.numpy as jnp
from jax import lax
from jax.experimental import pallas as pl
from jax.experimental.pallas import tpu as pltpu
from jax.sharding import PartitionSpec as P

GROUPS = 32
AXES = ("section", "tm", "tile")
VMEM_LIMIT = 48 * 1024 * 1024
RIM = 16


def params(limit=VMEM_LIMIT):
    return pltpu.CompilerParams(vmem_limit_bytes=limit)


def cost(flops, moved):
    return pl.CostEstimate(flops=flops, bytes_accessed=moved, transcendentals=0)


def vmem_specs(count):
    return [pl.BlockSpec(memory_space=pltpu.VMEM)] * count


def silu(u):
    half = 0.5 * u
    return half + half * jnp.tanh(half)


def moments_of(cells):
    mean = jnp.sum(cells, axis=0, keepdims=True) * (1.0 / cells.shape[0])
    off = cells - mean
    return jnp.concatenate([mean, jnp.sum(off * off, axis=0, keepdims=True)], axis=0)


def group_matrix(channels, width):
    shape = (channels, channels)
    row = lax.broadcasted_iota(jnp.int32, shape, 0) // width
    col = lax.broadcasted_iota(jnp.int32, shape, 1) // width
    return jnp.where(row == col, 1.0, 0.0).astype(jnp.bfloat16)


def group_sum(values, matrix):
    parts = []
    for _ in range(3):
        part = values.astype(jnp.bfloat16).astype(jnp.float32)
        parts.append(jnp.broadcast_to(part, (8, part.shape[-1])))
        values = values - part
    stacked = jnp.concatenate(parts + [jnp.zeros_like(parts[0])], axis=0).astype(jnp.bfloat16)
    summed = jnp.dot(stacked, matrix, preferred_element_type=jnp.float32)
    return summed[0:1] + summed[8:9] + summed[16:17]


def scale_and_offset(moments, cells, width, gain, shift, matrix):
    devices = moments.shape[0]
    means = moments[:, 0, :]
    mean = group_sum(jnp.sum(means, axis=0, keepdims=True), matrix) * (1.0 / (devices * width))
    off = means - mean
    total = jnp.sum(moments[:, 1, :] + float(cells) * (off * off), axis=0, keepdims=True)
    spread = group_sum(total, matrix) * (1.0 / (cells * devices * width))
    scale = lax.rsqrt(spread + 1e-6) * gain
    return mean, scale, shift


def apply_norm(values, norm):
    mean, scale, shift = norm
    return silu((values.astype(jnp.float32) - mean) * scale + shift).astype(jnp.bfloat16)


def matrix_kernel(width, matrix_ref):
    matrix_ref[...] = group_matrix(matrix_ref.shape[0], width)


def first_kernel(x_ref, order_ref, moments_ref):
    x = x_ref[...]
    cells = x.astype(jnp.float32).reshape(-1, x.shape[-1])
    moments_ref[...] = jnp.broadcast_to(moments_of(cells)[None], moments_ref.shape)


def rows_kernel(pairs, x_ref, prev_ref, for_x_ref, for_prev_ref, *edge_refs):
    frames, rows, columns = x_ref.shape[:3]
    width = for_x_ref.shape[2]
    start = (1 - lax.axis_index("section")) * (columns - width)
    theirs = pl.ds(pl.multiple_of(start, RIM), width)
    for_x_ref[...] = x_ref[:, :, theirs, :]
    for_prev_ref[...] = prev_ref[:, :, theirs, :]
    if pairs:
        starts = [(rows - 2) * (1 - lax.axis_index("tile"))]
    else:
        starts = [0, rows - 2]
    for start, edge_ref in zip(starts, edge_refs):
        edge_ref[:frames] = prev_ref[:, pl.ds(start, 2)]
        edge_ref[frames:] = x_ref[:, pl.ds(start, 2)]


def scales_kernel(cells, moments_ref, gain_ref, shift_ref, matrix_ref, norm_ref):
    sections, half = gain_ref.shape
    per_section = moments_ref.shape[0] // sections
    for k in range(sections):
        norm = scale_and_offset(
            moments_ref[k * per_section : (k + 1) * per_section],
            cells,
            sections * half // GROUPS,
            gain_ref[k : k + 1],
            shift_ref[k : k + 1],
            matrix_ref[...],
        )
        norm_ref[k] = jnp.concatenate(norm, axis=0)


def column_taps(weight_ref, t, h):
    return jnp.concatenate([weight_ref[t, h, w] for w in range(3)], axis=-1)


def shift_and_add(total, rows, width):
    outputs = total.shape[-1] // 3
    total = total.reshape(rows, width, 3 * outputs)
    before, middle, after = (total[..., k * outputs : (k + 1) * outputs] for k in range(3))
    before = jnp.concatenate([before[:, :1], before[:, :-1]], axis=1)
    after = jnp.concatenate([after[:, 1:], after[:, -1:]], axis=1)
    return middle + before + after


def conv_in_rows(act_ref, weight_ref, frames, top, rows, width):
    totals = [None] * frames
    for a in range(act_ref.shape[0]):
        reached = [f for f in range(frames) if 0 <= a - f <= 2]
        for h in range(3):
            cells = act_ref[a, pl.ds(top + h, rows)]
            cells = cells.reshape(rows * width, cells.shape[-1])
            taps = [column_taps(weight_ref, a - f, h) for f in reached]
            sums = jnp.dot(
                cells, jnp.concatenate(taps, axis=-1), preferred_element_type=jnp.float32
            )
            n = sums.shape[-1] // len(reached)
            for k, f in enumerate(reached):
                part = sums[:, k * n : (k + 1) * n]
                totals[f] = part if totals[f] is None else totals[f] + part
    return [shift_and_add(total, rows, width) for total in totals]


def conv_mid_rows(act_ref, weight_ref, taken, rows, width):
    cells, taps = [], []
    for t, frame in taken:
        for h in range(3):
            block = act_ref[frame, h : h + rows]
            cells.append(block.reshape(rows * width, block.shape[-1]))
            taps.append(column_taps(weight_ref, t, h))
    total = jnp.dot(
        jnp.concatenate(cells, axis=-1),
        jnp.concatenate(taps, axis=0),
        preferred_element_type=jnp.float32,
    )
    return shift_and_add(total, rows, width)


def first_row(tiles, tile):
    return 1 - tile if tiles == 2 else 0


def body_kernel(x_ref, prev_ref, other_x_ref, norm_ref, body_ref):
    section = lax.axis_index("section")
    frames, _, columns, half = x_ref.shape
    width = body_ref.shape[2]
    mine = pl.ds(pl.multiple_of(section * (columns - width), RIM), width)
    for which, first, ref, cols in (
        (section, 0, prev_ref, mine),
        (section, frames, x_ref, mine),
        (1 - section, frames, other_x_ref, slice(None)),
    ):
        norm = tuple(norm_ref[which, k : k + 1] for k in range(3))
        lanes = pl.ds(pl.multiple_of(which * half, half), half)
        for f in range(frames):
            body_ref[first + f, :, :, lanes] = apply_norm(ref[f, :, cols, :], norm)


def middle_kernel(tiles, sides, *refs):
    body_ref, other_prev_ref = refs[:2]
    rim_refs, other_rim_refs = refs[2 : 2 + sides], refs[2 + sides : 2 + 2 * sides]
    norm_ref, weight_ref, bias_ref, hidden_ref, out_moments_hbm = refs[2 + 2 * sides :][:5]
    act_ref, out_moments_ref, sem = refs[-3:]
    section, tm, tile = (lax.axis_index(axis) for axis in AXES)
    columns, half = rim_refs[0].shape[2:]
    frames, rows, width = body_ref.shape[0] // 2, body_ref.shape[1], body_ref.shape[2]
    own = columns // 2
    first = pl.multiple_of(section * (columns - width), RIM)
    cols = pl.ds(first, width)
    top = first_row(tiles, tile)
    rim_rows = (0, rows + 2) if sides == 2 else ((rows + 2) * (1 - tile),)
    act_ref[:, 2 : 2 + rows] = body_ref[...]
    for which, rims in ((section, rim_refs), (1 - section, other_rim_refs)):
        norm = tuple(norm_ref[which, k : k + 1] for k in range(3))
        lanes = pl.ds(pl.multiple_of(which * half, half), half)
        for f in range(2 * frames):
            for row, rim in zip(rim_rows, rims):
                act_ref[f, pl.ds(row, 2), :, lanes] = apply_norm(rim[f, :, cols, :], norm)
    for f in range(frames):
        act_ref[f, 2 : 2 + rows, :, lanes] = apply_norm(other_prev_ref[f], norm)

    @pl.when(tile == 0)
    def _():
        for f in range(2 * frames):
            act_ref[f, 1] = act_ref[f, 2]

    @pl.when(tile == tiles - 1)
    def _():
        for f in range(2 * frames):
            act_ref[f, rows + 2] = act_ref[f, rows + 1]

    @pl.when(tm == 0)
    def _():
        for f in range(frames):
            act_ref[f] = act_ref[frames]

    def hidden_rows(start, count, at):
        sums = conv_in_rows(act_ref, weight_ref, frames, start, count, width)
        for f, hidden in enumerate(sums):
            hidden_ref[f, pl.ds(at, count)] = (hidden + bias_ref[...]).astype(jnp.bfloat16)

    hidden_rows(1, rows, 1 - top)
    cells = hidden_ref[:, pl.ds(1 - top, rows), pl.ds(first, own), :]
    cells = cells.astype(jnp.float32).reshape(-1, cells.shape[-1])
    out_moments_ref[...] = jnp.broadcast_to(moments_of(cells)[None], out_moments_ref.shape)
    copy = pltpu.make_async_copy(out_moments_ref, out_moments_hbm, sem)
    copy.start()
    if sides == 2:
        hidden_rows(0, 1, 0)
        hidden_rows(rows + 1, 1, rows + 1)
    else:
        hidden_rows((rows + 1) * (1 - tile), 1, rows * (1 - tile))
    copy.wait()


def pack_kernel(hidden_ref, sent_ref):
    section = lax.axis_index("section")
    frames, kept, width, channels = hidden_ref.shape
    own = sent_ref.shape[2]
    first = pl.multiple_of(section * (width - own), RIM)
    for f in range(frames):
        sent_ref[f, :kept] = hidden_ref[f, :, pl.ds(first, own), :]
        hidden = hidden_ref[f].astype(jnp.float32)
        rim = jnp.where(section == 0, hidden[:, own, :], hidden[:, width - own - 1, :])
        spare = jnp.zeros((own - kept, channels), jnp.float32)
        sent_ref[f, kept] = jnp.concatenate([rim, spare], axis=0).astype(jnp.bfloat16)


def repeat_edges(act_ref, count, tiles, rows):
    tile = lax.axis_index("tile")

    @pl.when(tile == 0)
    def _():
        for f in range(count):
            act_ref[f, 0] = act_ref[f, 1]

    @pl.when(tile == tiles - 1)
    def _():
        for f in range(count):
            act_ref[f, rows + 1] = act_ref[f, rows]


def own_columns(values, own):
    section = lax.axis_index("section")
    width = values.shape[1]
    return jnp.where(section == 0, values[:, :own], values[:, width - own :])


def shortcut_kernel(x_ref, other_x_ref, skip_ref, skip_bias_ref, bias_ref, part_ref):
    section = lax.axis_index("section")
    frames, rows, columns, half = x_ref.shape
    own = columns // 2
    mine = pl.ds(pl.multiple_of(section * own, own), own)
    within = pl.ds(pl.multiple_of(section * (other_x_ref.shape[2] - own), RIM), own)
    skip_here = skip_ref[pl.ds(pl.multiple_of(section * half, half), half), :]
    skip_there = skip_ref[pl.ds(pl.multiple_of((1 - section) * half, half), half), :]
    for f in range(frames):
        here = x_ref[f, :, mine, :].reshape(rows * own, half)
        there = other_x_ref[f, :, within, :].reshape(rows * own, half)
        shortcut = jnp.dot(here, skip_here, preferred_element_type=jnp.float32)
        shortcut = shortcut + jnp.dot(there, skip_there, preferred_element_type=jnp.float32)
        part_ref[f] = (shortcut + (skip_bias_ref[...] + bias_ref[...])).reshape(rows, own, -1)


def own_frames_kernel(
    tiles,
    hidden_ref,
    moments_ref,
    gain_ref,
    shift_ref,
    weight_ref,
    shortcut_ref,
    part_ref,
    norm_ref,
    act_ref,
):
    frames, kept, width, outputs = hidden_ref.shape
    rows, own = part_ref.shape[1:3]
    top = first_row(tiles, lax.axis_index("tile"))
    norm = scale_and_offset(
        moments_ref[...],
        frames * rows * own,
        outputs // GROUPS,
        gain_ref[...],
        shift_ref[...],
        group_matrix(outputs, outputs // GROUPS),
    )
    norm_ref[...] = jnp.concatenate(norm, axis=0)
    for f in range(frames):
        act_ref[f, pl.ds(top, kept)] = apply_norm(hidden_ref[f], norm)
    repeat_edges(act_ref, frames, tiles, rows)
    for f in range(frames):
        taken = [(k - f + 2, k) for k in range(f - 2, f + 1) if k >= 0]
        residual = own_columns(conv_mid_rows(act_ref, weight_ref, taken, rows, width), own)
        part_ref[f] = shortcut_ref[f] + residual


def last_kernel(
    tiles, hidden_ref, before_ref, norm_ref, weight_ref, part_ref, out_hbm, act_ref, out_ref, sems
):
    section, tm, tile = (lax.axis_index(axis) for axis in AXES)
    frames, kept, width, outputs = hidden_ref.shape
    rows, own = part_ref.shape[1:3]
    top = first_row(tiles, tile)
    first = pl.multiple_of(section * (width - own), RIM)
    beside = pl.multiple_of((1 - section) * own, RIM)
    norm = tuple(norm_ref[k : k + 1] for k in range(3))
    @pl.when(tm > 0)
    def _():
        for f in range(frames):
            act_ref[f, pl.ds(top, kept), pl.ds(first, own), :] = apply_norm(before_ref[f, :kept], norm)
            rim = apply_norm(before_ref[f, kept], norm).astype(jnp.float32)[:kept]
            rim = jnp.broadcast_to(rim[:, None, :], (kept, width - own, outputs))
            act_ref[f, pl.ds(top, kept), pl.ds(beside, width - own), :] = rim.astype(jnp.bfloat16)

    @pl.when(tm == 0)
    def _():
        start = apply_norm(hidden_ref[0], norm)
        for f in range(frames):
            act_ref[f, pl.ds(top, kept)] = start

    repeat_edges(act_ref, frames, tiles, rows)
    copies = []
    for f in range(frames):
        taken = [(k - f, k) for k in range(f, f + 3) if k < frames]
        residual = own_columns(conv_mid_rows(act_ref, weight_ref, taken, rows, width), own)
        out_ref[f] = (part_ref[f] + residual).astype(jnp.bfloat16)
        copies.append(pltpu.make_async_copy(out_ref.at[f], out_hbm.at[f], sems.at[f]))
        copies[-1].start()
    for copy in copies:
        copy.wait()


def pairs_for(tm_count, tile_count, tm_step, tile_step):
    out = []
    for a in range(tm_count):
        for b in range(tile_count):
            c, d = a + tm_step, b + tile_step
            if 0 <= c < tm_count and 0 <= d < tile_count:
                out.append((a * tile_count + b, c * tile_count + d))
    return out


def to_everyone(moments):
    return lax.all_to_all(moments, AXES, 0, 0, tiled=True)


def shards(
    features,
    norm_gain_in,
    norm_shift_in,
    conv_in_weight,
    conv_in_bias,
    norm_gain_mid,
    norm_shift_mid,
    conv_mid_weight,
    conv_mid_bias,
    skip_weight,
    skip_bias,
):
    sections, tms, tiles = (lax.axis_size(axis) for axis in AXES)
    parties = sections * tms * tiles
    frames, rows, columns, half = features.shape
    own = columns // sections
    width = own + RIM
    middle = conv_in_weight.shape[-1]
    outputs = conv_mid_weight.shape[-1]
    grid_axes = ("tm", "tile")

    def shift(value, tm_step, tile_step):
        return lax.ppermute(value, grid_axes, pairs_for(tms, tiles, tm_step, tile_step))

    def swap(value):
        return lax.ppermute(value, "section", [(0, 1), (1, 0)])

    previous = shift(features, 1, 0)
    matrix = pl.pallas_call(
        functools.partial(matrix_kernel, half * sections // GROUPS),
        out_shape=jax.ShapeDtypeStruct((half, half), jnp.bfloat16),
        out_specs=pl.BlockSpec(memory_space=pltpu.VMEM),
        compiler_params=params(),
        cost_estimate=cost(1_000_000_000, 1_000_000),
        name="group_matrix",
    )()
    sums = pl.pallas_call(
        first_kernel,
        out_shape=jax.ShapeDtypeStruct((parties, 2, half), jnp.float32),
        in_specs=[*vmem_specs(1), pl.BlockSpec(memory_space=pl.ANY)],
        out_specs=pl.BlockSpec(memory_space=pltpu.VMEM),
        compiler_params=params(),
        cost_estimate=cost(1_000_000_000, 1_000_000),
        name="feature_moments",
    )(features, matrix)
    moments = to_everyone(sums)
    previous, _ = lax.optimization_barrier((previous, sums))
    edges = 1 if tiles == 2 else 2
    edge = jax.ShapeDtypeStruct((2 * frames, 2, columns, half), features.dtype)
    cut = jax.ShapeDtypeStruct((frames, rows, width, half), features.dtype)
    for_x, for_previous, *edge_rows = pl.pallas_call(
        functools.partial(rows_kernel, tiles == 2),
        out_shape=(cut, cut) + (edge,) * edges,
        in_specs=vmem_specs(2),
        out_specs=tuple(vmem_specs(2 + edges)),
        compiler_params=params(),
        cost_estimate=cost(500_000_000, 1_000_000),
        name="facing_rows",
    )(features, previous)
    if tiles == 2:
        rims = [lax.ppermute(edge_rows[0], "tile", [(0, 1), (1, 0)])]
    else:
        rims = [shift(edge_rows[1], 0, 1), shift(edge_rows[0], 0, -1)]
    other = swap(for_x)
    other_previous = swap(for_previous)
    norm_in = pl.pallas_call(
        functools.partial(scales_kernel, frames * rows * columns),
        out_shape=jax.ShapeDtypeStruct((sections, 3, half), jnp.float32),
        in_specs=vmem_specs(4),
        out_specs=pl.BlockSpec(memory_space=pltpu.VMEM),
        compiler_params=params(),
        cost_estimate=cost(2_000_000_000, 1_000_000),
        name="feature_scales",
    )(moments, norm_gain_in.reshape(sections, half), norm_shift_in.reshape(sections, half), matrix)
    norm_in, *rims = lax.optimization_barrier((norm_in, *rims))
    other_rims = [swap(rim) for rim in rims]

    kept = rows + edges
    body = pl.pallas_call(
        body_kernel,
        out_shape=jax.ShapeDtypeStruct((2 * frames, rows, width, 2 * half), jnp.bfloat16),
        in_specs=vmem_specs(4),
        out_specs=pl.BlockSpec(memory_space=pltpu.VMEM),
        compiler_params=params(),
        cost_estimate=cost(1_000_000_000, 1_000_000),
        name="norm_body",
    )(features, previous, other, norm_in)
    hidden, moments_mid = pl.pallas_call(
        functools.partial(middle_kernel, tiles, edges),
        out_shape=(
            jax.ShapeDtypeStruct((frames, kept, width, middle), jnp.bfloat16),
            jax.ShapeDtypeStruct((parties, 2, middle), jnp.float32),
        ),
        in_specs=vmem_specs(5 + 2 * edges),
        out_specs=(*vmem_specs(1), pl.BlockSpec(memory_space=pl.ANY)),
        scratch_shapes=[
            pltpu.VMEM((2 * frames, rows + 4, width, 2 * half), jnp.bfloat16),
            pltpu.VMEM((parties, 2, middle), jnp.float32),
            pltpu.SemaphoreType.DMA,
        ],
        compiler_params=params(),
        cost_estimate=cost(4_000_000_000, 1_000_000),
        name="conv_in",
    )(
        body,
        other_previous,
        *rims,
        *other_rims,
        norm_in,
        conv_in_weight,
        conv_in_bias.reshape(1, middle),
    )
    moments_mid = to_everyone(moments_mid)
    sent = pl.pallas_call(
        pack_kernel,
        out_shape=jax.ShapeDtypeStruct((frames, kept + 1, own, middle), jnp.bfloat16),
        in_specs=vmem_specs(1),
        out_specs=pl.BlockSpec(memory_space=pltpu.VMEM),
        compiler_params=params(),
        cost_estimate=cost(1_000_000_000, 1_000_000),
        name="pack_hidden",
    )(hidden)
    before = shift(sent, 1, 0)
    shown, _ = lax.optimization_barrier((other, sent))
    shortcut = pl.pallas_call(
        shortcut_kernel,
        out_shape=jax.ShapeDtypeStruct((frames, rows, own, outputs), jnp.float32),
        in_specs=vmem_specs(5),
        out_specs=pl.BlockSpec(memory_space=pltpu.VMEM),
        compiler_params=params(),
        cost_estimate=cost(300_000_000, 1_000_000),
        name="shortcut",
    )(
        features,
        shown,
        skip_weight,
        skip_bias.reshape(1, outputs),
        conv_mid_bias.reshape(1, outputs),
    )
    part, norm_mid = pl.pallas_call(
        functools.partial(own_frames_kernel, tiles),
        out_shape=(
            jax.ShapeDtypeStruct((frames, rows, own, outputs), jnp.float32),
            jax.ShapeDtypeStruct((3, middle), jnp.float32),
        ),
        in_specs=vmem_specs(6),
        out_specs=tuple(vmem_specs(2)),
        scratch_shapes=[pltpu.VMEM((frames, rows + 2, width, middle), jnp.bfloat16)],
        compiler_params=params(),
        cost_estimate=cost(2_000_000_000, 1_000_000),
        name="conv_mid_own_frames",
    )(
        hidden,
        moments_mid,
        norm_gain_mid.reshape(1, middle),
        norm_shift_mid.reshape(1, middle),
        conv_mid_weight,
        shortcut,
    )
    return pl.pallas_call(
        functools.partial(last_kernel, tiles),
        out_shape=jax.ShapeDtypeStruct((frames, rows, own, outputs), jnp.bfloat16),
        in_specs=vmem_specs(5),
        out_specs=pl.BlockSpec(memory_space=pl.ANY),
        scratch_shapes=[
            pltpu.VMEM((frames, rows + 2, width, middle), jnp.bfloat16),
            pltpu.VMEM((frames, rows, own, outputs), jnp.bfloat16),
            pltpu.SemaphoreType.DMA((frames,)),
        ],
        compiler_params=params(),
        cost_estimate=cost(2_000_000_000, 1_000_000),
        name="conv_mid_previous_frames",
    )(hidden, before, norm_mid, conv_mid_weight, part)


def solution(mesh):
    in_specs = (P("tm", "tile", None, "section"),) + (P(),) * 10
    out_specs = P("tm", "tile", "section", None)
    return jax.shard_map(shards, mesh=mesh, in_specs=in_specs, out_specs=out_specs, check_vma=False)
```

```python
import functools

import jax
import jax.numpy as jnp
from jax import lax
from jax.experimental import pallas as pl
from jax.experimental.pallas import tpu as pltpu
from jax.sharding import PartitionSpec as P

GROUPS = 32
AXES = ("section", "tm", "tile")
VMEM_LIMIT = 48 * 1024 * 1024
RIM = 16


def params(limit=VMEM_LIMIT):
    return pltpu.CompilerParams(vmem_limit_bytes=limit)


def cost(flops, moved):
    return pl.CostEstimate(flops=flops, bytes_accessed=moved, transcendentals=0)


def vmem_specs(count):
    return [pl.BlockSpec(memory_space=pltpu.VMEM)] * count


def silu(u):
    half = 0.5 * u
    return half + half * jnp.tanh(half)


def moments_of(cells):
    mean = jnp.sum(cells, axis=0, keepdims=True) * (1.0 / cells.shape[0])
    off = cells - mean
    return jnp.concatenate([mean, jnp.sum(off * off, axis=0, keepdims=True)], axis=0)


def group_matrix(channels, width):
    shape = (channels, channels)
    row = lax.broadcasted_iota(jnp.int32, shape, 0) // width
    col = lax.broadcasted_iota(jnp.int32, shape, 1) // width
    return jnp.where(row == col, 1.0, 0.0).astype(jnp.bfloat16)


def group_sum(values, matrix):
    parts = []
    for _ in range(3):
        part = values.astype(jnp.bfloat16).astype(jnp.float32)
        parts.append(jnp.broadcast_to(part, (8, part.shape[-1])))
        values = values - part
    stacked = jnp.concatenate(parts + [jnp.zeros_like(parts[0])], axis=0).astype(jnp.bfloat16)
    summed = jnp.dot(stacked, matrix, preferred_element_type=jnp.float32)
    return summed[0:1] + summed[8:9] + summed[16:17]


def scale_and_offset(moments, cells, width, gain, shift, matrix):
    devices = moments.shape[0]
    means = moments[:, 0, :]
    mean = group_sum(jnp.sum(means, axis=0, keepdims=True), matrix) * (1.0 / (devices * width))
    off = means - mean
    total = jnp.sum(moments[:, 1, :] + float(cells) * (off * off), axis=0, keepdims=True)
    spread = group_sum(total, matrix) * (1.0 / (cells * devices * width))
    scale = lax.rsqrt(spread + 1e-6) * gain
    return mean, scale, shift


def apply_norm(values, norm):
    mean, scale, shift = norm
    return silu((values.astype(jnp.float32) - mean) * scale + shift).astype(jnp.bfloat16)


def matrix_kernel(width, matrix_ref):
    matrix_ref[...] = group_matrix(matrix_ref.shape[0], width)


def first_kernel(x_ref, order_ref, moments_ref):
    x = x_ref[...]
    cells = x.astype(jnp.float32).reshape(-1, x.shape[-1])
    moments_ref[...] = jnp.broadcast_to(moments_of(cells)[None], moments_ref.shape)


def rows_kernel(pairs, x_ref, prev_ref, for_x_ref, for_prev_ref, *edge_refs):
    frames, rows, columns = x_ref.shape[:3]
    width = for_x_ref.shape[2]
    start = (1 - lax.axis_index("section")) * (columns - width)
    theirs = pl.ds(pl.multiple_of(start, RIM), width)
    for_x_ref[...] = x_ref[:, :, theirs, :]
    for_prev_ref[...] = prev_ref[:, :, theirs, :]
    if pairs:
        starts = [(rows - 2) * (1 - lax.axis_index("tile"))]
    else:
        starts = [0, rows - 2]
    for start, edge_ref in zip(starts, edge_refs):
        edge_ref[:frames] = prev_ref[:, pl.ds(start, 2)]
        edge_ref[frames:] = x_ref[:, pl.ds(start, 2)]


def scales_kernel(cells, moments_ref, gain_ref, shift_ref, matrix_ref, norm_ref):
    sections, half = gain_ref.shape
    per_section = moments_ref.shape[0] // sections
    for k in range(sections):
        norm = scale_and_offset(
            moments_ref[k * per_section : (k + 1) * per_section],
            cells,
            sections * half // GROUPS,
            gain_ref[k : k + 1],
            shift_ref[k : k + 1],
            matrix_ref[...],
        )
        norm_ref[k] = jnp.concatenate(norm, axis=0)


def column_taps(weight_ref, t, h):
    return jnp.concatenate([weight_ref[t, h, w] for w in range(3)], axis=-1)


def shift_and_add(total, rows, width):
    outputs = total.shape[-1] // 3
    total = total.reshape(rows, width, 3 * outputs)
    before, middle, after = (total[..., k * outputs : (k + 1) * outputs] for k in range(3))
    before = jnp.concatenate([before[:, :1], before[:, :-1]], axis=1)
    after = jnp.concatenate([after[:, 1:], after[:, -1:]], axis=1)
    return middle + before + after


def conv_in_rows(cells_of, weight_ref, frames, rows, width):
    totals = [None] * frames
    for a in range(frames + 2):
        reached = [f for f in range(frames) if 0 <= a - f <= 2]
        for h in range(3):
            cells = cells_of(a, h)
            cells = cells.reshape(rows * width, cells.shape[-1])
            taps = [column_taps(weight_ref, a - f, h) for f in reached]
            sums = jnp.dot(
                cells, jnp.concatenate(taps, axis=-1), preferred_element_type=jnp.float32
            )
            n = sums.shape[-1] // len(reached)
            for k, f in enumerate(reached):
                part = sums[:, k * n : (k + 1) * n]
                totals[f] = part if totals[f] is None else totals[f] + part
    return [shift_and_add(total, rows, width) for total in totals]


def conv_mid_rows(act_ref, weight_ref, taken, rows, width):
    cells, taps = [], []
    for t, frame in taken:
        for h in range(3):
            block = act_ref[frame, h : h + rows]
            cells.append(block.reshape(rows * width, block.shape[-1]))
            taps.append(column_taps(weight_ref, t, h))
    total = jnp.dot(
        jnp.concatenate(cells, axis=-1),
        jnp.concatenate(taps, axis=0),
        preferred_element_type=jnp.float32,
    )
    return shift_and_add(total, rows, width)


def first_row(tiles, tile):
    return 1 - tile if tiles == 2 else 0


def body_kernel(x_ref, prev_ref, other_x_ref, other_prev_ref, norm_ref, body_ref):
    section = lax.axis_index("section")
    frames, _, columns, half = x_ref.shape
    width = body_ref.shape[2]
    mine = pl.ds(pl.multiple_of(section * (columns - width), RIM), width)
    for which, first, ref, cols in (
        (section, 0, prev_ref, mine),
        (section, frames, x_ref, mine),
        (1 - section, frames, other_x_ref, slice(None)),
        (1 - section, 0, other_prev_ref, slice(None)),
    ):
        norm = tuple(norm_ref[which, k : k + 1] for k in range(3))
        lanes = pl.ds(pl.multiple_of(which * half, half), half)
        for f in range(frames):
            body_ref[first + f, :, :, lanes] = apply_norm(ref[f, :, cols, :], norm)

    @pl.when(lax.axis_index("tm") == 0)
    def _():
        for f in range(frames):
            body_ref[f] = body_ref[frames]


def inner_kernel(body_ref, weight_ref, bias_ref, inner_ref):
    frames, rows, width = inner_ref.shape[:3]
    sums = conv_in_rows(
        lambda a, h: body_ref[a, h : h + rows], weight_ref, frames, rows, width
    )
    for f, hidden in enumerate(sums):
        inner_ref[f] = (hidden + bias_ref[...]).astype(jnp.bfloat16)


def middle_kernel(tiles, sides, *refs):
    body_ref, inner_ref = refs[:2]
    rim_refs, other_rim_refs = refs[2 : 2 + sides], refs[2 + sides : 2 + 2 * sides]
    norm_ref, weight_ref, bias_ref, hidden_ref, out_moments_ref, act_ref = refs[2 + 2 * sides :]
    section, tm, tile = (lax.axis_index(axis) for axis in AXES)
    columns, half = rim_refs[0].shape[2:]
    frames, rows, width = body_ref.shape[0] // 2, body_ref.shape[1], body_ref.shape[2]
    own = columns // 2
    first = pl.multiple_of(section * (columns - width), RIM)
    cols = pl.ds(first, width)
    act_ref[:, 2:4] = body_ref[:, :2]
    act_ref[:, 4:6] = body_ref[:, rows - 2 :]
    rim_rows = (0, 6) if sides == 2 else (6 * (1 - tile),)
    for which, rims in ((section, rim_refs), (1 - section, other_rim_refs)):
        norm = tuple(norm_ref[which, k : k + 1] for k in range(3))
        lanes = pl.ds(pl.multiple_of(which * half, half), half)
        for f in range(2 * frames):
            for row, rim in zip(rim_rows, rims):
                act_ref[f, pl.ds(row, 2), :, lanes] = apply_norm(rim[f, :, cols, :], norm)

    @pl.when(tile == 0)
    def _():
        for f in range(2 * frames):
            act_ref[f, 1] = act_ref[f, 2]

    @pl.when(tile == tiles - 1)
    def _():
        for f in range(2 * frames):
            act_ref[f, 6] = act_ref[f, 5]

    @pl.when(tm == 0)
    def _():
        for f in range(frames):
            act_ref[f] = act_ref[frames]

    sums = conv_in_rows(
        lambda a, h: jnp.concatenate(
            [act_ref[a, h : h + 2], act_ref[a, 4 + h : 6 + h]], axis=0
        ),
        weight_ref,
        frames,
        4,
        width,
    )
    at = 1 - first_row(tiles, tile)
    for f, hidden in enumerate(sums):
        outer = (hidden + bias_ref[...]).astype(jnp.bfloat16)
        hidden_ref[f, pl.ds(at + 1, rows - 2)] = inner_ref[f]
        if sides == 2:
            hidden_ref[f, 0:1] = outer[0:1]
            hidden_ref[f, rows + 1 : rows + 2] = outer[3:4]
        else:
            rim = jnp.where(tile == 0, outer[3:4], outer[0:1])
            hidden_ref[f, pl.ds(rows * (1 - tile), 1)] = rim
        hidden_ref[f, pl.ds(at, 1)] = outer[1:2]
        hidden_ref[f, pl.ds(at + rows - 1, 1)] = outer[2:3]

    cells = hidden_ref[:, pl.ds(at, rows), pl.ds(first, own), :]
    cells = cells.astype(jnp.float32).reshape(-1, cells.shape[-1])
    out_moments_ref[...] = jnp.broadcast_to(moments_of(cells)[None], out_moments_ref.shape)


def pack_kernel(hidden_ref, sent_ref):
    section = lax.axis_index("section")
    frames, kept, width, channels = hidden_ref.shape
    own = sent_ref.shape[2]
    first = pl.multiple_of(section * (width - own), RIM)
    for f in range(frames):
        sent_ref[f, :kept] = hidden_ref[f, :, pl.ds(first, own), :]
        hidden = hidden_ref[f].astype(jnp.float32)
        rim = jnp.where(section == 0, hidden[:, own, :], hidden[:, width - own - 1, :])
        spare = jnp.zeros((own - kept, channels), jnp.float32)
        sent_ref[f, kept] = jnp.concatenate([rim, spare], axis=0).astype(jnp.bfloat16)


def repeat_edges(act_ref, count, tiles, rows):
    tile = lax.axis_index("tile")

    @pl.when(tile == 0)
    def _():
        for f in range(count):
            act_ref[f, 0] = act_ref[f, 1]

    @pl.when(tile == tiles - 1)
    def _():
        for f in range(count):
            act_ref[f, rows + 1] = act_ref[f, rows]


def own_columns(values, own):
    section = lax.axis_index("section")
    width = values.shape[1]
    return jnp.where(section == 0, values[:, :own], values[:, width - own :])


def shortcut_kernel(x_ref, other_x_ref, skip_ref, skip_bias_ref, bias_ref, part_ref):
    section = lax.axis_index("section")
    frames, rows, columns, half = x_ref.shape
    own = columns // 2
    mine = pl.ds(pl.multiple_of(section * own, own), own)
    within = pl.ds(pl.multiple_of(section * (other_x_ref.shape[2] - own), RIM), own)
    skip_here = skip_ref[pl.ds(pl.multiple_of(section * half, half), half), :]
    skip_there = skip_ref[pl.ds(pl.multiple_of((1 - section) * half, half), half), :]
    for f in range(frames):
        here = x_ref[f, :, mine, :].reshape(rows * own, half)
        there = other_x_ref[f, :, within, :].reshape(rows * own, half)
        shortcut = jnp.dot(here, skip_here, preferred_element_type=jnp.float32)
        shortcut = shortcut + jnp.dot(there, skip_there, preferred_element_type=jnp.float32)
        part_ref[f] = (shortcut + (skip_bias_ref[...] + bias_ref[...])).reshape(rows, own, -1)


def own_frames_kernel(
    tiles,
    hidden_ref,
    moments_ref,
    gain_ref,
    shift_ref,
    weight_ref,
    shortcut_ref,
    part_ref,
    norm_ref,
    act_ref,
):
    frames, kept, width, outputs = hidden_ref.shape
    rows, own = part_ref.shape[1:3]
    top = first_row(tiles, lax.axis_index("tile"))
    norm = scale_and_offset(
        moments_ref[...],
        frames * rows * own,
        outputs // GROUPS,
        gain_ref[...],
        shift_ref[...],
        group_matrix(outputs, outputs // GROUPS),
    )
    norm_ref[...] = jnp.concatenate(norm, axis=0)
    for f in range(frames):
        act_ref[f, pl.ds(top, kept)] = apply_norm(hidden_ref[f], norm)
    repeat_edges(act_ref, frames, tiles, rows)
    for f in range(frames):
        taken = [(k - f + 2, k) for k in range(f - 2, f + 1) if k >= 0]
        residual = own_columns(conv_mid_rows(act_ref, weight_ref, taken, rows, width), own)
        part_ref[f] = shortcut_ref[f] + residual


def last_kernel(
    tiles, hidden_ref, before_ref, norm_ref, weight_ref, part_ref, out_hbm, act_ref, out_ref, sems
):
    section, tm, tile = (lax.axis_index(axis) for axis in AXES)
    frames, kept, width, outputs = hidden_ref.shape
    rows, own = part_ref.shape[1:3]
    top = first_row(tiles, tile)
    first = pl.multiple_of(section * (width - own), RIM)
    beside = pl.multiple_of((1 - section) * own, RIM)
    norm = tuple(norm_ref[k : k + 1] for k in range(3))
    @pl.when(tm > 0)
    def _():
        for f in range(frames):
            act_ref[f, pl.ds(top, kept), pl.ds(first, own), :] = apply_norm(before_ref[f, :kept], norm)
            rim = apply_norm(before_ref[f, kept], norm).astype(jnp.float32)[:kept]
            rim = jnp.broadcast_to(rim[:, None, :], (kept, width - own, outputs))
            act_ref[f, pl.ds(top, kept), pl.ds(beside, width - own), :] = rim.astype(jnp.bfloat16)

    @pl.when(tm == 0)
    def _():
        start = apply_norm(hidden_ref[0], norm)
        for f in range(frames):
            act_ref[f, pl.ds(top, kept)] = start

    repeat_edges(act_ref, frames, tiles, rows)
    copies = []
    for f in range(frames):
        taken = [(k - f, k) for k in range(f, f + 3) if k < frames]
        residual = own_columns(conv_mid_rows(act_ref, weight_ref, taken, rows, width), own)
        out_ref[f] = (part_ref[f] + residual).astype(jnp.bfloat16)
        copies.append(pltpu.make_async_copy(out_ref.at[f], out_hbm.at[f], sems.at[f]))
        copies[-1].start()
    for copy in copies:
        copy.wait()


def pairs_for(tm_count, tile_count, tm_step, tile_step):
    out = []
    for a in range(tm_count):
        for b in range(tile_count):
            c, d = a + tm_step, b + tile_step
            if 0 <= c < tm_count and 0 <= d < tile_count:
                out.append((a * tile_count + b, c * tile_count + d))
    return out


def to_everyone(moments):
    return lax.all_to_all(moments, AXES, 0, 0, tiled=True)


def shards(
    features,
    norm_gain_in,
    norm_shift_in,
    conv_in_weight,
    conv_in_bias,
    norm_gain_mid,
    norm_shift_mid,
    conv_mid_weight,
    conv_mid_bias,
    skip_weight,
    skip_bias,
):
    sections, tms, tiles = (lax.axis_size(axis) for axis in AXES)
    parties = sections * tms * tiles
    frames, rows, columns, half = features.shape
    own = columns // sections
    width = own + RIM
    middle = conv_in_weight.shape[-1]
    outputs = conv_mid_weight.shape[-1]
    grid_axes = ("tm", "tile")

    def shift(value, tm_step, tile_step):
        return lax.ppermute(value, grid_axes, pairs_for(tms, tiles, tm_step, tile_step))

    def swap(value):
        return lax.ppermute(value, "section", [(0, 1), (1, 0)])

    previous = shift(features, 1, 0)
    matrix = pl.pallas_call(
        functools.partial(matrix_kernel, half * sections // GROUPS),
        out_shape=jax.ShapeDtypeStruct((half, half), jnp.bfloat16),
        out_specs=pl.BlockSpec(memory_space=pltpu.VMEM),
        compiler_params=params(),
        cost_estimate=cost(1_000_000_000, 1_000_000),
        name="group_matrix",
    )()
    sums = pl.pallas_call(
        first_kernel,
        out_shape=jax.ShapeDtypeStruct((parties, 2, half), jnp.float32),
        in_specs=[*vmem_specs(1), pl.BlockSpec(memory_space=pl.ANY)],
        out_specs=pl.BlockSpec(memory_space=pltpu.VMEM),
        compiler_params=params(),
        cost_estimate=cost(1_000_000_000, 1_000_000),
        name="feature_moments",
    )(features, matrix)
    moments = to_everyone(sums)
    previous, _ = lax.optimization_barrier((previous, sums))
    edges = 1 if tiles == 2 else 2
    edge = jax.ShapeDtypeStruct((2 * frames, 2, columns, half), features.dtype)
    cut = jax.ShapeDtypeStruct((frames, rows, width, half), features.dtype)
    for_x, for_previous, *edge_rows = pl.pallas_call(
        functools.partial(rows_kernel, tiles == 2),
        out_shape=(cut, cut) + (edge,) * edges,
        in_specs=vmem_specs(2),
        out_specs=tuple(vmem_specs(2 + edges)),
        compiler_params=params(),
        cost_estimate=cost(500_000_000, 1_000_000),
        name="facing_rows",
    )(features, previous)
    if tiles == 2:
        rims = [lax.ppermute(edge_rows[0], "tile", [(0, 1), (1, 0)])]
    else:
        rims = [shift(edge_rows[1], 0, 1), shift(edge_rows[0], 0, -1)]
    other = swap(for_x)
    other_previous = swap(for_previous)
    norm_in = pl.pallas_call(
        functools.partial(scales_kernel, frames * rows * columns),
        out_shape=jax.ShapeDtypeStruct((sections, 3, half), jnp.float32),
        in_specs=vmem_specs(4),
        out_specs=pl.BlockSpec(memory_space=pltpu.VMEM),
        compiler_params=params(),
        cost_estimate=cost(3_000_000_000, 1_000_000),
        name="feature_scales",
    )(moments, norm_gain_in.reshape(sections, half), norm_shift_in.reshape(sections, half), matrix)
    norm_in, *rims = lax.optimization_barrier((norm_in, *rims))
    other_rims = [swap(rim) for rim in rims]

    kept = rows + edges
    body = pl.pallas_call(
        body_kernel,
        out_shape=jax.ShapeDtypeStruct((2 * frames, rows, width, 2 * half), jnp.bfloat16),
        in_specs=vmem_specs(5),
        out_specs=pl.BlockSpec(memory_space=pltpu.VMEM),
        compiler_params=params(),
        cost_estimate=cost(1_000_000_000, 1_000_000),
        name="norm_body",
    )(features, previous, other, other_previous, norm_in)
    inner = pl.pallas_call(
        inner_kernel,
        out_shape=jax.ShapeDtypeStruct((frames, rows - 2, width, middle), jnp.bfloat16),
        in_specs=vmem_specs(3),
        out_specs=pl.BlockSpec(memory_space=pltpu.VMEM),
        compiler_params=params(),
        cost_estimate=cost(1_000_000_000, 1_000_000),
        name="conv_in_inner",
    )(body, conv_in_weight, conv_in_bias.reshape(1, middle))
    hidden, moments_mid = pl.pallas_call(
        functools.partial(middle_kernel, tiles, edges),
        out_shape=(
            jax.ShapeDtypeStruct((frames, kept, width, middle), jnp.bfloat16),
            jax.ShapeDtypeStruct((parties, 2, middle), jnp.float32),
        ),
        in_specs=vmem_specs(5 + 2 * edges),
        out_specs=tuple(vmem_specs(2)),
        scratch_shapes=[pltpu.VMEM((2 * frames, 8, width, 2 * half), jnp.bfloat16)],
        compiler_params=params(),
        cost_estimate=cost(4_000_000_000, 1_000_000),
        name="conv_in",
    )(
        body,
        inner,
        *rims,
        *other_rims,
        norm_in,
        conv_in_weight,
        conv_in_bias.reshape(1, middle),
    )
    moments_mid = to_everyone(moments_mid)
    sent = pl.pallas_call(
        pack_kernel,
        out_shape=jax.ShapeDtypeStruct((frames, kept + 1, own, middle), jnp.bfloat16),
        in_specs=vmem_specs(1),
        out_specs=pl.BlockSpec(memory_space=pltpu.VMEM),
        compiler_params=params(),
        cost_estimate=cost(1_000_000_000, 1_000_000),
        name="pack_hidden",
    )(hidden)
    before = shift(sent, 1, 0)
    shown, _ = lax.optimization_barrier((other, sent))
    shortcut = pl.pallas_call(
        shortcut_kernel,
        out_shape=jax.ShapeDtypeStruct((frames, rows, own, outputs), jnp.float32),
        in_specs=vmem_specs(5),
        out_specs=pl.BlockSpec(memory_space=pltpu.VMEM),
        compiler_params=params(),
        cost_estimate=cost(300_000_000, 1_000_000),
        name="shortcut",
    )(
        features,
        shown,
        skip_weight,
        skip_bias.reshape(1, outputs),
        conv_mid_bias.reshape(1, outputs),
    )
    part, norm_mid = pl.pallas_call(
        functools.partial(own_frames_kernel, tiles),
        out_shape=(
            jax.ShapeDtypeStruct((frames, rows, own, outputs), jnp.float32),
            jax.ShapeDtypeStruct((3, middle), jnp.float32),
        ),
        in_specs=vmem_specs(6),
        out_specs=tuple(vmem_specs(2)),
        scratch_shapes=[pltpu.VMEM((frames, rows + 2, width, middle), jnp.bfloat16)],
        compiler_params=params(),
        cost_estimate=cost(2_000_000_000, 1_000_000),
        name="conv_mid_own_frames",
    )(
        hidden,
        moments_mid,
        norm_gain_mid.reshape(1, middle),
        norm_shift_mid.reshape(1, middle),
        conv_mid_weight,
        shortcut,
    )
    return pl.pallas_call(
        functools.partial(last_kernel, tiles),
        out_shape=jax.ShapeDtypeStruct((frames, rows, own, outputs), jnp.bfloat16),
        in_specs=vmem_specs(5),
        out_specs=pl.BlockSpec(memory_space=pl.ANY),
        scratch_shapes=[
            pltpu.VMEM((frames, rows + 2, width, middle), jnp.bfloat16),
            pltpu.VMEM((frames, rows, own, outputs), jnp.bfloat16),
            pltpu.SemaphoreType.DMA((frames,)),
        ],
        compiler_params=params(),
        cost_estimate=cost(2_000_000_000, 1_000_000),
        name="conv_mid_previous_frames",
    )(hidden, before, norm_mid, conv_mid_weight, part)


def solution(mesh):
    in_specs = (P("tm", "tile", None, "section"),) + (P(),) * 10
    out_specs = P("tm", "tile", "section", None)
    return jax.shard_map(shards, mesh=mesh, in_specs=in_specs, out_specs=out_specs, check_vma=False)
```

```python
import functools

import jax
import jax.numpy as jnp
from jax import lax
from jax.experimental import pallas as pl
from jax.experimental.pallas import tpu as pltpu
from jax.sharding import PartitionSpec as P

GROUPS = 32
AXES = ("section", "tm", "tile")
VMEM_LIMIT = 48 * 1024 * 1024
RIM = 16


def params(limit=VMEM_LIMIT):
    return pltpu.CompilerParams(vmem_limit_bytes=limit)


def cost(flops, moved):
    return pl.CostEstimate(flops=flops, bytes_accessed=moved, transcendentals=0)


def vmem_specs(count):
    return [pl.BlockSpec(memory_space=pltpu.VMEM)] * count


def silu(u):
    half = 0.5 * u
    return half + half * jnp.tanh(half)


def moments_of(cells):
    mean = jnp.sum(cells, axis=0, keepdims=True) * (1.0 / cells.shape[0])
    off = cells - mean
    return jnp.concatenate([mean, jnp.sum(off * off, axis=0, keepdims=True)], axis=0)


def group_matrix(channels, width):
    shape = (channels, channels)
    row = lax.broadcasted_iota(jnp.int32, shape, 0) // width
    col = lax.broadcasted_iota(jnp.int32, shape, 1) // width
    return jnp.where(row == col, 1.0, 0.0).astype(jnp.bfloat16)


def group_sum(values, matrix):
    parts = []
    for _ in range(3):
        part = values.astype(jnp.bfloat16).astype(jnp.float32)
        parts.append(jnp.broadcast_to(part, (8, part.shape[-1])))
        values = values - part
    stacked = jnp.concatenate(parts + [jnp.zeros_like(parts[0])], axis=0).astype(jnp.bfloat16)
    summed = jnp.dot(stacked, matrix, preferred_element_type=jnp.float32)
    return summed[0:1] + summed[8:9] + summed[16:17]


def scale_and_offset(moments, cells, width, gain, shift, matrix):
    devices = moments.shape[0]
    means = moments[:, 0, :]
    mean = group_sum(jnp.sum(means, axis=0, keepdims=True), matrix) * (1.0 / (devices * width))
    off = means - mean
    total = jnp.sum(moments[:, 1, :] + float(cells) * (off * off), axis=0, keepdims=True)
    spread = group_sum(total, matrix) * (1.0 / (cells * devices * width))
    scale = lax.rsqrt(spread + 1e-6) * gain
    return mean, scale, shift


def apply_norm(values, norm):
    mean, scale, shift = norm
    return silu((values.astype(jnp.float32) - mean) * scale + shift).astype(jnp.bfloat16)


def matrix_kernel(width, matrix_ref):
    matrix_ref[...] = group_matrix(matrix_ref.shape[0], width)


def first_kernel(x_ref, order_ref, moments_ref):
    x = x_ref[...]
    cells = x.astype(jnp.float32).reshape(-1, x.shape[-1])
    moments_ref[...] = jnp.broadcast_to(moments_of(cells)[None], moments_ref.shape)


def rows_kernel(pairs, x_ref, prev_ref, for_x_ref, for_prev_ref, *edge_refs):
    frames, rows, columns = x_ref.shape[:3]
    width = for_x_ref.shape[2]
    start = (1 - lax.axis_index("section")) * (columns - width)
    theirs = pl.ds(pl.multiple_of(start, RIM), width)
    for_x_ref[...] = x_ref[:, :, theirs, :]
    for_prev_ref[...] = prev_ref[:, :, theirs, :]
    if pairs:
        starts = [(rows - 2) * (1 - lax.axis_index("tile"))]
    else:
        starts = [0, rows - 2]
    for start, edge_ref in zip(starts, edge_refs):
        edge_ref[:frames] = prev_ref[:, pl.ds(start, 2)]
        edge_ref[frames:] = x_ref[:, pl.ds(start, 2)]


def scales_kernel(cells, moments_ref, gain_ref, shift_ref, matrix_ref, norm_ref):
    sections, half = gain_ref.shape
    per_section = moments_ref.shape[0] // sections
    for k in range(sections):
        norm = scale_and_offset(
            moments_ref[k * per_section : (k + 1) * per_section],
            cells,
            sections * half // GROUPS,
            gain_ref[k : k + 1],
            shift_ref[k : k + 1],
            matrix_ref[...],
        )
        norm_ref[k] = jnp.concatenate(norm, axis=0)


def column_taps(weight_ref, t, h):
    return jnp.concatenate([weight_ref[t, h, w] for w in range(3)], axis=-1)


def shift_and_add(total, rows, width):
    outputs = total.shape[-1] // 3
    total = total.reshape(rows, width, 3 * outputs)
    before, middle, after = (total[..., k * outputs : (k + 1) * outputs] for k in range(3))
    before = jnp.concatenate([before[:, :1], before[:, :-1]], axis=1)
    after = jnp.concatenate([after[:, 1:], after[:, -1:]], axis=1)
    return middle + before + after


def conv_in_rows(cells_of, weight_ref, frames, rows, width):
    totals = [None] * frames
    for a in range(frames + 2):
        reached = [f for f in range(frames) if 0 <= a - f <= 2]
        for h in range(3):
            cells = cells_of(a, h)
            cells = cells.reshape(rows * width, cells.shape[-1])
            taps = [column_taps(weight_ref, a - f, h) for f in reached]
            sums = jnp.dot(
                cells, jnp.concatenate(taps, axis=-1), preferred_element_type=jnp.float32
            )
            n = sums.shape[-1] // len(reached)
            for k, f in enumerate(reached):
                part = sums[:, k * n : (k + 1) * n]
                totals[f] = part if totals[f] is None else totals[f] + part
    return [shift_and_add(total, rows, width) for total in totals]


def conv_mid_rows(act_ref, weight_ref, taken, rows, width):
    cells, taps = [], []
    for t, frame in taken:
        for h in range(3):
            block = act_ref[frame, h : h + rows]
            cells.append(block.reshape(rows * width, block.shape[-1]))
            taps.append(column_taps(weight_ref, t, h))
    total = jnp.dot(
        jnp.concatenate(cells, axis=-1),
        jnp.concatenate(taps, axis=0),
        preferred_element_type=jnp.float32,
    )
    return shift_and_add(total, rows, width)


def first_row(tiles, tile):
    return 1 - tile if tiles == 2 else 0


def body_kernel(x_ref, prev_ref, other_x_ref, other_prev_ref, norm_ref, body_ref):
    section = lax.axis_index("section")
    frames, _, columns, half = x_ref.shape
    width = body_ref.shape[2]
    mine = pl.ds(pl.multiple_of(section * (columns - width), RIM), width)
    for which, first, ref, cols in (
        (section, 0, prev_ref, mine),
        (section, frames, x_ref, mine),
        (1 - section, frames, other_x_ref, slice(None)),
        (1 - section, 0, other_prev_ref, slice(None)),
    ):
        norm = tuple(norm_ref[which, k : k + 1] for k in range(3))
        lanes = pl.ds(pl.multiple_of(which * half, half), half)
        for f in range(frames):
            body_ref[first + f, :, :, lanes] = apply_norm(ref[f, :, cols, :], norm)

    @pl.when(lax.axis_index("tm") == 0)
    def _():
        for f in range(frames):
            body_ref[f] = body_ref[frames]


def inner_kernel(body_ref, weight_ref, bias_ref, inner_ref):
    frames, rows, width = inner_ref.shape[:3]
    sums = conv_in_rows(
        lambda a, h: body_ref[a, h : h + rows], weight_ref, frames, rows, width
    )
    for f, hidden in enumerate(sums):
        inner_ref[f] = (hidden + bias_ref[...]).astype(jnp.bfloat16)


def middle_kernel(tiles, sides, *refs):
    body_ref, inner_ref = refs[:2]
    rim_refs, other_rim_refs = refs[2 : 2 + sides], refs[2 + sides : 2 + 2 * sides]
    norm_ref, weight_ref, bias_ref, hidden_ref, out_moments_ref, act_ref = refs[2 + 2 * sides :]
    section, tm, tile = (lax.axis_index(axis) for axis in AXES)
    columns, half = rim_refs[0].shape[2:]
    frames, rows, width = body_ref.shape[0] // 2, body_ref.shape[1], body_ref.shape[2]
    own = columns // 2
    first = pl.multiple_of(section * (columns - width), RIM)
    cols = pl.ds(first, width)
    act_ref[:, 2:4] = body_ref[:, :2]
    act_ref[:, 4:6] = body_ref[:, rows - 2 :]
    rim_rows = (0, 6) if sides == 2 else (6 * (1 - tile),)
    for which, rims in ((section, rim_refs), (1 - section, other_rim_refs)):
        norm = tuple(norm_ref[which, k : k + 1] for k in range(3))
        lanes = pl.ds(pl.multiple_of(which * half, half), half)
        for f in range(2 * frames):
            for row, rim in zip(rim_rows, rims):
                act_ref[f, pl.ds(row, 2), :, lanes] = apply_norm(rim[f, :, cols, :], norm)

    @pl.when(tile == 0)
    def _():
        for f in range(2 * frames):
            act_ref[f, 1] = act_ref[f, 2]

    @pl.when(tile == tiles - 1)
    def _():
        for f in range(2 * frames):
            act_ref[f, 6] = act_ref[f, 5]

    @pl.when(tm == 0)
    def _():
        for f in range(frames):
            act_ref[f] = act_ref[frames]

    sums = conv_in_rows(
        lambda a, h: jnp.concatenate(
            [act_ref[a, h : h + 2], act_ref[a, 4 + h : 6 + h]], axis=0
        ),
        weight_ref,
        frames,
        4,
        width,
    )
    at = 1 - first_row(tiles, tile)
    for f, hidden in enumerate(sums):
        outer = (hidden + bias_ref[...]).astype(jnp.bfloat16)
        hidden_ref[f, pl.ds(at + 1, rows - 2)] = inner_ref[f]
        if sides == 2:
            hidden_ref[f, 0:1] = outer[0:1]
            hidden_ref[f, rows + 1 : rows + 2] = outer[3:4]
        else:
            rim = jnp.where(tile == 0, outer[3:4], outer[0:1])
            hidden_ref[f, pl.ds(rows * (1 - tile), 1)] = rim
        hidden_ref[f, pl.ds(at, 1)] = outer[1:2]
        hidden_ref[f, pl.ds(at + rows - 1, 1)] = outer[2:3]

    cells = hidden_ref[:, pl.ds(at, rows), pl.ds(first, own), :]
    cells = cells.astype(jnp.float32).reshape(-1, cells.shape[-1])
    out_moments_ref[...] = jnp.broadcast_to(moments_of(cells)[None], out_moments_ref.shape)


def pack_kernel(hidden_ref, sent_ref):
    section = lax.axis_index("section")
    frames, kept, width, channels = hidden_ref.shape
    own = sent_ref.shape[2]
    first = pl.multiple_of(section * (width - own), RIM)
    for f in range(frames):
        sent_ref[f, :kept] = hidden_ref[f, :, pl.ds(first, own), :]
        hidden = hidden_ref[f].astype(jnp.float32)
        rim = jnp.where(section == 0, hidden[:, own, :], hidden[:, width - own - 1, :])
        spare = jnp.zeros((own - kept, channels), jnp.float32)
        sent_ref[f, kept] = jnp.concatenate([rim, spare], axis=0).astype(jnp.bfloat16)


def repeat_edges(act_ref, count, tiles, rows):
    tile = lax.axis_index("tile")

    @pl.when(tile == 0)
    def _():
        for f in range(count):
            act_ref[f, 0] = act_ref[f, 1]

    @pl.when(tile == tiles - 1)
    def _():
        for f in range(count):
            act_ref[f, rows + 1] = act_ref[f, rows]


def own_columns(values, own):
    section = lax.axis_index("section")
    width = values.shape[1]
    return jnp.where(section == 0, values[:, :own], values[:, width - own :])


def shortcut_kernel(x_ref, other_x_ref, skip_ref, skip_bias_ref, bias_ref, part_ref):
    section = lax.axis_index("section")
    frames, rows, columns, half = x_ref.shape
    own = columns // 2
    mine = pl.ds(pl.multiple_of(section * own, own), own)
    within = pl.ds(pl.multiple_of(section * (other_x_ref.shape[2] - own), RIM), own)
    skip_here = skip_ref[pl.ds(pl.multiple_of(section * half, half), half), :]
    skip_there = skip_ref[pl.ds(pl.multiple_of((1 - section) * half, half), half), :]
    for f in range(frames):
        here = x_ref[f, :, mine, :].reshape(rows * own, half)
        there = other_x_ref[f, :, within, :].reshape(rows * own, half)
        shortcut = jnp.dot(here, skip_here, preferred_element_type=jnp.float32)
        shortcut = shortcut + jnp.dot(there, skip_there, preferred_element_type=jnp.float32)
        part_ref[f] = (shortcut + (skip_bias_ref[...] + bias_ref[...])).reshape(rows, own, -1)


def own_frames_kernel(
    tiles,
    hidden_ref,
    moments_ref,
    gain_ref,
    shift_ref,
    weight_ref,
    shortcut_ref,
    part_ref,
    norm_ref,
    act_ref,
):
    frames, kept, width, outputs = hidden_ref.shape
    rows, own = part_ref.shape[1:3]
    top = first_row(tiles, lax.axis_index("tile"))
    norm = scale_and_offset(
        moments_ref[...],
        frames * rows * own,
        outputs // GROUPS,
        gain_ref[...],
        shift_ref[...],
        group_matrix(outputs, outputs // GROUPS),
    )
    norm_ref[...] = jnp.concatenate(norm, axis=0)
    for f in range(frames):
        act_ref[f, pl.ds(top, kept)] = apply_norm(hidden_ref[f], norm)
    repeat_edges(act_ref, frames, tiles, rows)
    for f in range(frames):
        taken = [(k - f + 2, k) for k in range(f - 2, f + 1) if k >= 0]
        residual = own_columns(conv_mid_rows(act_ref, weight_ref, taken, rows, width), own)
        part_ref[f] = shortcut_ref[f] + residual


def last_kernel(
    tiles, hidden_ref, before_ref, norm_ref, weight_ref, part_ref, out_hbm, act_ref, out_ref, sems
):
    section, tm, tile = (lax.axis_index(axis) for axis in AXES)
    frames, kept, width, outputs = hidden_ref.shape
    rows, own = part_ref.shape[1:3]
    top = first_row(tiles, tile)
    first = pl.multiple_of(section * (width - own), RIM)
    beside = pl.multiple_of((1 - section) * own, RIM)
    norm = tuple(norm_ref[k : k + 1] for k in range(3))
    @pl.when(tm > 0)
    def _():
        for f in range(frames):
            act_ref[f, pl.ds(top, kept), pl.ds(first, own), :] = apply_norm(before_ref[f, :kept], norm)
            rim = apply_norm(before_ref[f, kept], norm).astype(jnp.float32)[:kept]
            rim = jnp.broadcast_to(rim[:, None, :], (kept, width - own, outputs))
            act_ref[f, pl.ds(top, kept), pl.ds(beside, width - own), :] = rim.astype(jnp.bfloat16)

    @pl.when(tm == 0)
    def _():
        start = apply_norm(hidden_ref[0], norm)
        for f in range(frames):
            act_ref[f, pl.ds(top, kept)] = start

    repeat_edges(act_ref, frames, tiles, rows)
    copies = []
    for f in range(frames):
        taken = [(k - f, k) for k in range(f, f + 3) if k < frames]
        residual = own_columns(conv_mid_rows(act_ref, weight_ref, taken, rows, width), own)
        out_ref[f] = (part_ref[f] + residual).astype(jnp.bfloat16)
        copies.append(pltpu.make_async_copy(out_ref.at[f], out_hbm.at[f], sems.at[f]))
        copies[-1].start()
    for copy in copies:
        copy.wait()


def pairs_for(tm_count, tile_count, tm_step, tile_step):
    out = []
    for a in range(tm_count):
        for b in range(tile_count):
            c, d = a + tm_step, b + tile_step
            if 0 <= c < tm_count and 0 <= d < tile_count:
                out.append((a * tile_count + b, c * tile_count + d))
    return out


def to_everyone(moments):
    return lax.all_to_all(moments, AXES, 0, 0, tiled=True)


def shards(
    features,
    norm_gain_in,
    norm_shift_in,
    conv_in_weight,
    conv_in_bias,
    norm_gain_mid,
    norm_shift_mid,
    conv_mid_weight,
    conv_mid_bias,
    skip_weight,
    skip_bias,
):
    sections, tms, tiles = (lax.axis_size(axis) for axis in AXES)
    parties = sections * tms * tiles
    frames, rows, columns, half = features.shape
    own = columns // sections
    width = own + RIM
    middle = conv_in_weight.shape[-1]
    outputs = conv_mid_weight.shape[-1]
    grid_axes = ("tm", "tile")

    def shift(value, tm_step, tile_step):
        return lax.ppermute(value, grid_axes, pairs_for(tms, tiles, tm_step, tile_step))

    def swap(value):
        return lax.ppermute(value, "section", [(0, 1), (1, 0)])

    previous = shift(features, 1, 0)
    matrix = pl.pallas_call(
        functools.partial(matrix_kernel, half * sections // GROUPS),
        out_shape=jax.ShapeDtypeStruct((half, half), jnp.bfloat16),
        out_specs=pl.BlockSpec(memory_space=pltpu.VMEM),
        compiler_params=params(),
        cost_estimate=cost(1_000_000_000, 1_000_000),
        name="group_matrix",
    )()
    sums = pl.pallas_call(
        first_kernel,
        out_shape=jax.ShapeDtypeStruct((parties, 2, half), jnp.float32),
        in_specs=[*vmem_specs(1), pl.BlockSpec(memory_space=pl.ANY)],
        out_specs=pl.BlockSpec(memory_space=pltpu.VMEM),
        compiler_params=params(),
        cost_estimate=cost(1_000_000_000, 1_000_000),
        name="feature_moments",
    )(features, matrix)
    moments = to_everyone(sums)
    previous, _ = lax.optimization_barrier((previous, sums))
    edges = 1 if tiles == 2 else 2
    edge = jax.ShapeDtypeStruct((2 * frames, 2, columns, half), features.dtype)
    cut = jax.ShapeDtypeStruct((frames, rows, width, half), features.dtype)
    for_x, for_previous, *edge_rows = pl.pallas_call(
        functools.partial(rows_kernel, tiles == 2),
        out_shape=(cut, cut) + (edge,) * edges,
        in_specs=vmem_specs(2),
        out_specs=tuple(vmem_specs(2 + edges)),
        compiler_params=params(),
        cost_estimate=cost(500_000_000, 1_000_000),
        name="facing_rows",
    )(features, previous)
    if tiles == 2:
        rims = [lax.ppermute(edge_rows[0], "tile", [(0, 1), (1, 0)])]
    else:
        rims = [shift(edge_rows[1], 0, 1), shift(edge_rows[0], 0, -1)]
    other = swap(for_x)
    other_previous = swap(for_previous)
    norm_in = pl.pallas_call(
        functools.partial(scales_kernel, frames * rows * columns),
        out_shape=jax.ShapeDtypeStruct((sections, 3, half), jnp.float32),
        in_specs=vmem_specs(4),
        out_specs=pl.BlockSpec(memory_space=pltpu.VMEM),
        compiler_params=params(),
        cost_estimate=cost(3_000_000_000, 1_000_000),
        name="feature_scales",
    )(moments, norm_gain_in.reshape(sections, half), norm_shift_in.reshape(sections, half), matrix)

    kept = rows + edges
    body = pl.pallas_call(
        body_kernel,
        out_shape=jax.ShapeDtypeStruct((2 * frames, rows, width, 2 * half), jnp.bfloat16),
        in_specs=vmem_specs(5),
        out_specs=pl.BlockSpec(memory_space=pltpu.VMEM),
        compiler_params=params(),
        cost_estimate=cost(1_000_000_000, 1_000_000),
        name="norm_body",
    )(features, previous, other, other_previous, norm_in)
    body, *rims = lax.optimization_barrier((body, *rims))
    other_rims = [swap(rim) for rim in rims]
    inner = pl.pallas_call(
        inner_kernel,
        out_shape=jax.ShapeDtypeStruct((frames, rows - 2, width, middle), jnp.bfloat16),
        in_specs=vmem_specs(3),
        out_specs=pl.BlockSpec(memory_space=pltpu.VMEM),
        compiler_params=params(),
        cost_estimate=cost(1_000_000_000, 1_000_000),
        name="conv_in_inner",
    )(body, conv_in_weight, conv_in_bias.reshape(1, middle))
    hidden, moments_mid = pl.pallas_call(
        functools.partial(middle_kernel, tiles, edges),
        out_shape=(
            jax.ShapeDtypeStruct((frames, kept, width, middle), jnp.bfloat16),
            jax.ShapeDtypeStruct((parties, 2, middle), jnp.float32),
        ),
        in_specs=vmem_specs(5 + 2 * edges),
        out_specs=tuple(vmem_specs(2)),
        scratch_shapes=[pltpu.VMEM((2 * frames, 8, width, 2 * half), jnp.bfloat16)],
        compiler_params=params(),
        cost_estimate=cost(4_000_000_000, 1_000_000),
        name="conv_in",
    )(
        body,
        inner,
        *rims,
        *other_rims,
        norm_in,
        conv_in_weight,
        conv_in_bias.reshape(1, middle),
    )
    moments_mid = to_everyone(moments_mid)
    sent = pl.pallas_call(
        pack_kernel,
        out_shape=jax.ShapeDtypeStruct((frames, kept + 1, own, middle), jnp.bfloat16),
        in_specs=vmem_specs(1),
        out_specs=pl.BlockSpec(memory_space=pltpu.VMEM),
        compiler_params=params(),
        cost_estimate=cost(1_000_000_000, 1_000_000),
        name="pack_hidden",
    )(hidden)
    before = shift(sent, 1, 0)
    shown, _ = lax.optimization_barrier((other, sent))
    shortcut = pl.pallas_call(
        shortcut_kernel,
        out_shape=jax.ShapeDtypeStruct((frames, rows, own, outputs), jnp.float32),
        in_specs=vmem_specs(5),
        out_specs=pl.BlockSpec(memory_space=pltpu.VMEM),
        compiler_params=params(),
        cost_estimate=cost(300_000_000, 1_000_000),
        name="shortcut",
    )(
        features,
        shown,
        skip_weight,
        skip_bias.reshape(1, outputs),
        conv_mid_bias.reshape(1, outputs),
    )
    part, norm_mid = pl.pallas_call(
        functools.partial(own_frames_kernel, tiles),
        out_shape=(
            jax.ShapeDtypeStruct((frames, rows, own, outputs), jnp.float32),
            jax.ShapeDtypeStruct((3, middle), jnp.float32),
        ),
        in_specs=vmem_specs(6),
        out_specs=tuple(vmem_specs(2)),
        scratch_shapes=[pltpu.VMEM((frames, rows + 2, width, middle), jnp.bfloat16)],
        compiler_params=params(),
        cost_estimate=cost(2_000_000_000, 1_000_000),
        name="conv_mid_own_frames",
    )(
        hidden,
        moments_mid,
        norm_gain_mid.reshape(1, middle),
        norm_shift_mid.reshape(1, middle),
        conv_mid_weight,
        shortcut,
    )
    return pl.pallas_call(
        functools.partial(last_kernel, tiles),
        out_shape=jax.ShapeDtypeStruct((frames, rows, own, outputs), jnp.bfloat16),
        in_specs=vmem_specs(5),
        out_specs=pl.BlockSpec(memory_space=pl.ANY),
        scratch_shapes=[
            pltpu.VMEM((frames, rows + 2, width, middle), jnp.bfloat16),
            pltpu.VMEM((frames, rows, own, outputs), jnp.bfloat16),
            pltpu.SemaphoreType.DMA((frames,)),
        ],
        compiler_params=params(),
        cost_estimate=cost(2_000_000_000, 1_000_000),
        name="conv_mid_previous_frames",
    )(hidden, before, norm_mid, conv_mid_weight, part)


def solution(mesh):
    in_specs = (P("tm", "tile", None, "section"),) + (P(),) * 10
    out_specs = P("tm", "tile", "section", None)
    return jax.shard_map(shards, mesh=mesh, in_specs=in_specs, out_specs=out_specs, check_vma=False)
```

```python
import functools

import jax
import jax.numpy as jnp
from jax import lax
from jax.experimental import pallas as pl
from jax.experimental.pallas import tpu as pltpu
from jax.sharding import PartitionSpec as P

GROUPS = 32
AXES = ("section", "tm", "tile")
VMEM_LIMIT = 48 * 1024 * 1024
RIM = 16


def params(limit=VMEM_LIMIT):
    return pltpu.CompilerParams(vmem_limit_bytes=limit)


def cost(flops, moved):
    return pl.CostEstimate(flops=flops, bytes_accessed=moved, transcendentals=0)


def vmem_specs(count):
    return [pl.BlockSpec(memory_space=pltpu.VMEM)] * count


def silu(u):
    half = 0.5 * u
    return half + half * jnp.tanh(half)


def moments_of(cells):
    mean = jnp.sum(cells, axis=0, keepdims=True) * (1.0 / cells.shape[0])
    off = cells - mean
    return jnp.concatenate([mean, jnp.sum(off * off, axis=0, keepdims=True)], axis=0)


def group_matrix(channels, width):
    shape = (channels, channels)
    row = lax.broadcasted_iota(jnp.int32, shape, 0) // width
    col = lax.broadcasted_iota(jnp.int32, shape, 1) // width
    return jnp.where(row == col, 1.0, 0.0).astype(jnp.bfloat16)


def group_sum(values, matrix):
    parts = []
    for _ in range(3):
        part = values.astype(jnp.bfloat16).astype(jnp.float32)
        parts.append(jnp.broadcast_to(part, (8, part.shape[-1])))
        values = values - part
    stacked = jnp.concatenate(parts + [jnp.zeros_like(parts[0])], axis=0).astype(jnp.bfloat16)
    summed = jnp.dot(stacked, matrix, preferred_element_type=jnp.float32)
    return summed[0:1] + summed[8:9] + summed[16:17]


def scale_and_offset(moments, cells, width, gain, shift, matrix):
    devices = moments.shape[0]
    means = moments[:, 0, :]
    mean = group_sum(jnp.sum(means, axis=0, keepdims=True), matrix) * (1.0 / (devices * width))
    off = means - mean
    total = jnp.sum(moments[:, 1, :] + float(cells) * (off * off), axis=0, keepdims=True)
    spread = group_sum(total, matrix) * (1.0 / (cells * devices * width))
    scale = lax.rsqrt(spread + 1e-6) * gain
    return mean, scale, shift


def apply_norm(values, norm):
    mean, scale, shift = norm
    return silu((values.astype(jnp.float32) - mean) * scale + shift).astype(jnp.bfloat16)


def matrix_kernel(widths, *matrix_refs):
    for width, matrix_ref in zip(widths, matrix_refs):
        matrix_ref[...] = group_matrix(matrix_ref.shape[0], width)


def first_kernel(x_ref, order_ref, moments_ref):
    x = x_ref[...]
    cells = x.astype(jnp.float32).reshape(-1, x.shape[-1])
    moments_ref[...] = jnp.broadcast_to(moments_of(cells)[None], moments_ref.shape)


def rows_kernel(pairs, x_ref, prev_ref, for_x_ref, for_prev_ref, *edge_refs):
    frames, rows, columns = x_ref.shape[:3]
    width = for_x_ref.shape[2]
    start = (1 - lax.axis_index("section")) * (columns - width)
    theirs = pl.ds(pl.multiple_of(start, RIM), width)
    for_x_ref[...] = x_ref[:, :, theirs, :]
    for_prev_ref[...] = prev_ref[:, :, theirs, :]
    if pairs:
        starts = [(rows - 2) * (1 - lax.axis_index("tile"))]
    else:
        starts = [0, rows - 2]
    for start, edge_ref in zip(starts, edge_refs):
        edge_ref[:frames] = prev_ref[:, pl.ds(start, 2)]
        edge_ref[frames:] = x_ref[:, pl.ds(start, 2)]


def scales_kernel(cells, moments_ref, gain_ref, shift_ref, matrix_ref, norm_ref):
    sections, half = gain_ref.shape
    per_section = moments_ref.shape[0] // sections
    for k in range(sections):
        norm = scale_and_offset(
            moments_ref[k * per_section : (k + 1) * per_section],
            cells,
            sections * half // GROUPS,
            gain_ref[k : k + 1],
            shift_ref[k : k + 1],
            matrix_ref[...],
        )
        norm_ref[k] = jnp.concatenate(norm, axis=0)


def column_taps(weight_ref, t, h):
    return jnp.concatenate([weight_ref[t, h, w] for w in range(3)], axis=-1)


def shift_and_add(total, rows, width):
    outputs = total.shape[-1] // 3
    total = total.reshape(rows, width, 3 * outputs)
    before, middle, after = (total[..., k * outputs : (k + 1) * outputs] for k in range(3))
    before = jnp.concatenate([before[:, :1], before[:, :-1]], axis=1)
    after = jnp.concatenate([after[:, 1:], after[:, -1:]], axis=1)
    return middle + before + after


def conv_in_rows(cells_of, weight_ref, frames, rows, width):
    totals = [None] * frames
    for a in range(frames + 2):
        reached = [f for f in range(frames) if 0 <= a - f <= 2]
        for h in range(3):
            cells = cells_of(a, h)
            cells = cells.reshape(rows * width, cells.shape[-1])
            taps = [column_taps(weight_ref, a - f, h) for f in reached]
            sums = jnp.dot(
                cells, jnp.concatenate(taps, axis=-1), preferred_element_type=jnp.float32
            )
            n = sums.shape[-1] // len(reached)
            for k, f in enumerate(reached):
                part = sums[:, k * n : (k + 1) * n]
                totals[f] = part if totals[f] is None else totals[f] + part
    return [shift_and_add(total, rows, width) for total in totals]


def conv_mid_rows(act_ref, weight_ref, taken, rows, width):
    cells, taps = [], []
    for t, frame in taken:
        for h in range(3):
            block = act_ref[frame, h : h + rows]
            cells.append(block.reshape(rows * width, block.shape[-1]))
            taps.append(column_taps(weight_ref, t, h))
    total = jnp.dot(
        jnp.concatenate(cells, axis=-1),
        jnp.concatenate(taps, axis=0),
        preferred_element_type=jnp.float32,
    )
    return shift_and_add(total, rows, width)


def first_row(tiles, tile):
    return 1 - tile if tiles == 2 else 0


def body_kernel(x_ref, prev_ref, other_x_ref, other_prev_ref, norm_ref, body_ref):
    section = lax.axis_index("section")
    frames, _, columns, half = x_ref.shape
    width = body_ref.shape[2]
    mine = pl.ds(pl.multiple_of(section * (columns - width), RIM), width)
    for which, first, ref, cols in (
        (section, 0, prev_ref, mine),
        (section, frames, x_ref, mine),
        (1 - section, frames, other_x_ref, slice(None)),
        (1 - section, 0, other_prev_ref, slice(None)),
    ):
        norm = tuple(norm_ref[which, k : k + 1] for k in range(3))
        lanes = pl.ds(pl.multiple_of(which * half, half), half)
        for f in range(frames):
            body_ref[first + f, :, :, lanes] = apply_norm(ref[f, :, cols, :], norm)

    @pl.when(lax.axis_index("tm") == 0)
    def _():
        for f in range(frames):
            body_ref[f] = body_ref[frames]


def inner_kernel(body_ref, weight_ref, bias_ref, inner_ref):
    frames, rows, width = inner_ref.shape[:3]
    sums = conv_in_rows(
        lambda a, h: body_ref[a, h : h + rows], weight_ref, frames, rows, width
    )
    for f, hidden in enumerate(sums):
        inner_ref[f] = (hidden + bias_ref[...]).astype(jnp.bfloat16)


def middle_kernel(tiles, sides, *refs):
    body_ref, inner_ref = refs[:2]
    rim_refs, other_rim_refs = refs[2 : 2 + sides], refs[2 + sides : 2 + 2 * sides]
    norm_ref, weight_ref, bias_ref, hidden_ref, out_moments_ref, act_ref = refs[2 + 2 * sides :]
    section, tm, tile = (lax.axis_index(axis) for axis in AXES)
    columns, half = rim_refs[0].shape[2:]
    frames, rows, width = body_ref.shape[0] // 2, body_ref.shape[1], body_ref.shape[2]
    own = columns // 2
    first = pl.multiple_of(section * (columns - width), RIM)
    cols = pl.ds(first, width)
    act_ref[:, 2:4] = body_ref[:, :2]
    act_ref[:, 4:6] = body_ref[:, rows - 2 :]
    rim_rows = (0, 6) if sides == 2 else (6 * (1 - tile),)
    for which, rims in ((section, rim_refs), (1 - section, other_rim_refs)):
        norm = tuple(norm_ref[which, k : k + 1] for k in range(3))
        lanes = pl.ds(pl.multiple_of(which * half, half), half)
        for f in range(2 * frames):
            for row, rim in zip(rim_rows, rims):
                act_ref[f, pl.ds(row, 2), :, lanes] = apply_norm(rim[f, :, cols, :], norm)

    @pl.when(tile == 0)
    def _():
        for f in range(2 * frames):
            act_ref[f, 1] = act_ref[f, 2]

    @pl.when(tile == tiles - 1)
    def _():
        for f in range(2 * frames):
            act_ref[f, 6] = act_ref[f, 5]

    @pl.when(tm == 0)
    def _():
        for f in range(frames):
            act_ref[f] = act_ref[frames]

    sums = conv_in_rows(
        lambda a, h: jnp.concatenate(
            [act_ref[a, h : h + 2], act_ref[a, 4 + h : 6 + h]], axis=0
        ),
        weight_ref,
        frames,
        4,
        width,
    )
    at = 1 - first_row(tiles, tile)
    for f, hidden in enumerate(sums):
        outer = (hidden + bias_ref[...]).astype(jnp.bfloat16)
        hidden_ref[f, pl.ds(at + 1, rows - 2)] = inner_ref[f]
        if sides == 2:
            hidden_ref[f, 0:1] = outer[0:1]
            hidden_ref[f, rows + 1 : rows + 2] = outer[3:4]
        else:
            rim = jnp.where(tile == 0, outer[3:4], outer[0:1])
            hidden_ref[f, pl.ds(rows * (1 - tile), 1)] = rim
        hidden_ref[f, pl.ds(at, 1)] = outer[1:2]
        hidden_ref[f, pl.ds(at + rows - 1, 1)] = outer[2:3]

    cells = hidden_ref[:, pl.ds(at, rows), pl.ds(first, own), :]
    cells = cells.astype(jnp.float32).reshape(-1, cells.shape[-1])
    out_moments_ref[...] = jnp.broadcast_to(moments_of(cells)[None], out_moments_ref.shape)


def pack_kernel(hidden_ref, sent_ref):
    section = lax.axis_index("section")
    frames, kept, width, channels = hidden_ref.shape
    own = sent_ref.shape[2]
    first = pl.multiple_of(section * (width - own), RIM)
    for f in range(frames):
        sent_ref[f, :kept] = hidden_ref[f, :, pl.ds(first, own), :]
        hidden = hidden_ref[f].astype(jnp.float32)
        rim = jnp.where(section == 0, hidden[:, own, :], hidden[:, width - own - 1, :])
        spare = jnp.zeros((own - kept, channels), jnp.float32)
        sent_ref[f, kept] = jnp.concatenate([rim, spare], axis=0).astype(jnp.bfloat16)


def repeat_edges(act_ref, count, tiles, rows):
    tile = lax.axis_index("tile")

    @pl.when(tile == 0)
    def _():
        for f in range(count):
            act_ref[f, 0] = act_ref[f, 1]

    @pl.when(tile == tiles - 1)
    def _():
        for f in range(count):
            act_ref[f, rows + 1] = act_ref[f, rows]


def own_columns(values, own):
    section = lax.axis_index("section")
    width = values.shape[1]
    return jnp.where(section == 0, values[:, :own], values[:, width - own :])


def shortcut_kernel(x_ref, other_x_ref, skip_ref, skip_bias_ref, bias_ref, part_ref):
    section = lax.axis_index("section")
    frames, rows, columns, half = x_ref.shape
    own = columns // 2
    mine = pl.ds(pl.multiple_of(section * own, own), own)
    within = pl.ds(pl.multiple_of(section * (other_x_ref.shape[2] - own), RIM), own)
    skip_here = skip_ref[pl.ds(pl.multiple_of(section * half, half), half), :]
    skip_there = skip_ref[pl.ds(pl.multiple_of((1 - section) * half, half), half), :]
    for f in range(frames):
        here = x_ref[f, :, mine, :].reshape(rows * own, half)
        there = other_x_ref[f, :, within, :].reshape(rows * own, half)
        shortcut = jnp.dot(here, skip_here, preferred_element_type=jnp.float32)
        shortcut = shortcut + jnp.dot(there, skip_there, preferred_element_type=jnp.float32)
        part_ref[f] = (shortcut + (skip_bias_ref[...] + bias_ref[...])).reshape(rows, own, -1)


def own_frames_kernel(
    tiles,
    hidden_ref,
    moments_ref,
    gain_ref,
    shift_ref,
    weight_ref,
    shortcut_ref,
    matrix_ref,
    part_ref,
    norm_ref,
    act_ref,
):
    frames, kept, width, outputs = hidden_ref.shape
    rows, own = part_ref.shape[1:3]
    top = first_row(tiles, lax.axis_index("tile"))
    norm = scale_and_offset(
        moments_ref[...],
        frames * rows * own,
        outputs // GROUPS,
        gain_ref[...],
        shift_ref[...],
        matrix_ref[...],
    )
    norm_ref[...] = jnp.concatenate(norm, axis=0)
    for f in range(frames):
        act_ref[f, pl.ds(top, kept)] = apply_norm(hidden_ref[f], norm)
    repeat_edges(act_ref, frames, tiles, rows)
    for f in range(frames):
        taken = [(k - f + 2, k) for k in range(f - 2, f + 1) if k >= 0]
        residual = own_columns(conv_mid_rows(act_ref, weight_ref, taken, rows, width), own)
        part_ref[f] = shortcut_ref[f] + residual


def last_kernel(
    tiles, hidden_ref, before_ref, norm_ref, weight_ref, part_ref, out_hbm, act_ref, out_ref, sems
):
    section, tm, tile = (lax.axis_index(axis) for axis in AXES)
    frames, kept, width, outputs = hidden_ref.shape
    rows, own = part_ref.shape[1:3]
    top = first_row(tiles, tile)
    first = pl.multiple_of(section * (width - own), RIM)
    beside = pl.multiple_of((1 - section) * own, RIM)
    norm = tuple(norm_ref[k : k + 1] for k in range(3))
    @pl.when(tm > 0)
    def _():
        for f in range(frames):
            act_ref[f, pl.ds(top, kept), pl.ds(first, own), :] = apply_norm(before_ref[f, :kept], norm)
            rim = apply_norm(before_ref[f, kept], norm).astype(jnp.float32)[:kept]
            rim = jnp.broadcast_to(rim[:, None, :], (kept, width - own, outputs))
            act_ref[f, pl.ds(top, kept), pl.ds(beside, width - own), :] = rim.astype(jnp.bfloat16)

    @pl.when(tm == 0)
    def _():
        start = apply_norm(hidden_ref[0], norm)
        for f in range(frames):
            act_ref[f, pl.ds(top, kept)] = start

    repeat_edges(act_ref, frames, tiles, rows)
    copies = []
    for f in range(frames):
        taken = [(k - f, k) for k in range(f, f + 3) if k < frames]
        residual = own_columns(conv_mid_rows(act_ref, weight_ref, taken, rows, width), own)
        out_ref[f] = (part_ref[f] + residual).astype(jnp.bfloat16)
        copies.append(pltpu.make_async_copy(out_ref.at[f], out_hbm.at[f], sems.at[f]))
        copies[-1].start()
    for copy in copies:
        copy.wait()


def pairs_for(tm_count, tile_count, tm_step, tile_step):
    out = []
    for a in range(tm_count):
        for b in range(tile_count):
            c, d = a + tm_step, b + tile_step
            if 0 <= c < tm_count and 0 <= d < tile_count:
                out.append((a * tile_count + b, c * tile_count + d))
    return out


def to_everyone(moments):
    return lax.all_to_all(moments, AXES, 0, 0, tiled=True)


def shards(
    features,
    norm_gain_in,
    norm_shift_in,
    conv_in_weight,
    conv_in_bias,
    norm_gain_mid,
    norm_shift_mid,
    conv_mid_weight,
    conv_mid_bias,
    skip_weight,
    skip_bias,
):
    sections, tms, tiles = (lax.axis_size(axis) for axis in AXES)
    parties = sections * tms * tiles
    frames, rows, columns, half = features.shape
    own = columns // sections
    width = own + RIM
    middle = conv_in_weight.shape[-1]
    outputs = conv_mid_weight.shape[-1]
    grid_axes = ("tm", "tile")

    def shift(value, tm_step, tile_step):
        return lax.ppermute(value, grid_axes, pairs_for(tms, tiles, tm_step, tile_step))

    def swap(value):
        return lax.ppermute(value, "section", [(0, 1), (1, 0)])

    previous = shift(features, 1, 0)
    matrix, matrix_mid = pl.pallas_call(
        functools.partial(matrix_kernel, (half * sections // GROUPS, middle // GROUPS)),
        out_shape=(
            jax.ShapeDtypeStruct((half, half), jnp.bfloat16),
            jax.ShapeDtypeStruct((middle, middle), jnp.bfloat16),
        ),
        out_specs=tuple(vmem_specs(2)),
        compiler_params=params(),
        cost_estimate=cost(1_000_000_000, 1_000_000),
        name="group_matrix",
    )()
    sums = pl.pallas_call(
        first_kernel,
        out_shape=jax.ShapeDtypeStruct((parties, 2, half), jnp.float32),
        in_specs=[*vmem_specs(1), pl.BlockSpec(memory_space=pl.ANY)],
        out_specs=pl.BlockSpec(memory_space=pltpu.VMEM),
        compiler_params=params(),
        cost_estimate=cost(1_000_000_000, 1_000_000),
        name="feature_moments",
    )(features, matrix)
    moments = to_everyone(sums)
    previous, _ = lax.optimization_barrier((previous, sums))
    edges = 1 if tiles == 2 else 2
    edge = jax.ShapeDtypeStruct((2 * frames, 2, columns, half), features.dtype)
    cut = jax.ShapeDtypeStruct((frames, rows, width, half), features.dtype)
    for_x, for_previous, *edge_rows = pl.pallas_call(
        functools.partial(rows_kernel, tiles == 2),
        out_shape=(cut, cut) + (edge,) * edges,
        in_specs=vmem_specs(2),
        out_specs=tuple(vmem_specs(2 + edges)),
        compiler_params=params(),
        cost_estimate=cost(500_000_000, 1_000_000),
        name="facing_rows",
    )(features, previous)
    if tiles == 2:
        rims = [lax.ppermute(edge_rows[0], "tile", [(0, 1), (1, 0)])]
    else:
        rims = [shift(edge_rows[1], 0, 1), shift(edge_rows[0], 0, -1)]
    other = swap(for_x)
    other_previous = swap(for_previous)
    norm_in = pl.pallas_call(
        functools.partial(scales_kernel, frames * rows * columns),
        out_shape=jax.ShapeDtypeStruct((sections, 3, half), jnp.float32),
        in_specs=vmem_specs(4),
        out_specs=pl.BlockSpec(memory_space=pltpu.VMEM),
        compiler_params=params(),
        cost_estimate=cost(3_000_000_000, 1_000_000),
        name="feature_scales",
    )(moments, norm_gain_in.reshape(sections, half), norm_shift_in.reshape(sections, half), matrix)

    kept = rows + edges
    body = pl.pallas_call(
        body_kernel,
        out_shape=jax.ShapeDtypeStruct((2 * frames, rows, width, 2 * half), jnp.bfloat16),
        in_specs=vmem_specs(5),
        out_specs=pl.BlockSpec(memory_space=pltpu.VMEM),
        compiler_params=params(),
        cost_estimate=cost(1_000_000_000, 1_000_000),
        name="norm_body",
    )(features, previous, other, other_previous, norm_in)
    body, *rims = lax.optimization_barrier((body, *rims))
    other_rims = [swap(rim) for rim in rims]
    inner = pl.pallas_call(
        inner_kernel,
        out_shape=jax.ShapeDtypeStruct((frames, rows - 2, width, middle), jnp.bfloat16),
        in_specs=vmem_specs(3),
        out_specs=pl.BlockSpec(memory_space=pltpu.VMEM),
        compiler_params=params(),
        cost_estimate=cost(1_000_000_000, 1_000_000),
        name="conv_in_inner",
    )(body, conv_in_weight, conv_in_bias.reshape(1, middle))
    hidden, moments_mid = pl.pallas_call(
        functools.partial(middle_kernel, tiles, edges),
        out_shape=(
            jax.ShapeDtypeStruct((frames, kept, width, middle), jnp.bfloat16),
            jax.ShapeDtypeStruct((parties, 2, middle), jnp.float32),
        ),
        in_specs=vmem_specs(5 + 2 * edges),
        out_specs=tuple(vmem_specs(2)),
        scratch_shapes=[pltpu.VMEM((2 * frames, 8, width, 2 * half), jnp.bfloat16)],
        compiler_params=params(),
        cost_estimate=cost(4_000_000_000, 1_000_000),
        name="conv_in",
    )(
        body,
        inner,
        *rims,
        *other_rims,
        norm_in,
        conv_in_weight,
        conv_in_bias.reshape(1, middle),
    )
    moments_mid = to_everyone(moments_mid)
    sent = pl.pallas_call(
        pack_kernel,
        out_shape=jax.ShapeDtypeStruct((frames, kept + 1, own, middle), jnp.bfloat16),
        in_specs=vmem_specs(1),
        out_specs=pl.BlockSpec(memory_space=pltpu.VMEM),
        compiler_params=params(),
        cost_estimate=cost(1_000_000_000, 1_000_000),
        name="pack_hidden",
    )(hidden)
    before = shift(sent, 1, 0)
    shown, _ = lax.optimization_barrier((other, sent))
    shortcut = pl.pallas_call(
        shortcut_kernel,
        out_shape=jax.ShapeDtypeStruct((frames, rows, own, outputs), jnp.float32),
        in_specs=vmem_specs(5),
        out_specs=pl.BlockSpec(memory_space=pltpu.VMEM),
        compiler_params=params(),
        cost_estimate=cost(300_000_000, 1_000_000),
        name="shortcut",
    )(
        features,
        shown,
        skip_weight,
        skip_bias.reshape(1, outputs),
        conv_mid_bias.reshape(1, outputs),
    )
    part, norm_mid = pl.pallas_call(
        functools.partial(own_frames_kernel, tiles),
        out_shape=(
            jax.ShapeDtypeStruct((frames, rows, own, outputs), jnp.float32),
            jax.ShapeDtypeStruct((3, middle), jnp.float32),
        ),
        in_specs=vmem_specs(7),
        out_specs=tuple(vmem_specs(2)),
        scratch_shapes=[pltpu.VMEM((frames, rows + 2, width, middle), jnp.bfloat16)],
        compiler_params=params(),
        cost_estimate=cost(2_000_000_000, 1_000_000),
        name="conv_mid_own_frames",
    )(
        hidden,
        moments_mid,
        norm_gain_mid.reshape(1, middle),
        norm_shift_mid.reshape(1, middle),
        conv_mid_weight,
        shortcut,
        matrix_mid,
    )
    return pl.pallas_call(
        functools.partial(last_kernel, tiles),
        out_shape=jax.ShapeDtypeStruct((frames, rows, own, outputs), jnp.bfloat16),
        in_specs=vmem_specs(5),
        out_specs=pl.BlockSpec(memory_space=pl.ANY),
        scratch_shapes=[
            pltpu.VMEM((frames, rows + 2, width, middle), jnp.bfloat16),
            pltpu.VMEM((frames, rows, own, outputs), jnp.bfloat16),
            pltpu.SemaphoreType.DMA((frames,)),
        ],
        compiler_params=params(),
        cost_estimate=cost(2_000_000_000, 1_000_000),
        name="conv_mid_previous_frames",
    )(hidden, before, norm_mid, conv_mid_weight, part)


def solution(mesh):
    in_specs = (P("tm", "tile", None, "section"),) + (P(),) * 10
    out_specs = P("tm", "tile", "section", None)
    return jax.shard_map(shards, mesh=mesh, in_specs=in_specs, out_specs=out_specs, check_vma=False)
```
